32 devices in a mesh: runs: 2 (over y), sec: 8 (over z, x), env: 2 (over core).
Axes of the slice: x: 2, y: 2, z: 4, core: 2. Of those that a mesh axis runs over, the one named last changes fastest.
Arguments:
- amplitudes: bfloat16 [16, 128, 1024], P(('runs', 'sec'), None, 'env'), parts along dimension 0, may hold values from -6 to 6
- widths: int32 [16], P('runs'), parts along dimension 0, may hold values from 1 to 1024, 4096 in all
- holders: int32 [16], P('runs'), parts along dimension 0, may hold values from 0 to 7, each once
- left_env: bfloat16 [16, 3, 1024, 1024], P(('runs', 'sec'), None, None, 'env'), parts along dimension 0, may hold values from -1 to 4
- right_env: bfloat16 [6, 128, 128], P('runs'), parts along dimension 0, may hold values from -1 to 2
Outputs:
- first_product: bfloat16 [16, 128, 1024], P(('runs', 'sec'), None, 'env'), parts along dimension 0
- second_product: bfloat16 [16, 128, 1024], P(('runs', 'sec'), None, 'env'), parts along dimension 0
The draws below stay inside these ranges and needn't reach their ends.
There are 2 independent parts, one for each index of `runs`. The reference program is written for one: setup_inputs(seed, part) draws one part's arguments, and reference() takes and returns one part's arrays. A program takes and returns all parts, laid end to end along the dimension named above; each array names one. Nothing has to cross between parts.
Inputs may be any that keep to these rules, and one draw needn't show every extreme that they name: `holders`: each sector of 0 to 7 is held by exactly one slot; sector p has up charge p // 4 and down charge p % 4. The widths sum to 4096; the largest is exactly 1024.
All inputs are finite; a program needn't handle non-finite values.
Results may differ from the reference program's by a relative error of at most 0.0058.
Values may be sent and summed in bfloat16 or wider, within the bound.
No kernel may reach another device: no remote copies, remote signals or barrier semaphores. Data moves between devices by JAX's collectives and lax.ppermute only.
A program may use at most 64 MiB of HBM per device.

```python
import math
import jax
import jax.numpy as jnp
import numpy as np
from jax import lax

SW = 1024
CR = 128
TERMS = 3
QDOWN = 4
NSEC = 8
BOND = 4096


def draw_amplitudes(key, part):
    key = jax.random.fold_in(key, 11)
    shared_key, noise_key = jax.random.split(key)
    slope = 0.5 + jnp.arange(NSEC, dtype=jnp.float32)[:, None, None] / NSEC
    shared = jax.random.truncated_normal(shared_key, -4.0, 4.0, (1, CR, SW), jnp.float32)
    noise = jax.random.truncated_normal(noise_key, -4.0, 4.0, (NSEC, CR, SW), jnp.float32)
    mixed = 0.45 * shared + 0.45 * noise + 0.3
    return (mixed * slope).astype(jnp.bfloat16)


def draw_left_env(key, part):
    key = jax.random.fold_in(key, 23)
    noise_key, level_key, base_key = jax.random.split(key, 3)
    dims = (NSEC, TERMS, SW, SW)
    noise = jax.random.truncated_normal(noise_key, -3.0, 3.0, dims, jnp.float32)
    base = jax.random.uniform(base_key, (), jnp.float32, 0.5, 2.5)
    spread = jax.random.uniform(level_key, (NSEC, TERMS, SW, 1), jnp.float32, 0.0, 1.0)
    term_index = lax.broadcasted_iota(jnp.int32, (1, TERMS, 1, 1), 1)
    levels = jnp.where(term_index == 0, base + spread, 0.5 + spread)
    row_index = lax.broadcasted_iota(jnp.int32, (1, 1, SW, SW), 2)
    col_index = lax.broadcasted_iota(jnp.int32, (1, 1, SW, SW), 3)
    diagonal = jnp.where(row_index == col_index, levels, 2.0 / SW)
    return (noise * SW ** (-0.5) + diagonal).astype(jnp.bfloat16)


def draw_right_env(key, part):
    key = jax.random.fold_in(key, 37)
    noise_key, level_key = jax.random.split(key)
    dims = (TERMS, CR, CR)
    noise = jax.random.truncated_normal(noise_key, -4.0, 4.0, dims, jnp.float32)
    levels = jax.random.uniform(level_key, (TERMS, CR, 1), jnp.float32, 0.5, 1.5)
    row_index = lax.broadcasted_iota(jnp.int32, dims, 1)
    col_index = lax.broadcasted_iota(jnp.int32, dims, 2)
    diagonal = jnp.where(row_index == col_index, levels, 1.0 / CR)
    return (noise * CR ** (-0.5) + diagonal).astype(jnp.bfloat16)


def split_up(amount, total, bound, skew):
    weights = [(1 << 20) // math.isqrt(grade ** skew) + 1 for grade in range(2, amount + 1)]
    surplus, given = total - bound - (amount - 1), [1] * (amount - 1)
    while surplus > 0:
        free = [i for i in range(amount - 1) if given[i] < bound]
        pool, left = sum([weights[i] for i in free]), surplus
        for i in free:
            more = min(bound - given[i], max(1, left * weights[i] // pool), surplus)
            given[i] = given[i] + more
            surplus = surplus - more
    return np.array([bound] + given)


def ragged_sizes(stream_key, amount, total, limit, skew):
    if amount == 2:
        one = jax.random.randint(stream_key, (), max(1, total - limit), min(limit, total - 1) + 1)
        return jnp.stack([one, total - one])
    lengths = jnp.asarray(split_up(amount, total, limit, skew), jnp.int32)
    couples = (amount - 1) // 2
    donor, sink = lengths[1:1 + 2 * couples:2], lengths[2:2 + 2 * couples:2]
    margin = jnp.minimum(donor - 1, limit - sink)
    moved = jax.random.randint(jax.random.fold_in(stream_key, 1), (couples,), 0, 1 << 20) % (margin + 1)
    lengths = lengths.at[1:1 + 2 * couples:2].set(donor - moved).at[2:2 + 2 * couples:2].set(sink + moved)
    return lengths[jax.random.permutation(jax.random.fold_in(stream_key, 2), amount)]


def setup_inputs(seed: int = 0, part: int = 0) -> dict:
    arg_keys = jax.random.split(jax.random.key(seed), 6)
    part_keys = jax.random.split(jax.random.fold_in(arg_keys[5], part), 6)
    return {
        "amplitudes": draw_amplitudes(jax.random.fold_in(jax.random.fold_in(arg_keys[5], part), 71), part),
        "widths": ragged_sizes(part_keys[1], NSEC, BOND, SW, 2).astype(jnp.int32),
        "holders": jax.random.permutation(part_keys[2], NSEC).astype(jnp.int32),
        "left_env": draw_left_env(jax.random.fold_in(jax.random.fold_in(arg_keys[5], part), 71), part),
        "right_env": draw_right_env(jax.random.fold_in(jax.random.fold_in(arg_keys[5], part), 71), part),
    }


term_shifts = ((0, 0), (1, 0), (0, 1))

def routes(holders):
    slot_of = jnp.zeros((NSEC,), jnp.int32).at[holders].set(jnp.arange(NSEC, dtype=jnp.int32))
    sources = []
    allowed = []
    for shifted in term_shifts:
        up_charge = holders // QDOWN - shifted[0]
        down_charge = holders % QDOWN - shifted[1]
        permitted = (up_charge >= 0) & (up_charge < NSEC // QDOWN) & (down_charge >= 0) & (down_charge < QDOWN)
        wanted = jnp.clip(holders - QDOWN * shifted[0] - shifted[1], 0, NSEC - 1).astype(jnp.int32)
        sources.append(slot_of[wanted])
        allowed.append(permitted.astype(jnp.float32))
    return (jnp.stack(sources), jnp.stack(allowed))

def hamiltonian_product(vector, live_mask, source, allowed, left_env, right_env):
    right_f = right_env.astype(jnp.float32)

    def one_slot(slot_data):
        amps_slot, env_slot = slot_data
        products = jnp.einsum('tij,jw->tiw', right_f, amps_slot.astype(jnp.float32)).astype(jnp.bfloat16)
        return jnp.einsum('tiw,twv->tiv', products.astype(jnp.float32), env_slot.astype(jnp.float32)).astype(jnp.bfloat16)
    outgoing = lax.map(one_slot, (vector, left_env))
    running = jnp.zeros(vector.shape, jnp.float32)
    for term in range(TERMS):
        running = running + allowed[term][:, None, None] * outgoing[source[term], term].astype(jnp.float32)
    return (running * live_mask).astype(jnp.bfloat16)

def reference(amplitudes, widths, holders, left_env, right_env):
    sector_widths = widths[holders]
    live_mask = (jnp.arange(SW, dtype=jnp.int32)[None, None, :] < sector_widths[:, None, None]).astype(jnp.float32)
    source, allowed = routes(holders)
    start_vector = jnp.where(live_mask > 0, amplitudes, jnp.zeros_like(amplitudes))
    first_product = hamiltonian_product(start_vector, live_mask, source, allowed, left_env, right_env)
    basis_f = start_vector.astype(jnp.float32)
    first_f = first_product.astype(jnp.float32)
    quotient = jnp.sum(basis_f * first_f) / jnp.sum(basis_f * basis_f)
    residual = first_f - quotient * basis_f
    live_count = CR * jnp.sum(widths).astype(jnp.float32)
    probe_vector = (residual * lax.rsqrt(jnp.sum(residual * residual) / live_count + 1e-06)).astype(jnp.bfloat16)
    second_product = hamiltonian_product(probe_vector, live_mask, source, allowed, left_env, right_env)
    return (first_product, second_product)
```

```python
import jax
import jax.numpy as jnp
from jax import lax
from jax.sharding import PartitionSpec as P

QDOWN = 4

term_shifts = ((0, 0), (1, 0), (0, 1))


def route(holders):
    n_slots = holders.shape[0]
    sector_ids = jnp.arange(n_slots, dtype=jnp.int32)
    slot_of = jnp.argmax(holders[None, :] == sector_ids[:, None], axis=1)
    sources = []
    allowed = []
    for up, down in term_shifts[1:]:
        permitted = (holders // QDOWN - up >= 0) & (holders % QDOWN - down >= 0)
        wanted = jnp.clip(holders - QDOWN * up - down, 0, n_slots - 1)
        sources.append(slot_of[wanted])
        allowed.append(permitted)
    return sources, allowed


def contract(vector, left_env, right_env):
    products = jnp.einsum(
        "tij,jw->tiw", right_env, vector, preferred_element_type=jnp.float32
    ).astype(jnp.bfloat16)
    return jnp.einsum("tik,tkw->tiw", products, left_env, preferred_element_type=jnp.float32)


def spread(blocks, n_slots):
    terms, rows, width = blocks.shape
    pieces = blocks.reshape(terms, n_slots, rows // n_slots, width).swapaxes(0, 1)
    return lax.all_to_all(pieces, "sec", split_axis=0, concat_axis=0)


def collect(merged):
    n_slots, rows, width = merged.shape
    home = lax.all_to_all(merged, "sec", split_axis=0, concat_axis=0)
    return home.reshape(n_slots * rows, width)


def share(values, n_slots, me):
    lanes = jnp.zeros((1, 128), jnp.float32).at[0, : values.shape[0]].set(values)
    if n_slots & (n_slots - 1) or n_slots > 16:
        return lax.all_gather(lanes[0], "sec")
    table = jnp.where(jnp.arange(n_slots)[:, None] == me, lanes, 0.0)
    for offset in range(1, n_slots):
        pairs = [(i, i ^ offset) for i in range(n_slots)]
        other = lax.ppermute(lanes, "sec", pairs)
        table = jnp.where(jnp.arange(n_slots)[:, None] == (me ^ offset), other, table)
    return table


def merge(received, sources, allowed):
    total = 0.0
    for term, (source, permitted) in enumerate(zip(sources, allowed)):
        picked = received[source, term]
        total = total + jnp.where(permitted[:, None, None], picked, 0).astype(jnp.float32)
    return total


def on_device(amplitudes, widths, holders, left_env, right_env):
    slots_dev, right_dim, half_width = amplitudes.shape
    assert slots_dev == 1
    n_slots = holders.shape[0]
    me = lax.axis_index("sec")
    side = lax.axis_index("env")
    my_width = widths[holders[me]]
    row_index = side * half_width + jnp.arange(half_width, dtype=jnp.int32)
    live = (row_index < my_width)[None, :]
    sources, allowed = route(holders)
    envs = left_env[0]

    start = jnp.where(live, amplitudes[0], jnp.zeros_like(amplitudes[0]))
    start_full = lax.all_gather(start, "env", axis=1, tiled=True)
    outgoing = contract(start_full, envs, right_env).astype(jnp.bfloat16)
    stay = outgoing[0].astype(jnp.float32)
    received = spread(outgoing[1:], n_slots)
    arrived = collect(merge(received, sources, allowed).astype(jnp.bfloat16))
    first = jnp.where(live, stay + arrived.astype(jnp.float32), 0.0).astype(jnp.bfloat16)

    first_full = lax.all_gather(first, "env", axis=1, tiled=True).astype(jnp.float32)
    basis = start_full.astype(jnp.float32)
    overlap = jnp.sum(basis * first_full)
    norm = jnp.sum(basis * basis)
    own_quotient = jnp.where(norm > 0, overlap / jnp.where(norm > 0, norm, 1.0), 0.0)
    deflated = first_full - own_quotient * basis
    rest = jnp.sum(deflated * deflated)
    sums = share(jnp.stack([overlap, norm, own_quotient, rest]), n_slots, me)
    outgoing_2 = contract(deflated.astype(jnp.bfloat16), envs, right_env)
    received_2 = spread(outgoing_2[1:].astype(jnp.bfloat16), n_slots)

    quotient = jnp.sum(sums[:, 0]) / jnp.sum(sums[:, 1])
    shift = sums[:, 2] - quotient
    resid_norm = jnp.sum(sums[:, 3] + shift * shift * sums[:, 1])
    live_count = right_dim * jnp.sum(widths).astype(jnp.float32)
    scale = lax.rsqrt(resid_norm / live_count + 1e-06)
    mixed = received_2.astype(jnp.float32) + shift[:, None, None, None] * received.astype(
        jnp.float32
    )
    merged_2 = scale * merge(mixed, sources, allowed)
    arrived_2 = collect(merged_2.astype(jnp.bfloat16))
    stay_2 = scale * (outgoing_2[0] + (own_quotient - quotient) * stay)
    second = jnp.where(live, stay_2 + arrived_2.astype(jnp.float32), 0.0).astype(jnp.bfloat16)
    return first[None], second[None]


def solution(mesh):
    in_specs = (
        P(("runs", "sec"), None, "env"),
        P("runs"),
        P("runs"),
        P(("runs", "sec"), None, None, "env"),
        P("runs", None, None),
    )
    out_specs = (P(("runs", "sec"), None, "env"), P(("runs", "sec"), None, "env"))
    return jax.shard_map(
        on_device, mesh=mesh, in_specs=in_specs, out_specs=out_specs, check_vma=False
    )
```

```python
import jax
import jax.numpy as jnp
from jax import lax
from jax.experimental import pallas as pl
from jax.experimental.pallas import tpu as pltpu
from jax.sharding import PartitionSpec as P

QDOWN = 4

term_shifts = ((0, 0), (1, 0), (0, 1))


def route(holders):
    n_slots = holders.shape[0]
    sector_ids = jnp.arange(n_slots, dtype=jnp.int32)
    slot_of = jnp.argmax(holders[None, :] == sector_ids[:, None], axis=1)
    sources = []
    allowed = []
    for up, down in term_shifts[1:]:
        permitted = (holders // QDOWN - up >= 0) & (holders % QDOWN - down >= 0)
        wanted = jnp.clip(holders - QDOWN * up - down, 0, n_slots - 1)
        sources.append(slot_of[wanted])
        allowed.append(permitted)
    return sources, allowed


def contract(vector, left_env, right_env):
    products = jnp.einsum(
        "tij,jw->tiw", right_env, vector, preferred_element_type=jnp.float32
    ).astype(jnp.bfloat16)
    return jnp.einsum("tik,tkw->tiw", products, left_env, preferred_element_type=jnp.float32)


def spread(blocks, n_slots):
    terms, rows, width = blocks.shape
    pieces = blocks.reshape(terms, n_slots, rows // n_slots, width).swapaxes(0, 1)
    return lax.all_to_all(pieces, "sec", split_axis=0, concat_axis=0)


def collect(merged):
    n_slots, rows, width = merged.shape
    home = lax.all_to_all(merged, "sec", split_axis=0, concat_axis=0)
    return home.reshape(n_slots * rows, width)


def share(values, n_slots, me):
    lanes = jnp.zeros((1, 128), jnp.float32).at[0, : values.shape[0]].set(values)
    if n_slots & (n_slots - 1) or n_slots > 16:
        return lax.all_gather(lanes[0], "sec")
    table = jnp.where(jnp.arange(n_slots)[:, None] == me, lanes, 0.0)
    for offset in range(1, n_slots):
        pairs = [(i, i ^ offset) for i in range(n_slots)]
        other = lax.ppermute(lanes, "sec", pairs)
        table = jnp.where(jnp.arange(n_slots)[:, None] == (me ^ offset), other, table)
    return table


def merge(received, sources, allowed):
    total = 0.0
    for term, (source, permitted) in enumerate(zip(sources, allowed)):
        picked = received[source, term]
        total = total + jnp.where(permitted[:, None, None], picked, 0).astype(jnp.float32)
    return total


def on_device_any(amplitudes, widths, holders, left_env, right_env):
    slots_dev, right_dim, half_width = amplitudes.shape
    assert slots_dev == 1
    n_slots = holders.shape[0]
    me = lax.axis_index("sec")
    side = lax.axis_index("env")
    my_width = widths[holders[me]]
    row_index = side * half_width + jnp.arange(half_width, dtype=jnp.int32)
    live = (row_index < my_width)[None, :]
    sources, allowed = route(holders)
    envs = left_env[0]

    start = jnp.where(live, amplitudes[0], jnp.zeros_like(amplitudes[0]))
    start_full = lax.all_gather(start, "env", axis=1, tiled=True)
    outgoing = contract(start_full, envs, right_env).astype(jnp.bfloat16)
    stay = outgoing[0].astype(jnp.float32)
    received = spread(outgoing[1:], n_slots)
    arrived = collect(merge(received, sources, allowed).astype(jnp.bfloat16))
    first = jnp.where(live, stay + arrived.astype(jnp.float32), 0.0).astype(jnp.bfloat16)

    first_full = lax.all_gather(first, "env", axis=1, tiled=True).astype(jnp.float32)
    basis = start_full.astype(jnp.float32)
    overlap = jnp.sum(basis * first_full)
    norm = jnp.sum(basis * basis)
    own_quotient = jnp.where(norm > 0, overlap / jnp.where(norm > 0, norm, 1.0), 0.0)
    deflated = first_full - own_quotient * basis
    rest = jnp.sum(deflated * deflated)
    sums = share(jnp.stack([overlap, norm, own_quotient, rest]), n_slots, me)
    outgoing_2 = contract(deflated.astype(jnp.bfloat16), envs, right_env)
    received_2 = spread(outgoing_2[1:].astype(jnp.bfloat16), n_slots)

    quotient = jnp.sum(sums[:, 0]) / jnp.sum(sums[:, 1])
    shift = sums[:, 2] - quotient
    resid_norm = jnp.sum(sums[:, 3] + shift * shift * sums[:, 1])
    live_count = right_dim * jnp.sum(widths).astype(jnp.float32)
    scale = lax.rsqrt(resid_norm / live_count + 1e-06)
    mixed = received_2.astype(jnp.float32) + shift[:, None, None, None] * received.astype(
        jnp.float32
    )
    merged_2 = scale * merge(mixed, sources, allowed)
    arrived_2 = collect(merged_2.astype(jnp.bfloat16))
    stay_2 = scale * (outgoing_2[0] + (own_quotient - quotient) * stay)
    second = jnp.where(live, stay_2 + arrived_2.astype(jnp.float32), 0.0).astype(jnp.bfloat16)
    return first[None], second[None]


LANES = 128
TAG = 16


def find_slot(holders, sector):
    slot = jnp.int32(0)
    for s in range(holders.shape[0]):
        slot = slot + jnp.where(holders[s] == sector, s, 0)
    return slot


def live_columns(widths, holders, half, side):
    width = widths[holders[lax.axis_index("sec")]]
    columns = side * half + lax.broadcasted_iota(jnp.int32, (1, half), 1)
    return columns < width


def start_copies(left, left_vmem, sems):
    copies = []
    for term in (1, 2, 0):
        copy = pltpu.make_async_copy(left.at[0, term], left_vmem.at[term], sems.at[term])
        copy.start()
        copies.append((term, copy))
    return copies


def apply_term(right, left_vmem, vector, term):
    products = jnp.dot(right[term], vector, preferred_element_type=jnp.float32)
    return jnp.dot(
        products.astype(jnp.bfloat16), left_vmem[term], preferred_element_type=jnp.float32
    )


def store_chunks(message, first_row, block):
    rows = block.shape[0]
    for chunk in range(block.shape[1] // LANES):
        piece = block[:, chunk * LANES : (chunk + 1) * LANES]
        message[pl.ds(first_row + chunk * rows, rows), :] = piece


def load_chunks(message, first_row, rows):
    chunks = (message.shape[0] - first_row) // rows
    pieces = [message[pl.ds(first_row + c * rows, rows), :] for c in range(chunks)]
    return jnp.concatenate(pieces, axis=1)


def first_kernel(
    widths, holders, amps, right, left, message_1, message_2, stay, route, left_vmem, sems
):
    half = amps.shape[2]
    copies = start_copies(left, left_vmem, sems)
    me = lax.axis_index("sec")
    side = lax.axis_index("env")
    sector = holders[me]
    down = sector % QDOWN

    def needed(target):
        return widths[target] > side * half

    turn_1 = me ^ find_slot(holders, sector ^ QDOWN)
    turn_2 = me ^ find_slot(holders, sector ^ 1)
    turn_3 = me ^ find_slot(holders, sector ^ 3)
    route[0] = turn_1
    route[1] = turn_2
    route[2] = turn_3
    route[3] = jnp.where(needed(sector | QDOWN), turn_1, 0)
    route[4] = jnp.where(needed(sector | 1), turn_2, 0)
    inner = (down == 1) | (down == 2)
    route[5] = jnp.where(inner & needed(sector - down + 2), turn_3, 0)

    vector = jnp.concatenate(
        [
            jnp.where(live_columns(widths, holders, half, h), amps[h], jnp.zeros_like(amps[h]))
            for h in range(2)
        ],
        axis=1,
    )
    for term, copy in copies:
        copy.wait()
        block = apply_term(right, left_vmem, vector, term).astype(jnp.bfloat16)
        if term == 0:
            stay[...] = block
        else:
            store_chunks((message_1, message_2)[term - 1], 0, block)


def incoming(holders, arrived_1, arrived_2, arrived_3, first_row, rows):
    sector = holders[lax.axis_index("sec")]
    down = sector % QDOWN
    block_1 = load_chunks(arrived_1, first_row, rows).astype(jnp.float32)
    block_2 = load_chunks(arrived_2, first_row, rows).astype(jnp.float32)
    block_3 = load_chunks(arrived_3, first_row, rows).astype(jnp.float32)
    has_1 = sector >= QDOWN
    block_1 = jnp.where(has_1, block_1, 0.0)
    block_2 = jnp.where(down % 2 == 1, block_2, jnp.where(down == 2, block_3, 0.0))
    return block_1, block_2


def sum_kernel(widths, holders, stay, arrived_1, arrived_2, arrived_3, first):
    rows, half = stay.shape
    live = live_columns(widths, holders, half, lax.axis_index("env"))
    block_1, block_2 = incoming(holders, arrived_1, arrived_2, arrived_3, 0, rows)
    total = stay[...].astype(jnp.float32) + block_1 + block_2
    first[...] = jnp.where(live, total, 0.0).astype(jnp.bfloat16)


def total_of(array):
    return jnp.sum(jnp.sum(array, axis=0, keepdims=True), axis=1, keepdims=True)


def second_kernel(
    widths, holders, amps, first, right, left, message_1, message_2, tag, stay, left_vmem, sems
):
    half = amps.shape[2]
    copies = start_copies(left, left_vmem, sems)
    sector = holders[lax.axis_index("sec")]
    basis = [
        jnp.where(
            live_columns(widths, holders, half, h), amps[h].astype(jnp.float32), 0.0
        )
        for h in range(2)
    ]
    firsts = [first[h].astype(jnp.float32) for h in range(2)]
    overlap = total_of(basis[0] * firsts[0]) + total_of(basis[1] * firsts[1])
    norm = total_of(basis[0] * basis[0]) + total_of(basis[1] * basis[1])
    quotient = jnp.where(norm > 0, overlap / jnp.where(norm > 0, norm, 1.0), 0.0)
    deflated = [firsts[h] - quotient * basis[h] for h in range(2)]
    rest = total_of(deflated[0] * deflated[0]) + total_of(deflated[1] * deflated[1])
    vector = jnp.concatenate(deflated, axis=1).astype(jnp.bfloat16)

    row = lax.broadcasted_iota(jnp.int32, (TAG, LANES), 0)
    lane = lax.broadcasted_iota(jnp.int32, (TAG, LANES), 1)
    values = jnp.zeros((TAG, LANES), jnp.float32)
    for place, value in enumerate((overlap, norm, quotient, rest)):
        values = jnp.where(row // 3 == place, value, values)
    high = values.astype(jnp.bfloat16).astype(jnp.float32)
    middle = (values - high).astype(jnp.bfloat16).astype(jnp.float32)
    low = values - high - middle
    parts = jnp.where(row % 3 == 0, high, jnp.where(row % 3 == 1, middle, low))
    label = jnp.where((lane == sector) & (row < 12), parts, 0.0).astype(jnp.bfloat16)
    tag[...] = label
    message_1[pl.ds(0, TAG), :] = label
    message_2[pl.ds(0, TAG), :] = label

    for term, copy in copies:
        copy.wait()
        block = apply_term(right, left_vmem, vector, term)
        if term == 0:
            stay[...] = block
        else:
            store_chunks((message_1, message_2)[term - 1], TAG, block.astype(jnp.bfloat16))


def tag_kernel(tag, arrived, message, tag_out, message_out):
    joined = tag[...] + arrived[...]
    tag_out[...] = joined
    message_out[...] = joined


def final_kernel(
    widths,
    holders,
    tag,
    stay,
    old_1,
    old_2,
    old_3,
    stay_2,
    new_1,
    new_2,
    new_3,
    second,
):
    rows, half = stay.shape
    slots = holders.shape[0]
    sector = holders[lax.axis_index("sec")]
    live = live_columns(widths, holders, half, lax.axis_index("env"))
    total = jnp.int32(0)
    for s in range(slots):
        total = total + widths[s]
    live_count = rows * total.astype(jnp.float32)
    table = (tag[...] + new_3[pl.ds(0, TAG), :]).astype(jnp.float32)

    def value(place):
        parts = [table[3 * place + i : 3 * place + i + 1, :] for i in range(3)]
        return parts[0] + parts[1] + parts[2]

    overlaps, norms, quotients, rests = (value(place) for place in range(4))
    quotient = total_of(overlaps) / total_of(norms)
    lane = lax.broadcasted_iota(jnp.int32, (1, LANES), 1)
    shifts = jnp.where(lane < slots, quotients - quotient, 0.0)
    resid_norm = total_of(rests + shifts * shifts * norms)
    scale = lax.rsqrt(resid_norm / live_count + 1e-06)

    def shift_of(source):
        return total_of(jnp.where(lane == source, shifts, 0.0))

    old_block_1, old_block_2 = incoming(holders, old_1, old_2, old_3, 0, rows)
    new_block_1, new_block_2 = incoming(holders, new_1, new_2, new_3, TAG, rows)
    result = stay_2[...] + shift_of(sector) * stay[...].astype(jnp.float32)
    result = result + new_block_1 + shift_of(sector - QDOWN) * old_block_1
    result = result + new_block_2 + shift_of(sector - 1) * old_block_2
    second[...] = jnp.where(live, scale * result, 0.0).astype(jnp.bfloat16)


SMEM = pl.BlockSpec(memory_space=pltpu.SMEM)
VMEM = pl.BlockSpec(memory_space=pltpu.VMEM)
ANY = pl.BlockSpec(memory_space=pl.ANY)
PARAMS = pltpu.CompilerParams(vmem_limit_bytes=32 * 1024 * 1024)


def exchange(message, turn, n_slots):
    def turned(offset):
        pairs = [(i, i ^ offset) for i in range(n_slots)]
        return lambda sent: lax.ppermute(sent, "sec", pairs)

    branches = [lambda sent: sent] + [turned(offset) for offset in range(1, n_slots)]
    return lax.switch(turn, branches, message)


def on_device(amplitudes, widths, holders, left_env, right_env):
    slots_dev, right_dim, half = amplitudes.shape
    n_slots = holders.shape[0]
    assert slots_dev == 1
    if n_slots != 2 * QDOWN:
        return on_device_any(amplitudes, widths, holders, left_env, right_env)
    plain = jax.ShapeDtypeStruct((right_dim * half // LANES, LANES), jnp.bfloat16)
    tagged = jax.ShapeDtypeStruct((TAG + right_dim * half // LANES, LANES), jnp.bfloat16)
    label = jax.ShapeDtypeStruct((TAG, LANES), jnp.bfloat16)
    block = jax.ShapeDtypeStruct((right_dim, half), jnp.bfloat16)
    wide = jax.ShapeDtypeStruct((right_dim, half), jnp.float32)
    left_scratch = [
        pltpu.VMEM(left_env.shape[1:], jnp.bfloat16),
        pltpu.SemaphoreType.DMA((left_env.shape[1],)),
    ]

    amps_full = lax.all_gather(amplitudes[0], "env")
    message_1, message_2, stay, turns = pl.pallas_call(
        first_kernel,
        out_shape=(plain, plain, block, jax.ShapeDtypeStruct((6,), jnp.int32)),
        in_specs=[SMEM, SMEM, VMEM, VMEM, ANY],
        out_specs=(VMEM, VMEM, VMEM, SMEM),
        scratch_shapes=left_scratch,
        compiler_params=PARAMS,
    )(widths, holders, amps_full, right_env, left_env)
    old_1 = exchange(message_1, turns[3], n_slots)
    old_2 = exchange(message_2, turns[4], n_slots)
    old_3 = exchange(message_2, turns[5], n_slots)
    first = pl.pallas_call(
        sum_kernel,
        out_shape=block,
        in_specs=[SMEM, SMEM] + [VMEM] * 4,
        out_specs=VMEM,
        compiler_params=PARAMS,
    )(widths, holders, stay, old_1, old_2, old_3)

    first_full = lax.all_gather(first, "env")
    message_1, message_2, tag, stay_2 = pl.pallas_call(
        second_kernel,
        out_shape=(tagged, tagged, label, wide),
        in_specs=[SMEM, SMEM, VMEM, VMEM, VMEM, ANY],
        out_specs=(VMEM, VMEM, VMEM, VMEM),
        scratch_shapes=left_scratch,
        compiler_params=PARAMS,
    )(widths, holders, amps_full, first_full, right_env, left_env)
    new = []
    for step, message in enumerate((message_1, message_2, message_2)):
        if step:
            corner = pl.BlockSpec((TAG, LANES), lambda i: (0, 0))
            tag, message_2 = pl.pallas_call(
                tag_kernel,
                out_shape=(label, tagged),
                grid=(1,),
                in_specs=[corner, corner, ANY],
                out_specs=(corner, corner),
                input_output_aliases={2: 1},
                compiler_params=PARAMS,
            )(tag, new[-1], message_2)
            message = message_2
        new.append(exchange(message, turns[step], n_slots))
    second = pl.pallas_call(
        final_kernel,
        out_shape=block,
        in_specs=[SMEM, SMEM] + [VMEM] * 9,
        out_specs=VMEM,
        compiler_params=PARAMS,
    )(widths, holders, tag, stay, old_1, old_2, old_3, stay_2, *new)
    return first[None], second[None]


def solution(mesh):
    in_specs = (
        P(("runs", "sec"), None, "env"),
        P("runs"),
        P("runs"),
        P(("runs", "sec"), None, None, "env"),
        P("runs", None, None),
    )
    out_specs = (P(("runs", "sec"), None, "env"), P(("runs", "sec"), None, "env"))
    return jax.shard_map(
        on_device, mesh=mesh, in_specs=in_specs, out_specs=out_specs, check_vma=False
    )
```

```python
import jax
import jax.numpy as jnp
from jax import lax
from jax.experimental import pallas as pl
from jax.experimental.pallas import tpu as pltpu
from jax.sharding import PartitionSpec as P

QDOWN = 4

term_shifts = ((0, 0), (1, 0), (0, 1))


def route(holders):
    n_slots = holders.shape[0]
    sector_ids = jnp.arange(n_slots, dtype=jnp.int32)
    slot_of = jnp.argmax(holders[None, :] == sector_ids[:, None], axis=1)
    sources = []
    allowed = []
    for up, down in term_shifts[1:]:
        permitted = (holders // QDOWN - up >= 0) & (holders % QDOWN - down >= 0)
        wanted = jnp.clip(holders - QDOWN * up - down, 0, n_slots - 1)
        sources.append(slot_of[wanted])
        allowed.append(permitted)
    return sources, allowed


def contract(vector, left_env, right_env):
    products = jnp.einsum(
        "tij,jw->tiw", right_env, vector, preferred_element_type=jnp.float32
    ).astype(jnp.bfloat16)
    return jnp.einsum("tik,tkw->tiw", products, left_env, preferred_element_type=jnp.float32)


def spread(blocks, n_slots):
    terms, rows, width = blocks.shape
    pieces = blocks.reshape(terms, n_slots, rows // n_slots, width).swapaxes(0, 1)
    return lax.all_to_all(pieces, "sec", split_axis=0, concat_axis=0)


def collect(merged):
    n_slots, rows, width = merged.shape
    home = lax.all_to_all(merged, "sec", split_axis=0, concat_axis=0)
    return home.reshape(n_slots * rows, width)


def share(values, n_slots, me):
    lanes = jnp.zeros((1, 128), jnp.float32).at[0, : values.shape[0]].set(values)
    if n_slots & (n_slots - 1) or n_slots > 16:
        return lax.all_gather(lanes[0], "sec")
    table = jnp.where(jnp.arange(n_slots)[:, None] == me, lanes, 0.0)
    for offset in range(1, n_slots):
        pairs = [(i, i ^ offset) for i in range(n_slots)]
        other = lax.ppermute(lanes, "sec", pairs)
        table = jnp.where(jnp.arange(n_slots)[:, None] == (me ^ offset), other, table)
    return table


def merge(received, sources, allowed):
    total = 0.0
    for term, (source, permitted) in enumerate(zip(sources, allowed)):
        picked = received[source, term]
        total = total + jnp.where(permitted[:, None, None], picked, 0).astype(jnp.float32)
    return total


def on_device_any(amplitudes, widths, holders, left_env, right_env):
    slots_dev, right_dim, half_width = amplitudes.shape
    assert slots_dev == 1
    n_slots = holders.shape[0]
    me = lax.axis_index("sec")
    side = lax.axis_index("env")
    my_width = widths[holders[me]]
    row_index = side * half_width + jnp.arange(half_width, dtype=jnp.int32)
    live = (row_index < my_width)[None, :]
    sources, allowed = route(holders)
    envs = left_env[0]

    start = jnp.where(live, amplitudes[0], jnp.zeros_like(amplitudes[0]))
    start_full = lax.all_gather(start, "env", axis=1, tiled=True)
    outgoing = contract(start_full, envs, right_env).astype(jnp.bfloat16)
    stay = outgoing[0].astype(jnp.float32)
    received = spread(outgoing[1:], n_slots)
    arrived = collect(merge(received, sources, allowed).astype(jnp.bfloat16))
    first = jnp.where(live, stay + arrived.astype(jnp.float32), 0.0).astype(jnp.bfloat16)

    first_full = lax.all_gather(first, "env", axis=1, tiled=True).astype(jnp.float32)
    basis = start_full.astype(jnp.float32)
    overlap = jnp.sum(basis * first_full)
    norm = jnp.sum(basis * basis)
    own_quotient = jnp.where(norm > 0, overlap / jnp.where(norm > 0, norm, 1.0), 0.0)
    deflated = first_full - own_quotient * basis
    rest = jnp.sum(deflated * deflated)
    sums = share(jnp.stack([overlap, norm, own_quotient, rest]), n_slots, me)
    outgoing_2 = contract(deflated.astype(jnp.bfloat16), envs, right_env)
    received_2 = spread(outgoing_2[1:].astype(jnp.bfloat16), n_slots)

    quotient = jnp.sum(sums[:, 0]) / jnp.sum(sums[:, 1])
    shift = sums[:, 2] - quotient
    resid_norm = jnp.sum(sums[:, 3] + shift * shift * sums[:, 1])
    live_count = right_dim * jnp.sum(widths).astype(jnp.float32)
    scale = lax.rsqrt(resid_norm / live_count + 1e-06)
    mixed = received_2.astype(jnp.float32) + shift[:, None, None, None] * received.astype(
        jnp.float32
    )
    merged_2 = scale * merge(mixed, sources, allowed)
    arrived_2 = collect(merged_2.astype(jnp.bfloat16))
    stay_2 = scale * (outgoing_2[0] + (own_quotient - quotient) * stay)
    second = jnp.where(live, stay_2 + arrived_2.astype(jnp.float32), 0.0).astype(jnp.bfloat16)
    return first[None], second[None]


LANES = 128
PIECES = 2


def find_slot(holders, sector):
    slot = jnp.int32(0)
    for s in range(holders.shape[0]):
        slot = slot + jnp.where(holders[s] == sector, s, 0)
    return slot


def live_columns(widths, holders, half, side):
    width = widths[holders[lax.axis_index("sec")]]
    columns = side * half + lax.broadcasted_iota(jnp.int32, (1, half), 1)
    return columns < width


def start_copies(left, left_vmem, sems):
    copies = []
    for term in (1, 2, 0):
        copy = pltpu.make_async_copy(left.at[0, term], left_vmem.at[term], sems.at[term])
        copy.start()
        copies.append((term, copy))
    return copies


def apply_term(right, left_vmem, vector, term):
    products = jnp.dot(right[term], vector, preferred_element_type=jnp.float32)
    return jnp.dot(
        products.astype(jnp.bfloat16), left_vmem[term], preferred_element_type=jnp.float32
    )


def store_pieces(pieces, block):
    width = block.shape[1] // len(pieces)
    for i, piece in enumerate(pieces):
        piece[...] = block[:, i * width : (i + 1) * width].astype(piece.dtype)


def write_turns(widths, holders, half, turns):
    me = lax.axis_index("sec")
    sector = holders[me]
    down = sector % QDOWN
    inner = (down == 1) | (down == 2)
    group = sector - down
    plan = (
        (sector ^ QDOWN, sector & (QDOWN - 1), sector | QDOWN, True),
        (sector ^ 1, sector - sector % 2, sector | 1, True),
        (sector ^ 3, group + 1, group + 2, inner),
    )
    for step, (partner, sender, target, used) in enumerate(plan):
        offset = me ^ find_slot(holders, partner)
        backward = jnp.where(find_slot(holders, sender) > find_slot(holders, target), 1, 0)
        columns = widths[target] - lax.axis_index("env") * half
        count = jnp.int32(0)
        for i in range(PIECES):
            count = count + jnp.where(columns > i * (half // PIECES), 1, 0)
        count = jnp.where(used, count, 0)
        kind = jnp.where(count > 0, backward * PIECES + count, 0)
        turns[step][0] = jnp.where(kind > 0, (offset - 1) * 2 * PIECES + kind, 0)
        turns[step + 3][0] = (offset - 1) * (2 * PIECES + 1) + kind


def first_kernel(widths, holders, amps, right, left, *rest):
    half = amps.shape[2]
    pieces_1, pieces_2 = rest[:PIECES], rest[PIECES : 2 * PIECES]
    stay, *turns, left_vmem, sems = rest[2 * PIECES :]
    copies = start_copies(left, left_vmem, sems)
    write_turns(widths, holders, half, turns)
    vector = jnp.concatenate(
        [
            jnp.where(live_columns(widths, holders, half, h), amps[h], jnp.zeros_like(amps[h]))
            for h in range(2)
        ],
        axis=1,
    )
    for term, copy in copies:
        copy.wait()
        block = apply_term(right, left_vmem, vector, term)
        store_pieces(((stay,), pieces_1, pieces_2)[term], block)


def incoming(holders, arrived_1, arrived_2, arrived_3):
    sector = holders[lax.axis_index("sec")]
    down = sector % QDOWN
    block_1, block_2, block_3 = (
        jnp.concatenate([piece[...] for piece in pieces], axis=1).astype(jnp.float32)
        for pieces in (arrived_1, arrived_2, arrived_3)
    )
    block_1 = jnp.where(sector >= QDOWN, block_1, 0.0)
    block_2 = jnp.where(down % 2 == 1, block_2, jnp.where(down == 2, block_3, 0.0))
    return block_1, block_2


def thirds(refs):
    return refs[:PIECES], refs[PIECES : 2 * PIECES], refs[2 * PIECES :]


def sum_kernel(widths, holders, stay, *rest):
    *arrived, first = rest
    live = live_columns(widths, holders, stay.shape[1], lax.axis_index("env"))
    block_1, block_2 = incoming(holders, *thirds(arrived))
    total = stay[...].astype(jnp.float32) + block_1 + block_2
    first[...] = jnp.where(live, total, 0.0).astype(jnp.bfloat16)


def total_of(array):
    return jnp.sum(jnp.sum(array, axis=0, keepdims=True), axis=1, keepdims=True)


def second_kernel(widths, holders, amps, first, right, left, *outs):
    half = amps.shape[2]
    pieces_1, pieces_2 = outs[:PIECES], outs[PIECES : 2 * PIECES]
    stay, tag, left_vmem, sems = outs[2 * PIECES :]
    copies = start_copies(left, left_vmem, sems)
    sector = holders[lax.axis_index("sec")]
    basis = [
        jnp.where(
            live_columns(widths, holders, half, h), amps[h].astype(jnp.float32), 0.0
        )
        for h in range(2)
    ]
    firsts = [first[h].astype(jnp.float32) for h in range(2)]
    overlap = total_of(basis[0] * firsts[0]) + total_of(basis[1] * firsts[1])
    norm = total_of(basis[0] * basis[0]) + total_of(basis[1] * basis[1])
    quotient = jnp.where(norm > 0, overlap / jnp.where(norm > 0, norm, 1.0), 0.0)
    deflated = [firsts[h] - quotient * basis[h] for h in range(2)]
    rest = total_of(deflated[0] * deflated[0]) + total_of(deflated[1] * deflated[1])
    vector = jnp.concatenate(deflated, axis=1).astype(jnp.bfloat16)

    row = lax.broadcasted_iota(jnp.int32, tag.shape, 0)
    lane = lax.broadcasted_iota(jnp.int32, tag.shape, 1)
    values = jnp.zeros(tag.shape, jnp.float32)
    for place, value in enumerate((overlap, norm, quotient, rest)):
        values = jnp.where(row == place, value, values)
    tag[...] = jnp.where(lane == sector, values, 0.0)

    for term, copy in copies:
        copy.wait()
        block = apply_term(right, left_vmem, vector, term)
        store_pieces(((stay,), pieces_1, pieces_2)[term], block)


def final_kernel(widths, holders, tag, stay, stay_2, *rest):
    rows, half = stay.shape
    *arrived, second = rest
    old, new = arrived[: 3 * PIECES], arrived[3 * PIECES :]
    slots = holders.shape[0]
    sector = holders[lax.axis_index("sec")]
    live = live_columns(widths, holders, half, lax.axis_index("env"))
    total = jnp.int32(0)
    for s in range(slots):
        total = total + widths[s]
    live_count = rows * total.astype(jnp.float32)
    overlaps, norms, quotients, rests = (tag[i : i + 1, :] for i in range(4))
    quotient = total_of(overlaps) / total_of(norms)
    lane = lax.broadcasted_iota(jnp.int32, (1, LANES), 1)
    shifts = jnp.where(lane < slots, quotients - quotient, 0.0)
    resid_norm = total_of(rests + shifts * shifts * norms)
    scale = lax.rsqrt(resid_norm / live_count + 1e-06)

    def shift_of(source):
        return total_of(jnp.where(lane == source, shifts, 0.0))

    old_1, old_2 = incoming(holders, *thirds(old))
    new_1, new_2 = incoming(holders, *thirds(new))
    result = stay_2[...] + shift_of(sector) * stay[...].astype(jnp.float32)
    result = result + new_1 + shift_of(sector - QDOWN) * old_1
    result = result + new_2 + shift_of(sector - 1) * old_2
    second[...] = jnp.where(live, scale * result, 0.0).astype(jnp.bfloat16)


SMEM = pl.BlockSpec(memory_space=pltpu.SMEM)
VMEM = pl.BlockSpec(memory_space=pltpu.VMEM)
ANY = pl.BlockSpec(memory_space=pl.ANY)


def choose(index, branches, *operands):
    jaxprs = tuple(jax.make_jaxpr(branch)(*operands) for branch in branches)
    return lax.cond_p.bind(index.reshape(()), *operands, branches=jaxprs)


def send(pieces, offset, backward, count, n_slots):
    pairs = [(i, i ^ offset) for i in range(n_slots) if (i > i ^ offset) == bool(backward)]
    sent = [lax.ppermute(piece, "sec", pairs) for piece in pieces[:count]]
    return sent + [jnp.zeros_like(piece) for piece in pieces[count:]]


def exchange(turn, pieces, n_slots):
    branches = [lambda *sent: [jnp.zeros_like(piece) for piece in sent]]
    for offset in range(1, n_slots):
        for backward in range(2):
            for count in range(1, PIECES + 1):
                branches.append(
                    lambda *sent, o=offset, b=backward, c=count: send(sent, o, b, c, n_slots)
                )
    return choose(turn, branches, *pieces)


def exchange_tagged(turn, tag, pieces, n_slots):
    def swapped(tag, offset):
        return tag + lax.ppermute(tag, "sec", [(i, i ^ offset) for i in range(n_slots)])

    branches = []
    for offset in range(1, n_slots):
        for backward, count in [(0, 0)] + [
            (b, c) for b in range(2) for c in range(1, PIECES + 1)
        ]:
            branches.append(
                lambda tag, *sent, o=offset, b=backward, c=count: [swapped(tag, o)]
                + send(sent, o, b, c, n_slots)
            )
    tag, *arrived = choose(turn, branches, tag, *pieces)
    return tag, arrived


def on_device(amplitudes, widths, holders, left_env, right_env):
    slots_dev, right_dim, half = amplitudes.shape
    n_slots = holders.shape[0]
    assert slots_dev == 1
    if n_slots != 2 * QDOWN:
        return on_device_any(amplitudes, widths, holders, left_env, right_env)
    piece = jax.ShapeDtypeStruct((right_dim, half // PIECES), jnp.bfloat16)
    block = jax.ShapeDtypeStruct((right_dim, half), jnp.bfloat16)
    wide = jax.ShapeDtypeStruct((right_dim, half), jnp.float32)
    tag_shape = jax.ShapeDtypeStruct((8, LANES), jnp.float32)
    turn = jax.ShapeDtypeStruct((1,), jnp.int32)
    left_scratch = [
        pltpu.VMEM(left_env.shape[1:], jnp.bfloat16),
        pltpu.SemaphoreType.DMA((left_env.shape[1],)),
    ]

    amps_full = lax.all_gather(amplitudes[0], "env")
    *pieces, stay, turn_1, turn_2, turn_3, turn_4, turn_5, turn_6 = pl.pallas_call(
        first_kernel,
        out_shape=(piece,) * (2 * PIECES) + (block,) + (turn,) * 6,
        in_specs=[SMEM, SMEM, VMEM, VMEM, ANY],
        out_specs=(VMEM,) * (2 * PIECES + 1) + (SMEM,) * 6,
        scratch_shapes=left_scratch,
    )(widths, holders, amps_full, right_env, left_env)
    pieces_1, pieces_2 = pieces[:PIECES], pieces[PIECES:]
    old = [
        *exchange(turn_1, pieces_1, n_slots),
        *exchange(turn_2, pieces_2, n_slots),
        *exchange(turn_3, pieces_2, n_slots),
    ]
    first = pl.pallas_call(
        sum_kernel,
        out_shape=block,
        in_specs=[SMEM, SMEM] + [VMEM] * (1 + 3 * PIECES),
        out_specs=VMEM,
    )(widths, holders, stay, *old)

    first_full = lax.all_gather(first, "env")
    *pieces, stay_2, tag = pl.pallas_call(
        second_kernel,
        out_shape=(piece,) * (2 * PIECES) + (wide, tag_shape),
        in_specs=[SMEM, SMEM, VMEM, VMEM, VMEM, ANY],
        out_specs=(VMEM,) * (2 * PIECES + 2),
        scratch_shapes=left_scratch,
    )(widths, holders, amps_full, first_full, right_env, left_env)
    pieces_1, pieces_2 = pieces[:PIECES], pieces[PIECES:]
    tag, new_1 = exchange_tagged(turn_4, tag, pieces_1, n_slots)
    tag, new_2 = exchange_tagged(turn_5, tag, pieces_2, n_slots)
    tag, new_3 = exchange_tagged(turn_6, tag, pieces_2, n_slots)
    second = pl.pallas_call(
        final_kernel,
        out_shape=block,
        in_specs=[SMEM, SMEM] + [VMEM] * (3 + 6 * PIECES),
        out_specs=VMEM,
    )(widths, holders, tag, stay, stay_2, *old, *new_1, *new_2, *new_3)
    return first[None], second[None]


def solution(mesh):
    in_specs = (
        P(("runs", "sec"), None, "env"),
        P("runs"),
        P("runs"),
        P(("runs", "sec"), None, None, "env"),
        P("runs", None, None),
    )
    out_specs = (P(("runs", "sec"), None, "env"), P(("runs", "sec"), None, "env"))
    return jax.shard_map(
        on_device, mesh=mesh, in_specs=in_specs, out_specs=out_specs, check_vma=False
    )
```

```python
import jax
import jax.numpy as jnp
from jax import lax
from jax.experimental import pallas as pl
from jax.experimental.pallas import tpu as pltpu
from jax.sharding import PartitionSpec as P

QDOWN = 4

term_shifts = ((0, 0), (1, 0), (0, 1))


def route(holders):
    n_slots = holders.shape[0]
    sector_ids = jnp.arange(n_slots, dtype=jnp.int32)
    slot_of = jnp.argmax(holders[None, :] == sector_ids[:, None], axis=1)
    sources = []
    allowed = []
    for up, down in term_shifts[1:]:
        permitted = (holders // QDOWN - up >= 0) & (holders % QDOWN - down >= 0)
        wanted = jnp.clip(holders - QDOWN * up - down, 0, n_slots - 1)
        sources.append(slot_of[wanted])
        allowed.append(permitted)
    return sources, allowed


def contract(vector, left_env, right_env):
    products = jnp.einsum(
        "tij,jw->tiw", right_env, vector, preferred_element_type=jnp.float32
    ).astype(jnp.bfloat16)
    return jnp.einsum("tik,tkw->tiw", products, left_env, preferred_element_type=jnp.float32)


def spread(blocks, n_slots):
    terms, rows, width = blocks.shape
    pieces = blocks.reshape(terms, n_slots, rows // n_slots, width).swapaxes(0, 1)
    return lax.all_to_all(pieces, "sec", split_axis=0, concat_axis=0)


def collect(merged):
    n_slots, rows, width = merged.shape
    home = lax.all_to_all(merged, "sec", split_axis=0, concat_axis=0)
    return home.reshape(n_slots * rows, width)


def share(values, n_slots, me):
    lanes = jnp.zeros((1, 128), jnp.float32).at[0, : values.shape[0]].set(values)
    if n_slots & (n_slots - 1) or n_slots > 16:
        return lax.all_gather(lanes[0], "sec")
    table = jnp.where(jnp.arange(n_slots)[:, None] == me, lanes, 0.0)
    for offset in range(1, n_slots):
        pairs = [(i, i ^ offset) for i in range(n_slots)]
        other = lax.ppermute(lanes, "sec", pairs)
        table = jnp.where(jnp.arange(n_slots)[:, None] == (me ^ offset), other, table)
    return table


def merge(received, sources, allowed):
    total = 0.0
    for term, (source, permitted) in enumerate(zip(sources, allowed)):
        picked = received[source, term]
        total = total + jnp.where(permitted[:, None, None], picked, 0).astype(jnp.float32)
    return total


def on_device_any(amplitudes, widths, holders, left_env, right_env):
    slots_dev, right_dim, half_width = amplitudes.shape
    assert slots_dev == 1
    n_slots = holders.shape[0]
    me = lax.axis_index("sec")
    side = lax.axis_index("env")
    my_width = widths[holders[me]]
    row_index = side * half_width + jnp.arange(half_width, dtype=jnp.int32)
    live = (row_index < my_width)[None, :]
    sources, allowed = route(holders)
    envs = left_env[0]

    start = jnp.where(live, amplitudes[0], jnp.zeros_like(amplitudes[0]))
    start_full = lax.all_gather(start, "env", axis=1, tiled=True)
    outgoing = contract(start_full, envs, right_env).astype(jnp.bfloat16)
    stay = outgoing[0].astype(jnp.float32)
    received = spread(outgoing[1:], n_slots)
    arrived = collect(merge(received, sources, allowed).astype(jnp.bfloat16))
    first = jnp.where(live, stay + arrived.astype(jnp.float32), 0.0).astype(jnp.bfloat16)

    first_full = lax.all_gather(first, "env", axis=1, tiled=True).astype(jnp.float32)
    basis = start_full.astype(jnp.float32)
    overlap = jnp.sum(basis * first_full)
    norm = jnp.sum(basis * basis)
    own_quotient = jnp.where(norm > 0, overlap / jnp.where(norm > 0, norm, 1.0), 0.0)
    deflated = first_full - own_quotient * basis
    rest = jnp.sum(deflated * deflated)
    sums = share(jnp.stack([overlap, norm, own_quotient, rest]), n_slots, me)
    outgoing_2 = contract(deflated.astype(jnp.bfloat16), envs, right_env)
    received_2 = spread(outgoing_2[1:].astype(jnp.bfloat16), n_slots)

    quotient = jnp.sum(sums[:, 0]) / jnp.sum(sums[:, 1])
    shift = sums[:, 2] - quotient
    resid_norm = jnp.sum(sums[:, 3] + shift * shift * sums[:, 1])
    live_count = right_dim * jnp.sum(widths).astype(jnp.float32)
    scale = lax.rsqrt(resid_norm / live_count + 1e-06)
    mixed = received_2.astype(jnp.float32) + shift[:, None, None, None] * received.astype(
        jnp.float32
    )
    merged_2 = scale * merge(mixed, sources, allowed)
    arrived_2 = collect(merged_2.astype(jnp.bfloat16))
    stay_2 = scale * (outgoing_2[0] + (own_quotient - quotient) * stay)
    second = jnp.where(live, stay_2 + arrived_2.astype(jnp.float32), 0.0).astype(jnp.bfloat16)
    return first[None], second[None]


LANES = 128
PIECES = 2


def find_slot(holders, sector):
    slot = jnp.int32(0)
    for s in range(holders.shape[0]):
        slot = slot + jnp.where(holders[s] == sector, s, 0)
    return slot


def live_columns(widths, holders, half, side):
    width = widths[holders[lax.axis_index("sec")]]
    columns = side * half + lax.broadcasted_iota(jnp.int32, (1, half), 1)
    return columns < width


def start_copies(left, left_vmem, sems):
    copies = []
    for term in (1, 2, 0):
        copy = pltpu.make_async_copy(left.at[0, term], left_vmem.at[term], sems.at[term])
        copy.start()
        copies.append((term, copy))
    return copies


def apply_term(right, left_vmem, vector, term):
    products = jnp.dot(right[term], vector, preferred_element_type=jnp.float32)
    return jnp.dot(
        products.astype(jnp.bfloat16), left_vmem[term], preferred_element_type=jnp.float32
    )


def store_pieces(pieces, block):
    width = block.shape[1] // len(pieces)
    for i, piece in enumerate(pieces):
        piece[...] = block[:, i * width : (i + 1) * width].astype(piece.dtype)


def write_turns(widths, holders, half, turns):
    me = lax.axis_index("sec")
    sector = holders[me]
    down = sector % QDOWN
    inner = (down == 1) | (down == 2)
    group = sector - down
    plan = (
        (sector ^ QDOWN, sector & (QDOWN - 1), sector | QDOWN, True),
        (sector ^ 1, sector - sector % 2, sector | 1, True),
        (sector ^ 3, group + 1, group + 2, inner),
    )
    for step, (partner, sender, target, used) in enumerate(plan):
        offset = me ^ find_slot(holders, partner)
        backward = jnp.where(find_slot(holders, sender) > find_slot(holders, target), 1, 0)
        columns = widths[target] - lax.axis_index("env") * half
        count = jnp.int32(0)
        for i in range(PIECES):
            count = count + jnp.where(columns > i * (half // PIECES), 1, 0)
        count = jnp.where(used, count, 0)
        kind = jnp.where(count > 0, backward * PIECES + count, 0)
        turns[step][0] = jnp.where(kind > 0, (offset - 1) * 2 * PIECES + kind, 0)
        turns[step + 3][0] = (offset - 1) * (2 * PIECES + 1) + kind


def first_kernel(widths, holders, amps, right, left, *rest):
    half = amps.shape[2]
    pieces_1, pieces_2 = rest[:PIECES], rest[PIECES : 2 * PIECES]
    stay, *turns, left_vmem, sems = rest[2 * PIECES :]
    copies = start_copies(left, left_vmem, sems)
    write_turns(widths, holders, half, turns)
    vector = jnp.concatenate(
        [
            jnp.where(live_columns(widths, holders, half, h), amps[h], jnp.zeros_like(amps[h]))
            for h in range(2)
        ],
        axis=1,
    )
    for term, copy in copies:
        copy.wait()
        block = apply_term(right, left_vmem, vector, term)
        store_pieces(((stay,), pieces_1, pieces_2)[term], block)


def incoming(holders, arrived_1, arrived_2, arrived_3):
    sector = holders[lax.axis_index("sec")]
    down = sector % QDOWN
    block_1, block_2, block_3 = (
        jnp.concatenate([piece[...] for piece in pieces], axis=1).astype(jnp.float32)
        for pieces in (arrived_1, arrived_2, arrived_3)
    )
    block_1 = jnp.where(sector >= QDOWN, block_1, 0.0)
    block_2 = jnp.where(down % 2 == 1, block_2, jnp.where(down == 2, block_3, 0.0))
    return block_1, block_2


def thirds(refs):
    return refs[:PIECES], refs[PIECES : 2 * PIECES], refs[2 * PIECES :]


def sum_kernel(widths, holders, stay, *rest):
    *arrived, first = rest
    live = live_columns(widths, holders, stay.shape[1], lax.axis_index("env"))
    block_1, block_2 = incoming(holders, *thirds(arrived))
    total = stay[...].astype(jnp.float32) + block_1 + block_2
    first[...] = jnp.where(live, total, 0.0).astype(jnp.bfloat16)


def total_of(array):
    return jnp.sum(jnp.sum(array, axis=0, keepdims=True), axis=1, keepdims=True)


def second_kernel(widths, holders, amps, first, right, left, *outs):
    half = amps.shape[2]
    pieces_1, pieces_2 = outs[:PIECES], outs[PIECES : 2 * PIECES]
    stay, tag, left_vmem, sems = outs[2 * PIECES :]
    copies = start_copies(left, left_vmem, sems)
    sector = holders[lax.axis_index("sec")]
    basis = [
        jnp.where(
            live_columns(widths, holders, half, h), amps[h].astype(jnp.float32), 0.0
        )
        for h in range(2)
    ]
    firsts = [first[h].astype(jnp.float32) for h in range(2)]
    overlap = total_of(basis[0] * firsts[0]) + total_of(basis[1] * firsts[1])
    norm = total_of(basis[0] * basis[0]) + total_of(basis[1] * basis[1])
    quotient = jnp.where(norm > 0, overlap / jnp.where(norm > 0, norm, 1.0), 0.0)
    deflated = [firsts[h] - quotient * basis[h] for h in range(2)]
    rest = total_of(deflated[0] * deflated[0]) + total_of(deflated[1] * deflated[1])
    vector = jnp.concatenate(deflated, axis=1).astype(jnp.bfloat16)

    row = lax.broadcasted_iota(jnp.int32, tag.shape, 0)
    lane = lax.broadcasted_iota(jnp.int32, tag.shape, 1)
    values = jnp.zeros(tag.shape, jnp.float32)
    for place, value in enumerate((overlap, norm, quotient, rest)):
        values = jnp.where(row == place, value, values)
    tag[...] = jnp.where(lane == sector, values, 0.0)

    for term, copy in copies:
        copy.wait()
        block = apply_term(right, left_vmem, vector, term)
        store_pieces(((stay,), pieces_1, pieces_2)[term], block)


def final_kernel(widths, holders, tag, stay, stay_2, *rest):
    rows, half = stay.shape
    *arrived, second = rest
    old, new = arrived[: 3 * PIECES], arrived[3 * PIECES :]
    slots = holders.shape[0]
    sector = holders[lax.axis_index("sec")]
    live = live_columns(widths, holders, half, lax.axis_index("env"))
    total = jnp.int32(0)
    for s in range(slots):
        total = total + widths[s]
    live_count = rows * total.astype(jnp.float32)
    overlaps, norms, quotients, rests = (tag[i : i + 1, :] for i in range(4))
    quotient = total_of(overlaps) / total_of(norms)
    lane = lax.broadcasted_iota(jnp.int32, (1, LANES), 1)
    shifts = jnp.where(lane < slots, quotients - quotient, 0.0)
    resid_norm = total_of(rests + shifts * shifts * norms)
    scale = lax.rsqrt(resid_norm / live_count + 1e-06)

    def shift_of(source):
        return total_of(jnp.where(lane == source, shifts, 0.0))

    old_1, old_2 = incoming(holders, *thirds(old))
    new_1, new_2 = incoming(holders, *thirds(new))
    result = stay_2[...] + shift_of(sector) * stay[...].astype(jnp.float32)
    result = result + new_1 + shift_of(sector - QDOWN) * old_1
    result = result + new_2 + shift_of(sector - 1) * old_2
    second[...] = jnp.where(live, scale * result, 0.0).astype(jnp.bfloat16)


SMEM = pl.BlockSpec(memory_space=pltpu.SMEM)
VMEM = pl.BlockSpec(memory_space=pltpu.VMEM)
HBM = pl.BlockSpec(memory_space=pltpu.HBM)
PARAMS = pltpu.CompilerParams(vmem_limit_bytes=16 * 1024 * 1024)


def choose(index, branches, *operands):
    jaxprs = tuple(jax.make_jaxpr(branch)(*operands) for branch in branches)
    return lax.cond_p.bind(index.reshape(()), *operands, branches=jaxprs)


def send(pieces, offset, backward, count, n_slots):
    pairs = [(i, i ^ offset) for i in range(n_slots) if (i > i ^ offset) == bool(backward)]
    sent = [lax.ppermute(piece, "sec", pairs) for piece in pieces[:count]]
    return sent + [jnp.zeros_like(piece) for piece in pieces[count:]]


def exchange(turn, pieces, n_slots):
    branches = [lambda *sent: [jnp.zeros_like(piece) for piece in sent]]
    for offset in range(1, n_slots):
        for backward in range(2):
            for count in range(1, PIECES + 1):
                branches.append(
                    lambda *sent, o=offset, b=backward, c=count: send(sent, o, b, c, n_slots)
                )
    return choose(turn, branches, *pieces)


def exchange_tagged(turn, tag, pieces, n_slots):
    def swapped(tag, offset):
        return tag + lax.ppermute(tag, "sec", [(i, i ^ offset) for i in range(n_slots)])

    branches = []
    for offset in range(1, n_slots):
        for backward, count in [(0, 0)] + [
            (b, c) for b in range(2) for c in range(1, PIECES + 1)
        ]:
            branches.append(
                lambda tag, *sent, o=offset, b=backward, c=count: [swapped(tag, o)]
                + send(sent, o, b, c, n_slots)
            )
    tag, *arrived = choose(turn, branches, tag, *pieces)
    return tag, arrived


def on_device(amplitudes, widths, holders, left_env, right_env):
    slots_dev, right_dim, half = amplitudes.shape
    n_slots = holders.shape[0]
    assert slots_dev == 1
    if n_slots != 2 * QDOWN:
        return on_device_any(amplitudes, widths, holders, left_env, right_env)
    piece = jax.ShapeDtypeStruct((right_dim, half // PIECES), jnp.bfloat16)
    block = jax.ShapeDtypeStruct((right_dim, half), jnp.bfloat16)
    wide = jax.ShapeDtypeStruct((right_dim, half), jnp.float32)
    tag_shape = jax.ShapeDtypeStruct((8, LANES), jnp.float32)
    turn = jax.ShapeDtypeStruct((1,), jnp.int32)
    left_scratch = [
        pltpu.VMEM(left_env.shape[1:], jnp.bfloat16),
        pltpu.SemaphoreType.DMA((left_env.shape[1],)),
    ]

    amps_full = lax.all_gather(amplitudes[0], "env")
    *pieces, stay, turn_1, turn_2, turn_3, turn_4, turn_5, turn_6 = pl.pallas_call(
        first_kernel,
        out_shape=(piece,) * (2 * PIECES) + (block,) + (turn,) * 6,
        in_specs=[SMEM, SMEM, VMEM, VMEM, HBM],
        out_specs=(VMEM,) * (2 * PIECES + 1) + (SMEM,) * 6,
        scratch_shapes=left_scratch,
        compiler_params=PARAMS,
    )(widths, holders, amps_full, right_env, left_env)
    pieces_1, pieces_2 = pieces[:PIECES], pieces[PIECES:]
    old = [
        *exchange(turn_1, pieces_1, n_slots),
        *exchange(turn_2, pieces_2, n_slots),
        *exchange(turn_3, pieces_2, n_slots),
    ]
    first = pl.pallas_call(
        sum_kernel,
        out_shape=block,
        in_specs=[SMEM, SMEM] + [VMEM] * (1 + 3 * PIECES),
        out_specs=VMEM,
        compiler_params=PARAMS,
    )(widths, holders, stay, *old)

    first_full = lax.all_gather(first, "env")
    *pieces, stay_2, tag = pl.pallas_call(
        second_kernel,
        out_shape=(piece,) * (2 * PIECES) + (wide, tag_shape),
        in_specs=[SMEM, SMEM, VMEM, VMEM, VMEM, HBM],
        out_specs=(VMEM,) * (2 * PIECES + 2),
        scratch_shapes=left_scratch,
        compiler_params=PARAMS,
    )(widths, holders, amps_full, first_full, right_env, left_env)
    pieces_1, pieces_2 = pieces[:PIECES], pieces[PIECES:]
    tag, new_1 = exchange_tagged(turn_4, tag, pieces_1, n_slots)
    tag, new_2 = exchange_tagged(turn_5, tag, pieces_2, n_slots)
    tag, new_3 = exchange_tagged(turn_6, tag, pieces_2, n_slots)
    second = pl.pallas_call(
        final_kernel,
        out_shape=block,
        in_specs=[SMEM, SMEM] + [VMEM] * (3 + 6 * PIECES),
        out_specs=VMEM,
        compiler_params=PARAMS,
    )(widths, holders, tag, stay, stay_2, *old, *new_1, *new_2, *new_3)
    return first[None], second[None]


def solution(mesh):
    in_specs = (
        P(("runs", "sec"), None, "env"),
        P("runs"),
        P("runs"),
        P(("runs", "sec"), None, None, "env"),
        P("runs", None, None),
    )
    out_specs = (P(("runs", "sec"), None, "env"), P(("runs", "sec"), None, "env"))
    return jax.shard_map(
        on_device, mesh=mesh, in_specs=in_specs, out_specs=out_specs, check_vma=False
    )
```

```python
import jax
import jax.numpy as jnp
from jax import lax
from jax.experimental import pallas as pl
from jax.experimental.pallas import tpu as pltpu
from jax.sharding import PartitionSpec as P

QDOWN = 4

term_shifts = ((0, 0), (1, 0), (0, 1))


def route(holders):
    n_slots = holders.shape[0]
    sector_ids = jnp.arange(n_slots, dtype=jnp.int32)
    slot_of = jnp.argmax(holders[None, :] == sector_ids[:, None], axis=1)
    sources = []
    allowed = []
    for up, down in term_shifts[1:]:
        permitted = (holders // QDOWN - up >= 0) & (holders % QDOWN - down >= 0)
        wanted = jnp.clip(holders - QDOWN * up - down, 0, n_slots - 1)
        sources.append(slot_of[wanted])
        allowed.append(permitted)
    return sources, allowed


def contract(vector, left_env, right_env):
    products = jnp.einsum(
        "tij,jw->tiw", right_env, vector, preferred_element_type=jnp.float32
    ).astype(jnp.bfloat16)
    return jnp.einsum("tik,tkw->tiw", products, left_env, preferred_element_type=jnp.float32)


def spread(blocks, n_slots):
    terms, rows, width = blocks.shape
    pieces = blocks.reshape(terms, n_slots, rows // n_slots, width).swapaxes(0, 1)
    return lax.all_to_all(pieces, "sec", split_axis=0, concat_axis=0)


def collect(merged):
    n_slots, rows, width = merged.shape
    home = lax.all_to_all(merged, "sec", split_axis=0, concat_axis=0)
    return home.reshape(n_slots * rows, width)


def share(values, n_slots, me):
    lanes = jnp.zeros((1, 128), jnp.float32).at[0, : values.shape[0]].set(values)
    if n_slots & (n_slots - 1) or n_slots > 16:
        return lax.all_gather(lanes[0], "sec")
    table = jnp.where(jnp.arange(n_slots)[:, None] == me, lanes, 0.0)
    for offset in range(1, n_slots):
        pairs = [(i, i ^ offset) for i in range(n_slots)]
        other = lax.ppermute(lanes, "sec", pairs)
        table = jnp.where(jnp.arange(n_slots)[:, None] == (me ^ offset), other, table)
    return table


def merge(received, sources, allowed):
    total = 0.0
    for term, (source, permitted) in enumerate(zip(sources, allowed)):
        picked = received[source, term]
        total = total + jnp.where(permitted[:, None, None], picked, 0).astype(jnp.float32)
    return total


def on_device_any(amplitudes, widths, holders, left_env, right_env):
    slots_dev, right_dim, half_width = amplitudes.shape
    assert slots_dev == 1
    n_slots = holders.shape[0]
    me = lax.axis_index("sec")
    side = lax.axis_index("env")
    my_width = widths[holders[me]]
    row_index = side * half_width + jnp.arange(half_width, dtype=jnp.int32)
    live = (row_index < my_width)[None, :]
    sources, allowed = route(holders)
    envs = left_env[0]

    start = jnp.where(live, amplitudes[0], jnp.zeros_like(amplitudes[0]))
    start_full = lax.all_gather(start, "env", axis=1, tiled=True)
    outgoing = contract(start_full, envs, right_env).astype(jnp.bfloat16)
    stay = outgoing[0].astype(jnp.float32)
    received = spread(outgoing[1:], n_slots)
    arrived = collect(merge(received, sources, allowed).astype(jnp.bfloat16))
    first = jnp.where(live, stay + arrived.astype(jnp.float32), 0.0).astype(jnp.bfloat16)

    first_full = lax.all_gather(first, "env", axis=1, tiled=True).astype(jnp.float32)
    basis = start_full.astype(jnp.float32)
    overlap = jnp.sum(basis * first_full)
    norm = jnp.sum(basis * basis)
    own_quotient = jnp.where(norm > 0, overlap / jnp.where(norm > 0, norm, 1.0), 0.0)
    deflated = first_full - own_quotient * basis
    rest = jnp.sum(deflated * deflated)
    sums = share(jnp.stack([overlap, norm, own_quotient, rest]), n_slots, me)
    outgoing_2 = contract(deflated.astype(jnp.bfloat16), envs, right_env)
    received_2 = spread(outgoing_2[1:].astype(jnp.bfloat16), n_slots)

    quotient = jnp.sum(sums[:, 0]) / jnp.sum(sums[:, 1])
    shift = sums[:, 2] - quotient
    resid_norm = jnp.sum(sums[:, 3] + shift * shift * sums[:, 1])
    live_count = right_dim * jnp.sum(widths).astype(jnp.float32)
    scale = lax.rsqrt(resid_norm / live_count + 1e-06)
    mixed = received_2.astype(jnp.float32) + shift[:, None, None, None] * received.astype(
        jnp.float32
    )
    merged_2 = scale * merge(mixed, sources, allowed)
    arrived_2 = collect(merged_2.astype(jnp.bfloat16))
    stay_2 = scale * (outgoing_2[0] + (own_quotient - quotient) * stay)
    second = jnp.where(live, stay_2 + arrived_2.astype(jnp.float32), 0.0).astype(jnp.bfloat16)
    return first[None], second[None]


LANES = 128
TAG = 16


def find_slot(holders, sector):
    slot = jnp.int32(0)
    for s in range(holders.shape[0]):
        slot = slot + jnp.where(holders[s] == sector, s, 0)
    return slot


def live_columns(widths, holders, half, side):
    width = widths[holders[lax.axis_index("sec")]]
    columns = side * half + lax.broadcasted_iota(jnp.int32, (1, half), 1)
    return columns < width


def start_copies(left, left_vmem, sems):
    copies = []
    for term in (1, 2, 0):
        copy = pltpu.make_async_copy(left.at[0, term], left_vmem.at[term], sems.at[term])
        copy.start()
        copies.append((term, copy))
    return copies


def apply_term(right, left_vmem, vector, term):
    products = jnp.dot(right[term], vector, preferred_element_type=jnp.float32)
    return jnp.dot(
        products.astype(jnp.bfloat16), left_vmem[term], preferred_element_type=jnp.float32
    )


def first_kernel(widths, holders, amps, right, left, message, stay, left_vmem, sems):
    rows, half = stay.shape
    copies = start_copies(left, left_vmem, sems)
    vector = jnp.concatenate(
        [
            jnp.where(live_columns(widths, holders, half, h), amps[h], jnp.zeros_like(amps[h]))
            for h in range(2)
        ],
        axis=1,
    )
    for term, copy in copies:
        copy.wait()
        block = apply_term(right, left_vmem, vector, term).astype(jnp.bfloat16)
        if term == 0:
            stay[...] = block
        else:
            message[pl.ds((term - 1) * rows, rows), :] = block


def fetch(holders, gathered, first_row, rows, blocks, sems):
    sector = holders[lax.axis_index("sec")]
    sources = (find_slot(holders, sector & (QDOWN - 1)), find_slot(holders, sector - 1))
    copies = []
    for i, source in enumerate(sources):
        place = gathered.at[source, pl.ds(first_row + i * rows, rows)]
        copy = pltpu.make_async_copy(place, blocks.at[i], sems.at[i])
        copy.start()
        copies.append(copy)
    return copies


def incoming(holders, blocks):
    sector = holders[lax.axis_index("sec")]
    has = (sector >= QDOWN, sector % QDOWN > 0)
    return [jnp.where(has[i], blocks[i].astype(jnp.float32), 0.0) for i in range(2)]


def sum_kernel(widths, holders, stay, gathered, first, old, sems):
    rows, half = stay.shape
    copies = fetch(holders, gathered, 0, rows, old, sems)
    live = live_columns(widths, holders, half, lax.axis_index("env"))
    for copy in copies:
        copy.wait()
    block_1, block_2 = incoming(holders, old)
    total = stay[...].astype(jnp.float32) + block_1 + block_2
    first[...] = jnp.where(live, total, 0.0).astype(jnp.bfloat16)


def total_of(array):
    return jnp.sum(jnp.sum(array, axis=0, keepdims=True), axis=1, keepdims=True)


def make_tag(values, sector):
    row = lax.broadcasted_iota(jnp.int32, (TAG, LANES), 0)
    lane = lax.broadcasted_iota(jnp.int32, (TAG, LANES), 1)
    spread = jnp.zeros((TAG, LANES), jnp.float32)
    for place, value in enumerate(values):
        spread = jnp.where(row // 3 == place, value, spread)
    high = spread.astype(jnp.bfloat16).astype(jnp.float32)
    middle = (spread - high).astype(jnp.bfloat16).astype(jnp.float32)
    low = spread - high - middle
    parts = jnp.where(row % 3 == 0, high, jnp.where(row % 3 == 1, middle, low))
    return jnp.where((lane == sector) & (row < 3 * len(values)), parts, 0.0).astype(jnp.bfloat16)


def second_kernel(widths, holders, amps, first, right, left, message, stay, left_vmem, sems):
    rows, half = stay.shape
    copies = start_copies(left, left_vmem, sems)
    basis = [
        jnp.where(
            live_columns(widths, holders, half, h), amps[h].astype(jnp.float32), 0.0
        )
        for h in range(2)
    ]
    firsts = [first[h].astype(jnp.float32) for h in range(2)]
    overlap = total_of(basis[0] * firsts[0]) + total_of(basis[1] * firsts[1])
    norm = total_of(basis[0] * basis[0]) + total_of(basis[1] * basis[1])
    quotient = jnp.where(norm > 0, overlap / jnp.where(norm > 0, norm, 1.0), 0.0)
    deflated = [firsts[h] - quotient * basis[h] for h in range(2)]
    rest = total_of(deflated[0] * deflated[0]) + total_of(deflated[1] * deflated[1])
    vector = jnp.concatenate(deflated, axis=1).astype(jnp.bfloat16)
    sector = holders[lax.axis_index("sec")]
    message[pl.ds(0, TAG), pl.ds(0, LANES)] = make_tag((overlap, norm, quotient, rest), sector)
    message[pl.ds(0, TAG), pl.ds(LANES, half - LANES)] = jnp.zeros(
        (TAG, half - LANES), jnp.bfloat16
    )
    for term, copy in copies:
        copy.wait()
        block = apply_term(right, left_vmem, vector, term)
        if term == 0:
            stay[...] = block
        else:
            message[pl.ds(TAG + (term - 1) * rows, rows), :] = block.astype(jnp.bfloat16)


def final_kernel(widths, holders, stay, old, stay_2, gathered, second, tags, blocks, sems):
    rows, half = stay.shape
    slots = holders.shape[0]
    tag_copy = pltpu.make_async_copy(
        gathered.at[:, pl.ds(0, TAG), pl.ds(0, LANES)], tags, sems.at[2]
    )
    tag_copy.start()
    copies = fetch(holders, gathered, TAG, rows, blocks, sems)
    sector = holders[lax.axis_index("sec")]
    live = live_columns(widths, holders, half, lax.axis_index("env"))
    total = jnp.int32(0)
    for s in range(slots):
        total = total + widths[s]
    live_count = rows * total.astype(jnp.float32)
    tag_copy.wait()
    table = jnp.sum(tags[...].astype(jnp.float32), axis=0)

    def value(place):
        parts = [table[3 * place + i : 3 * place + i + 1, :] for i in range(3)]
        return parts[0] + parts[1] + parts[2]

    overlaps, norms, quotients, rests = (value(place) for place in range(4))
    quotient = total_of(overlaps) / total_of(norms)
    lane = lax.broadcasted_iota(jnp.int32, (1, LANES), 1)
    shifts = jnp.where(lane < slots, quotients - quotient, 0.0)
    resid_norm = total_of(rests + shifts * shifts * norms)
    scale = lax.rsqrt(resid_norm / live_count + 1e-06)

    def shift_of(source):
        return total_of(jnp.where(lane == source, shifts, 0.0))

    old_1, old_2 = incoming(holders, old)
    result = stay_2[...] + shift_of(sector) * stay[...].astype(jnp.float32)
    result = result + shift_of(sector - QDOWN) * old_1 + shift_of(sector - 1) * old_2
    for copy in copies:
        copy.wait()
    new_1, new_2 = incoming(holders, blocks)
    result = result + new_1 + new_2
    second[...] = jnp.where(live, scale * result, 0.0).astype(jnp.bfloat16)


SMEM = pl.BlockSpec(memory_space=pltpu.SMEM)
VMEM = pl.BlockSpec(memory_space=pltpu.VMEM)
HBM = pl.BlockSpec(memory_space=pltpu.HBM)
PARAMS = pltpu.CompilerParams(vmem_limit_bytes=16 * 1024 * 1024)


def on_device(amplitudes, widths, holders, left_env, right_env):
    slots_dev, right_dim, half = amplitudes.shape
    n_slots = holders.shape[0]
    assert slots_dev == 1
    if n_slots != 2 * QDOWN:
        return on_device_any(amplitudes, widths, holders, left_env, right_env)
    block = jax.ShapeDtypeStruct((right_dim, half), jnp.bfloat16)
    wide = jax.ShapeDtypeStruct((right_dim, half), jnp.float32)
    pair = jax.ShapeDtypeStruct((2, right_dim, half), jnp.bfloat16)
    plain = jax.ShapeDtypeStruct((2 * right_dim, half), jnp.bfloat16)
    tagged = jax.ShapeDtypeStruct((TAG + 2 * right_dim, half), jnp.bfloat16)
    left_scratch = [
        pltpu.VMEM(left_env.shape[1:], jnp.bfloat16),
        pltpu.SemaphoreType.DMA((left_env.shape[1],)),
    ]

    amps_full = lax.all_gather(amplitudes[0], "env")
    message, stay = pl.pallas_call(
        first_kernel,
        out_shape=(plain, block),
        in_specs=[SMEM, SMEM, VMEM, VMEM, HBM],
        out_specs=(VMEM, VMEM),
        scratch_shapes=left_scratch,
        compiler_params=PARAMS,
    )(widths, holders, amps_full, right_env, left_env)
    gathered = lax.all_gather(message, "sec")
    first, old = pl.pallas_call(
        sum_kernel,
        out_shape=(block, pair),
        in_specs=[SMEM, SMEM, VMEM, HBM],
        out_specs=(VMEM, VMEM),
        scratch_shapes=[pltpu.SemaphoreType.DMA((2,))],
        compiler_params=PARAMS,
    )(widths, holders, stay, gathered)

    first_full = lax.all_gather(first, "env")
    message, stay_2 = pl.pallas_call(
        second_kernel,
        out_shape=(tagged, wide),
        in_specs=[SMEM, SMEM, VMEM, VMEM, VMEM, HBM],
        out_specs=(VMEM, VMEM),
        scratch_shapes=left_scratch,
        compiler_params=PARAMS,
    )(widths, holders, amps_full, first_full, right_env, left_env)
    gathered = lax.all_gather(message, "sec")
    second = pl.pallas_call(
        final_kernel,
        out_shape=block,
        in_specs=[SMEM, SMEM, VMEM, VMEM, VMEM, HBM],
        out_specs=VMEM,
        scratch_shapes=[
            pltpu.VMEM((n_slots, TAG, LANES), jnp.bfloat16),
            pltpu.VMEM((2, right_dim, half), jnp.bfloat16),
            pltpu.SemaphoreType.DMA((3,)),
        ],
        compiler_params=PARAMS,
    )(widths, holders, stay, old, stay_2, gathered)
    return first[None], second[None]


def solution(mesh):
    in_specs = (
        P(("runs", "sec"), None, "env"),
        P("runs"),
        P("runs"),
        P(("runs", "sec"), None, None, "env"),
        P("runs", None, None),
    )
    out_specs = (P(("runs", "sec"), None, "env"), P(("runs", "sec"), None, "env"))
    return jax.shard_map(
        on_device, mesh=mesh, in_specs=in_specs, out_specs=out_specs, check_vma=False
    )
```

```python
import jax
import jax.numpy as jnp
from jax import lax
from jax.experimental import pallas as pl
from jax.experimental.pallas import tpu as pltpu
from jax.sharding import PartitionSpec as P

QDOWN = 4

term_shifts = ((0, 0), (1, 0), (0, 1))


def route(holders):
    n_slots = holders.shape[0]
    sector_ids = jnp.arange(n_slots, dtype=jnp.int32)
    slot_of = jnp.argmax(holders[None, :] == sector_ids[:, None], axis=1)
    sources = []
    allowed = []
    for up, down in term_shifts[1:]:
        permitted = (holders // QDOWN - up >= 0) & (holders % QDOWN - down >= 0)
        wanted = jnp.clip(holders - QDOWN * up - down, 0, n_slots - 1)
        sources.append(slot_of[wanted])
        allowed.append(permitted)
    return sources, allowed


def contract(vector, left_env, right_env):
    products = jnp.einsum(
        "tij,jw->tiw", right_env, vector, preferred_element_type=jnp.float32
    ).astype(jnp.bfloat16)
    return jnp.einsum("tik,tkw->tiw", products, left_env, preferred_element_type=jnp.float32)


def spread(blocks, n_slots):
    terms, rows, width = blocks.shape
    pieces = blocks.reshape(terms, n_slots, rows // n_slots, width).swapaxes(0, 1)
    return lax.all_to_all(pieces, "sec", split_axis=0, concat_axis=0)


def collect(merged):
    n_slots, rows, width = merged.shape
    home = lax.all_to_all(merged, "sec", split_axis=0, concat_axis=0)
    return home.reshape(n_slots * rows, width)


def share(values, n_slots, me):
    lanes = jnp.zeros((1, 128), jnp.float32).at[0, : values.shape[0]].set(values)
    if n_slots & (n_slots - 1) or n_slots > 16:
        return lax.all_gather(lanes[0], "sec")
    table = jnp.where(jnp.arange(n_slots)[:, None] == me, lanes, 0.0)
    for offset in range(1, n_slots):
        pairs = [(i, i ^ offset) for i in range(n_slots)]
        other = lax.ppermute(lanes, "sec", pairs)
        table = jnp.where(jnp.arange(n_slots)[:, None] == (me ^ offset), other, table)
    return table


def merge(received, sources, allowed):
    total = 0.0
    for term, (source, permitted) in enumerate(zip(sources, allowed)):
        picked = received[source, term]
        total = total + jnp.where(permitted[:, None, None], picked, 0).astype(jnp.float32)
    return total


def on_device_any(amplitudes, widths, holders, left_env, right_env):
    slots_dev, right_dim, half_width = amplitudes.shape
    assert slots_dev == 1
    n_slots = holders.shape[0]
    me = lax.axis_index("sec")
    side = lax.axis_index("env")
    my_width = widths[holders[me]]
    row_index = side * half_width + jnp.arange(half_width, dtype=jnp.int32)
    live = (row_index < my_width)[None, :]
    sources, allowed = route(holders)
    envs = left_env[0]

    start = jnp.where(live, amplitudes[0], jnp.zeros_like(amplitudes[0]))
    start_full = lax.all_gather(start, "env", axis=1, tiled=True)
    outgoing = contract(start_full, envs, right_env).astype(jnp.bfloat16)
    stay = outgoing[0].astype(jnp.float32)
    received = spread(outgoing[1:], n_slots)
    arrived = collect(merge(received, sources, allowed).astype(jnp.bfloat16))
    first = jnp.where(live, stay + arrived.astype(jnp.float32), 0.0).astype(jnp.bfloat16)

    first_full = lax.all_gather(first, "env", axis=1, tiled=True).astype(jnp.float32)
    basis = start_full.astype(jnp.float32)
    overlap = jnp.sum(basis * first_full)
    norm = jnp.sum(basis * basis)
    own_quotient = jnp.where(norm > 0, overlap / jnp.where(norm > 0, norm, 1.0), 0.0)
    deflated = first_full - own_quotient * basis
    rest = jnp.sum(deflated * deflated)
    sums = share(jnp.stack([overlap, norm, own_quotient, rest]), n_slots, me)
    outgoing_2 = contract(deflated.astype(jnp.bfloat16), envs, right_env)
    received_2 = spread(outgoing_2[1:].astype(jnp.bfloat16), n_slots)

    quotient = jnp.sum(sums[:, 0]) / jnp.sum(sums[:, 1])
    shift = sums[:, 2] - quotient
    resid_norm = jnp.sum(sums[:, 3] + shift * shift * sums[:, 1])
    live_count = right_dim * jnp.sum(widths).astype(jnp.float32)
    scale = lax.rsqrt(resid_norm / live_count + 1e-06)
    mixed = received_2.astype(jnp.float32) + shift[:, None, None, None] * received.astype(
        jnp.float32
    )
    merged_2 = scale * merge(mixed, sources, allowed)
    arrived_2 = collect(merged_2.astype(jnp.bfloat16))
    stay_2 = scale * (outgoing_2[0] + (own_quotient - quotient) * stay)
    second = jnp.where(live, stay_2 + arrived_2.astype(jnp.float32), 0.0).astype(jnp.bfloat16)
    return first[None], second[None]


LANES = 128


def find_slot(holders, sector):
    slot = jnp.int32(0)
    for s in range(holders.shape[0]):
        slot = slot + jnp.where(holders[s] == sector, s, 0)
    return slot


def live_columns(widths, holders, half, side):
    width = widths[holders[lax.axis_index("sec")]]
    columns = side * half + lax.broadcasted_iota(jnp.int32, (1, half), 1)
    return columns < width


def apply_term(right, left, vector, term):
    products = jnp.dot(right[term], vector, preferred_element_type=jnp.float32)
    return jnp.dot(products.astype(jnp.bfloat16), left, preferred_element_type=jnp.float32)


def store_message(full, part, block):
    block = block.astype(full.dtype)
    full[...] = block
    part[...] = block[:, : part.shape[1]]


def write_plan(widths, holders, half, turns, flags):
    me = lax.axis_index("sec")
    side = lax.axis_index("env")
    sector = holders[me]
    down = sector % QDOWN
    inner = (down == 1) | (down == 2)
    plan = (
        (sector ^ QDOWN, sector | QDOWN, True),
        (sector ^ 1, sector | 1, True),
        (sector ^ 3, sector - down + 2, inner),
    )
    for step, (partner, target, used) in enumerate(plan):
        offset = me ^ find_slot(holders, partner)
        columns = jnp.where(used, widths[target] - side * half, 0)
        kind = jnp.where(columns > half // 2, 2, 1)
        turns[step][0] = jnp.where(columns > 0, (offset - 1) * 2 + kind, 0)
    flags[0] = widths[sector] - side * half
    flags[1] = jnp.where(sector >= QDOWN, 1, 0)
    flags[2] = jnp.where(down % 2 == 1, 1, 0)
    flags[3] = jnp.where(down == 2, 1, 0)


def first_kernel(
    widths,
    holders,
    amps,
    right,
    left,
    full_1,
    part_1,
    full_2,
    part_2,
    stay,
    turn_1,
    turn_2,
    turn_3,
    flags,
    left_vmem,
    sems,
):
    half = amps.shape[2]
    copies = []
    for term in (1, 2, 0):
        copy = pltpu.make_async_copy(left.at[0, term], left_vmem.at[term], sems.at[term])
        copy.start()
        copies.append((term, copy))
    write_plan(widths, holders, half, (turn_1, turn_2, turn_3), flags)
    vector = jnp.concatenate(
        [
            jnp.where(live_columns(widths, holders, half, h), amps[h], jnp.zeros_like(amps[h]))
            for h in range(2)
        ],
        axis=1,
    )
    for term, copy in copies:
        copy.wait()
        block = apply_term(right, left_vmem[term], vector, term)
        if term == 0:
            stay[...] = block.astype(jnp.bfloat16)
        else:
            store_message(*((full_1, part_1), (full_2, part_2))[term - 1], block)


def total_of(array):
    return jnp.sum(jnp.sum(array, axis=0, keepdims=True), axis=1, keepdims=True)


def second_kernel(
    widths, holders, amps, first, right, left, full_1, part_1, full_2, part_2, stay, tag
):
    half = amps.shape[2]
    basis = [
        jnp.where(
            live_columns(widths, holders, half, h), amps[h].astype(jnp.float32), 0.0
        )
        for h in range(2)
    ]
    firsts = [first[h].astype(jnp.float32) for h in range(2)]
    overlap = total_of(basis[0] * firsts[0]) + total_of(basis[1] * firsts[1])
    norm = total_of(basis[0] * basis[0]) + total_of(basis[1] * basis[1])
    quotient = jnp.where(norm > 0, overlap / jnp.where(norm > 0, norm, 1.0), 0.0)
    deflated = [firsts[h] - quotient * basis[h] for h in range(2)]
    rest = total_of(deflated[0] * deflated[0]) + total_of(deflated[1] * deflated[1])
    vector = jnp.concatenate(deflated, axis=1).astype(jnp.bfloat16)

    row = lax.broadcasted_iota(jnp.int32, tag.shape, 0)
    values = jnp.zeros(tag.shape, jnp.float32)
    for place, value in enumerate((overlap, norm, quotient, rest)):
        values = jnp.where(row == place, value, values)
    tag[...] = values

    for term in (1, 2, 0):
        block = apply_term(right, left[0, term], vector, term)
        if term == 0:
            stay[...] = block
        else:
            store_message(*((full_1, part_1), (full_2, part_2))[term - 1], block)


def incoming(holders, arrived_1, arrived_2, arrived_3):
    sector = holders[lax.axis_index("sec")]
    down = sector % QDOWN
    block_1, block_2, block_3 = (
        arrived[...].astype(jnp.float32) for arrived in (arrived_1, arrived_2, arrived_3)
    )
    block_1 = jnp.where(sector >= QDOWN, block_1, 0.0)
    block_2 = jnp.where(down % 2 == 1, block_2, jnp.where(down == 2, block_3, 0.0))
    return block_1, block_2


def final_kernel(
    widths, holders, tags, stay, stay_2, old_1, old_2, old_3, new_1, new_2, new_3, second
):
    rows, half = stay.shape
    slots = holders.shape[0]
    me = lax.axis_index("sec")
    sector = holders[me]
    live = live_columns(widths, holders, half, lax.axis_index("env"))
    total = jnp.int32(0)
    for s in range(slots):
        total = total + widths[s]
    live_count = rows * total.astype(jnp.float32)
    overlaps, norms, quotients, rests = (tags[:, i, :] for i in range(4))
    quotient = jnp.sum(overlaps, axis=0, keepdims=True) / jnp.sum(norms, axis=0, keepdims=True)
    shifts = quotients - quotient
    resid_norm = jnp.sum(rests + shifts * shifts * norms, axis=0, keepdims=True)
    scale = lax.rsqrt(resid_norm / live_count + 1e-06)[:, :1]
    slot = lax.broadcasted_iota(jnp.int32, shifts.shape, 0)

    def shift_of(source):
        picked = jnp.where(slot == find_slot(holders, source), shifts, 0.0)
        return jnp.sum(picked, axis=0, keepdims=True)[:, :1]

    old_block_1, old_block_2 = incoming(holders, old_1, old_2, old_3)
    new_block_1, new_block_2 = incoming(holders, new_1, new_2, new_3)
    result = stay_2[...] + shift_of(sector) * stay[...].astype(jnp.float32)
    result = result + new_block_1 + shift_of(sector - QDOWN) * old_block_1
    result = result + new_block_2 + shift_of(sector - 1) * old_block_2
    second[...] = jnp.where(live, scale * result, 0.0).astype(jnp.bfloat16)


SMEM = pl.BlockSpec(memory_space=pltpu.SMEM)
VMEM = pl.BlockSpec(memory_space=pltpu.VMEM)
HBM = pl.BlockSpec(memory_space=pltpu.HBM)
SMALL = pltpu.CompilerParams(vmem_limit_bytes=16 * 1024 * 1024)
LARGE = pltpu.CompilerParams(vmem_limit_bytes=61 * 1024 * 1024)


def choose(index, branches, *operands):
    jaxprs = tuple(jax.make_jaxpr(branch)(*operands) for branch in branches)
    return lax.cond_p.bind(index.reshape(()), *operands, branches=jaxprs)


def exchange(turn, full, part, n_slots):
    def swap_part(offset):
        pairs = [(i, i ^ offset) for i in range(n_slots)]
        missing = full.shape[1] - part.shape[1]
        return lambda full, part: [
            jnp.pad(lax.ppermute(part, "sec", pairs), ((0, 0), (0, missing)))
        ]

    def swap_full(offset):
        pairs = [(i, i ^ offset) for i in range(n_slots)]
        return lambda full, part: [lax.ppermute(full, "sec", pairs)]

    branches = [lambda full, part: [jnp.zeros_like(full)]]
    for offset in range(1, n_slots):
        branches += [swap_part(offset), swap_full(offset)]
    (arrived,) = choose(turn, branches, full, part)
    return arrived


def on_device(amplitudes, widths, holders, left_env, right_env):
    slots_dev, right_dim, half = amplitudes.shape
    n_slots = holders.shape[0]
    assert slots_dev == 1
    if n_slots != 2 * QDOWN:
        return on_device_any(amplitudes, widths, holders, left_env, right_env)
    part = jax.ShapeDtypeStruct((right_dim, half // 2), jnp.bfloat16)
    block = jax.ShapeDtypeStruct((right_dim, half), jnp.bfloat16)
    wide = jax.ShapeDtypeStruct((right_dim, half), jnp.float32)
    tag_shape = jax.ShapeDtypeStruct((8, LANES), jnp.float32)
    turn = jax.ShapeDtypeStruct((1,), jnp.int32)

    amps_full = lax.all_gather(amplitudes[0], "env")
    full_1, part_1, full_2, part_2, stay, turn_1, turn_2, turn_3, flags = pl.pallas_call(
        first_kernel,
        out_shape=(block, part) * 2
        + (block, turn, turn, turn, jax.ShapeDtypeStruct((4,), jnp.int32)),
        in_specs=[SMEM, SMEM, VMEM, VMEM, HBM],
        out_specs=(VMEM,) * 5 + (SMEM,) * 4,
        scratch_shapes=[
            pltpu.VMEM(left_env.shape[1:], jnp.bfloat16),
            pltpu.SemaphoreType.DMA((left_env.shape[1],)),
        ],
        compiler_params=LARGE,
    )(widths, holders, amps_full, right_env, left_env)
    old_1 = exchange(turn_1, full_1, part_1, n_slots)
    old_2 = exchange(turn_2, full_2, part_2, n_slots)
    old_3 = exchange(turn_3, full_2, part_2, n_slots)
    live = lax.broadcasted_iota(jnp.int32, (right_dim, half), 1) < flags[0]
    total = stay.astype(jnp.float32) + jnp.where(flags[1] > 0, old_1, 0).astype(jnp.float32)
    side_block = jnp.where(flags[2] > 0, old_2, jnp.where(flags[3] > 0, old_3, 0))
    total = total + side_block.astype(jnp.float32)
    first = jnp.where(live, total, 0.0).astype(jnp.bfloat16)

    first_full = lax.all_gather(first, "env")
    full_1, part_1, full_2, part_2, stay_2, tag = pl.pallas_call(
        second_kernel,
        out_shape=(block, part) * 2 + (wide, tag_shape),
        in_specs=[SMEM, SMEM, VMEM, VMEM, VMEM, VMEM],
        out_specs=(VMEM,) * 6,
        compiler_params=SMALL,
    )(widths, holders, amps_full, first_full, right_env, left_env)
    tags = lax.all_gather(tag, "sec")
    new_1 = exchange(turn_1, full_1, part_1, n_slots)
    new_2 = exchange(turn_2, full_2, part_2, n_slots)
    new_3 = exchange(turn_3, full_2, part_2, n_slots)
    second = pl.pallas_call(
        final_kernel,
        out_shape=block,
        in_specs=[SMEM, SMEM] + [VMEM] * 9,
        out_specs=VMEM,
        compiler_params=SMALL,
    )(widths, holders, tags, stay, stay_2, old_1, old_2, old_3, new_1, new_2, new_3)
    return first[None], second[None]


def solution(mesh):
    in_specs = (
        P(("runs", "sec"), None, "env"),
        P("runs"),
        P("runs"),
        P(("runs", "sec"), None, None, "env"),
        P("runs", None, None),
    )
    out_specs = (P(("runs", "sec"), None, "env"), P(("runs", "sec"), None, "env"))
    return jax.shard_map(
        on_device, mesh=mesh, in_specs=in_specs, out_specs=out_specs, check_vma=False
    )
```

```python
import jax
import jax.numpy as jnp
from jax import lax
from jax.experimental import pallas as pl
from jax.experimental.pallas import tpu as pltpu
from jax.sharding import PartitionSpec as P

QDOWN = 4

term_shifts = ((0, 0), (1, 0), (0, 1))


def route(holders):
    n_slots = holders.shape[0]
    sector_ids = jnp.arange(n_slots, dtype=jnp.int32)
    slot_of = jnp.argmax(holders[None, :] == sector_ids[:, None], axis=1)
    sources = []
    allowed = []
    for up, down in term_shifts[1:]:
        permitted = (holders // QDOWN - up >= 0) & (holders % QDOWN - down >= 0)
        wanted = jnp.clip(holders - QDOWN * up - down, 0, n_slots - 1)
        sources.append(slot_of[wanted])
        allowed.append(permitted)
    return sources, allowed


def contract(vector, left_env, right_env):
    products = jnp.einsum(
        "tij,jw->tiw", right_env, vector, preferred_element_type=jnp.float32
    ).astype(jnp.bfloat16)
    return jnp.einsum("tik,tkw->tiw", products, left_env, preferred_element_type=jnp.float32)


def spread(blocks, n_slots):
    terms, rows, width = blocks.shape
    pieces = blocks.reshape(terms, n_slots, rows // n_slots, width).swapaxes(0, 1)
    return lax.all_to_all(pieces, "sec", split_axis=0, concat_axis=0)


def collect(merged):
    n_slots, rows, width = merged.shape
    home = lax.all_to_all(merged, "sec", split_axis=0, concat_axis=0)
    return home.reshape(n_slots * rows, width)


def share(values, n_slots, me):
    lanes = jnp.zeros((1, 128), jnp.float32).at[0, : values.shape[0]].set(values)
    if n_slots & (n_slots - 1) or n_slots > 16:
        return lax.all_gather(lanes[0], "sec")
    table = jnp.where(jnp.arange(n_slots)[:, None] == me, lanes, 0.0)
    for offset in range(1, n_slots):
        pairs = [(i, i ^ offset) for i in range(n_slots)]
        other = lax.ppermute(lanes, "sec", pairs)
        table = jnp.where(jnp.arange(n_slots)[:, None] == (me ^ offset), other, table)
    return table


def merge(received, sources, allowed):
    total = 0.0
    for term, (source, permitted) in enumerate(zip(sources, allowed)):
        picked = received[source, term]
        total = total + jnp.where(permitted[:, None, None], picked, 0).astype(jnp.float32)
    return total


def on_device_any(amplitudes, widths, holders, left_env, right_env):
    slots_dev, right_dim, half_width = amplitudes.shape
    assert slots_dev == 1
    n_slots = holders.shape[0]
    me = lax.axis_index("sec")
    side = lax.axis_index("env")
    my_width = widths[holders[me]]
    row_index = side * half_width + jnp.arange(half_width, dtype=jnp.int32)
    live = (row_index < my_width)[None, :]
    sources, allowed = route(holders)
    envs = left_env[0]

    start = jnp.where(live, amplitudes[0], jnp.zeros_like(amplitudes[0]))
    start_full = lax.all_gather(start, "env", axis=1, tiled=True)
    outgoing = contract(start_full, envs, right_env).astype(jnp.bfloat16)
    stay = outgoing[0].astype(jnp.float32)
    received = spread(outgoing[1:], n_slots)
    arrived = collect(merge(received, sources, allowed).astype(jnp.bfloat16))
    first = jnp.where(live, stay + arrived.astype(jnp.float32), 0.0).astype(jnp.bfloat16)

    first_full = lax.all_gather(first, "env", axis=1, tiled=True).astype(jnp.float32)
    basis = start_full.astype(jnp.float32)
    overlap = jnp.sum(basis * first_full)
    norm = jnp.sum(basis * basis)
    own_quotient = jnp.where(norm > 0, overlap / jnp.where(norm > 0, norm, 1.0), 0.0)
    deflated = first_full - own_quotient * basis
    rest = jnp.sum(deflated * deflated)
    sums = share(jnp.stack([overlap, norm, own_quotient, rest]), n_slots, me)
    outgoing_2 = contract(deflated.astype(jnp.bfloat16), envs, right_env)
    received_2 = spread(outgoing_2[1:].astype(jnp.bfloat16), n_slots)

    quotient = jnp.sum(sums[:, 0]) / jnp.sum(sums[:, 1])
    shift = sums[:, 2] - quotient
    resid_norm = jnp.sum(sums[:, 3] + shift * shift * sums[:, 1])
    live_count = right_dim * jnp.sum(widths).astype(jnp.float32)
    scale = lax.rsqrt(resid_norm / live_count + 1e-06)
    mixed = received_2.astype(jnp.float32) + shift[:, None, None, None] * received.astype(
        jnp.float32
    )
    merged_2 = scale * merge(mixed, sources, allowed)
    arrived_2 = collect(merged_2.astype(jnp.bfloat16))
    stay_2 = scale * (outgoing_2[0] + (own_quotient - quotient) * stay)
    second = jnp.where(live, stay_2 + arrived_2.astype(jnp.float32), 0.0).astype(jnp.bfloat16)
    return first[None], second[None]


LANES = 128
TAG = 16


def live_columns(widths, holders, half, side):
    width = widths[holders[lax.axis_index("sec")]]
    columns = side * half + lax.broadcasted_iota(jnp.int32, (1, half), 1)
    return columns < width


def start_copies(left, left_vmem, sems):
    copies = []
    for term in (1, 2, 0):
        copy = pltpu.make_async_copy(left.at[0, term], left_vmem.at[term], sems.at[term])
        copy.start()
        copies.append((term, copy))
    return copies


def apply_term(right, left, vector, term):
    products = jnp.dot(right[term], vector, preferred_element_type=jnp.float32)
    return jnp.dot(products.astype(jnp.bfloat16), left, preferred_element_type=jnp.float32)


def first_kernel(widths, holders, amps, right, left, *rest):
    slots = holders.shape[0]
    pieces = rest[:slots]
    stay, left_vmem, block_vmem, sems = rest[slots:]
    half = amps.shape[2]
    rows = pieces[0].shape[1]
    me = lax.axis_index("sec")
    copies = start_copies(left, left_vmem, sems)
    vector = jnp.concatenate(
        [
            jnp.where(live_columns(widths, holders, half, h), amps[h], jnp.zeros_like(amps[h]))
            for h in range(2)
        ],
        axis=1,
    )
    for term, copy in copies:
        copy.wait()
        block = apply_term(right, left_vmem[term], vector, term).astype(jnp.bfloat16)
        if term == 0:
            stay[...] = block
        else:
            block_vmem[...] = block.reshape(block_vmem.shape)
            for offset in range(slots):
                pieces[offset][term - 1] = block_vmem[me ^ offset]


def fill_slots(holders, slot_of):
    for s in range(holders.shape[0]):
        slot_of[holders[s]] = jnp.int32(s)


def sources_of(holders, slot_of, target):
    sector = holders[target]
    has = (sector >= QDOWN, sector % QDOWN > 0)
    source = (slot_of[sector & (QDOWN - 1)], slot_of[jnp.maximum(sector - 1, 0)])
    return has, source


def merge_kernel(holders, *rest):
    slots = holders.shape[0]
    pieces, outs = rest[:slots], rest[slots : 2 * slots]
    table, slot_of = rest[2 * slots :]
    me = lax.axis_index("sec")
    fill_slots(holders, slot_of)
    for offset in range(slots):
        table[me ^ offset] = pieces[offset][...]
    for offset in range(slots):
        has, source = sources_of(holders, slot_of, me ^ offset)
        total = 0.0
        for i in range(2):
            block = table[source[i], i].astype(jnp.float32)
            total = total + jnp.where(has[i], block, 0.0)
        outs[offset][...] = total.astype(jnp.bfloat16)


def sum_kernel(widths, holders, stay, *rest):
    *pieces, first = rest
    half = stay.shape[1]
    rows = pieces[0].shape[0]
    me = lax.axis_index("sec")
    live = live_columns(widths, holders, half, lax.axis_index("env"))
    for offset, piece in enumerate(pieces):
        place = pl.ds(pl.multiple_of((me ^ offset) * rows, rows), rows)
        total = stay[place, :].astype(jnp.float32) + piece[...].astype(jnp.float32)
        first[place, :] = jnp.where(live, total, 0.0).astype(jnp.bfloat16)


def total_of(array):
    return jnp.sum(jnp.sum(array, axis=0, keepdims=True), axis=1, keepdims=True)


def make_tag(values, me):
    row = lax.broadcasted_iota(jnp.int32, (TAG, LANES), 0)
    lane = lax.broadcasted_iota(jnp.int32, (TAG, LANES), 1)
    spread = jnp.zeros((TAG, LANES), jnp.float32)
    for place, value in enumerate(values):
        spread = jnp.where(row // 3 == place, value, spread)
    high = spread.astype(jnp.bfloat16).astype(jnp.float32)
    middle = (spread - high).astype(jnp.bfloat16).astype(jnp.float32)
    low = spread - high - middle
    parts = jnp.where(row % 3 == 0, high, jnp.where(row % 3 == 1, middle, low))
    return jnp.where((lane == me) & (row < 3 * len(values)), parts, 0.0).astype(jnp.bfloat16)


def second_kernel(widths, holders, amps, first, right, left, *rest):
    slots = holders.shape[0]
    pieces = rest[:slots]
    stay, block_vmem = rest[slots:]
    half = amps.shape[2]
    rows = block_vmem.shape[1]
    chunks = half // LANES
    me = lax.axis_index("sec")
    basis = [
        jnp.where(
            live_columns(widths, holders, half, h), amps[h].astype(jnp.float32), 0.0
        )
        for h in range(2)
    ]
    firsts = [first[h].astype(jnp.float32) for h in range(2)]
    overlap = total_of(basis[0] * firsts[0]) + total_of(basis[1] * firsts[1])
    norm = total_of(basis[0] * basis[0]) + total_of(basis[1] * basis[1])
    quotient = jnp.where(norm > 0, overlap / jnp.where(norm > 0, norm, 1.0), 0.0)
    deflated = [firsts[h] - quotient * basis[h] for h in range(2)]
    rest_norm = total_of(deflated[0] * deflated[0]) + total_of(deflated[1] * deflated[1])
    vector = jnp.concatenate(deflated, axis=1).astype(jnp.bfloat16)
    tag = make_tag((overlap, norm, quotient, rest_norm), me)
    for piece in pieces:
        piece[pl.ds(2 * chunks * rows, TAG), :] = tag
    for term in (1, 2, 0):
        block = apply_term(right, left[0, term], vector, term)
        if term == 0:
            stay[...] = block
        else:
            block_vmem[...] = block.astype(jnp.bfloat16).reshape(block_vmem.shape)
            for offset in range(slots):
                part = block_vmem[me ^ offset]
                for c in range(chunks):
                    place = pl.ds(((term - 1) * chunks + c) * rows, rows)
                    pieces[offset][place, :] = part[:, c * LANES : (c + 1) * LANES]


def mix_kernel(widths, holders, *rest):
    slots = holders.shape[0]
    old, new, outs = rest[:slots], rest[slots : 2 * slots], rest[2 * slots : 3 * slots]
    factors, old_table, new_table, slot_of = rest[3 * slots :]
    rows, half = outs[0].shape
    chunks = half // LANES
    me = lax.axis_index("sec")
    fill_slots(holders, slot_of)
    tag = jnp.zeros((TAG, LANES), jnp.float32)
    for offset in range(slots):
        old_table[me ^ offset] = old[offset][...]
        new_table[me ^ offset] = new[offset][...]
        tag = tag + new[offset][pl.ds(2 * chunks * rows, TAG), :].astype(jnp.float32)
    total = jnp.int32(0)
    for s in range(slots):
        total = total + widths[s]
    live_count = slots * rows * total.astype(jnp.float32)

    def value(place):
        parts = [tag[3 * place + i : 3 * place + i + 1, :] for i in range(3)]
        return parts[0] + parts[1] + parts[2]

    overlaps, norms, quotients, rests = (value(place) for place in range(4))
    quotient = total_of(overlaps) / total_of(norms)
    lane = lax.broadcasted_iota(jnp.int32, (1, LANES), 1)
    shifts = jnp.where(lane < slots, quotients - quotient, 0.0)
    resid_norm = total_of(rests + shifts * shifts * norms)
    scale = lax.rsqrt(resid_norm / live_count + 1e-06)

    def shift_of(slot):
        return total_of(jnp.where(lane == slot, shifts, 0.0))

    row = lax.broadcasted_iota(jnp.int32, factors.shape, 0)
    factors[...] = jnp.where(row == 0, scale, scale * shift_of(me))
    for offset in range(slots):
        has, source = sources_of(holders, slot_of, me ^ offset)
        total = 0.0
        for i in range(2):
            block = jnp.concatenate(
                [
                    new_table[source[i], pl.ds((i * chunks + c) * rows, rows), :]
                    for c in range(chunks)
                ],
                axis=1,
            ).astype(jnp.float32)
            block = block + shift_of(source[i]) * old_table[source[i], i].astype(jnp.float32)
            total = total + jnp.where(has[i], block, 0.0)
        outs[offset][...] = (scale * total).astype(jnp.bfloat16)


def final_kernel(widths, holders, factors, stay, stay_2, *rest):
    *pieces, second = rest
    half = stay.shape[1]
    rows = pieces[0].shape[0]
    me = lax.axis_index("sec")
    live = live_columns(widths, holders, half, lax.axis_index("env"))
    scale, shift = factors[0:1, 0:1], factors[1:2, 0:1]
    for offset, piece in enumerate(pieces):
        place = pl.ds(pl.multiple_of((me ^ offset) * rows, rows), rows)
        total = scale * stay_2[place, :] + shift * stay[place, :].astype(jnp.float32)
        total = total + piece[...].astype(jnp.float32)
        second[place, :] = jnp.where(live, total, 0.0).astype(jnp.bfloat16)


SMEM = pl.BlockSpec(memory_space=pltpu.SMEM)
VMEM = pl.BlockSpec(memory_space=pltpu.VMEM)
HBM = pl.BlockSpec(memory_space=pltpu.HBM)
SMALL = pltpu.CompilerParams(vmem_limit_bytes=16 * 1024 * 1024)
LARGE = pltpu.CompilerParams(vmem_limit_bytes=61 * 1024 * 1024)


def swap_all(pieces):
    slots = len(pieces)
    return [pieces[0]] + [
        lax.ppermute(pieces[offset], "sec", [(i, i ^ offset) for i in range(slots)])
        for offset in range(1, slots)
    ]


def on_device(amplitudes, widths, holders, left_env, right_env):
    slots_dev, right_dim, half = amplitudes.shape
    slots = holders.shape[0]
    assert slots_dev == 1
    if slots != 2 * QDOWN:
        return on_device_any(amplitudes, widths, holders, left_env, right_env)
    rows = right_dim // slots
    block = jax.ShapeDtypeStruct((right_dim, half), jnp.bfloat16)
    wide = jax.ShapeDtypeStruct((right_dim, half), jnp.float32)
    pair = jax.ShapeDtypeStruct((2, rows, half), jnp.bfloat16)
    single = jax.ShapeDtypeStruct((rows, half), jnp.bfloat16)
    tagged = jax.ShapeDtypeStruct((2 * rows * half // LANES + TAG, LANES), jnp.bfloat16)
    factor_shape = jax.ShapeDtypeStruct((8, LANES), jnp.float32)
    split = pltpu.VMEM((slots, rows, half), jnp.bfloat16)
    slot_table = pltpu.SMEM((slots,), jnp.int32)

    amps_full = lax.all_gather(amplitudes[0], "env")
    *pieces, stay = pl.pallas_call(
        first_kernel,
        out_shape=(pair,) * slots + (block,),
        in_specs=[SMEM, SMEM, VMEM, VMEM, HBM],
        out_specs=(VMEM,) * (slots + 1),
        scratch_shapes=[
            pltpu.VMEM(left_env.shape[1:], jnp.bfloat16),
            split,
            pltpu.SemaphoreType.DMA((left_env.shape[1],)),
        ],
        compiler_params=LARGE,
    )(widths, holders, amps_full, right_env, left_env)
    old = swap_all(pieces)
    merged = pl.pallas_call(
        merge_kernel,
        out_shape=(single,) * slots,
        in_specs=[SMEM] + [VMEM] * slots,
        out_specs=(VMEM,) * slots,
        scratch_shapes=[pltpu.VMEM((slots, *pair.shape), jnp.bfloat16), slot_table],
        compiler_params=SMALL,
    )(holders, *old)
    first = pl.pallas_call(
        sum_kernel,
        out_shape=block,
        in_specs=[SMEM, SMEM] + [VMEM] * (slots + 1),
        out_specs=VMEM,
        compiler_params=SMALL,
    )(widths, holders, stay, *swap_all(merged))

    first_full = lax.all_gather(first, "env")
    *pieces, stay_2 = pl.pallas_call(
        second_kernel,
        out_shape=(tagged,) * slots + (wide,),
        in_specs=[SMEM, SMEM, VMEM, VMEM, VMEM, VMEM],
        out_specs=(VMEM,) * (slots + 1),
        scratch_shapes=[split],
        compiler_params=SMALL,
    )(widths, holders, amps_full, first_full, right_env, left_env)
    new = swap_all(pieces)
    *mixed, factors = pl.pallas_call(
        mix_kernel,
        out_shape=(single,) * slots + (factor_shape,),
        in_specs=[SMEM, SMEM] + [VMEM] * (2 * slots),
        out_specs=(VMEM,) * (slots + 1),
        scratch_shapes=[
            pltpu.VMEM((slots, *pair.shape), jnp.bfloat16),
            pltpu.VMEM((slots, *tagged.shape), jnp.bfloat16),
            slot_table,
        ],
        compiler_params=SMALL,
    )(widths, holders, *old, *new)
    second = pl.pallas_call(
        final_kernel,
        out_shape=block,
        in_specs=[SMEM, SMEM] + [VMEM] * (slots + 3),
        out_specs=VMEM,
        compiler_params=SMALL,
    )(widths, holders, factors, stay, stay_2, *swap_all(mixed))
    return first[None], second[None]


def solution(mesh):
    in_specs = (
        P(("runs", "sec"), None, "env"),
        P("runs"),
        P("runs"),
        P(("runs", "sec"), None, None, "env"),
        P("runs", None, None),
    )
    out_specs = (P(("runs", "sec"), None, "env"), P(("runs", "sec"), None, "env"))
    return jax.shard_map(
        on_device, mesh=mesh, in_specs=in_specs, out_specs=out_specs, check_vma=False
    )
```

```python
import jax
import jax.numpy as jnp
from jax import lax
from jax.experimental import pallas as pl
from jax.experimental.pallas import tpu as pltpu
from jax.sharding import PartitionSpec as P

QDOWN = 4

term_shifts = ((0, 0), (1, 0), (0, 1))


def route(holders):
    n_slots = holders.shape[0]
    sector_ids = jnp.arange(n_slots, dtype=jnp.int32)
    slot_of = jnp.argmax(holders[None, :] == sector_ids[:, None], axis=1)
    sources = []
    allowed = []
    for up, down in term_shifts[1:]:
        permitted = (holders // QDOWN - up >= 0) & (holders % QDOWN - down >= 0)
        wanted = jnp.clip(holders - QDOWN * up - down, 0, n_slots - 1)
        sources.append(slot_of[wanted])
        allowed.append(permitted)
    return sources, allowed


def contract(vector, left_env, right_env):
    products = jnp.einsum(
        "tij,jw->tiw", right_env, vector, preferred_element_type=jnp.float32
    ).astype(jnp.bfloat16)
    return jnp.einsum("tik,tkw->tiw", products, left_env, preferred_element_type=jnp.float32)


def spread(blocks, n_slots):
    terms, rows, width = blocks.shape
    pieces = blocks.reshape(terms, n_slots, rows // n_slots, width).swapaxes(0, 1)
    return lax.all_to_all(pieces, "sec", split_axis=0, concat_axis=0)


def collect(merged):
    n_slots, rows, width = merged.shape
    home = lax.all_to_all(merged, "sec", split_axis=0, concat_axis=0)
    return home.reshape(n_slots * rows, width)


def share(values, n_slots, me):
    lanes = jnp.zeros((1, 128), jnp.float32).at[0, : values.shape[0]].set(values)
    if n_slots & (n_slots - 1) or n_slots > 16:
        return lax.all_gather(lanes[0], "sec")
    table = jnp.where(jnp.arange(n_slots)[:, None] == me, lanes, 0.0)
    for offset in range(1, n_slots):
        pairs = [(i, i ^ offset) for i in range(n_slots)]
        other = lax.ppermute(lanes, "sec", pairs)
        table = jnp.where(jnp.arange(n_slots)[:, None] == (me ^ offset), other, table)
    return table


def merge(received, sources, allowed):
    total = 0.0
    for term, (source, permitted) in enumerate(zip(sources, allowed)):
        picked = received[source, term]
        total = total + jnp.where(permitted[:, None, None], picked, 0).astype(jnp.float32)
    return total


def on_device_any(amplitudes, widths, holders, left_env, right_env):
    slots_dev, right_dim, half_width = amplitudes.shape
    assert slots_dev == 1
    n_slots = holders.shape[0]
    me = lax.axis_index("sec")
    side = lax.axis_index("env")
    my_width = widths[holders[me]]
    row_index = side * half_width + jnp.arange(half_width, dtype=jnp.int32)
    live = (row_index < my_width)[None, :]
    sources, allowed = route(holders)
    envs = left_env[0]

    start = jnp.where(live, amplitudes[0], jnp.zeros_like(amplitudes[0]))
    start_full = lax.all_gather(start, "env", axis=1, tiled=True)
    outgoing = contract(start_full, envs, right_env).astype(jnp.bfloat16)
    stay = outgoing[0].astype(jnp.float32)
    received = spread(outgoing[1:], n_slots)
    arrived = collect(merge(received, sources, allowed).astype(jnp.bfloat16))
    first = jnp.where(live, stay + arrived.astype(jnp.float32), 0.0).astype(jnp.bfloat16)

    first_full = lax.all_gather(first, "env", axis=1, tiled=True).astype(jnp.float32)
    basis = start_full.astype(jnp.float32)
    overlap = jnp.sum(basis * first_full)
    norm = jnp.sum(basis * basis)
    own_quotient = jnp.where(norm > 0, overlap / jnp.where(norm > 0, norm, 1.0), 0.0)
    deflated = first_full - own_quotient * basis
    rest = jnp.sum(deflated * deflated)
    sums = share(jnp.stack([overlap, norm, own_quotient, rest]), n_slots, me)
    outgoing_2 = contract(deflated.astype(jnp.bfloat16), envs, right_env)
    received_2 = spread(outgoing_2[1:].astype(jnp.bfloat16), n_slots)

    quotient = jnp.sum(sums[:, 0]) / jnp.sum(sums[:, 1])
    shift = sums[:, 2] - quotient
    resid_norm = jnp.sum(sums[:, 3] + shift * shift * sums[:, 1])
    live_count = right_dim * jnp.sum(widths).astype(jnp.float32)
    scale = lax.rsqrt(resid_norm / live_count + 1e-06)
    mixed = received_2.astype(jnp.float32) + shift[:, None, None, None] * received.astype(
        jnp.float32
    )
    merged_2 = scale * merge(mixed, sources, allowed)
    arrived_2 = collect(merged_2.astype(jnp.bfloat16))
    stay_2 = scale * (outgoing_2[0] + (own_quotient - quotient) * stay)
    second = jnp.where(live, stay_2 + arrived_2.astype(jnp.float32), 0.0).astype(jnp.bfloat16)
    return first[None], second[None]


LANES = 128
TAG = 16


def live_columns(widths, holders, half):
    width = widths[holders[lax.axis_index("sec")]]
    first_column = lax.axis_index("env") * half
    return first_column + lax.broadcasted_iota(jnp.int32, (1, half), 1) < width


def apply_term(right, left, vector, term):
    products = jnp.dot(right[term], vector, preferred_element_type=jnp.float32)
    return jnp.dot(products.astype(jnp.bfloat16), left, preferred_element_type=jnp.float32)


def mask_kernel(widths, holders, amps, start):
    live = live_columns(widths, holders, amps.shape[1])
    start[...] = jnp.where(live, amps[...], jnp.zeros_like(amps[...]))


def first_kernel(start, right, left, message, stay):
    slots, _, rows, _ = message.shape
    vector = jnp.concatenate([start[0], start[1]], axis=1)
    for term in (1, 2, 0):
        block = apply_term(right, left[0, term], vector, term).astype(jnp.bfloat16)
        if term == 0:
            stay[...] = block
        else:
            for slot in range(slots):
                message[slot, term - 1] = block[slot * rows : (slot + 1) * rows, :]


def fill_slots(holders, slot_of):
    for s in range(holders.shape[0]):
        slot_of[holders[s]] = jnp.int32(s)


def sources_of(holders, slot_of, target):
    sector = holders[target]
    has = (sector >= QDOWN, sector % QDOWN > 0)
    source = (slot_of[sector & (QDOWN - 1)], slot_of[jnp.maximum(sector - 1, 0)])
    return has, source


def merge_kernel(holders, table, out, slot_of):
    fill_slots(holders, slot_of)
    for slot in range(holders.shape[0]):
        has, source = sources_of(holders, slot_of, slot)
        total = 0.0
        for i in range(2):
            block = table[source[i], i].astype(jnp.float32)
            total = total + jnp.where(has[i], block, 0.0)
        out[slot] = total.astype(jnp.bfloat16)


def sum_kernel(widths, holders, stay, arrived, first):
    live = live_columns(widths, holders, stay.shape[1])
    total = stay[...].astype(jnp.float32) + arrived[...].astype(jnp.float32)
    first[...] = jnp.where(live, total, 0.0).astype(jnp.bfloat16)


def total_of(array):
    return jnp.sum(jnp.sum(array, axis=0, keepdims=True), axis=1, keepdims=True)


def make_tag(values, me):
    row = lax.broadcasted_iota(jnp.int32, (TAG, LANES), 0)
    lane = lax.broadcasted_iota(jnp.int32, (TAG, LANES), 1)
    spread = jnp.zeros((TAG, LANES), jnp.float32)
    for place, value in enumerate(values):
        spread = jnp.where(row // 3 == place, value, spread)
    high = spread.astype(jnp.bfloat16).astype(jnp.float32)
    middle = (spread - high).astype(jnp.bfloat16).astype(jnp.float32)
    low = spread - high - middle
    parts = jnp.where(row % 3 == 0, high, jnp.where(row % 3 == 1, middle, low))
    return jnp.where((lane == me) & (row < 3 * len(values)), parts, 0.0).astype(jnp.bfloat16)


def second_kernel(start, first, right, left, message, stay):
    slots = message.shape[0]
    half = stay.shape[1]
    rows = stay.shape[0] // slots
    chunks = half // LANES
    basis = [start[h].astype(jnp.float32) for h in range(2)]
    firsts = [first[h].astype(jnp.float32) for h in range(2)]
    overlap = total_of(basis[0] * firsts[0]) + total_of(basis[1] * firsts[1])
    norm = total_of(basis[0] * basis[0]) + total_of(basis[1] * basis[1])
    quotient = jnp.where(norm > 0, overlap / jnp.where(norm > 0, norm, 1.0), 0.0)
    deflated = [firsts[h] - quotient * basis[h] for h in range(2)]
    rest_norm = total_of(deflated[0] * deflated[0]) + total_of(deflated[1] * deflated[1])
    vector = jnp.concatenate(deflated, axis=1).astype(jnp.bfloat16)
    tag = make_tag((overlap, norm, quotient, rest_norm), lax.axis_index("sec"))
    for slot in range(slots):
        message[slot, pl.ds(2 * chunks * rows, TAG), :] = tag
    for term in (1, 2, 0):
        block = apply_term(right, left[0, term], vector, term)
        if term == 0:
            stay[...] = block
        else:
            block = block.astype(jnp.bfloat16)
            for slot in range(slots):
                for c in range(chunks):
                    place = pl.ds(((term - 1) * chunks + c) * rows, rows)
                    message[slot, place, :] = block[
                        slot * rows : (slot + 1) * rows, c * LANES : (c + 1) * LANES
                    ]


def mix_kernel(widths, holders, old, new, out, factors, slot_of):
    slots, rows, half = out.shape
    chunks = half // LANES
    fill_slots(holders, slot_of)
    tag = jnp.zeros((TAG, LANES), jnp.float32)
    total = jnp.int32(0)
    for slot in range(slots):
        tag = tag + new[slot, pl.ds(2 * chunks * rows, TAG), :].astype(jnp.float32)
        total = total + widths[slot]
    live_count = slots * rows * total.astype(jnp.float32)

    def value(place):
        parts = [tag[3 * place + i : 3 * place + i + 1, :] for i in range(3)]
        return parts[0] + parts[1] + parts[2]

    overlaps, norms, quotients, rests = (value(place) for place in range(4))
    quotient = total_of(overlaps) / total_of(norms)
    lane = lax.broadcasted_iota(jnp.int32, (1, LANES), 1)
    shifts = jnp.where(lane < slots, quotients - quotient, 0.0)
    resid_norm = total_of(rests + shifts * shifts * norms)
    scale = lax.rsqrt(resid_norm / live_count + 1e-06)

    def shift_of(slot):
        return total_of(jnp.where(lane == slot, shifts, 0.0))

    row = lax.broadcasted_iota(jnp.int32, factors.shape, 0)
    factors[...] = jnp.where(row == 0, scale, scale * shift_of(lax.axis_index("sec")))
    for slot in range(slots):
        has, source = sources_of(holders, slot_of, slot)
        total = 0.0
        for i in range(2):
            block = jnp.concatenate(
                [
                    new[source[i], pl.ds((i * chunks + c) * rows, rows), :]
                    for c in range(chunks)
                ],
                axis=1,
            ).astype(jnp.float32)
            block = block + shift_of(source[i]) * old[source[i], i].astype(jnp.float32)
            total = total + jnp.where(has[i], block, 0.0)
        out[slot] = (scale * total).astype(jnp.bfloat16)


def final_kernel(widths, holders, factors, stay, stay_2, arrived, second):
    live = live_columns(widths, holders, stay.shape[1])
    scale, shift = factors[0:1, 0:1], factors[1:2, 0:1]
    total = scale * stay_2[...] + shift * stay[...].astype(jnp.float32)
    total = total + arrived[...].astype(jnp.float32)
    second[...] = jnp.where(live, total, 0.0).astype(jnp.bfloat16)


SMEM = pl.BlockSpec(memory_space=pltpu.SMEM)
VMEM = pl.BlockSpec(memory_space=pltpu.VMEM)


def call(kernel, specs, outs, scratch=(), flops=0):
    return pl.pallas_call(
        kernel,
        out_shape=outs,
        in_specs=specs,
        out_specs=jax.tree.map(lambda _: VMEM, outs),
        scratch_shapes=scratch,
        compiler_params=pltpu.CompilerParams(vmem_limit_bytes=16 * 1024 * 1024),
        cost_estimate=pl.CostEstimate(flops=flops, bytes_accessed=1 << 18, transcendentals=0),
    )


def swap(pieces):
    return lax.all_to_all(pieces, "sec", split_axis=0, concat_axis=0)


def on_device(amplitudes, widths, holders, left_env, right_env):
    slots_dev, right_dim, half = amplitudes.shape
    slots = holders.shape[0]
    assert slots_dev == 1
    if slots != 2 * QDOWN:
        return on_device_any(amplitudes, widths, holders, left_env, right_env)
    rows = right_dim // slots
    dots = 6 * right_dim * half * (right_dim + 2 * half)
    block = jax.ShapeDtypeStruct((right_dim, half), jnp.bfloat16)
    wide = jax.ShapeDtypeStruct((right_dim, half), jnp.float32)
    pairs = jax.ShapeDtypeStruct((slots, 2, rows, half), jnp.bfloat16)
    singles = jax.ShapeDtypeStruct((slots, rows, half), jnp.bfloat16)
    tagged = jax.ShapeDtypeStruct((slots, 2 * rows * half // LANES + TAG, LANES), jnp.bfloat16)
    factor_shape = jax.ShapeDtypeStruct((8, LANES), jnp.float32)
    slot_table = [pltpu.SMEM((slots,), jnp.int32)]

    start = call(mask_kernel, [SMEM, SMEM, VMEM], block, flops=dots)(
        widths, holders, amplitudes[0]
    )
    start_full = lax.all_gather(start, "env")
    message, stay = call(first_kernel, [VMEM] * 3, (pairs, block), flops=dots)(
        start_full, right_env, left_env
    )
    old = swap(message)
    merged = call(merge_kernel, [SMEM, VMEM], singles, slot_table)(holders, old)
    arrived = swap(merged).reshape(right_dim, half)
    first = call(sum_kernel, [SMEM, SMEM, VMEM, VMEM], block)(widths, holders, stay, arrived)

    first_full = lax.all_gather(first, "env")
    message, stay_2 = call(second_kernel, [VMEM] * 4, (tagged, wide), flops=dots)(
        start_full, first_full, right_env, left_env
    )
    new = swap(message)
    mixed, factors = call(
        mix_kernel, [SMEM, SMEM, VMEM, VMEM], (singles, factor_shape), slot_table
    )(widths, holders, old, new)
    arrived = swap(mixed).reshape(right_dim, half)
    second = call(final_kernel, [SMEM, SMEM] + [VMEM] * 4, block)(
        widths, holders, factors, stay, stay_2, arrived
    )
    return first[None], second[None]


def solution(mesh):
    in_specs = (
        P(("runs", "sec"), None, "env"),
        P("runs"),
        P("runs"),
        P(("runs", "sec"), None, None, "env"),
        P("runs", None, None),
    )
    out_specs = (P(("runs", "sec"), None, "env"), P(("runs", "sec"), None, "env"))
    return jax.shard_map(
        on_device, mesh=mesh, in_specs=in_specs, out_specs=out_specs, check_vma=False
    )
```

```python
import jax
import jax.numpy as jnp
from jax import lax
from jax.experimental import pallas as pl
from jax.experimental.pallas import tpu as pltpu
from jax.sharding import PartitionSpec as P

QDOWN = 4

term_shifts = ((0, 0), (1, 0), (0, 1))


def route(holders):
    n_slots = holders.shape[0]
    sector_ids = jnp.arange(n_slots, dtype=jnp.int32)
    slot_of = jnp.argmax(holders[None, :] == sector_ids[:, None], axis=1)
    sources = []
    allowed = []
    for up, down in term_shifts[1:]:
        permitted = (holders // QDOWN - up >= 0) & (holders % QDOWN - down >= 0)
        wanted = jnp.clip(holders - QDOWN * up - down, 0, n_slots - 1)
        sources.append(slot_of[wanted])
        allowed.append(permitted)
    return sources, allowed


def contract(vector, left_env, right_env):
    products = jnp.einsum(
        "tij,jw->tiw", right_env, vector, preferred_element_type=jnp.float32
    ).astype(jnp.bfloat16)
    return jnp.einsum("tik,tkw->tiw", products, left_env, preferred_element_type=jnp.float32)


def spread(blocks, n_slots):
    terms, rows, width = blocks.shape
    pieces = blocks.reshape(terms, n_slots, rows // n_slots, width).swapaxes(0, 1)
    return lax.all_to_all(pieces, "sec", split_axis=0, concat_axis=0)


def collect(merged):
    n_slots, rows, width = merged.shape
    home = lax.all_to_all(merged, "sec", split_axis=0, concat_axis=0)
    return home.reshape(n_slots * rows, width)


def share(values, n_slots, me):
    lanes = jnp.zeros((1, 128), jnp.float32).at[0, : values.shape[0]].set(values)
    if n_slots & (n_slots - 1) or n_slots > 16:
        return lax.all_gather(lanes[0], "sec")
    table = jnp.where(jnp.arange(n_slots)[:, None] == me, lanes, 0.0)
    for offset in range(1, n_slots):
        pairs = [(i, i ^ offset) for i in range(n_slots)]
        other = lax.ppermute(lanes, "sec", pairs)
        table = jnp.where(jnp.arange(n_slots)[:, None] == (me ^ offset), other, table)
    return table


def merge(received, sources, allowed):
    total = 0.0
    for term, (source, permitted) in enumerate(zip(sources, allowed)):
        picked = received[source, term]
        total = total + jnp.where(permitted[:, None, None], picked, 0).astype(jnp.float32)
    return total


def on_device_any(amplitudes, widths, holders, left_env, right_env):
    slots_dev, right_dim, half_width = amplitudes.shape
    assert slots_dev == 1
    n_slots = holders.shape[0]
    me = lax.axis_index("sec")
    side = lax.axis_index("env")
    my_width = widths[holders[me]]
    row_index = side * half_width + jnp.arange(half_width, dtype=jnp.int32)
    live = (row_index < my_width)[None, :]
    sources, allowed = route(holders)
    envs = left_env[0]

    start = jnp.where(live, amplitudes[0], jnp.zeros_like(amplitudes[0]))
    start_full = lax.all_gather(start, "env", axis=1, tiled=True)
    outgoing = contract(start_full, envs, right_env).astype(jnp.bfloat16)
    stay = outgoing[0].astype(jnp.float32)
    received = spread(outgoing[1:], n_slots)
    arrived = collect(merge(received, sources, allowed).astype(jnp.bfloat16))
    first = jnp.where(live, stay + arrived.astype(jnp.float32), 0.0).astype(jnp.bfloat16)

    first_full = lax.all_gather(first, "env", axis=1, tiled=True).astype(jnp.float32)
    basis = start_full.astype(jnp.float32)
    overlap = jnp.sum(basis * first_full)
    norm = jnp.sum(basis * basis)
    own_quotient = jnp.where(norm > 0, overlap / jnp.where(norm > 0, norm, 1.0), 0.0)
    deflated = first_full - own_quotient * basis
    rest = jnp.sum(deflated * deflated)
    sums = share(jnp.stack([overlap, norm, own_quotient, rest]), n_slots, me)
    outgoing_2 = contract(deflated.astype(jnp.bfloat16), envs, right_env)
    received_2 = spread(outgoing_2[1:].astype(jnp.bfloat16), n_slots)

    quotient = jnp.sum(sums[:, 0]) / jnp.sum(sums[:, 1])
    shift = sums[:, 2] - quotient
    resid_norm = jnp.sum(sums[:, 3] + shift * shift * sums[:, 1])
    live_count = right_dim * jnp.sum(widths).astype(jnp.float32)
    scale = lax.rsqrt(resid_norm / live_count + 1e-06)
    mixed = received_2.astype(jnp.float32) + shift[:, None, None, None] * received.astype(
        jnp.float32
    )
    merged_2 = scale * merge(mixed, sources, allowed)
    arrived_2 = collect(merged_2.astype(jnp.bfloat16))
    stay_2 = scale * (outgoing_2[0] + (own_quotient - quotient) * stay)
    second = jnp.where(live, stay_2 + arrived_2.astype(jnp.float32), 0.0).astype(jnp.bfloat16)
    return first[None], second[None]


LANES = 128
TAG = 16


def live_columns(widths, holders, half):
    width = widths[holders[lax.axis_index("sec")]]
    first_column = lax.axis_index("env") * half
    return first_column + lax.broadcasted_iota(jnp.int32, (1, half), 1) < width


def apply_term(right, left, vector, term):
    products = jnp.dot(right[term], vector, preferred_element_type=jnp.float32)
    return jnp.dot(products.astype(jnp.bfloat16), left, preferred_element_type=jnp.float32)


def first_kernel(
    widths_in,
    holders_in,
    amps_in,
    right_in,
    left_in,
    message,
    stay,
    start,
    widths,
    holders,
    amps,
    right,
    left,
    sems,
):
    slots, _, rows, half = message.shape
    small = ((widths_in, widths), (holders_in, holders), (amps_in, amps), (right_in, right))
    large = [(left_in.at[0, term], left.at[term]) for term in range(3)]
    copies = [
        pltpu.make_async_copy(source, target, sems.at[i])
        for i, (source, target) in enumerate([*small, *large])
    ]
    for i in (0, 1, 2, 3, 5, 6, 4):
        copies[i].start()
    for copy in copies[:4]:
        copy.wait()
    width = widths[holders[lax.axis_index("sec")]]
    columns = lax.broadcasted_iota(jnp.int32, (1, half), 1)
    for h in range(2):
        live = h * half + columns < width
        start[h] = jnp.where(live, amps[h], jnp.zeros_like(amps[h]))
    vector = jnp.concatenate([start[0], start[1]], axis=1)
    for term in (1, 2, 0):
        copies[4 + term].wait()
        block = apply_term(right, left[term], vector, term).astype(jnp.bfloat16)
        if term == 0:
            stay[...] = block
        else:
            for slot in range(slots):
                message[slot, term - 1] = block[slot * rows : (slot + 1) * rows, :]


def fill_slots(holders, slot_of):
    for s in range(holders.shape[0]):
        slot_of[holders[s]] = jnp.int32(s)


def sources_of(holders, slot_of, target):
    sector = holders[target]
    has = (sector >= QDOWN, sector % QDOWN > 0)
    source = (slot_of[sector & (QDOWN - 1)], slot_of[jnp.maximum(sector - 1, 0)])
    return has, source


def merge_kernel(holders, table, out, slot_of):
    fill_slots(holders, slot_of)
    for slot in range(holders.shape[0]):
        has, source = sources_of(holders, slot_of, slot)
        total = 0.0
        for i in range(2):
            block = table[source[i], i].astype(jnp.float32)
            total = total + jnp.where(has[i], block, 0.0)
        out[slot] = total.astype(jnp.bfloat16)


def sum_kernel(widths, holders, stay, arrived, first):
    live = live_columns(widths, holders, stay.shape[1])
    total = stay[...].astype(jnp.float32) + arrived[...].astype(jnp.float32)
    first[...] = jnp.where(live, total, 0.0).astype(jnp.bfloat16)


def total_of(array):
    return jnp.sum(jnp.sum(array, axis=0, keepdims=True), axis=1, keepdims=True)


def make_tag(values, me):
    row = lax.broadcasted_iota(jnp.int32, (TAG, LANES), 0)
    lane = lax.broadcasted_iota(jnp.int32, (TAG, LANES), 1)
    spread = jnp.zeros((TAG, LANES), jnp.float32)
    for place, value in enumerate(values):
        spread = jnp.where(row // 3 == place, value, spread)
    high = spread.astype(jnp.bfloat16).astype(jnp.float32)
    middle = (spread - high).astype(jnp.bfloat16).astype(jnp.float32)
    low = spread - high - middle
    parts = jnp.where(row % 3 == 0, high, jnp.where(row % 3 == 1, middle, low))
    return jnp.where((lane == me) & (row < 3 * len(values)), parts, 0.0).astype(jnp.bfloat16)


def second_kernel(start, first, right, left, message, stay):
    slots = message.shape[0]
    half = stay.shape[1]
    rows = stay.shape[0] // slots
    chunks = half // LANES
    basis = [start[h].astype(jnp.float32) for h in range(2)]
    firsts = [first[h].astype(jnp.float32) for h in range(2)]
    overlap = total_of(basis[0] * firsts[0]) + total_of(basis[1] * firsts[1])
    norm = total_of(basis[0] * basis[0]) + total_of(basis[1] * basis[1])
    quotient = jnp.where(norm > 0, overlap / jnp.where(norm > 0, norm, 1.0), 0.0)
    deflated = [firsts[h] - quotient * basis[h] for h in range(2)]
    rest_norm = total_of(deflated[0] * deflated[0]) + total_of(deflated[1] * deflated[1])
    vector = jnp.concatenate(deflated, axis=1).astype(jnp.bfloat16)
    tag = make_tag((overlap, norm, quotient, rest_norm), lax.axis_index("sec"))
    for slot in range(slots):
        message[slot, pl.ds(2 * chunks * rows, TAG), :] = tag
    for term in (1, 2, 0):
        block = apply_term(right, left[0, term], vector, term)
        if term == 0:
            stay[...] = block
        else:
            block = block.astype(jnp.bfloat16)
            for slot in range(slots):
                for c in range(chunks):
                    place = pl.ds(((term - 1) * chunks + c) * rows, rows)
                    message[slot, place, :] = block[
                        slot * rows : (slot + 1) * rows, c * LANES : (c + 1) * LANES
                    ]


def mix_kernel(widths, holders, old, new, out, factors, slot_of):
    slots, rows, half = out.shape
    chunks = half // LANES
    fill_slots(holders, slot_of)
    tag = jnp.zeros((TAG, LANES), jnp.float32)
    total = jnp.int32(0)
    for slot in range(slots):
        tag = tag + new[slot, pl.ds(2 * chunks * rows, TAG), :].astype(jnp.float32)
        total = total + widths[slot]
    live_count = slots * rows * total.astype(jnp.float32)

    def value(place):
        parts = [tag[3 * place + i : 3 * place + i + 1, :] for i in range(3)]
        return parts[0] + parts[1] + parts[2]

    overlaps, norms, quotients, rests = (value(place) for place in range(4))
    quotient = total_of(overlaps) / total_of(norms)
    lane = lax.broadcasted_iota(jnp.int32, (1, LANES), 1)
    shifts = jnp.where(lane < slots, quotients - quotient, 0.0)
    resid_norm = total_of(rests + shifts * shifts * norms)
    scale = lax.rsqrt(resid_norm / live_count + 1e-06)

    def shift_of(slot):
        return total_of(jnp.where(lane == slot, shifts, 0.0))

    row = lax.broadcasted_iota(jnp.int32, factors.shape, 0)
    factors[...] = jnp.where(row == 0, scale, scale * shift_of(lax.axis_index("sec")))
    for slot in range(slots):
        has, source = sources_of(holders, slot_of, slot)
        total = 0.0
        for i in range(2):
            block = jnp.concatenate(
                [
                    new[source[i], pl.ds((i * chunks + c) * rows, rows), :]
                    for c in range(chunks)
                ],
                axis=1,
            ).astype(jnp.float32)
            block = block + shift_of(source[i]) * old[source[i], i].astype(jnp.float32)
            total = total + jnp.where(has[i], block, 0.0)
        out[slot] = (scale * total).astype(jnp.bfloat16)


def final_kernel(widths, holders, factors, stay, stay_2, arrived, first, second, first_out):
    first_out[...] = first[...]
    live = live_columns(widths, holders, stay.shape[1])
    scale, shift = factors[0:1, 0:1], factors[1:2, 0:1]
    total = scale * stay_2[...] + shift * stay[...].astype(jnp.float32)
    total = total + arrived[...].astype(jnp.float32)
    second[...] = jnp.where(live, total, 0.0).astype(jnp.bfloat16)


SMEM = pl.BlockSpec(memory_space=pltpu.SMEM)
VMEM = pl.BlockSpec(memory_space=pltpu.VMEM)


ANY = pl.BlockSpec(memory_space=pl.ANY)


def call(kernel, specs, outs, scratch=(), flops=0, vmem=16):
    return pl.pallas_call(
        kernel,
        out_shape=outs,
        in_specs=specs,
        out_specs=jax.tree.map(lambda _: VMEM, outs),
        scratch_shapes=scratch,
        compiler_params=pltpu.CompilerParams(vmem_limit_bytes=vmem * 1024 * 1024),
        cost_estimate=pl.CostEstimate(flops=flops, bytes_accessed=1 << 18, transcendentals=0),
    )


def swap(pieces):
    return lax.all_to_all(pieces, "sec", split_axis=0, concat_axis=0)


def on_device(amplitudes, widths, holders, left_env, right_env):
    slots_dev, right_dim, half = amplitudes.shape
    slots = holders.shape[0]
    assert slots_dev == 1
    if slots != 2 * QDOWN:
        return on_device_any(amplitudes, widths, holders, left_env, right_env)
    rows = right_dim // slots
    dots = 6 * right_dim * half * (right_dim + 2 * half)
    block = jax.ShapeDtypeStruct((right_dim, half), jnp.bfloat16)
    wide = jax.ShapeDtypeStruct((right_dim, half), jnp.float32)
    pairs = jax.ShapeDtypeStruct((slots, 2, rows, half), jnp.bfloat16)
    singles = jax.ShapeDtypeStruct((slots, rows, half), jnp.bfloat16)
    tagged = jax.ShapeDtypeStruct((slots, 2 * rows * half // LANES + TAG, LANES), jnp.bfloat16)
    factor_shape = jax.ShapeDtypeStruct((8, LANES), jnp.float32)
    slot_table = [pltpu.SMEM((slots,), jnp.int32)]

    amps_full = lax.all_gather(amplitudes[0], "env")
    both = jax.ShapeDtypeStruct(amps_full.shape, jnp.bfloat16)
    scratch = [
        pltpu.SMEM((slots,), jnp.int32),
        pltpu.SMEM((slots,), jnp.int32),
        pltpu.VMEM(amps_full.shape, jnp.bfloat16),
        pltpu.VMEM(right_env.shape, jnp.bfloat16),
        pltpu.VMEM(left_env.shape[1:], jnp.bfloat16),
        pltpu.SemaphoreType.DMA((7,)),
    ]
    message, stay, start_full = call(
        first_kernel, [ANY] * 5, (pairs, block, both), scratch, dots, vmem=59
    )(widths, holders, amps_full, right_env, left_env)
    old = swap(message)
    merged = call(merge_kernel, [SMEM, VMEM], singles, slot_table)(holders, old)
    arrived = swap(merged).reshape(right_dim, half)
    first = call(sum_kernel, [SMEM, SMEM, VMEM, VMEM], block)(widths, holders, stay, arrived)

    first_full = lax.all_gather(first, "env")
    message, stay_2 = call(second_kernel, [VMEM] * 4, (tagged, wide), flops=dots)(
        start_full, first_full, right_env, left_env
    )
    new = swap(message)
    mixed, factors = call(
        mix_kernel, [SMEM, SMEM, VMEM, VMEM], (singles, factor_shape), slot_table
    )(widths, holders, old, new)
    arrived = swap(mixed).reshape(right_dim, half)
    second, first = call(final_kernel, [SMEM, SMEM] + [VMEM] * 5, (block, block))(
        widths, holders, factors, stay, stay_2, arrived, first
    )
    return first[None], second[None]


def solution(mesh):
    in_specs = (
        P(("runs", "sec"), None, "env"),
        P("runs"),
        P("runs"),
        P(("runs", "sec"), None, None, "env"),
        P("runs", None, None),
    )
    out_specs = (P(("runs", "sec"), None, "env"), P(("runs", "sec"), None, "env"))
    return jax.shard_map(
        on_device, mesh=mesh, in_specs=in_specs, out_specs=out_specs, check_vma=False
    )
```

```python
import jax
import jax.numpy as jnp
from jax import lax
from jax.experimental import pallas as pl
from jax.experimental.pallas import tpu as pltpu
from jax.sharding import PartitionSpec as P

QDOWN = 4

term_shifts = ((0, 0), (1, 0), (0, 1))


def route(holders):
    n_slots = holders.shape[0]
    sector_ids = jnp.arange(n_slots, dtype=jnp.int32)
    slot_of = jnp.argmax(holders[None, :] == sector_ids[:, None], axis=1)
    sources = []
    allowed = []
    for up, down in term_shifts[1:]:
        permitted = (holders // QDOWN - up >= 0) & (holders % QDOWN - down >= 0)
        wanted = jnp.clip(holders - QDOWN * up - down, 0, n_slots - 1)
        sources.append(slot_of[wanted])
        allowed.append(permitted)
    return sources, allowed


def contract(vector, left_env, right_env):
    products = jnp.einsum(
        "tij,jw->tiw", right_env, vector, preferred_element_type=jnp.float32
    ).astype(jnp.bfloat16)
    return jnp.einsum("tik,tkw->tiw", products, left_env, preferred_element_type=jnp.float32)


def spread(blocks, n_slots):
    terms, rows, width = blocks.shape
    pieces = blocks.reshape(terms, n_slots, rows // n_slots, width).swapaxes(0, 1)
    return lax.all_to_all(pieces, "sec", split_axis=0, concat_axis=0)


def collect(merged):
    n_slots, rows, width = merged.shape
    home = lax.all_to_all(merged, "sec", split_axis=0, concat_axis=0)
    return home.reshape(n_slots * rows, width)


def share(values, n_slots, me):
    lanes = jnp.zeros((1, 128), jnp.float32).at[0, : values.shape[0]].set(values)
    if n_slots & (n_slots - 1) or n_slots > 16:
        return lax.all_gather(lanes[0], "sec")
    table = jnp.where(jnp.arange(n_slots)[:, None] == me, lanes, 0.0)
    for offset in range(1, n_slots):
        pairs = [(i, i ^ offset) for i in range(n_slots)]
        other = lax.ppermute(lanes, "sec", pairs)
        table = jnp.where(jnp.arange(n_slots)[:, None] == (me ^ offset), other, table)
    return table


def merge(received, sources, allowed):
    total = 0.0
    for term, (source, permitted) in enumerate(zip(sources, allowed)):
        picked = received[source, term]
        total = total + jnp.where(permitted[:, None, None], picked, 0).astype(jnp.float32)
    return total


def on_device_any(amplitudes, widths, holders, left_env, right_env):
    slots_dev, right_dim, half_width = amplitudes.shape
    assert slots_dev == 1
    n_slots = holders.shape[0]
    me = lax.axis_index("sec")
    side = lax.axis_index("env")
    my_width = widths[holders[me]]
    row_index = side * half_width + jnp.arange(half_width, dtype=jnp.int32)
    live = (row_index < my_width)[None, :]
    sources, allowed = route(holders)
    envs = left_env[0]

    start = jnp.where(live, amplitudes[0], jnp.zeros_like(amplitudes[0]))
    start_full = lax.all_gather(start, "env", axis=1, tiled=True)
    outgoing = contract(start_full, envs, right_env).astype(jnp.bfloat16)
    stay = outgoing[0].astype(jnp.float32)
    received = spread(outgoing[1:], n_slots)
    arrived = collect(merge(received, sources, allowed).astype(jnp.bfloat16))
    first = jnp.where(live, stay + arrived.astype(jnp.float32), 0.0).astype(jnp.bfloat16)

    first_full = lax.all_gather(first, "env", axis=1, tiled=True).astype(jnp.float32)
    basis = start_full.astype(jnp.float32)
    overlap = jnp.sum(basis * first_full)
    norm = jnp.sum(basis * basis)
    own_quotient = jnp.where(norm > 0, overlap / jnp.where(norm > 0, norm, 1.0), 0.0)
    deflated = first_full - own_quotient * basis
    rest = jnp.sum(deflated * deflated)
    sums = share(jnp.stack([overlap, norm, own_quotient, rest]), n_slots, me)
    outgoing_2 = contract(deflated.astype(jnp.bfloat16), envs, right_env)
    received_2 = spread(outgoing_2[1:].astype(jnp.bfloat16), n_slots)

    quotient = jnp.sum(sums[:, 0]) / jnp.sum(sums[:, 1])
    shift = sums[:, 2] - quotient
    resid_norm = jnp.sum(sums[:, 3] + shift * shift * sums[:, 1])
    live_count = right_dim * jnp.sum(widths).astype(jnp.float32)
    scale = lax.rsqrt(resid_norm / live_count + 1e-06)
    mixed = received_2.astype(jnp.float32) + shift[:, None, None, None] * received.astype(
        jnp.float32
    )
    merged_2 = scale * merge(mixed, sources, allowed)
    arrived_2 = collect(merged_2.astype(jnp.bfloat16))
    stay_2 = scale * (outgoing_2[0] + (own_quotient - quotient) * stay)
    second = jnp.where(live, stay_2 + arrived_2.astype(jnp.float32), 0.0).astype(jnp.bfloat16)
    return first[None], second[None]


LANES = 128
TAG = 16


def live_columns(widths, holders, half):
    width = widths[holders[lax.axis_index("sec")]]
    first_column = lax.axis_index("env") * half
    return first_column + lax.broadcasted_iota(jnp.int32, (1, half), 1) < width


def apply_term(right, left, vector, term):
    products = jnp.dot(right[term], vector, preferred_element_type=jnp.float32)
    return jnp.dot(products.astype(jnp.bfloat16), left, preferred_element_type=jnp.float32)


def stage_kernel(amps, staged):
    staged[...] = amps[...]


def first_kernel(widths, holders, amps, right, left, message, stay, start):
    slots, _, rows, half = message.shape
    width = widths[holders[lax.axis_index("sec")]]
    columns = lax.broadcasted_iota(jnp.int32, (1, half), 1)
    for h in range(2):
        live = h * half + columns < width
        start[h] = jnp.where(live, amps[h], jnp.zeros_like(amps[h]))
    vector = jnp.concatenate([start[0], start[1]], axis=1)
    for term in (1, 2, 0):
        block = apply_term(right, left[0, term], vector, term).astype(jnp.bfloat16)
        if term == 0:
            stay[...] = block
        else:
            for slot in range(slots):
                message[slot, term - 1] = block[slot * rows : (slot + 1) * rows, :]


def fill_slots(holders, slot_of):
    for s in range(holders.shape[0]):
        slot_of[holders[s]] = jnp.int32(s)


def sources_of(holders, slot_of, target):
    sector = holders[target]
    has = (sector >= QDOWN, sector % QDOWN > 0)
    source = (slot_of[sector & (QDOWN - 1)], slot_of[jnp.maximum(sector - 1, 0)])
    return has, source


def merge_kernel(holders, table, out, slot_of):
    fill_slots(holders, slot_of)
    for slot in range(holders.shape[0]):
        has, source = sources_of(holders, slot_of, slot)
        total = 0.0
        for i in range(2):
            block = table[source[i], i].astype(jnp.float32)
            total = total + jnp.where(has[i], block, 0.0)
        out[slot] = total.astype(jnp.bfloat16)


def sum_kernel(widths, holders, stay, arrived, first):
    live = live_columns(widths, holders, stay.shape[1])
    total = stay[...].astype(jnp.float32) + arrived[...].astype(jnp.float32)
    first[...] = jnp.where(live, total, 0.0).astype(jnp.bfloat16)


def total_of(array):
    return jnp.sum(jnp.sum(array, axis=0, keepdims=True), axis=1, keepdims=True)


def make_tag(values, me):
    row = lax.broadcasted_iota(jnp.int32, (TAG, LANES), 0)
    lane = lax.broadcasted_iota(jnp.int32, (TAG, LANES), 1)
    spread = jnp.zeros((TAG, LANES), jnp.float32)
    for place, value in enumerate(values):
        spread = jnp.where(row // 3 == place, value, spread)
    high = spread.astype(jnp.bfloat16).astype(jnp.float32)
    middle = (spread - high).astype(jnp.bfloat16).astype(jnp.float32)
    low = spread - high - middle
    parts = jnp.where(row % 3 == 0, high, jnp.where(row % 3 == 1, middle, low))
    return jnp.where((lane == me) & (row < 3 * len(values)), parts, 0.0).astype(jnp.bfloat16)


def second_kernel(start, first, right, left, message, stay):
    slots = message.shape[0]
    half = stay.shape[1]
    rows = stay.shape[0] // slots
    chunks = half // LANES
    basis = [start[h].astype(jnp.float32) for h in range(2)]
    firsts = [first[h].astype(jnp.float32) for h in range(2)]
    overlap = total_of(basis[0] * firsts[0]) + total_of(basis[1] * firsts[1])
    norm = total_of(basis[0] * basis[0]) + total_of(basis[1] * basis[1])
    quotient = jnp.where(norm > 0, overlap / jnp.where(norm > 0, norm, 1.0), 0.0)
    deflated = [firsts[h] - quotient * basis[h] for h in range(2)]
    rest_norm = total_of(deflated[0] * deflated[0]) + total_of(deflated[1] * deflated[1])
    vector = jnp.concatenate(deflated, axis=1).astype(jnp.bfloat16)
    tag = make_tag((overlap, norm, quotient, rest_norm), lax.axis_index("sec"))
    for slot in range(slots):
        message[slot, pl.ds(2 * chunks * rows, TAG), :] = tag
    for term in (1, 2, 0):
        block = apply_term(right, left[0, term], vector, term)
        if term == 0:
            stay[...] = block
        else:
            block = block.astype(jnp.bfloat16)
            for slot in range(slots):
                for c in range(chunks):
                    place = pl.ds(((term - 1) * chunks + c) * rows, rows)
                    message[slot, place, :] = block[
                        slot * rows : (slot + 1) * rows, c * LANES : (c + 1) * LANES
                    ]


def mix_kernel(widths, holders, old, new, out, factors, slot_of):
    slots, rows, half = out.shape
    chunks = half // LANES
    fill_slots(holders, slot_of)
    tag = jnp.zeros((TAG, LANES), jnp.float32)
    total = jnp.int32(0)
    for slot in range(slots):
        tag = tag + new[slot, pl.ds(2 * chunks * rows, TAG), :].astype(jnp.float32)
        total = total + widths[slot]
    live_count = slots * rows * total.astype(jnp.float32)

    def value(place):
        parts = [tag[3 * place + i : 3 * place + i + 1, :] for i in range(3)]
        return parts[0] + parts[1] + parts[2]

    overlaps, norms, quotients, rests = (value(place) for place in range(4))
    quotient = total_of(overlaps) / total_of(norms)
    lane = lax.broadcasted_iota(jnp.int32, (1, LANES), 1)
    shifts = jnp.where(lane < slots, quotients - quotient, 0.0)
    resid_norm = total_of(rests + shifts * shifts * norms)
    scale = lax.rsqrt(resid_norm / live_count + 1e-06)

    def shift_of(slot):
        return total_of(jnp.where(lane == slot, shifts, 0.0))

    row = lax.broadcasted_iota(jnp.int32, factors.shape, 0)
    factors[...] = jnp.where(row == 0, scale, scale * shift_of(lax.axis_index("sec")))
    for slot in range(slots):
        has, source = sources_of(holders, slot_of, slot)
        total = 0.0
        for i in range(2):
            block = jnp.concatenate(
                [
                    new[source[i], pl.ds((i * chunks + c) * rows, rows), :]
                    for c in range(chunks)
                ],
                axis=1,
            ).astype(jnp.float32)
            block = block + shift_of(source[i]) * old[source[i], i].astype(jnp.float32)
            total = total + jnp.where(has[i], block, 0.0)
        out[slot] = (scale * total).astype(jnp.bfloat16)


def final_kernel(widths, holders, factors, stay, stay_2, arrived, first, second, first_out):
    first_out[...] = first[...]
    live = live_columns(widths, holders, stay.shape[1])
    scale, shift = factors[0:1, 0:1], factors[1:2, 0:1]
    total = scale * stay_2[...] + shift * stay[...].astype(jnp.float32)
    total = total + arrived[...].astype(jnp.float32)
    second[...] = jnp.where(live, total, 0.0).astype(jnp.bfloat16)


SMEM = pl.BlockSpec(memory_space=pltpu.SMEM)
VMEM = pl.BlockSpec(memory_space=pltpu.VMEM)


def call(kernel, specs, outs, scratch=(), flops=0):
    return pl.pallas_call(
        kernel,
        out_shape=outs,
        in_specs=specs,
        out_specs=jax.tree.map(lambda _: VMEM, outs),
        scratch_shapes=scratch,
        compiler_params=pltpu.CompilerParams(vmem_limit_bytes=16 * 1024 * 1024),
        cost_estimate=pl.CostEstimate(flops=flops, bytes_accessed=1 << 18, transcendentals=0),
    )


def swap(pieces):
    return lax.all_to_all(pieces, "sec", split_axis=0, concat_axis=0)


def on_device(amplitudes, widths, holders, left_env, right_env):
    slots_dev, right_dim, half = amplitudes.shape
    slots = holders.shape[0]
    assert slots_dev == 1
    if slots != 2 * QDOWN:
        return on_device_any(amplitudes, widths, holders, left_env, right_env)
    rows = right_dim // slots
    dots = 6 * right_dim * half * (right_dim + 2 * half)
    block = jax.ShapeDtypeStruct((right_dim, half), jnp.bfloat16)
    wide = jax.ShapeDtypeStruct((right_dim, half), jnp.float32)
    pairs = jax.ShapeDtypeStruct((slots, 2, rows, half), jnp.bfloat16)
    singles = jax.ShapeDtypeStruct((slots, rows, half), jnp.bfloat16)
    tagged = jax.ShapeDtypeStruct((slots, 2 * rows * half // LANES + TAG, LANES), jnp.bfloat16)
    factor_shape = jax.ShapeDtypeStruct((8, LANES), jnp.float32)
    slot_table = [pltpu.SMEM((slots,), jnp.int32)]

    staged = call(stage_kernel, [VMEM], block, flops=4 << 30)(amplitudes[0])
    amps_full = lax.all_gather(staged, "env")
    both = jax.ShapeDtypeStruct(amps_full.shape, jnp.bfloat16)
    message, stay, start_full = call(
        first_kernel, [SMEM, SMEM] + [VMEM] * 3, (pairs, block, both), flops=dots
    )(widths, holders, amps_full, right_env, left_env)
    old = swap(message)
    merged = call(merge_kernel, [SMEM, VMEM], singles, slot_table)(holders, old)
    arrived = swap(merged).reshape(right_dim, half)
    first = call(sum_kernel, [SMEM, SMEM, VMEM, VMEM], block)(widths, holders, stay, arrived)

    first_full = lax.all_gather(first, "env")
    message, stay_2 = call(second_kernel, [VMEM] * 4, (tagged, wide), flops=dots)(
        start_full, first_full, right_env, left_env
    )
    new = swap(message)
    mixed, factors = call(
        mix_kernel, [SMEM, SMEM, VMEM, VMEM], (singles, factor_shape), slot_table
    )(widths, holders, old, new)
    arrived = swap(mixed).reshape(right_dim, half)
    second, first = call(final_kernel, [SMEM, SMEM] + [VMEM] * 5, (block, block))(
        widths, holders, factors, stay, stay_2, arrived, first
    )
    return first[None], second[None]


def solution(mesh):
    in_specs = (
        P(("runs", "sec"), None, "env"),
        P("runs"),
        P("runs"),
        P(("runs", "sec"), None, None, "env"),
        P("runs", None, None),
    )
    out_specs = (P(("runs", "sec"), None, "env"), P(("runs", "sec"), None, "env"))
    return jax.shard_map(
        on_device, mesh=mesh, in_specs=in_specs, out_specs=out_specs, check_vma=False
    )
```

```python
import jax
import jax.numpy as jnp
from jax import lax
from jax.experimental import pallas as pl
from jax.experimental.pallas import tpu as pltpu
from jax.sharding import PartitionSpec as P

QDOWN = 4

term_shifts = ((0, 0), (1, 0), (0, 1))


def route(holders):
    n_slots = holders.shape[0]
    sector_ids = jnp.arange(n_slots, dtype=jnp.int32)
    slot_of = jnp.argmax(holders[None, :] == sector_ids[:, None], axis=1)
    sources = []
    allowed = []
    for up, down in term_shifts[1:]:
        permitted = (holders // QDOWN - up >= 0) & (holders % QDOWN - down >= 0)
        wanted = jnp.clip(holders - QDOWN * up - down, 0, n_slots - 1)
        sources.append(slot_of[wanted])
        allowed.append(permitted)
    return sources, allowed


def contract(vector, left_env, right_env):
    products = jnp.einsum(
        "tij,jw->tiw", right_env, vector, preferred_element_type=jnp.float32
    ).astype(jnp.bfloat16)
    return jnp.einsum("tik,tkw->tiw", products, left_env, preferred_element_type=jnp.float32)


def spread(blocks, n_slots):
    terms, rows, width = blocks.shape
    pieces = blocks.reshape(terms, n_slots, rows // n_slots, width).swapaxes(0, 1)
    return lax.all_to_all(pieces, "sec", split_axis=0, concat_axis=0)


def collect(merged):
    n_slots, rows, width = merged.shape
    home = lax.all_to_all(merged, "sec", split_axis=0, concat_axis=0)
    return home.reshape(n_slots * rows, width)


def share(values, n_slots, me):
    lanes = jnp.zeros((1, 128), jnp.float32).at[0, : values.shape[0]].set(values)
    if n_slots & (n_slots - 1) or n_slots > 16:
        return lax.all_gather(lanes[0], "sec")
    table = jnp.where(jnp.arange(n_slots)[:, None] == me, lanes, 0.0)
    for offset in range(1, n_slots):
        pairs = [(i, i ^ offset) for i in range(n_slots)]
        other = lax.ppermute(lanes, "sec", pairs)
        table = jnp.where(jnp.arange(n_slots)[:, None] == (me ^ offset), other, table)
    return table


def merge(received, sources, allowed):
    total = 0.0
    for term, (source, permitted) in enumerate(zip(sources, allowed)):
        picked = received[source, term]
        total = total + jnp.where(permitted[:, None, None], picked, 0).astype(jnp.float32)
    return total


def on_device_any(amplitudes, widths, holders, left_env, right_env):
    slots_dev, right_dim, half_width = amplitudes.shape
    assert slots_dev == 1
    n_slots = holders.shape[0]
    me = lax.axis_index("sec")
    side = lax.axis_index("env")
    my_width = widths[holders[me]]
    row_index = side * half_width + jnp.arange(half_width, dtype=jnp.int32)
    live = (row_index < my_width)[None, :]
    sources, allowed = route(holders)
    envs = left_env[0]

    start = jnp.where(live, amplitudes[0], jnp.zeros_like(amplitudes[0]))
    start_full = lax.all_gather(start, "env", axis=1, tiled=True)
    outgoing = contract(start_full, envs, right_env).astype(jnp.bfloat16)
    stay = outgoing[0].astype(jnp.float32)
    received = spread(outgoing[1:], n_slots)
    arrived = collect(merge(received, sources, allowed).astype(jnp.bfloat16))
    first = jnp.where(live, stay + arrived.astype(jnp.float32), 0.0).astype(jnp.bfloat16)

    first_full = lax.all_gather(first, "env", axis=1, tiled=True).astype(jnp.float32)
    basis = start_full.astype(jnp.float32)
    overlap = jnp.sum(basis * first_full)
    norm = jnp.sum(basis * basis)
    own_quotient = jnp.where(norm > 0, overlap / jnp.where(norm > 0, norm, 1.0), 0.0)
    deflated = first_full - own_quotient * basis
    rest = jnp.sum(deflated * deflated)
    sums = share(jnp.stack([overlap, norm, own_quotient, rest]), n_slots, me)
    outgoing_2 = contract(deflated.astype(jnp.bfloat16), envs, right_env)
    received_2 = spread(outgoing_2[1:].astype(jnp.bfloat16), n_slots)

    quotient = jnp.sum(sums[:, 0]) / jnp.sum(sums[:, 1])
    shift = sums[:, 2] - quotient
    resid_norm = jnp.sum(sums[:, 3] + shift * shift * sums[:, 1])
    live_count = right_dim * jnp.sum(widths).astype(jnp.float32)
    scale = lax.rsqrt(resid_norm / live_count + 1e-06)
    mixed = received_2.astype(jnp.float32) + shift[:, None, None, None] * received.astype(
        jnp.float32
    )
    merged_2 = scale * merge(mixed, sources, allowed)
    arrived_2 = collect(merged_2.astype(jnp.bfloat16))
    stay_2 = scale * (outgoing_2[0] + (own_quotient - quotient) * stay)
    second = jnp.where(live, stay_2 + arrived_2.astype(jnp.float32), 0.0).astype(jnp.bfloat16)
    return first[None], second[None]


LANES = 128
TAG = 16
LINES = 2


def live_columns(widths, holders, half):
    width = widths[holders[lax.axis_index("sec")]]
    first_column = lax.axis_index("env") * half
    return first_column + lax.broadcasted_iota(jnp.int32, (1, half), 1) < width


def apply_term(right, left, vector, term):
    products = jnp.dot(right[term], vector, preferred_element_type=jnp.float32)
    return jnp.dot(products.astype(jnp.bfloat16), left, preferred_element_type=jnp.float32)


def stage_kernel(amps, staged):
    staged[...] = amps[...]


def first_kernel(widths, holders, amps, right, left, message, stay, start):
    slots, _, rows, half = message.shape
    width = widths[holders[lax.axis_index("sec")]]
    columns = lax.broadcasted_iota(jnp.int32, (1, half), 1)
    for h in range(2):
        live = h * half + columns < width
        start[h] = jnp.where(live, amps[h], jnp.zeros_like(amps[h]))
    vector = jnp.concatenate([start[0], start[1]], axis=1)
    for term in (1, 2, 0):
        block = apply_term(right, left[0, term], vector, term).astype(jnp.bfloat16)
        if term == 0:
            stay[...] = block
        else:
            for slot in range(slots):
                message[slot, term - 1] = block[slot * rows : (slot + 1) * rows, :]


def fill_slots(holders, slot_of):
    for s in range(holders.shape[0]):
        slot_of[holders[s]] = jnp.int32(s)


def sources_of(holders, slot_of, target):
    sector = holders[target]
    has = (sector >= QDOWN, sector % QDOWN > 0)
    source = (slot_of[sector & (QDOWN - 1)], slot_of[jnp.maximum(sector - 1, 0)])
    return has, source


def line_targets(holders, slot_of):
    line = lax.axis_index("sec") % LINES
    for place in range(holders.shape[0] // LINES):
        for crossing in range(2):
            has, source = sources_of(holders, slot_of, place * LINES + (line ^ crossing))
            here = [has[i] & (source[i] % LINES == line) for i in range(2)]
            yield place, crossing, here, source


def merge_kernel(holders, table, keep, cross, slot_of):
    fill_slots(holders, slot_of)
    for place, crossing, here, source in line_targets(holders, slot_of):
        total = 0.0
        for i in range(2):
            block = table[source[i] // LINES, i].astype(jnp.float32)
            total = total + jnp.where(here[i], block, 0.0)
        (keep, cross)[crossing][place] = total.astype(jnp.bfloat16)


def join_kernel(keep, arrived, out):
    total = keep[...].astype(jnp.float32) + arrived[...].astype(jnp.float32)
    out[...] = total.astype(jnp.bfloat16)


def sum_kernel(widths, holders, stay, arrived, first):
    live = live_columns(widths, holders, stay.shape[1])
    total = stay[...].astype(jnp.float32) + arrived[...].astype(jnp.float32)
    first[...] = jnp.where(live, total, 0.0).astype(jnp.bfloat16)


def total_of(array):
    return jnp.sum(jnp.sum(array, axis=0, keepdims=True), axis=1, keepdims=True)


def make_tag(values, me):
    row = lax.broadcasted_iota(jnp.int32, (TAG, LANES), 0)
    lane = lax.broadcasted_iota(jnp.int32, (TAG, LANES), 1)
    spread = jnp.zeros((TAG, LANES), jnp.float32)
    for place, value in enumerate(values):
        spread = jnp.where(row // 3 == place, value, spread)
    high = spread.astype(jnp.bfloat16).astype(jnp.float32)
    middle = (spread - high).astype(jnp.bfloat16).astype(jnp.float32)
    low = spread - high - middle
    parts = jnp.where(row % 3 == 0, high, jnp.where(row % 3 == 1, middle, low))
    return jnp.where((lane == me) & (row < 3 * len(values)), parts, 0.0).astype(jnp.bfloat16)


def second_kernel(start, first, right, left, message, stay):
    slots = message.shape[0]
    half = stay.shape[1]
    rows = stay.shape[0] // slots
    chunks = half // LANES
    basis = [start[h].astype(jnp.float32) for h in range(2)]
    firsts = [first[h].astype(jnp.float32) for h in range(2)]
    overlap = total_of(basis[0] * firsts[0]) + total_of(basis[1] * firsts[1])
    norm = total_of(basis[0] * basis[0]) + total_of(basis[1] * basis[1])
    quotient = jnp.where(norm > 0, overlap / jnp.where(norm > 0, norm, 1.0), 0.0)
    deflated = [firsts[h] - quotient * basis[h] for h in range(2)]
    rest_norm = total_of(deflated[0] * deflated[0]) + total_of(deflated[1] * deflated[1])
    vector = jnp.concatenate(deflated, axis=1).astype(jnp.bfloat16)
    tag = make_tag((overlap, norm, quotient, rest_norm), lax.axis_index("sec"))
    for slot in range(slots):
        message[slot, pl.ds(2 * chunks * rows, TAG), :] = tag
    for term in (1, 2, 0):
        block = apply_term(right, left[0, term], vector, term)
        if term == 0:
            stay[...] = block
        else:
            block = block.astype(jnp.bfloat16)
            for slot in range(slots):
                for c in range(chunks):
                    place = pl.ds(((term - 1) * chunks + c) * rows, rows)
                    message[slot, place, :] = block[
                        slot * rows : (slot + 1) * rows, c * LANES : (c + 1) * LANES
                    ]


def read_tag(tag):
    def value(place):
        parts = [tag[3 * place + i : 3 * place + i + 1, :] for i in range(3)]
        return parts[0] + parts[1] + parts[2]

    return [value(place) for place in range(4)]


def line_quotient(overlaps, norms, line):
    inside = lax.broadcasted_iota(jnp.int32, (1, LANES), 1) % LINES == line
    overlap = total_of(jnp.where(inside, overlaps, 0.0))
    norm = total_of(jnp.where(inside, norms, 0.0))
    return jnp.where(norm > 0, overlap / jnp.where(norm > 0, norm, 1.0), 0.0)


def mix_kernel(holders, old, new, keep, cross, tag_out, slot_of):
    places, rows, half = keep.shape
    chunks = half // LANES
    fill_slots(holders, slot_of)
    tag = jnp.zeros((TAG, LANES), jnp.float32)
    for place in range(places):
        tag = tag + new[place, pl.ds(2 * chunks * rows, TAG), :].astype(jnp.float32)
    tag_out[...] = tag.astype(jnp.bfloat16)
    cross[pl.ds(places * chunks * rows, TAG), :] = tag.astype(jnp.bfloat16)
    overlaps, norms, quotients, _ = read_tag(tag)
    shifts = quotients - line_quotient(overlaps, norms, lax.axis_index("sec") % LINES)
    lane = lax.broadcasted_iota(jnp.int32, (1, LANES), 1)
    for place, crossing, here, source in line_targets(holders, slot_of):
        total = 0.0
        for i in range(2):
            where = source[i] // LINES
            block = jnp.concatenate(
                [new[where, pl.ds((i * chunks + c) * rows, rows), :] for c in range(chunks)],
                axis=1,
            ).astype(jnp.float32)
            shift = total_of(jnp.where(lane == source[i], shifts, 0.0))
            block = block + shift * old[where, i].astype(jnp.float32)
            total = total + jnp.where(here[i], block, 0.0)
        if crossing:
            total = total.astype(jnp.bfloat16)
            for c in range(chunks):
                target = pl.ds((place * chunks + c) * rows, rows)
                cross[target, :] = total[:, c * LANES : (c + 1) * LANES]
        else:
            keep[place] = total


def join_mixed_kernel(widths, tag_line, keep, arrived, old_keep, old_arrived, out, factors):
    places, rows, half = keep.shape
    chunks = half // LANES
    slots = widths.shape[0]
    me = lax.axis_index("sec")
    total = jnp.int32(0)
    for slot in range(slots):
        total = total + widths[slot]
    live_count = places * rows * total.astype(jnp.float32)
    tag = tag_line[...].astype(jnp.float32)
    tag = tag + arrived[pl.ds(places * chunks * rows, TAG), :].astype(jnp.float32)
    overlaps, norms, quotients, rests = read_tag(tag)
    quotient = total_of(overlaps) / total_of(norms)
    lane = lax.broadcasted_iota(jnp.int32, (1, LANES), 1)
    shifts = jnp.where(lane < slots, quotients - quotient, 0.0)
    resid_norm = total_of(rests + shifts * shifts * norms)
    scale = lax.rsqrt(resid_norm / live_count + 1e-06)
    row = lax.broadcasted_iota(jnp.int32, factors.shape, 0)
    own_shift = total_of(jnp.where(lane == me, shifts, 0.0))
    factors[...] = jnp.where(row == 0, scale, scale * own_shift)
    line = me % LINES
    shift_here = line_quotient(overlaps, norms, line) - quotient
    shift_there = line_quotient(overlaps, norms, 1 - line) - quotient
    for place in range(places):
        block = jnp.concatenate(
            [arrived[pl.ds((place * chunks + c) * rows, rows), :] for c in range(chunks)],
            axis=1,
        ).astype(jnp.float32)
        block = block + shift_there * old_arrived[place].astype(jnp.float32)
        block = block + keep[place] + shift_here * old_keep[place].astype(jnp.float32)
        out[place] = (scale * block).astype(jnp.bfloat16)


def final_kernel(widths, holders, factors, stay, stay_2, arrived, first, second, first_out):
    first_out[...] = first[...]
    live = live_columns(widths, holders, stay.shape[1])
    scale, shift = factors[0:1, 0:1], factors[1:2, 0:1]
    total = scale * stay_2[...] + shift * stay[...].astype(jnp.float32)
    total = total + arrived[...].astype(jnp.float32)
    second[...] = jnp.where(live, total, 0.0).astype(jnp.bfloat16)


SMEM = pl.BlockSpec(memory_space=pltpu.SMEM)
VMEM = pl.BlockSpec(memory_space=pltpu.VMEM)


def call(kernel, specs, outs, scratch=(), flops=0):
    return pl.pallas_call(
        kernel,
        out_shape=outs,
        in_specs=specs,
        out_specs=jax.tree.map(lambda _: VMEM, outs),
        scratch_shapes=scratch,
        compiler_params=pltpu.CompilerParams(vmem_limit_bytes=16 * 1024 * 1024),
        cost_estimate=pl.CostEstimate(flops=flops, bytes_accessed=1 << 18, transcendentals=0),
    )


def along_line(pieces):
    places = pieces.shape[0]
    groups = [[place * LINES + line for place in range(places)] for line in range(LINES)]
    return lax.all_to_all(pieces, "sec", 0, 0, axis_index_groups=groups)


def across(piece, slots):
    return lax.ppermute(piece, "sec", [(slot, slot ^ 1) for slot in range(slots)])


def on_device(amplitudes, widths, holders, left_env, right_env):
    slots_dev, right_dim, half = amplitudes.shape
    slots = holders.shape[0]
    assert slots_dev == 1
    if slots != 2 * QDOWN:
        return on_device_any(amplitudes, widths, holders, left_env, right_env)
    places = slots // LINES
    rows = right_dim // places
    dots = 6 * right_dim * half * (right_dim + 2 * half)
    block = jax.ShapeDtypeStruct((right_dim, half), jnp.bfloat16)
    wide = jax.ShapeDtypeStruct((right_dim, half), jnp.float32)
    pairs = jax.ShapeDtypeStruct((places, 2, rows, half), jnp.bfloat16)
    singles = jax.ShapeDtypeStruct((places, rows, half), jnp.bfloat16)
    wides = jax.ShapeDtypeStruct((places, rows, half), jnp.float32)
    chunked = rows * half // LANES
    tagged = jax.ShapeDtypeStruct((places, 2 * chunked + TAG, LANES), jnp.bfloat16)
    crossing = jax.ShapeDtypeStruct((places * chunked + TAG, LANES), jnp.bfloat16)
    label = jax.ShapeDtypeStruct((TAG, LANES), jnp.bfloat16)
    factor_shape = jax.ShapeDtypeStruct((8, LANES), jnp.float32)
    slot_table = [pltpu.SMEM((slots,), jnp.int32)]

    staged = call(stage_kernel, [VMEM], block, flops=4 << 30)(amplitudes[0])
    amps_full = lax.all_gather(staged, "env")
    both = jax.ShapeDtypeStruct(amps_full.shape, jnp.bfloat16)
    message, stay, start_full = call(
        first_kernel, [SMEM, SMEM] + [VMEM] * 3, (pairs, block, both), flops=dots
    )(widths, holders, amps_full, right_env, left_env)
    old = along_line(message)
    old_keep, cross = call(merge_kernel, [SMEM, VMEM], (singles, singles), slot_table)(holders, old)
    old_arrived = across(cross, slots)
    joined = call(join_kernel, [VMEM, VMEM], singles)(old_keep, old_arrived)
    arrived = along_line(joined).reshape(right_dim, half)
    first = call(sum_kernel, [SMEM, SMEM, VMEM, VMEM], block)(widths, holders, stay, arrived)

    first_full = lax.all_gather(first, "env")
    message, stay_2 = call(second_kernel, [VMEM] * 4, (tagged, wide), flops=dots)(
        start_full, first_full, right_env, left_env
    )
    new = along_line(message)
    keep, cross, tag = call(
        mix_kernel, [SMEM, VMEM, VMEM], (wides, crossing, label), slot_table
    )(holders, old, new)
    joined, factors = call(join_mixed_kernel, [SMEM] + [VMEM] * 5, (singles, factor_shape))(
        widths, tag, keep, across(cross, slots), old_keep, old_arrived
    )
    arrived = along_line(joined).reshape(right_dim, half)
    second, first = call(final_kernel, [SMEM, SMEM] + [VMEM] * 5, (block, block))(
        widths, holders, factors, stay, stay_2, arrived, first
    )
    return first[None], second[None]


def solution(mesh):
    in_specs = (
        P(("runs", "sec"), None, "env"),
        P("runs"),
        P("runs"),
        P(("runs", "sec"), None, None, "env"),
        P("runs", None, None),
    )
    out_specs = (P(("runs", "sec"), None, "env"), P(("runs", "sec"), None, "env"))
    return jax.shard_map(
        on_device, mesh=mesh, in_specs=in_specs, out_specs=out_specs, check_vma=False
    )
```

```python
import jax
import jax.numpy as jnp
from jax import lax
from jax.experimental import pallas as pl
from jax.experimental.pallas import tpu as pltpu
from jax.sharding import PartitionSpec as P

QDOWN = 4

term_shifts = ((0, 0), (1, 0), (0, 1))


def route(holders):
    n_slots = holders.shape[0]
    sector_ids = jnp.arange(n_slots, dtype=jnp.int32)
    slot_of = jnp.argmax(holders[None, :] == sector_ids[:, None], axis=1)
    sources = []
    allowed = []
    for up, down in term_shifts[1:]:
        permitted = (holders // QDOWN - up >= 0) & (holders % QDOWN - down >= 0)
        wanted = jnp.clip(holders - QDOWN * up - down, 0, n_slots - 1)
        sources.append(slot_of[wanted])
        allowed.append(permitted)
    return sources, allowed


def contract(vector, left_env, right_env):
    products = jnp.einsum(
        "tij,jw->tiw", right_env, vector, preferred_element_type=jnp.float32
    ).astype(jnp.bfloat16)
    return jnp.einsum("tik,tkw->tiw", products, left_env, preferred_element_type=jnp.float32)


def spread(blocks, n_slots):
    terms, rows, width = blocks.shape
    pieces = blocks.reshape(terms, n_slots, rows // n_slots, width).swapaxes(0, 1)
    return lax.all_to_all(pieces, "sec", split_axis=0, concat_axis=0)


def collect(merged):
    n_slots, rows, width = merged.shape
    home = lax.all_to_all(merged, "sec", split_axis=0, concat_axis=0)
    return home.reshape(n_slots * rows, width)


def share(values, n_slots, me):
    lanes = jnp.zeros((1, 128), jnp.float32).at[0, : values.shape[0]].set(values)
    if n_slots & (n_slots - 1) or n_slots > 16:
        return lax.all_gather(lanes[0], "sec")
    table = jnp.where(jnp.arange(n_slots)[:, None] == me, lanes, 0.0)
    for offset in range(1, n_slots):
        pairs = [(i, i ^ offset) for i in range(n_slots)]
        other = lax.ppermute(lanes, "sec", pairs)
        table = jnp.where(jnp.arange(n_slots)[:, None] == (me ^ offset), other, table)
    return table


def merge(received, sources, allowed):
    total = 0.0
    for term, (source, permitted) in enumerate(zip(sources, allowed)):
        picked = received[source, term]
        total = total + jnp.where(permitted[:, None, None], picked, 0).astype(jnp.float32)
    return total


def on_device_any(amplitudes, widths, holders, left_env, right_env):
    slots_dev, right_dim, half_width = amplitudes.shape
    assert slots_dev == 1
    n_slots = holders.shape[0]
    me = lax.axis_index("sec")
    side = lax.axis_index("env")
    my_width = widths[holders[me]]
    row_index = side * half_width + jnp.arange(half_width, dtype=jnp.int32)
    live = (row_index < my_width)[None, :]
    sources, allowed = route(holders)
    envs = left_env[0]

    start = jnp.where(live, amplitudes[0], jnp.zeros_like(amplitudes[0]))
    start_full = lax.all_gather(start, "env", axis=1, tiled=True)
    outgoing = contract(start_full, envs, right_env).astype(jnp.bfloat16)
    stay = outgoing[0].astype(jnp.float32)
    received = spread(outgoing[1:], n_slots)
    arrived = collect(merge(received, sources, allowed).astype(jnp.bfloat16))
    first = jnp.where(live, stay + arrived.astype(jnp.float32), 0.0).astype(jnp.bfloat16)

    first_full = lax.all_gather(first, "env", axis=1, tiled=True).astype(jnp.float32)
    basis = start_full.astype(jnp.float32)
    overlap = jnp.sum(basis * first_full)
    norm = jnp.sum(basis * basis)
    own_quotient = jnp.where(norm > 0, overlap / jnp.where(norm > 0, norm, 1.0), 0.0)
    deflated = first_full - own_quotient * basis
    rest = jnp.sum(deflated * deflated)
    sums = share(jnp.stack([overlap, norm, own_quotient, rest]), n_slots, me)
    outgoing_2 = contract(deflated.astype(jnp.bfloat16), envs, right_env)
    received_2 = spread(outgoing_2[1:].astype(jnp.bfloat16), n_slots)

    quotient = jnp.sum(sums[:, 0]) / jnp.sum(sums[:, 1])
    shift = sums[:, 2] - quotient
    resid_norm = jnp.sum(sums[:, 3] + shift * shift * sums[:, 1])
    live_count = right_dim * jnp.sum(widths).astype(jnp.float32)
    scale = lax.rsqrt(resid_norm / live_count + 1e-06)
    mixed = received_2.astype(jnp.float32) + shift[:, None, None, None] * received.astype(
        jnp.float32
    )
    merged_2 = scale * merge(mixed, sources, allowed)
    arrived_2 = collect(merged_2.astype(jnp.bfloat16))
    stay_2 = scale * (outgoing_2[0] + (own_quotient - quotient) * stay)
    second = jnp.where(live, stay_2 + arrived_2.astype(jnp.float32), 0.0).astype(jnp.bfloat16)
    return first[None], second[None]


LANES = 128
TAG = 16


def live_columns(widths, holders, half):
    width = widths[holders[lax.axis_index("sec")]]
    first_column = lax.axis_index("env") * half
    return first_column + lax.broadcasted_iota(jnp.int32, (1, half), 1) < width


def apply_term(right, left, vector, term):
    products = jnp.dot(right[term], vector, preferred_element_type=jnp.float32)
    return jnp.dot(products.astype(jnp.bfloat16), left, preferred_element_type=jnp.float32)


def columns_kernel(columns):
    columns[...] = lax.broadcasted_iota(jnp.int32, columns.shape, 1)


def masked(widths, holders, columns, amps):
    half = amps.shape[2]
    width = widths[holders[lax.axis_index("sec")]]
    return [
        jnp.where(columns[0:1, :] < width - h * half, amps[h], jnp.zeros_like(amps[h]))
        for h in range(2)
    ]


def first_kernel(widths, holders, columns, amps, right, left, message, stay):
    slots, _, rows, half = message.shape
    vector = jnp.concatenate(masked(widths, holders, columns, amps), axis=1)
    for term in (1, 2, 0):
        block = apply_term(right, left[0, term], vector, term).astype(jnp.bfloat16)
        if term == 0:
            stay[...] = block
        else:
            for slot in range(slots):
                message[slot, term - 1] = block[slot * rows : (slot + 1) * rows, :]


def fill_slots(holders, slot_of):
    for s in range(holders.shape[0]):
        slot_of[holders[s]] = jnp.int32(s)


def sources_of(holders, slot_of, target):
    sector = holders[target]
    has = (sector >= QDOWN, sector % QDOWN > 0)
    source = (slot_of[sector & (QDOWN - 1)], slot_of[jnp.maximum(sector - 1, 0)])
    return has, source


def merge_kernel(holders, table, out, slot_of):
    fill_slots(holders, slot_of)
    for slot in range(holders.shape[0]):
        has, source = sources_of(holders, slot_of, slot)
        total = 0.0
        for i in range(2):
            block = table[source[i], i].astype(jnp.float32)
            total = total + jnp.where(has[i], block, 0.0)
        out[slot] = total.astype(jnp.bfloat16)


def sum_kernel(widths, holders, stay, arrived, first):
    live = live_columns(widths, holders, stay.shape[1])
    total = stay[...].astype(jnp.float32) + arrived[...].astype(jnp.float32)
    first[...] = jnp.where(live, total, 0.0).astype(jnp.bfloat16)


def total_of(array):
    return jnp.sum(jnp.sum(array, axis=0, keepdims=True), axis=1, keepdims=True)


def make_tag(values, me):
    row = lax.broadcasted_iota(jnp.int32, (TAG, LANES), 0)
    lane = lax.broadcasted_iota(jnp.int32, (TAG, LANES), 1)
    spread = jnp.zeros((TAG, LANES), jnp.float32)
    for place, value in enumerate(values):
        spread = jnp.where(row // 3 == place, value, spread)
    high = spread.astype(jnp.bfloat16).astype(jnp.float32)
    middle = (spread - high).astype(jnp.bfloat16).astype(jnp.float32)
    low = spread - high - middle
    parts = jnp.where(row % 3 == 0, high, jnp.where(row % 3 == 1, middle, low))
    return jnp.where((lane == me) & (row < 3 * len(values)), parts, 0.0).astype(jnp.bfloat16)


def second_kernel(widths, holders, columns, amps, first, right, left, message, stay):
    slots = message.shape[0]
    half = stay.shape[1]
    rows = stay.shape[0] // slots
    chunks = half // LANES
    basis = [part.astype(jnp.float32) for part in masked(widths, holders, columns, amps)]
    firsts = [first[h].astype(jnp.float32) for h in range(2)]
    overlap = total_of(basis[0] * firsts[0]) + total_of(basis[1] * firsts[1])
    norm = total_of(basis[0] * basis[0]) + total_of(basis[1] * basis[1])
    quotient = jnp.where(norm > 0, overlap / jnp.where(norm > 0, norm, 1.0), 0.0)
    deflated = [firsts[h] - quotient * basis[h] for h in range(2)]
    rest_norm = total_of(deflated[0] * deflated[0]) + total_of(deflated[1] * deflated[1])
    vector = jnp.concatenate(deflated, axis=1).astype(jnp.bfloat16)
    tag = make_tag((overlap, norm, quotient, rest_norm), lax.axis_index("sec"))
    for slot in range(slots):
        message[slot, pl.ds(2 * chunks * rows, TAG), :] = tag
    for term in (1, 2, 0):
        block = apply_term(right, left[0, term], vector, term)
        if term == 0:
            stay[...] = block
        else:
            block = block.astype(jnp.bfloat16)
            for slot in range(slots):
                for c in range(chunks):
                    place = pl.ds(((term - 1) * chunks + c) * rows, rows)
                    message[slot, place, :] = block[
                        slot * rows : (slot + 1) * rows, c * LANES : (c + 1) * LANES
                    ]


def mix_kernel(widths, holders, old, new, out, factors, slot_of):
    slots, rows, half = out.shape
    chunks = half // LANES
    fill_slots(holders, slot_of)
    tag = jnp.zeros((TAG, LANES), jnp.float32)
    total = jnp.int32(0)
    for slot in range(slots):
        tag = tag + new[slot, pl.ds(2 * chunks * rows, TAG), :].astype(jnp.float32)
        total = total + widths[slot]
    live_count = slots * rows * total.astype(jnp.float32)

    def value(place):
        parts = [tag[3 * place + i : 3 * place + i + 1, :] for i in range(3)]
        return parts[0] + parts[1] + parts[2]

    overlaps, norms, quotients, rests = (value(place) for place in range(4))
    quotient = total_of(overlaps) / total_of(norms)
    lane = lax.broadcasted_iota(jnp.int32, (1, LANES), 1)
    shifts = jnp.where(lane < slots, quotients - quotient, 0.0)
    resid_norm = total_of(rests + shifts * shifts * norms)
    scale = lax.rsqrt(resid_norm / live_count + 1e-06)

    def shift_of(slot):
        return total_of(jnp.where(lane == slot, shifts, 0.0))

    row = lax.broadcasted_iota(jnp.int32, factors.shape, 0)
    me = lax.axis_index("sec")
    bound = widths[holders[me]] - lax.axis_index("env") * half
    factors[...] = jnp.where(
        row == 0, scale, jnp.where(row == 1, scale * shift_of(me), bound.astype(jnp.float32))
    )
    for slot in range(slots):
        has, source = sources_of(holders, slot_of, slot)
        total = 0.0
        for i in range(2):
            block = jnp.concatenate(
                [
                    new[source[i], pl.ds((i * chunks + c) * rows, rows), :]
                    for c in range(chunks)
                ],
                axis=1,
            ).astype(jnp.float32)
            block = block + shift_of(source[i]) * old[source[i], i].astype(jnp.float32)
            total = total + jnp.where(has[i], block, 0.0)
        out[slot] = (scale * total).astype(jnp.bfloat16)


SMEM = pl.BlockSpec(memory_space=pltpu.SMEM)
VMEM = pl.BlockSpec(memory_space=pltpu.VMEM)


def call(kernel, specs, outs, scratch=(), flops=0):
    return pl.pallas_call(
        kernel,
        out_shape=outs,
        in_specs=specs,
        out_specs=jax.tree.map(lambda _: VMEM, outs),
        scratch_shapes=scratch,
        compiler_params=pltpu.CompilerParams(vmem_limit_bytes=16 * 1024 * 1024),
        cost_estimate=pl.CostEstimate(flops=flops, bytes_accessed=1 << 18, transcendentals=0),
    )


def swap(pieces):
    return lax.all_to_all(pieces, "sec", split_axis=0, concat_axis=0)


def on_device(amplitudes, widths, holders, left_env, right_env):
    slots_dev, right_dim, half = amplitudes.shape
    slots = holders.shape[0]
    assert slots_dev == 1
    if slots != 2 * QDOWN:
        return on_device_any(amplitudes, widths, holders, left_env, right_env)
    rows = right_dim // slots
    dots = 6 * right_dim * half * (right_dim + 2 * half)
    block = jax.ShapeDtypeStruct((right_dim, half), jnp.bfloat16)
    wide = jax.ShapeDtypeStruct((right_dim, half), jnp.float32)
    pairs = jax.ShapeDtypeStruct((slots, 2, rows, half), jnp.bfloat16)
    singles = jax.ShapeDtypeStruct((slots, rows, half), jnp.bfloat16)
    tagged = jax.ShapeDtypeStruct((slots, 2 * rows * half // LANES + TAG, LANES), jnp.bfloat16)
    factor_shape = jax.ShapeDtypeStruct((8, LANES), jnp.float32)
    slot_table = [pltpu.SMEM((slots,), jnp.int32)]

    number = jax.ShapeDtypeStruct((8, half), jnp.int32)
    columns = call(columns_kernel, [], number, flops=4 << 30)()
    columns, amps = lax.optimization_barrier((columns, amplitudes[0]))
    amps_full = lax.all_gather(amps, "env")
    message, stay = call(first_kernel, [SMEM, SMEM] + [VMEM] * 4, (pairs, block), flops=dots)(
        widths, holders, columns, amps_full, right_env, left_env
    )
    old = swap(message)
    merged = call(merge_kernel, [SMEM, VMEM], singles, slot_table)(holders, old)
    arrived = swap(merged).reshape(right_dim, half)
    first = call(sum_kernel, [SMEM, SMEM, VMEM, VMEM], block)(widths, holders, stay, arrived)

    first_full = lax.all_gather(first, "env")
    message, stay_2 = call(
        second_kernel, [SMEM, SMEM] + [VMEM] * 5, (tagged, wide), flops=dots
    )(widths, holders, columns, amps_full, first_full, right_env, left_env)
    new = swap(message)
    mixed, factors = call(
        mix_kernel, [SMEM, SMEM, VMEM, VMEM], (singles, factor_shape), slot_table
    )(widths, holders, old, new)
    arrived = swap(mixed).reshape(right_dim, half)
    total = factors[0:1, 0:1] * stay_2 + factors[1:2, 0:1] * stay.astype(jnp.float32)
    total = total + arrived.astype(jnp.float32)
    live = lax.broadcasted_iota(jnp.int32, (right_dim, half), 1).astype(jnp.float32) < factors[2:3, 0:1]
    second = jnp.where(live, total, 0.0).astype(jnp.bfloat16)
    first = jnp.where(live, first, jnp.zeros_like(first))
    return first[None], second[None]


def solution(mesh):
    in_specs = (
        P(("runs", "sec"), None, "env"),
        P("runs"),
        P("runs"),
        P(("runs", "sec"), None, None, "env"),
        P("runs", None, None),
    )
    out_specs = (P(("runs", "sec"), None, "env"), P(("runs", "sec"), None, "env"))
    return jax.shard_map(
        on_device, mesh=mesh, in_specs=in_specs, out_specs=out_specs, check_vma=False
    )
```

```python
import jax
import jax.numpy as jnp
from jax import lax
from jax.experimental import pallas as pl
from jax.experimental.pallas import tpu as pltpu
from jax.sharding import PartitionSpec as P

QDOWN = 4

term_shifts = ((0, 0), (1, 0), (0, 1))


def route(holders):
    n_slots = holders.shape[0]
    sector_ids = jnp.arange(n_slots, dtype=jnp.int32)
    slot_of = jnp.argmax(holders[None, :] == sector_ids[:, None], axis=1)
    sources = []
    allowed = []
    for up, down in term_shifts[1:]:
        permitted = (holders // QDOWN - up >= 0) & (holders % QDOWN - down >= 0)
        wanted = jnp.clip(holders - QDOWN * up - down, 0, n_slots - 1)
        sources.append(slot_of[wanted])
        allowed.append(permitted)
    return sources, allowed


def contract(vector, left_env, right_env):
    products = jnp.einsum(
        "tij,jw->tiw", right_env, vector, preferred_element_type=jnp.float32
    ).astype(jnp.bfloat16)
    return jnp.einsum("tik,tkw->tiw", products, left_env, preferred_element_type=jnp.float32)


def spread(blocks, n_slots):
    terms, rows, width = blocks.shape
    pieces = blocks.reshape(terms, n_slots, rows // n_slots, width).swapaxes(0, 1)
    return lax.all_to_all(pieces, "sec", split_axis=0, concat_axis=0)


def collect(merged):
    n_slots, rows, width = merged.shape
    home = lax.all_to_all(merged, "sec", split_axis=0, concat_axis=0)
    return home.reshape(n_slots * rows, width)


def share(values, n_slots, me):
    lanes = jnp.zeros((1, 128), jnp.float32).at[0, : values.shape[0]].set(values)
    if n_slots & (n_slots - 1) or n_slots > 16:
        return lax.all_gather(lanes[0], "sec")
    table = jnp.where(jnp.arange(n_slots)[:, None] == me, lanes, 0.0)
    for offset in range(1, n_slots):
        pairs = [(i, i ^ offset) for i in range(n_slots)]
        other = lax.ppermute(lanes, "sec", pairs)
        table = jnp.where(jnp.arange(n_slots)[:, None] == (me ^ offset), other, table)
    return table


def merge(received, sources, allowed):
    total = 0.0
    for term, (source, permitted) in enumerate(zip(sources, allowed)):
        picked = received[source, term]
        total = total + jnp.where(permitted[:, None, None], picked, 0).astype(jnp.float32)
    return total


def on_device_any(amplitudes, widths, holders, left_env, right_env):
    slots_dev, right_dim, half_width = amplitudes.shape
    assert slots_dev == 1
    n_slots = holders.shape[0]
    me = lax.axis_index("sec")
    side = lax.axis_index("env")
    my_width = widths[holders[me]]
    row_index = side * half_width + jnp.arange(half_width, dtype=jnp.int32)
    live = (row_index < my_width)[None, :]
    sources, allowed = route(holders)
    envs = left_env[0]

    start = jnp.where(live, amplitudes[0], jnp.zeros_like(amplitudes[0]))
    start_full = lax.all_gather(start, "env", axis=1, tiled=True)
    outgoing = contract(start_full, envs, right_env).astype(jnp.bfloat16)
    stay = outgoing[0].astype(jnp.float32)
    received = spread(outgoing[1:], n_slots)
    arrived = collect(merge(received, sources, allowed).astype(jnp.bfloat16))
    first = jnp.where(live, stay + arrived.astype(jnp.float32), 0.0).astype(jnp.bfloat16)

    first_full = lax.all_gather(first, "env", axis=1, tiled=True).astype(jnp.float32)
    basis = start_full.astype(jnp.float32)
    overlap = jnp.sum(basis * first_full)
    norm = jnp.sum(basis * basis)
    own_quotient = jnp.where(norm > 0, overlap / jnp.where(norm > 0, norm, 1.0), 0.0)
    deflated = first_full - own_quotient * basis
    rest = jnp.sum(deflated * deflated)
    sums = share(jnp.stack([overlap, norm, own_quotient, rest]), n_slots, me)
    outgoing_2 = contract(deflated.astype(jnp.bfloat16), envs, right_env)
    received_2 = spread(outgoing_2[1:].astype(jnp.bfloat16), n_slots)

    quotient = jnp.sum(sums[:, 0]) / jnp.sum(sums[:, 1])
    shift = sums[:, 2] - quotient
    resid_norm = jnp.sum(sums[:, 3] + shift * shift * sums[:, 1])
    live_count = right_dim * jnp.sum(widths).astype(jnp.float32)
    scale = lax.rsqrt(resid_norm / live_count + 1e-06)
    mixed = received_2.astype(jnp.float32) + shift[:, None, None, None] * received.astype(
        jnp.float32
    )
    merged_2 = scale * merge(mixed, sources, allowed)
    arrived_2 = collect(merged_2.astype(jnp.bfloat16))
    stay_2 = scale * (outgoing_2[0] + (own_quotient - quotient) * stay)
    second = jnp.where(live, stay_2 + arrived_2.astype(jnp.float32), 0.0).astype(jnp.bfloat16)
    return first[None], second[None]


LANES = 128
TAG = 16
LINES = 2


def live_columns(widths, holders, half):
    width = widths[holders[lax.axis_index("sec")]]
    first_column = lax.axis_index("env") * half
    return first_column + lax.broadcasted_iota(jnp.int32, (1, half), 1) < width


def apply_term(right, left, vector, term):
    products = jnp.dot(right[term], vector, preferred_element_type=jnp.float32)
    return jnp.dot(products.astype(jnp.bfloat16), left, preferred_element_type=jnp.float32)


def stage_kernel(amps, staged):
    staged[...] = amps[...]


def own_place():
    return lax.axis_index("sec") // LINES


def first_kernel(widths, holders, amps, right, left, *rest):
    *pieces, stay, start, block_vmem = rest
    half = stay.shape[1]
    width = widths[holders[lax.axis_index("sec")]]
    columns = lax.broadcasted_iota(jnp.int32, (1, half), 1)
    for h in range(2):
        live = h * half + columns < width
        start[h] = jnp.where(live, amps[h], jnp.zeros_like(amps[h]))
    vector = jnp.concatenate([start[0], start[1]], axis=1)
    for term in (1, 2, 0):
        block = apply_term(right, left[0, term], vector, term).astype(jnp.bfloat16)
        if term == 0:
            stay[...] = block
        else:
            block_vmem[...] = block.reshape(block_vmem.shape)
            for step, piece in enumerate(pieces):
                piece[term - 1] = block_vmem[own_place() ^ step]


def fill_slots(holders, slot_of):
    for s in range(holders.shape[0]):
        slot_of[holders[s]] = jnp.int32(s)


def sources_of(holders, slot_of, target):
    sector = holders[target]
    has = (sector >= QDOWN, sector % QDOWN > 0)
    source = (slot_of[sector & (QDOWN - 1)], slot_of[jnp.maximum(sector - 1, 0)])
    return has, source


def line_targets(holders, slot_of):
    line = lax.axis_index("sec") % LINES
    for place in range(holders.shape[0] // LINES):
        for crossing in range(2):
            has, source = sources_of(holders, slot_of, place * LINES + (line ^ crossing))
            here = [has[i] & (source[i] % LINES == line) for i in range(2)]
            yield place, crossing, here, source


def merge_kernel(holders, *rest):
    *pieces, keep, cross, table, slot_of = rest
    fill_slots(holders, slot_of)
    for step, piece in enumerate(pieces):
        table[own_place() ^ step] = piece[...]
    for place, crossing, here, source in line_targets(holders, slot_of):
        total = 0.0
        for i in range(2):
            block = table[source[i] // LINES, i].astype(jnp.float32)
            total = total + jnp.where(here[i], block, 0.0)
        (keep, cross)[crossing][place] = total.astype(jnp.bfloat16)


def join_kernel(keep, arrived, *outs):
    for step, out in enumerate(outs):
        place = own_place() ^ step
        total = keep[place].astype(jnp.float32) + arrived[place].astype(jnp.float32)
        out[...] = total.astype(jnp.bfloat16)


def piece_rows(step, rows):
    return pl.ds(pl.multiple_of((own_place() ^ step) * rows, rows), rows)


def sum_kernel(widths, holders, stay, *rest):
    *pieces, first = rest
    live = live_columns(widths, holders, stay.shape[1])
    for step, piece in enumerate(pieces):
        place = piece_rows(step, piece.shape[0])
        total = stay[place, :].astype(jnp.float32) + piece[...].astype(jnp.float32)
        first[place, :] = jnp.where(live, total, 0.0).astype(jnp.bfloat16)


def total_of(array):
    return jnp.sum(jnp.sum(array, axis=0, keepdims=True), axis=1, keepdims=True)


def make_tag(values, me):
    row = lax.broadcasted_iota(jnp.int32, (TAG, LANES), 0)
    lane = lax.broadcasted_iota(jnp.int32, (TAG, LANES), 1)
    spread = jnp.zeros((TAG, LANES), jnp.float32)
    for place, value in enumerate(values):
        spread = jnp.where(row // 3 == place, value, spread)
    high = spread.astype(jnp.bfloat16).astype(jnp.float32)
    middle = (spread - high).astype(jnp.bfloat16).astype(jnp.float32)
    low = spread - high - middle
    parts = jnp.where(row % 3 == 0, high, jnp.where(row % 3 == 1, middle, low))
    return jnp.where((lane == me) & (row < 3 * len(values)), parts, 0.0).astype(jnp.bfloat16)


def second_kernel(start, first, right, left, *rest):
    *pieces, stay, block_vmem = rest
    half = stay.shape[1]
    rows = block_vmem.shape[1]
    chunks = half // LANES
    basis = [start[h].astype(jnp.float32) for h in range(2)]
    firsts = [first[h].astype(jnp.float32) for h in range(2)]
    overlap = total_of(basis[0] * firsts[0]) + total_of(basis[1] * firsts[1])
    norm = total_of(basis[0] * basis[0]) + total_of(basis[1] * basis[1])
    quotient = jnp.where(norm > 0, overlap / jnp.where(norm > 0, norm, 1.0), 0.0)
    deflated = [firsts[h] - quotient * basis[h] for h in range(2)]
    rest_norm = total_of(deflated[0] * deflated[0]) + total_of(deflated[1] * deflated[1])
    vector = jnp.concatenate(deflated, axis=1).astype(jnp.bfloat16)
    tag = make_tag((overlap, norm, quotient, rest_norm), lax.axis_index("sec"))
    for piece in pieces:
        piece[pl.ds(2 * chunks * rows, TAG), :] = tag
    for term in (1, 2, 0):
        block = apply_term(right, left[0, term], vector, term)
        if term == 0:
            stay[...] = block
        else:
            block_vmem[...] = block.astype(jnp.bfloat16).reshape(block_vmem.shape)
            for step, piece in enumerate(pieces):
                part = block_vmem[own_place() ^ step]
                for c in range(chunks):
                    place = pl.ds(((term - 1) * chunks + c) * rows, rows)
                    piece[place, :] = part[:, c * LANES : (c + 1) * LANES]


def read_tag(tag):
    def value(place):
        parts = [tag[3 * place + i : 3 * place + i + 1, :] for i in range(3)]
        return parts[0] + parts[1] + parts[2]

    return [value(place) for place in range(4)]


def line_quotient(overlaps, norms, line):
    inside = lax.broadcasted_iota(jnp.int32, (1, LANES), 1) % LINES == line
    overlap = total_of(jnp.where(inside, overlaps, 0.0))
    norm = total_of(jnp.where(inside, norms, 0.0))
    return jnp.where(norm > 0, overlap / jnp.where(norm > 0, norm, 1.0), 0.0)


def mix_kernel(holders, *rest):
    keep, cross, tag_out, old, new, slot_of = rest[-6:]
    places, rows, half = keep.shape
    chunks = half // LANES
    fill_slots(holders, slot_of)
    tag = jnp.zeros((TAG, LANES), jnp.float32)
    for step in range(places):
        old[own_place() ^ step] = rest[step][...]
        new[own_place() ^ step] = rest[places + step][...]
        label = rest[places + step][pl.ds(2 * chunks * rows, TAG), :]
        tag = tag + label.astype(jnp.float32)
    tag_out[...] = tag.astype(jnp.bfloat16)
    cross[pl.ds(places * chunks * rows, TAG), :] = tag.astype(jnp.bfloat16)
    overlaps, norms, quotients, _ = read_tag(tag)
    shifts = quotients - line_quotient(overlaps, norms, lax.axis_index("sec") % LINES)
    lane = lax.broadcasted_iota(jnp.int32, (1, LANES), 1)
    for place, crossing, here, source in line_targets(holders, slot_of):
        total = 0.0
        for i in range(2):
            where = source[i] // LINES
            block = jnp.concatenate(
                [new[where, pl.ds((i * chunks + c) * rows, rows), :] for c in range(chunks)],
                axis=1,
            ).astype(jnp.float32)
            shift = total_of(jnp.where(lane == source[i], shifts, 0.0))
            block = block + shift * old[where, i].astype(jnp.float32)
            total = total + jnp.where(here[i], block, 0.0)
        if crossing:
            total = total.astype(jnp.bfloat16)
            for c in range(chunks):
                target = pl.ds((place * chunks + c) * rows, rows)
                cross[target, :] = total[:, c * LANES : (c + 1) * LANES]
        else:
            keep[place] = total


def join_mixed_kernel(widths, tag_line, keep, arrived, old_keep, old_arrived, *rest):
    *outs, factors = rest
    places, rows, half = keep.shape
    chunks = half // LANES
    slots = widths.shape[0]
    me = lax.axis_index("sec")
    total = jnp.int32(0)
    for slot in range(slots):
        total = total + widths[slot]
    live_count = places * rows * total.astype(jnp.float32)
    tag = tag_line[...].astype(jnp.float32)
    tag = tag + arrived[pl.ds(places * chunks * rows, TAG), :].astype(jnp.float32)
    overlaps, norms, quotients, rests = read_tag(tag)
    quotient = total_of(overlaps) / total_of(norms)
    lane = lax.broadcasted_iota(jnp.int32, (1, LANES), 1)
    shifts = jnp.where(lane < slots, quotients - quotient, 0.0)
    resid_norm = total_of(rests + shifts * shifts * norms)
    scale = lax.rsqrt(resid_norm / live_count + 1e-06)
    row = lax.broadcasted_iota(jnp.int32, factors.shape, 0)
    own_shift = total_of(jnp.where(lane == me, shifts, 0.0))
    factors[...] = jnp.where(row == 0, scale, scale * own_shift)
    line = me % LINES
    shift_here = line_quotient(overlaps, norms, line) - quotient
    shift_there = line_quotient(overlaps, norms, 1 - line) - quotient
    for step, out in enumerate(outs):
        place = own_place() ^ step
        starts = [pl.multiple_of((place * chunks + c) * rows, rows) for c in range(chunks)]
        block = jnp.concatenate(
            [arrived[pl.ds(start, rows), :] for start in starts], axis=1
        ).astype(jnp.float32)
        block = block + shift_there * old_arrived[place].astype(jnp.float32)
        block = block + keep[place] + shift_here * old_keep[place].astype(jnp.float32)
        out[...] = (scale * block).astype(jnp.bfloat16)


def final_kernel(widths, holders, factors, stay, stay_2, first, *rest):
    *pieces, second, first_out = rest
    first_out[...] = first[...]
    live = live_columns(widths, holders, stay.shape[1])
    scale, shift = factors[0:1, 0:1], factors[1:2, 0:1]
    for step, piece in enumerate(pieces):
        place = piece_rows(step, piece.shape[0])
        total = scale * stay_2[place, :] + shift * stay[place, :].astype(jnp.float32)
        total = total + piece[...].astype(jnp.float32)
        second[place, :] = jnp.where(live, total, 0.0).astype(jnp.bfloat16)


SMEM = pl.BlockSpec(memory_space=pltpu.SMEM)
VMEM = pl.BlockSpec(memory_space=pltpu.VMEM)


def call(kernel, specs, outs, scratch=(), flops=0):
    return pl.pallas_call(
        kernel,
        out_shape=outs,
        in_specs=specs,
        out_specs=jax.tree.map(lambda _: VMEM, outs),
        scratch_shapes=scratch,
        compiler_params=pltpu.CompilerParams(vmem_limit_bytes=16 * 1024 * 1024),
        cost_estimate=pl.CostEstimate(flops=flops, bytes_accessed=1 << 18, transcendentals=0),
    )


def along_line(pieces, slots):
    sent = [pieces[0]]
    for step in range(1, len(pieces)):
        pairs = [(slot, slot ^ (step * LINES)) for slot in range(slots)]
        sent.append(lax.ppermute(pieces[step], "sec", pairs))
    return sent


def across(piece, slots):
    return lax.ppermute(piece, "sec", [(slot, slot ^ 1) for slot in range(slots)])


def on_device(amplitudes, widths, holders, left_env, right_env):
    slots_dev, right_dim, half = amplitudes.shape
    slots = holders.shape[0]
    assert slots_dev == 1
    if slots != 2 * QDOWN:
        return on_device_any(amplitudes, widths, holders, left_env, right_env)
    places = slots // LINES
    rows = right_dim // places
    dots = 6 * right_dim * half * (right_dim + 2 * half)
    block = jax.ShapeDtypeStruct((right_dim, half), jnp.bfloat16)
    wide = jax.ShapeDtypeStruct((right_dim, half), jnp.float32)
    pair = jax.ShapeDtypeStruct((2, rows, half), jnp.bfloat16)
    single = jax.ShapeDtypeStruct((rows, half), jnp.bfloat16)
    singles = jax.ShapeDtypeStruct((places, rows, half), jnp.bfloat16)
    wides = jax.ShapeDtypeStruct((places, rows, half), jnp.float32)
    chunked = rows * half // LANES
    tagged = jax.ShapeDtypeStruct((2 * chunked + TAG, LANES), jnp.bfloat16)
    crossing = jax.ShapeDtypeStruct((places * chunked + TAG, LANES), jnp.bfloat16)
    label = jax.ShapeDtypeStruct((TAG, LANES), jnp.bfloat16)
    factor_shape = jax.ShapeDtypeStruct((8, LANES), jnp.float32)
    slot_table = pltpu.SMEM((slots,), jnp.int32)
    split = [pltpu.VMEM((places, rows, half), jnp.bfloat16)]
    tables = [pltpu.VMEM((places, *shape.shape), jnp.bfloat16) for shape in (pair, tagged)]

    staged = call(stage_kernel, [VMEM], block, flops=4 << 30)(amplitudes[0])
    amps_full = lax.all_gather(staged, "env")
    both = jax.ShapeDtypeStruct(amps_full.shape, jnp.bfloat16)
    *pieces, stay, start_full = call(
        first_kernel, [SMEM, SMEM] + [VMEM] * 3, (pair,) * places + (block, both), split, dots
    )(widths, holders, amps_full, right_env, left_env)
    old = along_line(pieces, slots)
    old_keep, cross = call(
        merge_kernel, [SMEM] + [VMEM] * places, (singles, singles), [tables[0], slot_table]
    )(holders, *old)
    old_arrived = across(cross, slots)
    joined = call(join_kernel, [VMEM, VMEM], (single,) * places)(old_keep, old_arrived)
    first = call(sum_kernel, [SMEM, SMEM] + [VMEM] * (1 + places), block)(
        widths, holders, stay, *along_line(joined, slots)
    )

    first_full = lax.all_gather(first, "env")
    *pieces, stay_2 = call(
        second_kernel, [VMEM] * 4, (tagged,) * places + (wide,), split, dots
    )(start_full, first_full, right_env, left_env)
    new = along_line(pieces, slots)
    keep, cross, tag = call(
        mix_kernel,
        [SMEM] + [VMEM] * (2 * places),
        (wides, crossing, label),
        [*tables, slot_table],
    )(holders, *old, *new)
    *joined, factors = call(
        join_mixed_kernel, [SMEM] + [VMEM] * 5, (single,) * places + (factor_shape,)
    )(widths, tag, keep, across(cross, slots), old_keep, old_arrived)
    second, first = call(final_kernel, [SMEM, SMEM] + [VMEM] * (4 + places), (block, block))(
        widths, holders, factors, stay, stay_2, first, *along_line(joined, slots)
    )
    return first[None], second[None]


def solution(mesh):
    in_specs = (
        P(("runs", "sec"), None, "env"),
        P("runs"),
        P("runs"),
        P(("runs", "sec"), None, None, "env"),
        P("runs", None, None),
    )
    out_specs = (P(("runs", "sec"), None, "env"), P(("runs", "sec"), None, "env"))
    return jax.shard_map(
        on_device, mesh=mesh, in_specs=in_specs, out_specs=out_specs, check_vma=False
    )
```

```python
import jax
import jax.numpy as jnp
from jax import lax
from jax.experimental import pallas as pl
from jax.experimental.pallas import tpu as pltpu
from jax.sharding import PartitionSpec as P

QDOWN = 4

term_shifts = ((0, 0), (1, 0), (0, 1))


def route(holders):
    n_slots = holders.shape[0]
    sector_ids = jnp.arange(n_slots, dtype=jnp.int32)
    slot_of = jnp.argmax(holders[None, :] == sector_ids[:, None], axis=1)
    sources = []
    allowed = []
    for up, down in term_shifts[1:]:
        permitted = (holders // QDOWN - up >= 0) & (holders % QDOWN - down >= 0)
        wanted = jnp.clip(holders - QDOWN * up - down, 0, n_slots - 1)
        sources.append(slot_of[wanted])
        allowed.append(permitted)
    return sources, allowed


def contract(vector, left_env, right_env):
    products = jnp.einsum(
        "tij,jw->tiw", right_env, vector, preferred_element_type=jnp.float32
    ).astype(jnp.bfloat16)
    return jnp.einsum("tik,tkw->tiw", products, left_env, preferred_element_type=jnp.float32)


def spread(blocks, n_slots):
    terms, rows, width = blocks.shape
    pieces = blocks.reshape(terms, n_slots, rows // n_slots, width).swapaxes(0, 1)
    return lax.all_to_all(pieces, "sec", split_axis=0, concat_axis=0)


def collect(merged):
    n_slots, rows, width = merged.shape
    home = lax.all_to_all(merged, "sec", split_axis=0, concat_axis=0)
    return home.reshape(n_slots * rows, width)


def share(values, n_slots, me):
    lanes = jnp.zeros((1, 128), jnp.float32).at[0, : values.shape[0]].set(values)
    if n_slots & (n_slots - 1) or n_slots > 16:
        return lax.all_gather(lanes[0], "sec")
    table = jnp.where(jnp.arange(n_slots)[:, None] == me, lanes, 0.0)
    for offset in range(1, n_slots):
        pairs = [(i, i ^ offset) for i in range(n_slots)]
        other = lax.ppermute(lanes, "sec", pairs)
        table = jnp.where(jnp.arange(n_slots)[:, None] == (me ^ offset), other, table)
    return table


def merge(received, sources, allowed):
    total = 0.0
    for term, (source, permitted) in enumerate(zip(sources, allowed)):
        picked = received[source, term]
        total = total + jnp.where(permitted[:, None, None], picked, 0).astype(jnp.float32)
    return total


def on_device_any(amplitudes, widths, holders, left_env, right_env):
    slots_dev, right_dim, half_width = amplitudes.shape
    assert slots_dev == 1
    n_slots = holders.shape[0]
    me = lax.axis_index("sec")
    side = lax.axis_index("env")
    my_width = widths[holders[me]]
    row_index = side * half_width + jnp.arange(half_width, dtype=jnp.int32)
    live = (row_index < my_width)[None, :]
    sources, allowed = route(holders)
    envs = left_env[0]

    start = jnp.where(live, amplitudes[0], jnp.zeros_like(amplitudes[0]))
    start_full = lax.all_gather(start, "env", axis=1, tiled=True)
    outgoing = contract(start_full, envs, right_env).astype(jnp.bfloat16)
    stay = outgoing[0].astype(jnp.float32)
    received = spread(outgoing[1:], n_slots)
    arrived = collect(merge(received, sources, allowed).astype(jnp.bfloat16))
    first = jnp.where(live, stay + arrived.astype(jnp.float32), 0.0).astype(jnp.bfloat16)

    first_full = lax.all_gather(first, "env", axis=1, tiled=True).astype(jnp.float32)
    basis = start_full.astype(jnp.float32)
    overlap = jnp.sum(basis * first_full)
    norm = jnp.sum(basis * basis)
    own_quotient = jnp.where(norm > 0, overlap / jnp.where(norm > 0, norm, 1.0), 0.0)
    deflated = first_full - own_quotient * basis
    rest = jnp.sum(deflated * deflated)
    sums = share(jnp.stack([overlap, norm, own_quotient, rest]), n_slots, me)
    outgoing_2 = contract(deflated.astype(jnp.bfloat16), envs, right_env)
    received_2 = spread(outgoing_2[1:].astype(jnp.bfloat16), n_slots)

    quotient = jnp.sum(sums[:, 0]) / jnp.sum(sums[:, 1])
    shift = sums[:, 2] - quotient
    resid_norm = jnp.sum(sums[:, 3] + shift * shift * sums[:, 1])
    live_count = right_dim * jnp.sum(widths).astype(jnp.float32)
    scale = lax.rsqrt(resid_norm / live_count + 1e-06)
    mixed = received_2.astype(jnp.float32) + shift[:, None, None, None] * received.astype(
        jnp.float32
    )
    merged_2 = scale * merge(mixed, sources, allowed)
    arrived_2 = collect(merged_2.astype(jnp.bfloat16))
    stay_2 = scale * (outgoing_2[0] + (own_quotient - quotient) * stay)
    second = jnp.where(live, stay_2 + arrived_2.astype(jnp.float32), 0.0).astype(jnp.bfloat16)
    return first[None], second[None]


LANES = 128
TAG = 16
LINES = 2


def live_columns(widths, holders, half):
    width = widths[holders[lax.axis_index("sec")]]
    first_column = lax.axis_index("env") * half
    return first_column + lax.broadcasted_iota(jnp.int32, (1, half), 1) < width


def apply_term(right, left, vector, term):
    products = jnp.dot(right[term], vector, preferred_element_type=jnp.float32)
    return jnp.dot(products.astype(jnp.bfloat16), left, preferred_element_type=jnp.float32)


def stage_kernel(amps, staged):
    staged[...] = amps[...]


def own_place():
    return lax.axis_index("sec") // LINES


def first_kernel(widths, holders, amps, right, left, *rest):
    *pieces, stay, start, block_vmem = rest
    half = stay.shape[1]
    width = widths[holders[lax.axis_index("sec")]]
    columns = lax.broadcasted_iota(jnp.int32, (1, half), 1)
    for h in range(2):
        live = h * half + columns < width
        start[h] = jnp.where(live, amps[h], jnp.zeros_like(amps[h]))
    vector = jnp.concatenate([start[0], start[1]], axis=1)
    for term in (1, 2, 0):
        block = apply_term(right, left[0, term], vector, term).astype(jnp.bfloat16)
        if term == 0:
            stay[...] = block
        else:
            block_vmem[...] = block.reshape(block_vmem.shape)
            for step, piece in enumerate(pieces):
                piece[term - 1] = block_vmem[own_place() ^ step]


def fill_slots(holders, slot_of):
    for s in range(holders.shape[0]):
        slot_of[holders[s]] = jnp.int32(s)


def sources_of(holders, slot_of, target):
    sector = holders[target]
    has = (sector >= QDOWN, sector % QDOWN > 0)
    source = (slot_of[sector & (QDOWN - 1)], slot_of[jnp.maximum(sector - 1, 0)])
    return has, source


def line_targets(holders, slot_of):
    line = lax.axis_index("sec") % LINES
    for place in range(holders.shape[0] // LINES):
        for crossing in range(2):
            has, source = sources_of(holders, slot_of, place * LINES + (line ^ crossing))
            here = [has[i] & (source[i] % LINES == line) for i in range(2)]
            yield place, crossing, here, source


def merge_kernel(holders, *rest):
    *pieces, keep, cross, table, slot_of = rest
    fill_slots(holders, slot_of)
    for step, piece in enumerate(pieces):
        table[own_place() ^ step] = piece[...]
    for place, crossing, here, source in line_targets(holders, slot_of):
        total = 0.0
        for i in range(2):
            block = table[source[i] // LINES, i].astype(jnp.float32)
            total = total + jnp.where(here[i], block, 0.0)
        (keep, cross)[crossing][place] = total.astype(jnp.bfloat16)


def join_kernel(keep, arrived, *outs):
    for step, out in enumerate(outs):
        place = own_place() ^ step
        total = keep[place].astype(jnp.float32) + arrived[place].astype(jnp.float32)
        out[...] = total.astype(jnp.bfloat16)


def piece_rows(step, rows):
    return pl.ds(pl.multiple_of((own_place() ^ step) * rows, rows), rows)


def sum_kernel(widths, holders, stay, *rest):
    *pieces, first = rest
    live = live_columns(widths, holders, stay.shape[1])
    for step, piece in enumerate(pieces):
        place = piece_rows(step, piece.shape[0])
        total = stay[place, :].astype(jnp.float32) + piece[...].astype(jnp.float32)
        first[place, :] = jnp.where(live, total, 0.0).astype(jnp.bfloat16)


def total_of(array):
    return jnp.sum(jnp.sum(array, axis=0, keepdims=True), axis=1, keepdims=True)


def make_tag(values, me):
    row = lax.broadcasted_iota(jnp.int32, (TAG, LANES), 0)
    lane = lax.broadcasted_iota(jnp.int32, (TAG, LANES), 1)
    spread = jnp.zeros((TAG, LANES), jnp.float32)
    for place, value in enumerate(values):
        spread = jnp.where(row // 3 == place, value, spread)
    high = spread.astype(jnp.bfloat16).astype(jnp.float32)
    middle = (spread - high).astype(jnp.bfloat16).astype(jnp.float32)
    low = spread - high - middle
    parts = jnp.where(row % 3 == 0, high, jnp.where(row % 3 == 1, middle, low))
    return jnp.where((lane == me) & (row < 3 * len(values)), parts, 0.0).astype(jnp.bfloat16)


def second_kernel(start, first, right, left, *rest):
    *pieces, stay, block_vmem = rest
    half = stay.shape[1]
    rows = block_vmem.shape[1]
    chunks = half // LANES
    basis = [start[h].astype(jnp.float32) for h in range(2)]
    firsts = [first[h].astype(jnp.float32) for h in range(2)]
    overlap = total_of(basis[0] * firsts[0]) + total_of(basis[1] * firsts[1])
    norm = total_of(basis[0] * basis[0]) + total_of(basis[1] * basis[1])
    quotient = jnp.where(norm > 0, overlap / jnp.where(norm > 0, norm, 1.0), 0.0)
    deflated = [firsts[h] - quotient * basis[h] for h in range(2)]
    rest_norm = total_of(deflated[0] * deflated[0]) + total_of(deflated[1] * deflated[1])
    vector = jnp.concatenate(deflated, axis=1).astype(jnp.bfloat16)
    tag = make_tag((overlap, norm, quotient, rest_norm), lax.axis_index("sec"))
    for piece in pieces:
        piece[pl.ds(2 * chunks * rows, TAG), :] = tag
    for term in (1, 2, 0):
        block = apply_term(right, left[0, term], vector, term)
        if term == 0:
            stay[...] = block
        else:
            block_vmem[...] = block.astype(jnp.bfloat16).reshape(block_vmem.shape)
            for step, piece in enumerate(pieces):
                part = block_vmem[own_place() ^ step]
                for c in range(chunks):
                    place = pl.ds(((term - 1) * chunks + c) * rows, rows)
                    piece[place, :] = part[:, c * LANES : (c + 1) * LANES]


def read_tag(tag):
    def value(place):
        parts = [tag[3 * place + i : 3 * place + i + 1, :] for i in range(3)]
        return parts[0] + parts[1] + parts[2]

    return [value(place) for place in range(4)]


def line_quotient(overlaps, norms, line):
    inside = lax.broadcasted_iota(jnp.int32, (1, LANES), 1) % LINES == line
    overlap = total_of(jnp.where(inside, overlaps, 0.0))
    norm = total_of(jnp.where(inside, norms, 0.0))
    return jnp.where(norm > 0, overlap / jnp.where(norm > 0, norm, 1.0), 0.0)


def mix_kernel(holders, *rest):
    keep, cross, tag_out, old, new, slot_of = rest[-6:]
    places, rows, half = keep.shape
    chunks = half // LANES
    fill_slots(holders, slot_of)
    tag = jnp.zeros((TAG, LANES), jnp.float32)
    for step in range(places):
        old[own_place() ^ step] = rest[step][...]
        new[own_place() ^ step] = rest[places + step][...]
        label = rest[places + step][pl.ds(2 * chunks * rows, TAG), :]
        tag = tag + label.astype(jnp.float32)
    tag_out[...] = tag.astype(jnp.bfloat16)
    cross[pl.ds(places * chunks * rows, TAG), :] = tag.astype(jnp.bfloat16)
    overlaps, norms, quotients, _ = read_tag(tag)
    shifts = quotients - line_quotient(overlaps, norms, lax.axis_index("sec") % LINES)
    lane = lax.broadcasted_iota(jnp.int32, (1, LANES), 1)
    for place, crossing, here, source in line_targets(holders, slot_of):
        total = 0.0
        for i in range(2):
            where = source[i] // LINES
            block = jnp.concatenate(
                [new[where, pl.ds((i * chunks + c) * rows, rows), :] for c in range(chunks)],
                axis=1,
            ).astype(jnp.float32)
            shift = total_of(jnp.where(lane == source[i], shifts, 0.0))
            block = block + shift * old[where, i].astype(jnp.float32)
            total = total + jnp.where(here[i], block, 0.0)
        if crossing:
            total = total.astype(jnp.bfloat16)
            for c in range(chunks):
                target = pl.ds((place * chunks + c) * rows, rows)
                cross[target, :] = total[:, c * LANES : (c + 1) * LANES]
        else:
            keep[place] = total


def join_mixed_kernel(widths, tag_line, keep, arrived, old_keep, old_arrived, *rest):
    *outs, factors = rest
    places, rows, half = keep.shape
    chunks = half // LANES
    slots = widths.shape[0]
    me = lax.axis_index("sec")
    total = jnp.int32(0)
    for slot in range(slots):
        total = total + widths[slot]
    live_count = places * rows * total.astype(jnp.float32)
    tag = tag_line[...].astype(jnp.float32)
    tag = tag + arrived[pl.ds(places * chunks * rows, TAG), :].astype(jnp.float32)
    overlaps, norms, quotients, rests = read_tag(tag)
    quotient = total_of(overlaps) / total_of(norms)
    lane = lax.broadcasted_iota(jnp.int32, (1, LANES), 1)
    shifts = jnp.where(lane < slots, quotients - quotient, 0.0)
    resid_norm = total_of(rests + shifts * shifts * norms)
    scale = lax.rsqrt(resid_norm / live_count + 1e-06)
    row = lax.broadcasted_iota(jnp.int32, factors.shape, 0)
    own_shift = total_of(jnp.where(lane == me, shifts, 0.0))
    factors[...] = jnp.where(row == 0, scale, scale * own_shift)
    line = me % LINES
    shift_here = line_quotient(overlaps, norms, line) - quotient
    shift_there = line_quotient(overlaps, norms, 1 - line) - quotient
    for step, out in enumerate(outs):
        place = own_place() ^ step
        starts = [pl.multiple_of((place * chunks + c) * rows, rows) for c in range(chunks)]
        block = jnp.concatenate(
            [arrived[pl.ds(start, rows), :] for start in starts], axis=1
        ).astype(jnp.float32)
        block = block + shift_there * old_arrived[place].astype(jnp.float32)
        block = block + keep[place] + shift_here * old_keep[place].astype(jnp.float32)
        out[...] = (scale * block).astype(jnp.bfloat16)


def final_kernel(widths, holders, factors, stay, stay_2, first, *rest):
    *pieces, second, first_out = rest
    first_out[...] = first[...]
    live = live_columns(widths, holders, stay.shape[1])
    scale, shift = factors[0:1, 0:1], factors[1:2, 0:1]
    for step, piece in enumerate(pieces):
        place = piece_rows(step, piece.shape[0])
        total = scale * stay_2[place, :] + shift * stay[place, :].astype(jnp.float32)
        total = total + piece[...].astype(jnp.float32)
        second[place, :] = jnp.where(live, total, 0.0).astype(jnp.bfloat16)


SMEM = pl.BlockSpec(memory_space=pltpu.SMEM)
VMEM = pl.BlockSpec(memory_space=pltpu.VMEM)


def call(kernel, specs, outs, scratch=(), flops=0):
    return pl.pallas_call(
        kernel,
        out_shape=outs,
        in_specs=specs,
        out_specs=jax.tree.map(lambda _: VMEM, outs),
        scratch_shapes=scratch,
        compiler_params=pltpu.CompilerParams(vmem_limit_bytes=16 * 1024 * 1024),
        cost_estimate=pl.CostEstimate(flops=flops, bytes_accessed=1 << 18, transcendentals=0),
    )


def along_line(pieces, slots):
    places = len(pieces)
    sent = {0: pieces[0]}
    for step in sorted(range(1, places), key=lambda step: step < places // 2):
        pairs = [(slot, slot ^ (step * LINES)) for slot in range(slots)]
        sent[step] = lax.ppermute(pieces[step], "sec", pairs)
    return [sent[step] for step in range(places)]


def across(piece, slots):
    return lax.ppermute(piece, "sec", [(slot, slot ^ 1) for slot in range(slots)])


def on_device(amplitudes, widths, holders, left_env, right_env):
    slots_dev, right_dim, half = amplitudes.shape
    slots = holders.shape[0]
    assert slots_dev == 1
    if slots != 2 * QDOWN:
        return on_device_any(amplitudes, widths, holders, left_env, right_env)
    places = slots // LINES
    rows = right_dim // places
    dots = 6 * right_dim * half * (right_dim + 2 * half)
    block = jax.ShapeDtypeStruct((right_dim, half), jnp.bfloat16)
    wide = jax.ShapeDtypeStruct((right_dim, half), jnp.float32)
    pair = jax.ShapeDtypeStruct((2, rows, half), jnp.bfloat16)
    single = jax.ShapeDtypeStruct((rows, half), jnp.bfloat16)
    singles = jax.ShapeDtypeStruct((places, rows, half), jnp.bfloat16)
    wides = jax.ShapeDtypeStruct((places, rows, half), jnp.float32)
    chunked = rows * half // LANES
    tagged = jax.ShapeDtypeStruct((2 * chunked + TAG, LANES), jnp.bfloat16)
    crossing = jax.ShapeDtypeStruct((places * chunked + TAG, LANES), jnp.bfloat16)
    label = jax.ShapeDtypeStruct((TAG, LANES), jnp.bfloat16)
    factor_shape = jax.ShapeDtypeStruct((8, LANES), jnp.float32)
    slot_table = pltpu.SMEM((slots,), jnp.int32)
    split = [pltpu.VMEM((places, rows, half), jnp.bfloat16)]
    tables = [pltpu.VMEM((places, *shape.shape), jnp.bfloat16) for shape in (pair, tagged)]

    staged = call(stage_kernel, [VMEM], block, flops=4 << 30)(amplitudes[0])
    amps_full = lax.all_gather(staged, "env")
    both = jax.ShapeDtypeStruct(amps_full.shape, jnp.bfloat16)
    *pieces, stay, start_full = call(
        first_kernel, [SMEM, SMEM] + [VMEM] * 3, (pair,) * places + (block, both), split, dots
    )(widths, holders, amps_full, right_env, left_env)
    old = along_line(pieces, slots)
    old_keep, cross = call(
        merge_kernel, [SMEM] + [VMEM] * places, (singles, singles), [tables[0], slot_table]
    )(holders, *old)
    old_arrived = across(cross, slots)
    joined = call(join_kernel, [VMEM, VMEM], (single,) * places)(old_keep, old_arrived)
    first = call(sum_kernel, [SMEM, SMEM] + [VMEM] * (1 + places), block)(
        widths, holders, stay, *along_line(joined, slots)
    )

    first_full = lax.all_gather(first, "env")
    *pieces, stay_2 = call(
        second_kernel, [VMEM] * 4, (tagged,) * places + (wide,), split, dots
    )(start_full, first_full, right_env, left_env)
    new = along_line(pieces, slots)
    keep, cross, tag = call(
        mix_kernel,
        [SMEM] + [VMEM] * (2 * places),
        (wides, crossing, label),
        [*tables, slot_table],
    )(holders, *old, *new)
    *joined, factors = call(
        join_mixed_kernel, [SMEM] + [VMEM] * 5, (single,) * places + (factor_shape,)
    )(widths, tag, keep, across(cross, slots), old_keep, old_arrived)
    second, first = call(final_kernel, [SMEM, SMEM] + [VMEM] * (4 + places), (block, block))(
        widths, holders, factors, stay, stay_2, first, *along_line(joined, slots)
    )
    return first[None], second[None]


def solution(mesh):
    in_specs = (
        P(("runs", "sec"), None, "env"),
        P("runs"),
        P("runs"),
        P(("runs", "sec"), None, None, "env"),
        P("runs", None, None),
    )
    out_specs = (P(("runs", "sec"), None, "env"), P(("runs", "sec"), None, "env"))
    return jax.shard_map(
        on_device, mesh=mesh, in_specs=in_specs, out_specs=out_specs, check_vma=False
    )
```

```python
import jax
import jax.numpy as jnp
from jax import lax
from jax.experimental import pallas as pl
from jax.experimental.pallas import tpu as pltpu
from jax.sharding import PartitionSpec as P

QDOWN = 4

term_shifts = ((0, 0), (1, 0), (0, 1))


def route(holders):
    n_slots = holders.shape[0]
    sector_ids = jnp.arange(n_slots, dtype=jnp.int32)
    slot_of = jnp.argmax(holders[None, :] == sector_ids[:, None], axis=1)
    sources = []
    allowed = []
    for up, down in term_shifts[1:]:
        permitted = (holders // QDOWN - up >= 0) & (holders % QDOWN - down >= 0)
        wanted = jnp.clip(holders - QDOWN * up - down, 0, n_slots - 1)
        sources.append(slot_of[wanted])
        allowed.append(permitted)
    return sources, allowed


def contract(vector, left_env, right_env):
    products = jnp.einsum(
        "tij,jw->tiw", right_env, vector, preferred_element_type=jnp.float32
    ).astype(jnp.bfloat16)
    return jnp.einsum("tik,tkw->tiw", products, left_env, preferred_element_type=jnp.float32)


def spread(blocks, n_slots):
    terms, rows, width = blocks.shape
    pieces = blocks.reshape(terms, n_slots, rows // n_slots, width).swapaxes(0, 1)
    return lax.all_to_all(pieces, "sec", split_axis=0, concat_axis=0)


def collect(merged):
    n_slots, rows, width = merged.shape
    home = lax.all_to_all(merged, "sec", split_axis=0, concat_axis=0)
    return home.reshape(n_slots * rows, width)


def share(values, n_slots, me):
    lanes = jnp.zeros((1, 128), jnp.float32).at[0, : values.shape[0]].set(values)
    if n_slots & (n_slots - 1) or n_slots > 16:
        return lax.all_gather(lanes[0], "sec")
    table = jnp.where(jnp.arange(n_slots)[:, None] == me, lanes, 0.0)
    for offset in range(1, n_slots):
        pairs = [(i, i ^ offset) for i in range(n_slots)]
        other = lax.ppermute(lanes, "sec", pairs)
        table = jnp.where(jnp.arange(n_slots)[:, None] == (me ^ offset), other, table)
    return table


def merge(received, sources, allowed):
    total = 0.0
    for term, (source, permitted) in enumerate(zip(sources, allowed)):
        picked = received[source, term]
        total = total + jnp.where(permitted[:, None, None], picked, 0).astype(jnp.float32)
    return total


def on_device_any(amplitudes, widths, holders, left_env, right_env):
    slots_dev, right_dim, half_width = amplitudes.shape
    assert slots_dev == 1
    n_slots = holders.shape[0]
    me = lax.axis_index("sec")
    side = lax.axis_index("env")
    my_width = widths[holders[me]]
    row_index = side * half_width + jnp.arange(half_width, dtype=jnp.int32)
    live = (row_index < my_width)[None, :]
    sources, allowed = route(holders)
    envs = left_env[0]

    start = jnp.where(live, amplitudes[0], jnp.zeros_like(amplitudes[0]))
    start_full = lax.all_gather(start, "env", axis=1, tiled=True)
    outgoing = contract(start_full, envs, right_env).astype(jnp.bfloat16)
    stay = outgoing[0].astype(jnp.float32)
    received = spread(outgoing[1:], n_slots)
    arrived = collect(merge(received, sources, allowed).astype(jnp.bfloat16))
    first = jnp.where(live, stay + arrived.astype(jnp.float32), 0.0).astype(jnp.bfloat16)

    first_full = lax.all_gather(first, "env", axis=1, tiled=True).astype(jnp.float32)
    basis = start_full.astype(jnp.float32)
    overlap = jnp.sum(basis * first_full)
    norm = jnp.sum(basis * basis)
    own_quotient = jnp.where(norm > 0, overlap / jnp.where(norm > 0, norm, 1.0), 0.0)
    deflated = first_full - own_quotient * basis
    rest = jnp.sum(deflated * deflated)
    sums = share(jnp.stack([overlap, norm, own_quotient, rest]), n_slots, me)
    outgoing_2 = contract(deflated.astype(jnp.bfloat16), envs, right_env)
    received_2 = spread(outgoing_2[1:].astype(jnp.bfloat16), n_slots)

    quotient = jnp.sum(sums[:, 0]) / jnp.sum(sums[:, 1])
    shift = sums[:, 2] - quotient
    resid_norm = jnp.sum(sums[:, 3] + shift * shift * sums[:, 1])
    live_count = right_dim * jnp.sum(widths).astype(jnp.float32)
    scale = lax.rsqrt(resid_norm / live_count + 1e-06)
    mixed = received_2.astype(jnp.float32) + shift[:, None, None, None] * received.astype(
        jnp.float32
    )
    merged_2 = scale * merge(mixed, sources, allowed)
    arrived_2 = collect(merged_2.astype(jnp.bfloat16))
    stay_2 = scale * (outgoing_2[0] + (own_quotient - quotient) * stay)
    second = jnp.where(live, stay_2 + arrived_2.astype(jnp.float32), 0.0).astype(jnp.bfloat16)
    return first[None], second[None]


LANES = 128
TAG = 16
LINES = 2
STEPS = (0, 2, 3, 1)


def live_columns(widths, holders, half):
    width = widths[holders[lax.axis_index("sec")]]
    first_column = lax.axis_index("env") * half
    return first_column + lax.broadcasted_iota(jnp.int32, (1, half), 1) < width


def apply_term(right, left, vector, term):
    products = jnp.dot(right[term], vector, preferred_element_type=jnp.float32)
    return jnp.dot(products.astype(jnp.bfloat16), left, preferred_element_type=jnp.float32)


def stage_kernel(amps, staged):
    staged[...] = amps[...]


def own_place():
    return lax.axis_index("sec") // LINES


def first_kernel(widths, holders, amps, right, left, *rest):
    *pieces, stay, start, block_vmem = rest
    half = stay.shape[1]
    width = widths[holders[lax.axis_index("sec")]]
    columns = lax.broadcasted_iota(jnp.int32, (1, half), 1)
    for h in range(2):
        live = h * half + columns < width
        start[h] = jnp.where(live, amps[h], jnp.zeros_like(amps[h]))
    vector = jnp.concatenate([start[0], start[1]], axis=1)
    for term in (1, 2, 0):
        block = apply_term(right, left[0, term], vector, term).astype(jnp.bfloat16)
        if term == 0:
            stay[...] = block
        else:
            block_vmem[...] = block.reshape(block_vmem.shape)
            for step, piece in zip(STEPS, pieces):
                piece[term - 1] = block_vmem[own_place() ^ step]


def fill_slots(holders, slot_of):
    for s in range(holders.shape[0]):
        slot_of[holders[s]] = jnp.int32(s)


def sources_of(holders, slot_of, target):
    sector = holders[target]
    has = (sector >= QDOWN, sector % QDOWN > 0)
    source = (slot_of[sector & (QDOWN - 1)], slot_of[jnp.maximum(sector - 1, 0)])
    return has, source


def line_targets(holders, slot_of):
    line = lax.axis_index("sec") % LINES
    for place in range(holders.shape[0] // LINES):
        for crossing in range(2):
            has, source = sources_of(holders, slot_of, place * LINES + (line ^ crossing))
            here = [has[i] & (source[i] % LINES == line) for i in range(2)]
            yield place, crossing, here, source


def merge_kernel(holders, *rest):
    *pieces, keep, cross, table, slot_of = rest
    fill_slots(holders, slot_of)
    for step, piece in zip(STEPS, pieces):
        table[own_place() ^ step] = piece[...]
    for place, crossing, here, source in line_targets(holders, slot_of):
        total = 0.0
        for i in range(2):
            block = table[source[i] // LINES, i].astype(jnp.float32)
            total = total + jnp.where(here[i], block, 0.0)
        (keep, cross)[crossing][place] = total.astype(jnp.bfloat16)


def join_kernel(keep, arrived, *outs):
    for step, out in zip(STEPS, outs):
        place = own_place() ^ step
        total = keep[place].astype(jnp.float32) + arrived[place].astype(jnp.float32)
        out[...] = total.astype(jnp.bfloat16)


def piece_rows(step, rows):
    return pl.ds(pl.multiple_of((own_place() ^ step) * rows, rows), rows)


def sum_kernel(widths, holders, stay, *rest):
    *pieces, first = rest
    live = live_columns(widths, holders, stay.shape[1])
    for step, piece in zip(STEPS, pieces):
        place = piece_rows(step, piece.shape[0])
        total = stay[place, :].astype(jnp.float32) + piece[...].astype(jnp.float32)
        first[place, :] = jnp.where(live, total, 0.0).astype(jnp.bfloat16)


def total_of(array):
    return jnp.sum(jnp.sum(array, axis=0, keepdims=True), axis=1, keepdims=True)


def make_tag(values, me):
    row = lax.broadcasted_iota(jnp.int32, (TAG, LANES), 0)
    lane = lax.broadcasted_iota(jnp.int32, (TAG, LANES), 1)
    spread = jnp.zeros((TAG, LANES), jnp.float32)
    for place, value in enumerate(values):
        spread = jnp.where(row // 3 == place, value, spread)
    high = spread.astype(jnp.bfloat16).astype(jnp.float32)
    middle = (spread - high).astype(jnp.bfloat16).astype(jnp.float32)
    low = spread - high - middle
    parts = jnp.where(row % 3 == 0, high, jnp.where(row % 3 == 1, middle, low))
    return jnp.where((lane == me) & (row < 3 * len(values)), parts, 0.0).astype(jnp.bfloat16)


def second_kernel(start, first, right, left, *rest):
    *pieces, stay, block_vmem = rest
    half = stay.shape[1]
    rows = block_vmem.shape[1]
    chunks = half // LANES
    basis = [start[h].astype(jnp.float32) for h in range(2)]
    firsts = [first[h].astype(jnp.float32) for h in range(2)]
    overlap = total_of(basis[0] * firsts[0]) + total_of(basis[1] * firsts[1])
    norm = total_of(basis[0] * basis[0]) + total_of(basis[1] * basis[1])
    quotient = jnp.where(norm > 0, overlap / jnp.where(norm > 0, norm, 1.0), 0.0)
    deflated = [firsts[h] - quotient * basis[h] for h in range(2)]
    rest_norm = total_of(deflated[0] * deflated[0]) + total_of(deflated[1] * deflated[1])
    vector = jnp.concatenate(deflated, axis=1).astype(jnp.bfloat16)
    tag = make_tag((overlap, norm, quotient, rest_norm), lax.axis_index("sec"))
    for piece in pieces:
        piece[pl.ds(2 * chunks * rows, TAG), :] = tag
    for term in (1, 2, 0):
        block = apply_term(right, left[0, term], vector, term)
        if term == 0:
            stay[...] = block
        else:
            block_vmem[...] = block.astype(jnp.bfloat16).reshape(block_vmem.shape)
            for step, piece in zip(STEPS, pieces):
                part = block_vmem[own_place() ^ step]
                for c in range(chunks):
                    place = pl.ds(((term - 1) * chunks + c) * rows, rows)
                    piece[place, :] = part[:, c * LANES : (c + 1) * LANES]


def read_tag(tag):
    def value(place):
        parts = [tag[3 * place + i : 3 * place + i + 1, :] for i in range(3)]
        return parts[0] + parts[1] + parts[2]

    return [value(place) for place in range(4)]


def line_quotient(overlaps, norms, line):
    inside = lax.broadcasted_iota(jnp.int32, (1, LANES), 1) % LINES == line
    overlap = total_of(jnp.where(inside, overlaps, 0.0))
    norm = total_of(jnp.where(inside, norms, 0.0))
    return jnp.where(norm > 0, overlap / jnp.where(norm > 0, norm, 1.0), 0.0)


def mix_kernel(holders, *rest):
    keep, cross, tag_out, old, new, slot_of = rest[-6:]
    places, rows, half = keep.shape
    chunks = half // LANES
    fill_slots(holders, slot_of)
    tag = jnp.zeros((TAG, LANES), jnp.float32)
    for i, step in enumerate(STEPS):
        old[own_place() ^ step] = rest[i][...]
        new[own_place() ^ step] = rest[places + i][...]
        label = rest[places + i][pl.ds(2 * chunks * rows, TAG), :]
        tag = tag + label.astype(jnp.float32)
    tag_out[...] = tag.astype(jnp.bfloat16)
    cross[pl.ds(places * chunks * rows, TAG), :] = tag.astype(jnp.bfloat16)
    overlaps, norms, quotients, _ = read_tag(tag)
    shifts = quotients - line_quotient(overlaps, norms, lax.axis_index("sec") % LINES)
    lane = lax.broadcasted_iota(jnp.int32, (1, LANES), 1)
    for place, crossing, here, source in line_targets(holders, slot_of):
        total = 0.0
        for i in range(2):
            where = source[i] // LINES
            block = jnp.concatenate(
                [new[where, pl.ds((i * chunks + c) * rows, rows), :] for c in range(chunks)],
                axis=1,
            ).astype(jnp.float32)
            shift = total_of(jnp.where(lane == source[i], shifts, 0.0))
            block = block + shift * old[where, i].astype(jnp.float32)
            total = total + jnp.where(here[i], block, 0.0)
        if crossing:
            total = total.astype(jnp.bfloat16)
            for c in range(chunks):
                target = pl.ds((place * chunks + c) * rows, rows)
                cross[target, :] = total[:, c * LANES : (c + 1) * LANES]
        else:
            keep[place] = total


def join_mixed_kernel(widths, tag_line, keep, arrived, old_keep, old_arrived, *rest):
    *outs, factors = rest
    places, rows, half = keep.shape
    chunks = half // LANES
    slots = widths.shape[0]
    me = lax.axis_index("sec")
    total = jnp.int32(0)
    for slot in range(slots):
        total = total + widths[slot]
    live_count = places * rows * total.astype(jnp.float32)
    tag = tag_line[...].astype(jnp.float32)
    tag = tag + arrived[pl.ds(places * chunks * rows, TAG), :].astype(jnp.float32)
    overlaps, norms, quotients, rests = read_tag(tag)
    quotient = total_of(overlaps) / total_of(norms)
    lane = lax.broadcasted_iota(jnp.int32, (1, LANES), 1)
    shifts = jnp.where(lane < slots, quotients - quotient, 0.0)
    resid_norm = total_of(rests + shifts * shifts * norms)
    scale = lax.rsqrt(resid_norm / live_count + 1e-06)
    row = lax.broadcasted_iota(jnp.int32, factors.shape, 0)
    own_shift = total_of(jnp.where(lane == me, shifts, 0.0))
    factors[...] = jnp.where(row == 0, scale, scale * own_shift)
    line = me % LINES
    shift_here = line_quotient(overlaps, norms, line) - quotient
    shift_there = line_quotient(overlaps, norms, 1 - line) - quotient
    for step, out in zip(STEPS, outs):
        place = own_place() ^ step
        starts = [pl.multiple_of((place * chunks + c) * rows, rows) for c in range(chunks)]
        block = jnp.concatenate(
            [arrived[pl.ds(start, rows), :] for start in starts], axis=1
        ).astype(jnp.float32)
        block = block + shift_there * old_arrived[place].astype(jnp.float32)
        block = block + keep[place] + shift_here * old_keep[place].astype(jnp.float32)
        out[...] = (scale * block).astype(jnp.bfloat16)


def final_kernel(widths, holders, factors, stay, stay_2, first, *rest):
    *pieces, second, first_out = rest
    first_out[...] = first[...]
    live = live_columns(widths, holders, stay.shape[1])
    scale, shift = factors[0:1, 0:1], factors[1:2, 0:1]
    for step, piece in zip(STEPS, pieces):
        place = piece_rows(step, piece.shape[0])
        total = scale * stay_2[place, :] + shift * stay[place, :].astype(jnp.float32)
        total = total + piece[...].astype(jnp.float32)
        second[place, :] = jnp.where(live, total, 0.0).astype(jnp.bfloat16)


SMEM = pl.BlockSpec(memory_space=pltpu.SMEM)
VMEM = pl.BlockSpec(memory_space=pltpu.VMEM)


def call(kernel, specs, outs, scratch=(), flops=0):
    return pl.pallas_call(
        kernel,
        out_shape=outs,
        in_specs=specs,
        out_specs=jax.tree.map(lambda _: VMEM, outs),
        scratch_shapes=scratch,
        compiler_params=pltpu.CompilerParams(vmem_limit_bytes=16 * 1024 * 1024),
        cost_estimate=pl.CostEstimate(flops=flops, bytes_accessed=1 << 18, transcendentals=0),
    )


def along_line(pieces, slots):
    sent = []
    for step, piece in zip(STEPS, pieces):
        pairs = [(slot, slot ^ (step * LINES)) for slot in range(slots)]
        sent.append(lax.ppermute(piece, "sec", pairs) if step else piece)
    return sent


def across(piece, slots):
    return lax.ppermute(piece, "sec", [(slot, slot ^ 1) for slot in range(slots)])


def on_device(amplitudes, widths, holders, left_env, right_env):
    slots_dev, right_dim, half = amplitudes.shape
    slots = holders.shape[0]
    assert slots_dev == 1
    if slots != 2 * QDOWN:
        return on_device_any(amplitudes, widths, holders, left_env, right_env)
    places = slots // LINES
    rows = right_dim // places
    dots = 6 * right_dim * half * (right_dim + 2 * half)
    block = jax.ShapeDtypeStruct((right_dim, half), jnp.bfloat16)
    wide = jax.ShapeDtypeStruct((right_dim, half), jnp.float32)
    pair = jax.ShapeDtypeStruct((2, rows, half), jnp.bfloat16)
    single = jax.ShapeDtypeStruct((rows, half), jnp.bfloat16)
    singles = jax.ShapeDtypeStruct((places, rows, half), jnp.bfloat16)
    wides = jax.ShapeDtypeStruct((places, rows, half), jnp.float32)
    chunked = rows * half // LANES
    tagged = jax.ShapeDtypeStruct((2 * chunked + TAG, LANES), jnp.bfloat16)
    crossing = jax.ShapeDtypeStruct((places * chunked + TAG, LANES), jnp.bfloat16)
    label = jax.ShapeDtypeStruct((TAG, LANES), jnp.bfloat16)
    factor_shape = jax.ShapeDtypeStruct((8, LANES), jnp.float32)
    slot_table = pltpu.SMEM((slots,), jnp.int32)
    split = [pltpu.VMEM((places, rows, half), jnp.bfloat16)]
    tables = [pltpu.VMEM((places, *shape.shape), jnp.bfloat16) for shape in (pair, tagged)]

    staged = call(stage_kernel, [VMEM], block, flops=4 << 30)(amplitudes[0])
    amps_full = lax.all_gather(staged, "env")
    both = jax.ShapeDtypeStruct(amps_full.shape, jnp.bfloat16)
    *pieces, stay, start_full = call(
        first_kernel, [SMEM, SMEM] + [VMEM] * 3, (pair,) * places + (block, both), split, dots
    )(widths, holders, amps_full, right_env, left_env)
    old = along_line(pieces, slots)
    old_keep, cross = call(
        merge_kernel, [SMEM] + [VMEM] * places, (singles, singles), [tables[0], slot_table]
    )(holders, *old)
    old_arrived = across(cross, slots)
    joined = call(join_kernel, [VMEM, VMEM], (single,) * places)(old_keep, old_arrived)
    first = call(sum_kernel, [SMEM, SMEM] + [VMEM] * (1 + places), block)(
        widths, holders, stay, *along_line(joined, slots)
    )

    first_full = lax.all_gather(first, "env")
    *pieces, stay_2 = call(
        second_kernel, [VMEM] * 4, (tagged,) * places + (wide,), split, dots
    )(start_full, first_full, right_env, left_env)
    new = along_line(pieces, slots)
    keep, cross, tag = call(
        mix_kernel,
        [SMEM] + [VMEM] * (2 * places),
        (wides, crossing, label),
        [*tables, slot_table],
    )(holders, *old, *new)
    *joined, factors = call(
        join_mixed_kernel, [SMEM] + [VMEM] * 5, (single,) * places + (factor_shape,)
    )(widths, tag, keep, across(cross, slots), old_keep, old_arrived)
    second, first = call(final_kernel, [SMEM, SMEM] + [VMEM] * (4 + places), (block, block))(
        widths, holders, factors, stay, stay_2, first, *along_line(joined, slots)
    )
    return first[None], second[None]


def solution(mesh):
    in_specs = (
        P(("runs", "sec"), None, "env"),
        P("runs"),
        P("runs"),
        P(("runs", "sec"), None, None, "env"),
        P("runs", None, None),
    )
    out_specs = (P(("runs", "sec"), None, "env"), P(("runs", "sec"), None, "env"))
    return jax.shard_map(
        on_device, mesh=mesh, in_specs=in_specs, out_specs=out_specs, check_vma=False
    )
```

```python
import jax
import jax.numpy as jnp
from jax import lax
from jax.experimental import pallas as pl
from jax.experimental.pallas import tpu as pltpu
from jax.sharding import PartitionSpec as P

QDOWN = 4

term_shifts = ((0, 0), (1, 0), (0, 1))


def route(holders):
    n_slots = holders.shape[0]
    sector_ids = jnp.arange(n_slots, dtype=jnp.int32)
    slot_of = jnp.argmax(holders[None, :] == sector_ids[:, None], axis=1)
    sources = []
    allowed = []
    for up, down in term_shifts[1:]:
        permitted = (holders // QDOWN - up >= 0) & (holders % QDOWN - down >= 0)
        wanted = jnp.clip(holders - QDOWN * up - down, 0, n_slots - 1)
        sources.append(slot_of[wanted])
        allowed.append(permitted)
    return sources, allowed


def contract(vector, left_env, right_env):
    products = jnp.einsum(
        "tij,jw->tiw", right_env, vector, preferred_element_type=jnp.float32
    ).astype(jnp.bfloat16)
    return jnp.einsum("tik,tkw->tiw", products, left_env, preferred_element_type=jnp.float32)


def spread(blocks, n_slots):
    terms, rows, width = blocks.shape
    pieces = blocks.reshape(terms, n_slots, rows // n_slots, width).swapaxes(0, 1)
    return lax.all_to_all(pieces, "sec", split_axis=0, concat_axis=0)


def collect(merged):
    n_slots, rows, width = merged.shape
    home = lax.all_to_all(merged, "sec", split_axis=0, concat_axis=0)
    return home.reshape(n_slots * rows, width)


def share(values, n_slots, me):
    lanes = jnp.zeros((1, 128), jnp.float32).at[0, : values.shape[0]].set(values)
    if n_slots & (n_slots - 1) or n_slots > 16:
        return lax.all_gather(lanes[0], "sec")
    table = jnp.where(jnp.arange(n_slots)[:, None] == me, lanes, 0.0)
    for offset in range(1, n_slots):
        pairs = [(i, i ^ offset) for i in range(n_slots)]
        other = lax.ppermute(lanes, "sec", pairs)
        table = jnp.where(jnp.arange(n_slots)[:, None] == (me ^ offset), other, table)
    return table


def merge(received, sources, allowed):
    total = 0.0
    for term, (source, permitted) in enumerate(zip(sources, allowed)):
        picked = received[source, term]
        total = total + jnp.where(permitted[:, None, None], picked, 0).astype(jnp.float32)
    return total


def on_device_any(amplitudes, widths, holders, left_env, right_env):
    slots_dev, right_dim, half_width = amplitudes.shape
    assert slots_dev == 1
    n_slots = holders.shape[0]
    me = lax.axis_index("sec")
    side = lax.axis_index("env")
    my_width = widths[holders[me]]
    row_index = side * half_width + jnp.arange(half_width, dtype=jnp.int32)
    live = (row_index < my_width)[None, :]
    sources, allowed = route(holders)
    envs = left_env[0]

    start = jnp.where(live, amplitudes[0], jnp.zeros_like(amplitudes[0]))
    start_full = lax.all_gather(start, "env", axis=1, tiled=True)
    outgoing = contract(start_full, envs, right_env).astype(jnp.bfloat16)
    stay = outgoing[0].astype(jnp.float32)
    received = spread(outgoing[1:], n_slots)
    arrived = collect(merge(received, sources, allowed).astype(jnp.bfloat16))
    first = jnp.where(live, stay + arrived.astype(jnp.float32), 0.0).astype(jnp.bfloat16)

    first_full = lax.all_gather(first, "env", axis=1, tiled=True).astype(jnp.float32)
    basis = start_full.astype(jnp.float32)
    overlap = jnp.sum(basis * first_full)
    norm = jnp.sum(basis * basis)
    own_quotient = jnp.where(norm > 0, overlap / jnp.where(norm > 0, norm, 1.0), 0.0)
    deflated = first_full - own_quotient * basis
    rest = jnp.sum(deflated * deflated)
    sums = share(jnp.stack([overlap, norm, own_quotient, rest]), n_slots, me)
    outgoing_2 = contract(deflated.astype(jnp.bfloat16), envs, right_env)
    received_2 = spread(outgoing_2[1:].astype(jnp.bfloat16), n_slots)

    quotient = jnp.sum(sums[:, 0]) / jnp.sum(sums[:, 1])
    shift = sums[:, 2] - quotient
    resid_norm = jnp.sum(sums[:, 3] + shift * shift * sums[:, 1])
    live_count = right_dim * jnp.sum(widths).astype(jnp.float32)
    scale = lax.rsqrt(resid_norm / live_count + 1e-06)
    mixed = received_2.astype(jnp.float32) + shift[:, None, None, None] * received.astype(
        jnp.float32
    )
    merged_2 = scale * merge(mixed, sources, allowed)
    arrived_2 = collect(merged_2.astype(jnp.bfloat16))
    stay_2 = scale * (outgoing_2[0] + (own_quotient - quotient) * stay)
    second = jnp.where(live, stay_2 + arrived_2.astype(jnp.float32), 0.0).astype(jnp.bfloat16)
    return first[None], second[None]


LANES = 128
TAG = 16
LINES = 2
STEPS = (0, 2, 3, 1)


def plan_kernel(widths, holders, plan, slot_of):
    slots = holders.shape[0]
    me = lax.axis_index("sec")
    total = jnp.int32(0)
    for s in range(slots):
        slot_of[holders[s]] = jnp.int32(s)
        total = total + widths[s]
    codes = [jnp.int32(0), jnp.int32(0)]
    for target in range(slots):
        sector = holders[target]
        has = (sector >= QDOWN, sector % QDOWN > 0)
        source = (slot_of[sector & (QDOWN - 1)], slot_of[jnp.maximum(sector - 1, 0)])
        for i in range(2):
            entry = jnp.where(has[i], source[i] + slots, 0)
            codes[i] = codes[i] | (entry << (target * 4))
    row = lax.broadcasted_iota(jnp.int32, plan.shape, 0)
    values = jnp.where(row == 0, widths[holders[me]], total)
    values = jnp.where(row == 2, codes[0], values)
    plan[...] = jnp.where(row == 3, codes[1], values)


def live_columns(plan, half):
    first_column = lax.axis_index("env") * half
    return first_column + lax.broadcasted_iota(jnp.int32, (1, half), 1) < plan[0:1, 0:1]


def apply_term(right, left, vector, term):
    products = jnp.dot(right[term], vector, preferred_element_type=jnp.float32)
    return jnp.dot(products.astype(jnp.bfloat16), left, preferred_element_type=jnp.float32)


def stage_kernel(amps, staged):
    staged[...] = amps[...]


def own_place():
    return lax.axis_index("sec") // LINES


def first_kernel(widths, holders, amps, right, left, *rest):
    *pieces, stay, start, block_vmem = rest
    half = stay.shape[1]
    slot = lax.broadcasted_iota(jnp.int32, widths.shape, 1)
    mine = jnp.where(slot == lax.axis_index("sec"), holders[...], 0)
    sector = jnp.sum(mine, axis=1, keepdims=True)
    width = jnp.sum(jnp.where(slot == sector, widths[...], 0), axis=1, keepdims=True)
    columns = lax.broadcasted_iota(jnp.int32, (1, half), 1)
    for h in range(2):
        live = h * half + columns < width
        start[h] = jnp.where(live, amps[h], jnp.zeros_like(amps[h]))
    vector = jnp.concatenate([start[0], start[1]], axis=1)
    for term in (1, 2, 0):
        block = apply_term(right, left[0, term], vector, term).astype(jnp.bfloat16)
        if term == 0:
            stay[...] = block
        else:
            block_vmem[...] = block.reshape(block_vmem.shape)
            for step, piece in zip(STEPS, pieces):
                piece[term - 1] = block_vmem[own_place() ^ step]


def line_targets(plan, places):
    line = lax.axis_index("sec") % LINES
    codes = [jnp.max(plan[2 + i : 3 + i, :]) for i in range(2)]
    for place in range(places):
        for crossing in range(2):
            target = place * LINES + (line ^ crossing)
            entries = [(code >> (target * 4)) & (2 * LINES * places - 1) for code in codes]
            source = [entry & (LINES * places - 1) for entry in entries]
            here = [
                (entry >= LINES * places) & (slot % LINES == line)
                for entry, slot in zip(entries, source)
            ]
            yield place, crossing, here, source


def merge_kernel(plan, *rest):
    *pieces, keep, cross, table = rest
    for step, piece in zip(STEPS, pieces):
        table[own_place() ^ step] = piece[...]
    for place, crossing, here, source in line_targets(plan, keep.shape[0]):
        total = 0.0
        for i in range(2):
            block = table[source[i] // LINES, i].astype(jnp.float32)
            total = total + jnp.where(here[i], block, 0.0)
        (keep, cross)[crossing][place] = total.astype(jnp.bfloat16)


def join_kernel(keep, arrived, *outs):
    for step, out in zip(STEPS, outs):
        place = own_place() ^ step
        total = keep[place].astype(jnp.float32) + arrived[place].astype(jnp.float32)
        out[...] = total.astype(jnp.bfloat16)


def piece_rows(step, rows):
    return pl.ds(pl.multiple_of((own_place() ^ step) * rows, rows), rows)


def sum_kernel(plan, stay, *rest):
    *pieces, first = rest
    live = live_columns(plan, stay.shape[1])
    for step, piece in zip(STEPS, pieces):
        place = piece_rows(step, piece.shape[0])
        total = stay[place, :].astype(jnp.float32) + piece[...].astype(jnp.float32)
        first[place, :] = jnp.where(live, total, 0.0).astype(jnp.bfloat16)


def total_of(array):
    return jnp.sum(jnp.sum(array, axis=0, keepdims=True), axis=1, keepdims=True)


def make_tag(values, me):
    row = lax.broadcasted_iota(jnp.int32, (TAG, LANES), 0)
    lane = lax.broadcasted_iota(jnp.int32, (TAG, LANES), 1)
    spread = jnp.zeros((TAG, LANES), jnp.float32)
    for place, value in enumerate(values):
        spread = jnp.where(row // 3 == place, value, spread)
    high = spread.astype(jnp.bfloat16).astype(jnp.float32)
    middle = (spread - high).astype(jnp.bfloat16).astype(jnp.float32)
    low = spread - high - middle
    parts = jnp.where(row % 3 == 0, high, jnp.where(row % 3 == 1, middle, low))
    return jnp.where((lane == me) & (row < 3 * len(values)), parts, 0.0).astype(jnp.bfloat16)


def second_kernel(start, first, right, left, *rest):
    *pieces, stay, block_vmem = rest
    half = stay.shape[1]
    rows = block_vmem.shape[1]
    chunks = half // LANES
    basis = [start[h].astype(jnp.float32) for h in range(2)]
    firsts = [first[h].astype(jnp.float32) for h in range(2)]
    overlap = total_of(basis[0] * firsts[0]) + total_of(basis[1] * firsts[1])
    norm = total_of(basis[0] * basis[0]) + total_of(basis[1] * basis[1])
    quotient = jnp.where(norm > 0, overlap / jnp.where(norm > 0, norm, 1.0), 0.0)
    deflated = [firsts[h] - quotient * basis[h] for h in range(2)]
    rest_norm = total_of(deflated[0] * deflated[0]) + total_of(deflated[1] * deflated[1])
    vector = jnp.concatenate(deflated, axis=1).astype(jnp.bfloat16)
    tag = make_tag((overlap, norm, quotient, rest_norm), lax.axis_index("sec"))
    for piece in pieces:
        piece[pl.ds(2 * chunks * rows, TAG), :] = tag
    for term in (1, 2, 0):
        block = apply_term(right, left[0, term], vector, term)
        if term == 0:
            stay[...] = block
        else:
            block_vmem[...] = block.astype(jnp.bfloat16).reshape(block_vmem.shape)
            for step, piece in zip(STEPS, pieces):
                part = block_vmem[own_place() ^ step]
                for c in range(chunks):
                    place = pl.ds(((term - 1) * chunks + c) * rows, rows)
                    piece[place, :] = part[:, c * LANES : (c + 1) * LANES]


def read_tag(tag):
    def value(place):
        parts = [tag[3 * place + i : 3 * place + i + 1, :] for i in range(3)]
        return parts[0] + parts[1] + parts[2]

    return [value(place) for place in range(4)]


def line_quotient(overlaps, norms, line):
    inside = lax.broadcasted_iota(jnp.int32, (1, LANES), 1) % LINES == line
    overlap = total_of(jnp.where(inside, overlaps, 0.0))
    norm = total_of(jnp.where(inside, norms, 0.0))
    return jnp.where(norm > 0, overlap / jnp.where(norm > 0, norm, 1.0), 0.0)


def mix_kernel(plan, *rest):
    keep, cross, tag_out, old, new = rest[-5:]
    places, rows, half = keep.shape
    chunks = half // LANES
    tag = jnp.zeros((TAG, LANES), jnp.float32)
    for i, step in enumerate(STEPS):
        old[own_place() ^ step] = rest[i][...]
        new[own_place() ^ step] = rest[places + i][...]
        label = rest[places + i][pl.ds(2 * chunks * rows, TAG), :]
        tag = tag + label.astype(jnp.float32)
    tag_out[...] = tag.astype(jnp.bfloat16)
    cross[pl.ds(places * chunks * rows, TAG), :] = tag.astype(jnp.bfloat16)
    overlaps, norms, quotients, _ = read_tag(tag)
    shifts = quotients - line_quotient(overlaps, norms, lax.axis_index("sec") % LINES)
    lane = lax.broadcasted_iota(jnp.int32, (1, LANES), 1)
    for place, crossing, here, source in line_targets(plan, keep.shape[0]):
        total = 0.0
        for i in range(2):
            where = source[i] // LINES
            block = jnp.concatenate(
                [new[where, pl.ds((i * chunks + c) * rows, rows), :] for c in range(chunks)],
                axis=1,
            ).astype(jnp.float32)
            shift = total_of(jnp.where(lane == source[i], shifts, 0.0))
            block = block + shift * old[where, i].astype(jnp.float32)
            total = total + jnp.where(here[i], block, 0.0)
        if crossing:
            total = total.astype(jnp.bfloat16)
            for c in range(chunks):
                target = pl.ds((place * chunks + c) * rows, rows)
                cross[target, :] = total[:, c * LANES : (c + 1) * LANES]
        else:
            keep[place] = total


def join_mixed_kernel(plan, tag_line, keep, arrived, old_keep, old_arrived, *rest):
    *outs, factors = rest
    places, rows, half = keep.shape
    chunks = half // LANES
    slots = places * LINES
    me = lax.axis_index("sec")
    live_count = places * rows * plan[1:2, 0:1].astype(jnp.float32)
    tag = tag_line[...].astype(jnp.float32)
    tag = tag + arrived[pl.ds(places * chunks * rows, TAG), :].astype(jnp.float32)
    overlaps, norms, quotients, rests = read_tag(tag)
    quotient = total_of(overlaps) / total_of(norms)
    lane = lax.broadcasted_iota(jnp.int32, (1, LANES), 1)
    shifts = jnp.where(lane < slots, quotients - quotient, 0.0)
    resid_norm = total_of(rests + shifts * shifts * norms)
    scale = lax.rsqrt(resid_norm / live_count + 1e-06)
    row = lax.broadcasted_iota(jnp.int32, factors.shape, 0)
    own_shift = total_of(jnp.where(lane == me, shifts, 0.0))
    factors[...] = jnp.where(row == 0, scale, scale * own_shift)
    line = me % LINES
    shift_here = line_quotient(overlaps, norms, line) - quotient
    shift_there = line_quotient(overlaps, norms, 1 - line) - quotient
    for step, out in zip(STEPS, outs):
        place = own_place() ^ step
        starts = [pl.multiple_of((place * chunks + c) * rows, rows) for c in range(chunks)]
        block = jnp.concatenate(
            [arrived[pl.ds(start, rows), :] for start in starts], axis=1
        ).astype(jnp.float32)
        block = block + shift_there * old_arrived[place].astype(jnp.float32)
        block = block + keep[place] + shift_here * old_keep[place].astype(jnp.float32)
        out[...] = (scale * block).astype(jnp.bfloat16)


def final_kernel(plan, factors, stay, stay_2, first, *rest):
    *pieces, second, first_out = rest
    first_out[...] = first[...]
    live = live_columns(plan, stay.shape[1])
    scale, shift = factors[0:1, 0:1], factors[1:2, 0:1]
    for step, piece in zip(STEPS, pieces):
        place = piece_rows(step, piece.shape[0])
        total = scale * stay_2[place, :] + shift * stay[place, :].astype(jnp.float32)
        total = total + piece[...].astype(jnp.float32)
        second[place, :] = jnp.where(live, total, 0.0).astype(jnp.bfloat16)


SMEM = pl.BlockSpec(memory_space=pltpu.SMEM)
VMEM = pl.BlockSpec(memory_space=pltpu.VMEM)


def call(kernel, specs, outs, scratch=(), flops=0):
    return pl.pallas_call(
        kernel,
        out_shape=outs,
        in_specs=specs,
        out_specs=jax.tree.map(lambda _: VMEM, outs),
        scratch_shapes=scratch,
        compiler_params=pltpu.CompilerParams(vmem_limit_bytes=16 * 1024 * 1024),
        cost_estimate=pl.CostEstimate(flops=flops, bytes_accessed=1 << 18, transcendentals=0),
    )


def along_line(pieces, slots):
    sent = []
    for step, piece in zip(STEPS, pieces):
        pairs = [(slot, slot ^ (step * LINES)) for slot in range(slots)]
        sent.append(lax.ppermute(piece, "sec", pairs) if step else piece)
    return sent


def across(piece, slots):
    return lax.ppermute(piece, "sec", [(slot, slot ^ 1) for slot in range(slots)])


def on_device(amplitudes, widths, holders, left_env, right_env):
    slots_dev, right_dim, half = amplitudes.shape
    slots = holders.shape[0]
    assert slots_dev == 1
    if slots != 2 * QDOWN:
        return on_device_any(amplitudes, widths, holders, left_env, right_env)
    places = slots // LINES
    rows = right_dim // places
    dots = 6 * right_dim * half * (right_dim + 2 * half)
    block = jax.ShapeDtypeStruct((right_dim, half), jnp.bfloat16)
    wide = jax.ShapeDtypeStruct((right_dim, half), jnp.float32)
    pair = jax.ShapeDtypeStruct((2, rows, half), jnp.bfloat16)
    single = jax.ShapeDtypeStruct((rows, half), jnp.bfloat16)
    singles = jax.ShapeDtypeStruct((places, rows, half), jnp.bfloat16)
    wides = jax.ShapeDtypeStruct((places, rows, half), jnp.float32)
    chunked = rows * half // LANES
    tagged = jax.ShapeDtypeStruct((2 * chunked + TAG, LANES), jnp.bfloat16)
    crossing = jax.ShapeDtypeStruct((places * chunked + TAG, LANES), jnp.bfloat16)
    label = jax.ShapeDtypeStruct((TAG, LANES), jnp.bfloat16)
    factor_shape = jax.ShapeDtypeStruct((8, LANES), jnp.float32)
    plan_shape = jax.ShapeDtypeStruct((8, LANES), jnp.int32)
    split = [pltpu.VMEM((places, rows, half), jnp.bfloat16)]
    tables = [pltpu.VMEM((places, *shape.shape), jnp.bfloat16) for shape in (pair, tagged)]

    slot_table = [pltpu.SMEM((slots,), jnp.int32)]
    plan = call(plan_kernel, [SMEM, SMEM], plan_shape, slot_table)(widths, holders)
    staged = call(stage_kernel, [VMEM], block, flops=4 << 30)(amplitudes[0])
    amps_full = lax.all_gather(staged, "env")
    both = jax.ShapeDtypeStruct(amps_full.shape, jnp.bfloat16)
    *pieces, stay, start_full = call(
        first_kernel, [VMEM] * 5, (pair,) * places + (block, both), split, dots
    )(widths[None], holders[None], amps_full, right_env, left_env)
    old = along_line(pieces, slots)
    old_keep, cross = call(
        merge_kernel, [VMEM] * (1 + places), (singles, singles), tables[:1]
    )(plan, *old)
    old_arrived = across(cross, slots)
    joined = call(join_kernel, [VMEM, VMEM], (single,) * places)(old_keep, old_arrived)
    first = call(sum_kernel, [VMEM] * (2 + places), block)(
        plan, stay, *along_line(joined, slots)
    )

    first_full = lax.all_gather(first, "env")
    *pieces, stay_2 = call(
        second_kernel, [VMEM] * 4, (tagged,) * places + (wide,), split, dots
    )(start_full, first_full, right_env, left_env)
    new = along_line(pieces, slots)
    keep, cross, tag = call(
        mix_kernel, [VMEM] * (1 + 2 * places), (wides, crossing, label), tables
    )(plan, *old, *new)
    *joined, factors = call(
        join_mixed_kernel, [VMEM] * 6, (single,) * places + (factor_shape,)
    )(plan, tag, keep, across(cross, slots), old_keep, old_arrived)
    second, first = call(final_kernel, [VMEM] * (5 + places), (block, block))(
        plan, factors, stay, stay_2, first, *along_line(joined, slots)
    )
    return first[None], second[None]


def solution(mesh):
    in_specs = (
        P(("runs", "sec"), None, "env"),
        P("runs"),
        P("runs"),
        P(("runs", "sec"), None, None, "env"),
        P("runs", None, None),
    )
    out_specs = (P(("runs", "sec"), None, "env"), P(("runs", "sec"), None, "env"))
    return jax.shard_map(
        on_device, mesh=mesh, in_specs=in_specs, out_specs=out_specs, check_vma=False
    )
```

```python
import jax
import jax.numpy as jnp
from jax import lax
from jax.experimental import pallas as pl
from jax.experimental.pallas import tpu as pltpu
from jax.sharding import PartitionSpec as P

QDOWN = 4

term_shifts = ((0, 0), (1, 0), (0, 1))


def route(holders):
    n_slots = holders.shape[0]
    sector_ids = jnp.arange(n_slots, dtype=jnp.int32)
    slot_of = jnp.argmax(holders[None, :] == sector_ids[:, None], axis=1)
    sources = []
    allowed = []
    for up, down in term_shifts[1:]:
        permitted = (holders // QDOWN - up >= 0) & (holders % QDOWN - down >= 0)
        wanted = jnp.clip(holders - QDOWN * up - down, 0, n_slots - 1)
        sources.append(slot_of[wanted])
        allowed.append(permitted)
    return sources, allowed


def contract(vector, left_env, right_env):
    products = jnp.einsum(
        "tij,jw->tiw", right_env, vector, preferred_element_type=jnp.float32
    ).astype(jnp.bfloat16)
    return jnp.einsum("tik,tkw->tiw", products, left_env, preferred_element_type=jnp.float32)


def spread(blocks, n_slots):
    terms, rows, width = blocks.shape
    pieces = blocks.reshape(terms, n_slots, rows // n_slots, width).swapaxes(0, 1)
    return lax.all_to_all(pieces, "sec", split_axis=0, concat_axis=0)


def collect(merged):
    n_slots, rows, width = merged.shape
    home = lax.all_to_all(merged, "sec", split_axis=0, concat_axis=0)
    return home.reshape(n_slots * rows, width)


def share(values, n_slots, me):
    lanes = jnp.zeros((1, 128), jnp.float32).at[0, : values.shape[0]].set(values)
    if n_slots & (n_slots - 1) or n_slots > 16:
        return lax.all_gather(lanes[0], "sec")
    table = jnp.where(jnp.arange(n_slots)[:, None] == me, lanes, 0.0)
    for offset in range(1, n_slots):
        pairs = [(i, i ^ offset) for i in range(n_slots)]
        other = lax.ppermute(lanes, "sec", pairs)
        table = jnp.where(jnp.arange(n_slots)[:, None] == (me ^ offset), other, table)
    return table


def merge(received, sources, allowed):
    total = 0.0
    for term, (source, permitted) in enumerate(zip(sources, allowed)):
        picked = received[source, term]
        total = total + jnp.where(permitted[:, None, None], picked, 0).astype(jnp.float32)
    return total


def on_device_any(amplitudes, widths, holders, left_env, right_env):
    slots_dev, right_dim, half_width = amplitudes.shape
    assert slots_dev == 1
    n_slots = holders.shape[0]
    me = lax.axis_index("sec")
    side = lax.axis_index("env")
    my_width = widths[holders[me]]
    row_index = side * half_width + jnp.arange(half_width, dtype=jnp.int32)
    live = (row_index < my_width)[None, :]
    sources, allowed = route(holders)
    envs = left_env[0]

    start = jnp.where(live, amplitudes[0], jnp.zeros_like(amplitudes[0]))
    start_full = lax.all_gather(start, "env", axis=1, tiled=True)
    outgoing = contract(start_full, envs, right_env).astype(jnp.bfloat16)
    stay = outgoing[0].astype(jnp.float32)
    received = spread(outgoing[1:], n_slots)
    arrived = collect(merge(received, sources, allowed).astype(jnp.bfloat16))
    first = jnp.where(live, stay + arrived.astype(jnp.float32), 0.0).astype(jnp.bfloat16)

    first_full = lax.all_gather(first, "env", axis=1, tiled=True).astype(jnp.float32)
    basis = start_full.astype(jnp.float32)
    overlap = jnp.sum(basis * first_full)
    norm = jnp.sum(basis * basis)
    own_quotient = jnp.where(norm > 0, overlap / jnp.where(norm > 0, norm, 1.0), 0.0)
    deflated = first_full - own_quotient * basis
    rest = jnp.sum(deflated * deflated)
    sums = share(jnp.stack([overlap, norm, own_quotient, rest]), n_slots, me)
    outgoing_2 = contract(deflated.astype(jnp.bfloat16), envs, right_env)
    received_2 = spread(outgoing_2[1:].astype(jnp.bfloat16), n_slots)

    quotient = jnp.sum(sums[:, 0]) / jnp.sum(sums[:, 1])
    shift = sums[:, 2] - quotient
    resid_norm = jnp.sum(sums[:, 3] + shift * shift * sums[:, 1])
    live_count = right_dim * jnp.sum(widths).astype(jnp.float32)
    scale = lax.rsqrt(resid_norm / live_count + 1e-06)
    mixed = received_2.astype(jnp.float32) + shift[:, None, None, None] * received.astype(
        jnp.float32
    )
    merged_2 = scale * merge(mixed, sources, allowed)
    arrived_2 = collect(merged_2.astype(jnp.bfloat16))
    stay_2 = scale * (outgoing_2[0] + (own_quotient - quotient) * stay)
    second = jnp.where(live, stay_2 + arrived_2.astype(jnp.float32), 0.0).astype(jnp.bfloat16)
    return first[None], second[None]


LANES = 128
TAG = 16
LINES = 2
STEPS = (0, 2, 3, 1)


def plan_kernel(widths, holders, plan, slot_of):
    slots = holders.shape[0]
    me = lax.axis_index("sec")
    total = jnp.int32(0)
    for s in range(slots):
        slot_of[holders[s]] = jnp.int32(s)
        total = total + widths[s]
    codes = [jnp.int32(0), jnp.int32(0)]
    for target in range(slots):
        sector = holders[target]
        has = (sector >= QDOWN, sector % QDOWN > 0)
        source = (slot_of[sector & (QDOWN - 1)], slot_of[jnp.maximum(sector - 1, 0)])
        for i in range(2):
            entry = jnp.where(has[i], source[i] + slots, 0)
            codes[i] = codes[i] | (entry << (target * 4))
    row = lax.broadcasted_iota(jnp.int32, plan.shape, 0)
    values = jnp.where(row == 0, widths[holders[me]], total)
    values = jnp.where(row == 2, codes[0], values)
    plan[...] = jnp.where(row == 3, codes[1], values)


def live_columns(plan, half):
    first_column = lax.axis_index("env") * half
    return first_column + lax.broadcasted_iota(jnp.int32, (1, half), 1) < plan[0:1, 0:1]


def apply_term(right, left, vector, term):
    products = jnp.dot(right[term], vector, preferred_element_type=jnp.float32)
    return jnp.dot(products.astype(jnp.bfloat16), left, preferred_element_type=jnp.float32)


def in_order(own, other):
    upper = lax.axis_index("env") > 0
    return [jnp.where(upper, other, own), jnp.where(upper, own, other)]


def own_place():
    return lax.axis_index("sec") // LINES


def first_kernel(widths, holders, own, other, right, left, *rest):
    *pieces, stay, start, block_vmem = rest
    half = stay.shape[1]
    slot = lax.broadcasted_iota(jnp.int32, widths.shape, 1)
    mine = jnp.where(slot == lax.axis_index("sec"), holders[...], 0)
    sector = jnp.sum(mine, axis=1, keepdims=True)
    width = jnp.sum(jnp.where(slot == sector, widths[...], 0), axis=1, keepdims=True)
    columns = lax.broadcasted_iota(jnp.int32, (1, half), 1)
    for h, part in enumerate(in_order(own[...], other[...])):
        live = h * half + columns < width
        start[h] = jnp.where(live, part, jnp.zeros_like(part))
    vector = jnp.concatenate([start[0], start[1]], axis=1)
    for term in (1, 2, 0):
        block = apply_term(right, left[0, term], vector, term).astype(jnp.bfloat16)
        if term == 0:
            stay[...] = block
        else:
            block_vmem[...] = block.reshape(block_vmem.shape)
            for step, piece in zip(STEPS, pieces):
                piece[term - 1] = block_vmem[own_place() ^ step]


def line_targets(plan, places):
    line = lax.axis_index("sec") % LINES
    codes = [jnp.max(plan[2 + i : 3 + i, :]) for i in range(2)]
    for place in range(places):
        for crossing in range(2):
            target = place * LINES + (line ^ crossing)
            entries = [(code >> (target * 4)) & (2 * LINES * places - 1) for code in codes]
            source = [entry & (LINES * places - 1) for entry in entries]
            here = [
                (entry >= LINES * places) & (slot % LINES == line)
                for entry, slot in zip(entries, source)
            ]
            yield place, crossing, here, source


def merge_kernel(plan, *rest):
    *pieces, keep, cross, table = rest
    for step, piece in zip(STEPS, pieces):
        table[own_place() ^ step] = piece[...]
    for place, crossing, here, source in line_targets(plan, keep.shape[0]):
        total = 0.0
        for i in range(2):
            block = table[source[i] // LINES, i].astype(jnp.float32)
            total = total + jnp.where(here[i], block, 0.0)
        (keep, cross)[crossing][place] = total.astype(jnp.bfloat16)


def join_kernel(keep, arrived, *outs):
    for step, out in zip(STEPS, outs):
        place = own_place() ^ step
        total = keep[place].astype(jnp.float32) + arrived[place].astype(jnp.float32)
        out[...] = total.astype(jnp.bfloat16)


def piece_rows(step, rows):
    return pl.ds(pl.multiple_of((own_place() ^ step) * rows, rows), rows)


def sum_kernel(plan, stay, *rest):
    *pieces, first = rest
    live = live_columns(plan, stay.shape[1])
    for step, piece in zip(STEPS, pieces):
        place = piece_rows(step, piece.shape[0])
        total = stay[place, :].astype(jnp.float32) + piece[...].astype(jnp.float32)
        first[place, :] = jnp.where(live, total, 0.0).astype(jnp.bfloat16)


def total_of(array):
    return jnp.sum(jnp.sum(array, axis=0, keepdims=True), axis=1, keepdims=True)


def make_tag(values, me):
    row = lax.broadcasted_iota(jnp.int32, (TAG, LANES), 0)
    lane = lax.broadcasted_iota(jnp.int32, (TAG, LANES), 1)
    spread = jnp.zeros((TAG, LANES), jnp.float32)
    for place, value in enumerate(values):
        spread = jnp.where(row // 3 == place, value, spread)
    high = spread.astype(jnp.bfloat16).astype(jnp.float32)
    middle = (spread - high).astype(jnp.bfloat16).astype(jnp.float32)
    low = spread - high - middle
    parts = jnp.where(row % 3 == 0, high, jnp.where(row % 3 == 1, middle, low))
    return jnp.where((lane == me) & (row < 3 * len(values)), parts, 0.0).astype(jnp.bfloat16)


def second_kernel(start, own, other, right, left, *rest):
    *pieces, stay, block_vmem = rest
    half = stay.shape[1]
    rows = block_vmem.shape[1]
    chunks = half // LANES
    basis = [start[h].astype(jnp.float32) for h in range(2)]
    firsts = [part.astype(jnp.float32) for part in in_order(own[...], other[...])]
    overlap = total_of(basis[0] * firsts[0]) + total_of(basis[1] * firsts[1])
    norm = total_of(basis[0] * basis[0]) + total_of(basis[1] * basis[1])
    quotient = jnp.where(norm > 0, overlap / jnp.where(norm > 0, norm, 1.0), 0.0)
    deflated = [firsts[h] - quotient * basis[h] for h in range(2)]
    rest_norm = total_of(deflated[0] * deflated[0]) + total_of(deflated[1] * deflated[1])
    vector = jnp.concatenate(deflated, axis=1).astype(jnp.bfloat16)
    tag = make_tag((overlap, norm, quotient, rest_norm), lax.axis_index("sec"))
    for piece in pieces:
        piece[pl.ds(2 * chunks * rows, TAG), :] = tag
    for term in (1, 2, 0):
        block = apply_term(right, left[0, term], vector, term)
        if term == 0:
            stay[...] = block
        else:
            block_vmem[...] = block.astype(jnp.bfloat16).reshape(block_vmem.shape)
            for step, piece in zip(STEPS, pieces):
                part = block_vmem[own_place() ^ step]
                for c in range(chunks):
                    place = pl.ds(((term - 1) * chunks + c) * rows, rows)
                    piece[place, :] = part[:, c * LANES : (c + 1) * LANES]


def read_tag(tag):
    def value(place):
        parts = [tag[3 * place + i : 3 * place + i + 1, :] for i in range(3)]
        return parts[0] + parts[1] + parts[2]

    return [value(place) for place in range(4)]


def line_quotient(overlaps, norms, line):
    inside = lax.broadcasted_iota(jnp.int32, (1, LANES), 1) % LINES == line
    overlap = total_of(jnp.where(inside, overlaps, 0.0))
    norm = total_of(jnp.where(inside, norms, 0.0))
    return jnp.where(norm > 0, overlap / jnp.where(norm > 0, norm, 1.0), 0.0)


def mix_kernel(plan, *rest):
    keep, cross, tag_out, old, new = rest[-5:]
    places, rows, half = keep.shape
    chunks = half // LANES
    tag = jnp.zeros((TAG, LANES), jnp.float32)
    for i, step in enumerate(STEPS):
        old[own_place() ^ step] = rest[i][...]
        new[own_place() ^ step] = rest[places + i][...]
        label = rest[places + i][pl.ds(2 * chunks * rows, TAG), :]
        tag = tag + label.astype(jnp.float32)
    tag_out[...] = tag.astype(jnp.bfloat16)
    cross[pl.ds(places * chunks * rows, TAG), :] = tag.astype(jnp.bfloat16)
    overlaps, norms, quotients, _ = read_tag(tag)
    shifts = quotients - line_quotient(overlaps, norms, lax.axis_index("sec") % LINES)
    lane = lax.broadcasted_iota(jnp.int32, (1, LANES), 1)
    for place, crossing, here, source in line_targets(plan, keep.shape[0]):
        total = 0.0
        for i in range(2):
            where = source[i] // LINES
            block = jnp.concatenate(
                [new[where, pl.ds((i * chunks + c) * rows, rows), :] for c in range(chunks)],
                axis=1,
            ).astype(jnp.float32)
            shift = total_of(jnp.where(lane == source[i], shifts, 0.0))
            block = block + shift * old[where, i].astype(jnp.float32)
            total = total + jnp.where(here[i], block, 0.0)
        if crossing:
            total = total.astype(jnp.bfloat16)
            for c in range(chunks):
                target = pl.ds((place * chunks + c) * rows, rows)
                cross[target, :] = total[:, c * LANES : (c + 1) * LANES]
        else:
            keep[place] = total


def join_mixed_kernel(plan, tag_line, keep, arrived, old_keep, old_arrived, *rest):
    *outs, factors = rest
    places, rows, half = keep.shape
    chunks = half // LANES
    slots = places * LINES
    me = lax.axis_index("sec")
    live_count = places * rows * plan[1:2, 0:1].astype(jnp.float32)
    tag = tag_line[...].astype(jnp.float32)
    tag = tag + arrived[pl.ds(places * chunks * rows, TAG), :].astype(jnp.float32)
    overlaps, norms, quotients, rests = read_tag(tag)
    quotient = total_of(overlaps) / total_of(norms)
    lane = lax.broadcasted_iota(jnp.int32, (1, LANES), 1)
    shifts = jnp.where(lane < slots, quotients - quotient, 0.0)
    resid_norm = total_of(rests + shifts * shifts * norms)
    scale = lax.rsqrt(resid_norm / live_count + 1e-06)
    row = lax.broadcasted_iota(jnp.int32, factors.shape, 0)
    own_shift = total_of(jnp.where(lane == me, shifts, 0.0))
    factors[...] = jnp.where(row == 0, scale, scale * own_shift)
    line = me % LINES
    shift_here = line_quotient(overlaps, norms, line) - quotient
    shift_there = line_quotient(overlaps, norms, 1 - line) - quotient
    for step, out in zip(STEPS, outs):
        place = own_place() ^ step
        starts = [pl.multiple_of((place * chunks + c) * rows, rows) for c in range(chunks)]
        block = jnp.concatenate(
            [arrived[pl.ds(start, rows), :] for start in starts], axis=1
        ).astype(jnp.float32)
        block = block + shift_there * old_arrived[place].astype(jnp.float32)
        block = block + keep[place] + shift_here * old_keep[place].astype(jnp.float32)
        out[...] = (scale * block).astype(jnp.bfloat16)


def final_kernel(plan, factors, stay, stay_2, first, *rest):
    *pieces, second, first_out = rest
    first_out[...] = first[...]
    live = live_columns(plan, stay.shape[1])
    scale, shift = factors[0:1, 0:1], factors[1:2, 0:1]
    for step, piece in zip(STEPS, pieces):
        place = piece_rows(step, piece.shape[0])
        total = scale * stay_2[place, :] + shift * stay[place, :].astype(jnp.float32)
        total = total + piece[...].astype(jnp.float32)
        second[place, :] = jnp.where(live, total, 0.0).astype(jnp.bfloat16)


SMEM = pl.BlockSpec(memory_space=pltpu.SMEM)
VMEM = pl.BlockSpec(memory_space=pltpu.VMEM)


def call(kernel, specs, outs, scratch=(), flops=0):
    return pl.pallas_call(
        kernel,
        out_shape=outs,
        in_specs=specs,
        out_specs=jax.tree.map(lambda _: VMEM, outs),
        scratch_shapes=scratch,
        compiler_params=pltpu.CompilerParams(vmem_limit_bytes=16 * 1024 * 1024),
        cost_estimate=pl.CostEstimate(flops=flops, bytes_accessed=1 << 18, transcendentals=0),
    )


def along_line(pieces, slots):
    sent = []
    for step, piece in zip(STEPS, pieces):
        pairs = [(slot, slot ^ (step * LINES)) for slot in range(slots)]
        sent.append(lax.ppermute(piece, "sec", pairs) if step else piece)
    return sent


def other_core(block):
    return lax.ppermute(block, "env", [(0, 1), (1, 0)])


def across(piece, slots):
    return lax.ppermute(piece, "sec", [(slot, slot ^ 1) for slot in range(slots)])


def on_device(amplitudes, widths, holders, left_env, right_env):
    slots_dev, right_dim, half = amplitudes.shape
    slots = holders.shape[0]
    assert slots_dev == 1
    if slots != 2 * QDOWN:
        return on_device_any(amplitudes, widths, holders, left_env, right_env)
    places = slots // LINES
    rows = right_dim // places
    dots = 6 * right_dim * half * (right_dim + 2 * half)
    block = jax.ShapeDtypeStruct((right_dim, half), jnp.bfloat16)
    wide = jax.ShapeDtypeStruct((right_dim, half), jnp.float32)
    pair = jax.ShapeDtypeStruct((2, rows, half), jnp.bfloat16)
    single = jax.ShapeDtypeStruct((rows, half), jnp.bfloat16)
    singles = jax.ShapeDtypeStruct((places, rows, half), jnp.bfloat16)
    wides = jax.ShapeDtypeStruct((places, rows, half), jnp.float32)
    chunked = rows * half // LANES
    tagged = jax.ShapeDtypeStruct((2 * chunked + TAG, LANES), jnp.bfloat16)
    crossing = jax.ShapeDtypeStruct((places * chunked + TAG, LANES), jnp.bfloat16)
    label = jax.ShapeDtypeStruct((TAG, LANES), jnp.bfloat16)
    factor_shape = jax.ShapeDtypeStruct((8, LANES), jnp.float32)
    plan_shape = jax.ShapeDtypeStruct((8, LANES), jnp.int32)
    split = [pltpu.VMEM((places, rows, half), jnp.bfloat16)]
    tables = [pltpu.VMEM((places, *shape.shape), jnp.bfloat16) for shape in (pair, tagged)]

    slot_table = [pltpu.SMEM((slots,), jnp.int32)]
    plan = call(plan_kernel, [SMEM, SMEM], plan_shape, slot_table)(widths, holders)
    both = jax.ShapeDtypeStruct((2, right_dim, half), jnp.bfloat16)
    *pieces, stay, start_full = call(
        first_kernel, [VMEM] * 6, (pair,) * places + (block, both), split, dots
    )(widths[None], holders[None], amplitudes[0], other_core(amplitudes[0]), right_env, left_env)
    old = along_line(pieces, slots)
    old_keep, cross = call(
        merge_kernel, [VMEM] * (1 + places), (singles, singles), tables[:1]
    )(plan, *old)
    old_arrived = across(cross, slots)
    joined = call(join_kernel, [VMEM, VMEM], (single,) * places)(old_keep, old_arrived)
    first = call(sum_kernel, [VMEM] * (2 + places), block)(
        plan, stay, *along_line(joined, slots)
    )

    *pieces, stay_2 = call(
        second_kernel, [VMEM] * 5, (tagged,) * places + (wide,), split, dots
    )(start_full, first, other_core(first), right_env, left_env)
    new = along_line(pieces, slots)
    keep, cross, tag = call(
        mix_kernel, [VMEM] * (1 + 2 * places), (wides, crossing, label), tables
    )(plan, *old, *new)
    *joined, factors = call(
        join_mixed_kernel, [VMEM] * 6, (single,) * places + (factor_shape,)
    )(plan, tag, keep, across(cross, slots), old_keep, old_arrived)
    second, first = call(final_kernel, [VMEM] * (5 + places), (block, block))(
        plan, factors, stay, stay_2, first, *along_line(joined, slots)
    )
    return first[None], second[None]


def solution(mesh):
    in_specs = (
        P(("runs", "sec"), None, "env"),
        P("runs"),
        P("runs"),
        P(("runs", "sec"), None, None, "env"),
        P("runs", None, None),
    )
    out_specs = (P(("runs", "sec"), None, "env"), P(("runs", "sec"), None, "env"))
    return jax.shard_map(
        on_device, mesh=mesh, in_specs=in_specs, out_specs=out_specs, check_vma=False
    )
```

```python
import jax
import jax.numpy as jnp
from jax import lax
from jax.experimental import pallas as pl
from jax.experimental.pallas import tpu as pltpu
from jax.sharding import PartitionSpec as P

QDOWN = 4

term_shifts = ((0, 0), (1, 0), (0, 1))


def route(holders):
    n_slots = holders.shape[0]
    sector_ids = jnp.arange(n_slots, dtype=jnp.int32)
    slot_of = jnp.argmax(holders[None, :] == sector_ids[:, None], axis=1)
    sources = []
    allowed = []
    for up, down in term_shifts[1:]:
        permitted = (holders // QDOWN - up >= 0) & (holders % QDOWN - down >= 0)
        wanted = jnp.clip(holders - QDOWN * up - down, 0, n_slots - 1)
        sources.append(slot_of[wanted])
        allowed.append(permitted)
    return sources, allowed


def contract(vector, left_env, right_env):
    products = jnp.einsum(
        "tij,jw->tiw", right_env, vector, preferred_element_type=jnp.float32
    ).astype(jnp.bfloat16)
    return jnp.einsum("tik,tkw->tiw", products, left_env, preferred_element_type=jnp.float32)


def spread(blocks, n_slots):
    terms, rows, width = blocks.shape
    pieces = blocks.reshape(terms, n_slots, rows // n_slots, width).swapaxes(0, 1)
    return lax.all_to_all(pieces, "sec", split_axis=0, concat_axis=0)


def collect(merged):
    n_slots, rows, width = merged.shape
    home = lax.all_to_all(merged, "sec", split_axis=0, concat_axis=0)
    return home.reshape(n_slots * rows, width)


def share(values, n_slots, me):
    lanes = jnp.zeros((1, 128), jnp.float32).at[0, : values.shape[0]].set(values)
    if n_slots & (n_slots - 1) or n_slots > 16:
        return lax.all_gather(lanes[0], "sec")
    table = jnp.where(jnp.arange(n_slots)[:, None] == me, lanes, 0.0)
    for offset in range(1, n_slots):
        pairs = [(i, i ^ offset) for i in range(n_slots)]
        other = lax.ppermute(lanes, "sec", pairs)
        table = jnp.where(jnp.arange(n_slots)[:, None] == (me ^ offset), other, table)
    return table


def merge(received, sources, allowed):
    total = 0.0
    for term, (source, permitted) in enumerate(zip(sources, allowed)):
        picked = received[source, term]
        total = total + jnp.where(permitted[:, None, None], picked, 0).astype(jnp.float32)
    return total


def on_device_any(amplitudes, widths, holders, left_env, right_env):
    slots_dev, right_dim, half_width = amplitudes.shape
    assert slots_dev == 1
    n_slots = holders.shape[0]
    me = lax.axis_index("sec")
    side = lax.axis_index("env")
    my_width = widths[holders[me]]
    row_index = side * half_width + jnp.arange(half_width, dtype=jnp.int32)
    live = (row_index < my_width)[None, :]
    sources, allowed = route(holders)
    envs = left_env[0]

    start = jnp.where(live, amplitudes[0], jnp.zeros_like(amplitudes[0]))
    start_full = lax.all_gather(start, "env", axis=1, tiled=True)
    outgoing = contract(start_full, envs, right_env).astype(jnp.bfloat16)
    stay = outgoing[0].astype(jnp.float32)
    received = spread(outgoing[1:], n_slots)
    arrived = collect(merge(received, sources, allowed).astype(jnp.bfloat16))
    first = jnp.where(live, stay + arrived.astype(jnp.float32), 0.0).astype(jnp.bfloat16)

    first_full = lax.all_gather(first, "env", axis=1, tiled=True).astype(jnp.float32)
    basis = start_full.astype(jnp.float32)
    overlap = jnp.sum(basis * first_full)
    norm = jnp.sum(basis * basis)
    own_quotient = jnp.where(norm > 0, overlap / jnp.where(norm > 0, norm, 1.0), 0.0)
    deflated = first_full - own_quotient * basis
    rest = jnp.sum(deflated * deflated)
    sums = share(jnp.stack([overlap, norm, own_quotient, rest]), n_slots, me)
    outgoing_2 = contract(deflated.astype(jnp.bfloat16), envs, right_env)
    received_2 = spread(outgoing_2[1:].astype(jnp.bfloat16), n_slots)

    quotient = jnp.sum(sums[:, 0]) / jnp.sum(sums[:, 1])
    shift = sums[:, 2] - quotient
    resid_norm = jnp.sum(sums[:, 3] + shift * shift * sums[:, 1])
    live_count = right_dim * jnp.sum(widths).astype(jnp.float32)
    scale = lax.rsqrt(resid_norm / live_count + 1e-06)
    mixed = received_2.astype(jnp.float32) + shift[:, None, None, None] * received.astype(
        jnp.float32
    )
    merged_2 = scale * merge(mixed, sources, allowed)
    arrived_2 = collect(merged_2.astype(jnp.bfloat16))
    stay_2 = scale * (outgoing_2[0] + (own_quotient - quotient) * stay)
    second = jnp.where(live, stay_2 + arrived_2.astype(jnp.float32), 0.0).astype(jnp.bfloat16)
    return first[None], second[None]


LANES = 128
TAG = 16
LINES = 2
STEPS = (0, 2, 3, 1)


def plan_kernel(widths, holders, plan, slot_of):
    slots = holders.shape[0]
    me = lax.axis_index("sec")
    total = jnp.int32(0)
    for s in range(slots):
        slot_of[holders[s]] = jnp.int32(s)
        total = total + widths[s]
    codes = [jnp.int32(0), jnp.int32(0)]
    for target in range(slots):
        sector = holders[target]
        has = (sector >= QDOWN, sector % QDOWN > 0)
        source = (slot_of[sector & (QDOWN - 1)], slot_of[jnp.maximum(sector - 1, 0)])
        for i in range(2):
            entry = jnp.where(has[i], source[i] + slots, 0)
            codes[i] = codes[i] | (entry << (target * 4))
    row = lax.broadcasted_iota(jnp.int32, plan.shape, 0)
    values = jnp.where(row == 0, widths[holders[me]], total)
    values = jnp.where(row == 2, codes[0], values)
    plan[...] = jnp.where(row == 3, codes[1], values)


def live_columns(plan, half):
    first_column = lax.axis_index("env") * half
    return first_column + lax.broadcasted_iota(jnp.int32, (1, half), 1) < plan[0:1, 0:1]


def apply_term(right, left, vector, term):
    products = jnp.dot(right[term], vector, preferred_element_type=jnp.float32)
    return jnp.dot(products.astype(jnp.bfloat16), left, preferred_element_type=jnp.float32)


def in_order(own, other):
    upper = lax.axis_index("env") > 0
    return [jnp.where(upper, other, own), jnp.where(upper, own, other)]


def own_place():
    return lax.axis_index("sec") // LINES


def columns_kernel(columns):
    columns[...] = lax.broadcasted_iota(jnp.int32, columns.shape, 1)


def first_kernel(columns, widths, holders, own, other, right, left, *rest):
    *pieces, stay, start, block_vmem = rest
    half = stay.shape[1]
    slot = lax.broadcasted_iota(jnp.int32, widths.shape, 1)
    mine = jnp.where(slot == lax.axis_index("sec"), holders[...], 0)
    sector = jnp.sum(mine, axis=1, keepdims=True)
    width = jnp.sum(jnp.where(slot == sector, widths[...], 0), axis=1, keepdims=True)
    for h, part in enumerate(in_order(own[...], other[...])):
        live = h * half + columns[0:1, :] < width
        start[h] = jnp.where(live, part, jnp.zeros_like(part))
    vector = jnp.concatenate([start[0], start[1]], axis=1)
    for term in (1, 2, 0):
        block = apply_term(right, left[0, term], vector, term).astype(jnp.bfloat16)
        if term == 0:
            stay[...] = block
        else:
            block_vmem[...] = block.reshape(block_vmem.shape)
            for step, piece in zip(STEPS, pieces):
                piece[term - 1] = block_vmem[own_place() ^ step]


def line_targets(plan, places):
    line = lax.axis_index("sec") % LINES
    codes = [jnp.max(plan[2 + i : 3 + i, :]) for i in range(2)]
    for place in range(places):
        for crossing in range(2):
            target = place * LINES + (line ^ crossing)
            entries = [(code >> (target * 4)) & (2 * LINES * places - 1) for code in codes]
            source = [entry & (LINES * places - 1) for entry in entries]
            here = [
                (entry >= LINES * places) & (slot % LINES == line)
                for entry, slot in zip(entries, source)
            ]
            yield place, crossing, here, source


def merge_kernel(plan, *rest):
    *pieces, keep, cross, table = rest
    for step, piece in zip(STEPS, pieces):
        table[own_place() ^ step] = piece[...]
    for place, crossing, here, source in line_targets(plan, keep.shape[0]):
        total = 0.0
        for i in range(2):
            block = table[source[i] // LINES, i].astype(jnp.float32)
            total = total + jnp.where(here[i], block, 0.0)
        (keep, cross)[crossing][place] = total.astype(jnp.bfloat16)


def join_kernel(keep, arrived, *outs):
    for step, out in zip(STEPS, outs):
        place = own_place() ^ step
        total = keep[place].astype(jnp.float32) + arrived[place].astype(jnp.float32)
        out[...] = total.astype(jnp.bfloat16)


def piece_rows(step, rows):
    return pl.ds(pl.multiple_of((own_place() ^ step) * rows, rows), rows)


def sum_kernel(plan, stay, *rest):
    *pieces, first = rest
    live = live_columns(plan, stay.shape[1])
    for step, piece in zip(STEPS, pieces):
        place = piece_rows(step, piece.shape[0])
        total = stay[place, :].astype(jnp.float32) + piece[...].astype(jnp.float32)
        first[place, :] = jnp.where(live, total, 0.0).astype(jnp.bfloat16)


def total_of(array):
    return jnp.sum(jnp.sum(array, axis=0, keepdims=True), axis=1, keepdims=True)


def make_tag(values, me):
    row = lax.broadcasted_iota(jnp.int32, (TAG, LANES), 0)
    lane = lax.broadcasted_iota(jnp.int32, (TAG, LANES), 1)
    spread = jnp.zeros((TAG, LANES), jnp.float32)
    for place, value in enumerate(values):
        spread = jnp.where(row // 3 == place, value, spread)
    high = spread.astype(jnp.bfloat16).astype(jnp.float32)
    middle = (spread - high).astype(jnp.bfloat16).astype(jnp.float32)
    low = spread - high - middle
    parts = jnp.where(row % 3 == 0, high, jnp.where(row % 3 == 1, middle, low))
    return jnp.where((lane == me) & (row < 3 * len(values)), parts, 0.0).astype(jnp.bfloat16)


def second_kernel(start, own, other, right, left, *rest):
    *pieces, stay, block_vmem = rest
    half = stay.shape[1]
    rows = block_vmem.shape[1]
    chunks = half // LANES
    basis = [start[h].astype(jnp.float32) for h in range(2)]
    firsts = [part.astype(jnp.float32) for part in in_order(own[...], other[...])]
    overlap = total_of(basis[0] * firsts[0]) + total_of(basis[1] * firsts[1])
    norm = total_of(basis[0] * basis[0]) + total_of(basis[1] * basis[1])
    quotient = jnp.where(norm > 0, overlap / jnp.where(norm > 0, norm, 1.0), 0.0)
    deflated = [firsts[h] - quotient * basis[h] for h in range(2)]
    rest_norm = total_of(deflated[0] * deflated[0]) + total_of(deflated[1] * deflated[1])
    vector = jnp.concatenate(deflated, axis=1).astype(jnp.bfloat16)
    tag = make_tag((overlap, norm, quotient, rest_norm), lax.axis_index("sec"))
    for piece in pieces:
        piece[pl.ds(2 * chunks * rows, TAG), :] = tag
    for term in (1, 2, 0):
        block = apply_term(right, left[0, term], vector, term)
        if term == 0:
            stay[...] = block
        else:
            block_vmem[...] = block.astype(jnp.bfloat16).reshape(block_vmem.shape)
            for step, piece in zip(STEPS, pieces):
                part = block_vmem[own_place() ^ step]
                for c in range(chunks):
                    place = pl.ds(((term - 1) * chunks + c) * rows, rows)
                    piece[place, :] = part[:, c * LANES : (c + 1) * LANES]


def read_tag(tag):
    def value(place):
        parts = [tag[3 * place + i : 3 * place + i + 1, :] for i in range(3)]
        return parts[0] + parts[1] + parts[2]

    return [value(place) for place in range(4)]


def line_quotient(overlaps, norms, line):
    inside = lax.broadcasted_iota(jnp.int32, (1, LANES), 1) % LINES == line
    overlap = total_of(jnp.where(inside, overlaps, 0.0))
    norm = total_of(jnp.where(inside, norms, 0.0))
    return jnp.where(norm > 0, overlap / jnp.where(norm > 0, norm, 1.0), 0.0)


def mix_kernel(plan, *rest):
    keep, cross, tag_out, old, new = rest[-5:]
    places, rows, half = keep.shape
    chunks = half // LANES
    tag = jnp.zeros((TAG, LANES), jnp.float32)
    for i, step in enumerate(STEPS):
        old[own_place() ^ step] = rest[i][...]
        new[own_place() ^ step] = rest[places + i][...]
        label = rest[places + i][pl.ds(2 * chunks * rows, TAG), :]
        tag = tag + label.astype(jnp.float32)
    tag_out[...] = tag.astype(jnp.bfloat16)
    cross[pl.ds(places * chunks * rows, TAG), :] = tag.astype(jnp.bfloat16)
    overlaps, norms, quotients, _ = read_tag(tag)
    shifts = quotients - line_quotient(overlaps, norms, lax.axis_index("sec") % LINES)
    lane = lax.broadcasted_iota(jnp.int32, (1, LANES), 1)
    for place, crossing, here, source in line_targets(plan, keep.shape[0]):
        total = 0.0
        for i in range(2):
            where = source[i] // LINES
            block = jnp.concatenate(
                [new[where, pl.ds((i * chunks + c) * rows, rows), :] for c in range(chunks)],
                axis=1,
            ).astype(jnp.float32)
            shift = total_of(jnp.where(lane == source[i], shifts, 0.0))
            block = block + shift * old[where, i].astype(jnp.float32)
            total = total + jnp.where(here[i], block, 0.0)
        if crossing:
            total = total.astype(jnp.bfloat16)
            for c in range(chunks):
                target = pl.ds((place * chunks + c) * rows, rows)
                cross[target, :] = total[:, c * LANES : (c + 1) * LANES]
        else:
            keep[place] = total


def join_mixed_kernel(plan, tag_line, keep, arrived, old_keep, old_arrived, *rest):
    *outs, factors = rest
    places, rows, half = keep.shape
    chunks = half // LANES
    slots = places * LINES
    me = lax.axis_index("sec")
    live_count = places * rows * plan[1:2, 0:1].astype(jnp.float32)
    tag = tag_line[...].astype(jnp.float32)
    tag = tag + arrived[pl.ds(places * chunks * rows, TAG), :].astype(jnp.float32)
    overlaps, norms, quotients, rests = read_tag(tag)
    quotient = total_of(overlaps) / total_of(norms)
    lane = lax.broadcasted_iota(jnp.int32, (1, LANES), 1)
    shifts = jnp.where(lane < slots, quotients - quotient, 0.0)
    resid_norm = total_of(rests + shifts * shifts * norms)
    scale = lax.rsqrt(resid_norm / live_count + 1e-06)
    row = lax.broadcasted_iota(jnp.int32, factors.shape, 0)
    own_shift = total_of(jnp.where(lane == me, shifts, 0.0))
    factors[...] = jnp.where(row == 0, scale, scale * own_shift)
    line = me % LINES
    shift_here = line_quotient(overlaps, norms, line) - quotient
    shift_there = line_quotient(overlaps, norms, 1 - line) - quotient
    for step, out in zip(STEPS, outs):
        place = own_place() ^ step
        starts = [pl.multiple_of((place * chunks + c) * rows, rows) for c in range(chunks)]
        block = jnp.concatenate(
            [arrived[pl.ds(start, rows), :] for start in starts], axis=1
        ).astype(jnp.float32)
        block = block + shift_there * old_arrived[place].astype(jnp.float32)
        block = block + keep[place] + shift_here * old_keep[place].astype(jnp.float32)
        out[...] = (scale * block).astype(jnp.bfloat16)


def final_kernel(plan, factors, stay, stay_2, first, *rest):
    *pieces, second, first_out = rest
    first_out[...] = first[...]
    live = live_columns(plan, stay.shape[1])
    scale, shift = factors[0:1, 0:1], factors[1:2, 0:1]
    for step, piece in zip(STEPS, pieces):
        place = piece_rows(step, piece.shape[0])
        total = scale * stay_2[place, :] + shift * stay[place, :].astype(jnp.float32)
        total = total + piece[...].astype(jnp.float32)
        second[place, :] = jnp.where(live, total, 0.0).astype(jnp.bfloat16)


SMEM = pl.BlockSpec(memory_space=pltpu.SMEM)
VMEM = pl.BlockSpec(memory_space=pltpu.VMEM)


def call(kernel, specs, outs, scratch=(), flops=0):
    return pl.pallas_call(
        kernel,
        out_shape=outs,
        in_specs=specs,
        out_specs=jax.tree.map(lambda _: VMEM, outs),
        scratch_shapes=scratch,
        compiler_params=pltpu.CompilerParams(vmem_limit_bytes=16 * 1024 * 1024),
        cost_estimate=pl.CostEstimate(flops=flops, bytes_accessed=1 << 18, transcendentals=0),
    )


def along_line(pieces, slots):
    sent = []
    for step, piece in zip(STEPS, pieces):
        pairs = [(slot, slot ^ (step * LINES)) for slot in range(slots)]
        sent.append(lax.ppermute(piece, "sec", pairs) if step else piece)
    return sent


def other_core(block):
    return lax.ppermute(block, "env", [(0, 1), (1, 0)])


def across(piece, slots):
    return lax.ppermute(piece, "sec", [(slot, slot ^ 1) for slot in range(slots)])


def on_device(amplitudes, widths, holders, left_env, right_env):
    slots_dev, right_dim, half = amplitudes.shape
    slots = holders.shape[0]
    assert slots_dev == 1
    if slots != 2 * QDOWN:
        return on_device_any(amplitudes, widths, holders, left_env, right_env)
    places = slots // LINES
    rows = right_dim // places
    dots = 6 * right_dim * half * (right_dim + 2 * half)
    block = jax.ShapeDtypeStruct((right_dim, half), jnp.bfloat16)
    wide = jax.ShapeDtypeStruct((right_dim, half), jnp.float32)
    pair = jax.ShapeDtypeStruct((2, rows, half), jnp.bfloat16)
    single = jax.ShapeDtypeStruct((rows, half), jnp.bfloat16)
    singles = jax.ShapeDtypeStruct((places, rows, half), jnp.bfloat16)
    wides = jax.ShapeDtypeStruct((places, rows, half), jnp.float32)
    chunked = rows * half // LANES
    tagged = jax.ShapeDtypeStruct((2 * chunked + TAG, LANES), jnp.bfloat16)
    crossing = jax.ShapeDtypeStruct((places * chunked + TAG, LANES), jnp.bfloat16)
    label = jax.ShapeDtypeStruct((TAG, LANES), jnp.bfloat16)
    factor_shape = jax.ShapeDtypeStruct((8, LANES), jnp.float32)
    plan_shape = jax.ShapeDtypeStruct((8, LANES), jnp.int32)
    split = [pltpu.VMEM((places, rows, half), jnp.bfloat16)]
    tables = [pltpu.VMEM((places, *shape.shape), jnp.bfloat16) for shape in (pair, tagged)]

    slot_table = [pltpu.SMEM((slots,), jnp.int32)]
    plan = call(plan_kernel, [SMEM, SMEM], plan_shape, slot_table)(widths, holders)
    both = jax.ShapeDtypeStruct((2, right_dim, half), jnp.bfloat16)
    number = jax.ShapeDtypeStruct((8, half), jnp.int32)
    columns = call(columns_kernel, [], number, flops=4 << 30)()
    *pieces, stay, start_full = call(
        first_kernel, [VMEM] * 7, (pair,) * places + (block, both), split, dots
    )(
        columns,
        widths[None],
        holders[None],
        amplitudes[0],
        other_core(amplitudes[0]),
        right_env,
        left_env,
    )
    old = along_line(pieces, slots)
    old_keep, cross = call(
        merge_kernel, [VMEM] * (1 + places), (singles, singles), tables[:1]
    )(plan, *old)
    old_arrived = across(cross, slots)
    joined = call(join_kernel, [VMEM, VMEM], (single,) * places)(old_keep, old_arrived)
    first = call(sum_kernel, [VMEM] * (2 + places), block)(
        plan, stay, *along_line(joined, slots)
    )

    *pieces, stay_2 = call(
        second_kernel, [VMEM] * 5, (tagged,) * places + (wide,), split, dots
    )(start_full, first, other_core(first), right_env, left_env)
    new = along_line(pieces, slots)
    keep, cross, tag = call(
        mix_kernel, [VMEM] * (1 + 2 * places), (wides, crossing, label), tables
    )(plan, *old, *new)
    *joined, factors = call(
        join_mixed_kernel, [VMEM] * 6, (single,) * places + (factor_shape,)
    )(plan, tag, keep, across(cross, slots), old_keep, old_arrived)
    second, first = call(final_kernel, [VMEM] * (5 + places), (block, block))(
        plan, factors, stay, stay_2, first, *along_line(joined, slots)
    )
    return first[None], second[None]


def solution(mesh):
    in_specs = (
        P(("runs", "sec"), None, "env"),
        P("runs"),
        P("runs"),
        P(("runs", "sec"), None, None, "env"),
        P("runs", None, None),
    )
    out_specs = (P(("runs", "sec"), None, "env"), P(("runs", "sec"), None, "env"))
    return jax.shard_map(
        on_device, mesh=mesh, in_specs=in_specs, out_specs=out_specs, check_vma=False
    )
```

```python
import jax
import jax.numpy as jnp
from jax import lax
from jax.experimental import pallas as pl
from jax.experimental.pallas import tpu as pltpu
from jax.sharding import PartitionSpec as P

QDOWN = 4

term_shifts = ((0, 0), (1, 0), (0, 1))


def route(holders):
    n_slots = holders.shape[0]
    sector_ids = jnp.arange(n_slots, dtype=jnp.int32)
    slot_of = jnp.argmax(holders[None, :] == sector_ids[:, None], axis=1)
    sources = []
    allowed = []
    for up, down in term_shifts[1:]:
        permitted = (holders // QDOWN - up >= 0) & (holders % QDOWN - down >= 0)
        wanted = jnp.clip(holders - QDOWN * up - down, 0, n_slots - 1)
        sources.append(slot_of[wanted])
        allowed.append(permitted)
    return sources, allowed


def contract(vector, left_env, right_env):
    products = jnp.einsum(
        "tij,jw->tiw", right_env, vector, preferred_element_type=jnp.float32
    ).astype(jnp.bfloat16)
    return jnp.einsum("tik,tkw->tiw", products, left_env, preferred_element_type=jnp.float32)


def spread(blocks, n_slots):
    terms, rows, width = blocks.shape
    pieces = blocks.reshape(terms, n_slots, rows // n_slots, width).swapaxes(0, 1)
    return lax.all_to_all(pieces, "sec", split_axis=0, concat_axis=0)


def collect(merged):
    n_slots, rows, width = merged.shape
    home = lax.all_to_all(merged, "sec", split_axis=0, concat_axis=0)
    return home.reshape(n_slots * rows, width)


def share(values, n_slots, me):
    lanes = jnp.zeros((1, 128), jnp.float32).at[0, : values.shape[0]].set(values)
    if n_slots & (n_slots - 1) or n_slots > 16:
        return lax.all_gather(lanes[0], "sec")
    table = jnp.where(jnp.arange(n_slots)[:, None] == me, lanes, 0.0)
    for offset in range(1, n_slots):
        pairs = [(i, i ^ offset) for i in range(n_slots)]
        other = lax.ppermute(lanes, "sec", pairs)
        table = jnp.where(jnp.arange(n_slots)[:, None] == (me ^ offset), other, table)
    return table


def merge(received, sources, allowed):
    total = 0.0
    for term, (source, permitted) in enumerate(zip(sources, allowed)):
        picked = received[source, term]
        total = total + jnp.where(permitted[:, None, None], picked, 0).astype(jnp.float32)
    return total


def on_device_any(amplitudes, widths, holders, left_env, right_env):
    slots_dev, right_dim, half_width = amplitudes.shape
    assert slots_dev == 1
    n_slots = holders.shape[0]
    me = lax.axis_index("sec")
    side = lax.axis_index("env")
    my_width = widths[holders[me]]
    row_index = side * half_width + jnp.arange(half_width, dtype=jnp.int32)
    live = (row_index < my_width)[None, :]
    sources, allowed = route(holders)
    envs = left_env[0]

    start = jnp.where(live, amplitudes[0], jnp.zeros_like(amplitudes[0]))
    start_full = lax.all_gather(start, "env", axis=1, tiled=True)
    outgoing = contract(start_full, envs, right_env).astype(jnp.bfloat16)
    stay = outgoing[0].astype(jnp.float32)
    received = spread(outgoing[1:], n_slots)
    arrived = collect(merge(received, sources, allowed).astype(jnp.bfloat16))
    first = jnp.where(live, stay + arrived.astype(jnp.float32), 0.0).astype(jnp.bfloat16)

    first_full = lax.all_gather(first, "env", axis=1, tiled=True).astype(jnp.float32)
    basis = start_full.astype(jnp.float32)
    overlap = jnp.sum(basis * first_full)
    norm = jnp.sum(basis * basis)
    own_quotient = jnp.where(norm > 0, overlap / jnp.where(norm > 0, norm, 1.0), 0.0)
    deflated = first_full - own_quotient * basis
    rest = jnp.sum(deflated * deflated)
    sums = share(jnp.stack([overlap, norm, own_quotient, rest]), n_slots, me)
    outgoing_2 = contract(deflated.astype(jnp.bfloat16), envs, right_env)
    received_2 = spread(outgoing_2[1:].astype(jnp.bfloat16), n_slots)

    quotient = jnp.sum(sums[:, 0]) / jnp.sum(sums[:, 1])
    shift = sums[:, 2] - quotient
    resid_norm = jnp.sum(sums[:, 3] + shift * shift * sums[:, 1])
    live_count = right_dim * jnp.sum(widths).astype(jnp.float32)
    scale = lax.rsqrt(resid_norm / live_count + 1e-06)
    mixed = received_2.astype(jnp.float32) + shift[:, None, None, None] * received.astype(
        jnp.float32
    )
    merged_2 = scale * merge(mixed, sources, allowed)
    arrived_2 = collect(merged_2.astype(jnp.bfloat16))
    stay_2 = scale * (outgoing_2[0] + (own_quotient - quotient) * stay)
    second = jnp.where(live, stay_2 + arrived_2.astype(jnp.float32), 0.0).astype(jnp.bfloat16)
    return first[None], second[None]


LANES = 128
TAG = 16
LINES = 2
STEPS = (0, 3, 2, 1)


def plan_kernel(widths, holders, plan, slot_of):
    slots = holders.shape[0]
    me = lax.axis_index("sec")
    total = jnp.int32(0)
    for s in range(slots):
        slot_of[holders[s]] = jnp.int32(s)
        total = total + widths[s]
    codes = [jnp.int32(0), jnp.int32(0)]
    for target in range(slots):
        sector = holders[target]
        has = (sector >= QDOWN, sector % QDOWN > 0)
        source = (slot_of[sector & (QDOWN - 1)], slot_of[jnp.maximum(sector - 1, 0)])
        for i in range(2):
            entry = jnp.where(has[i], source[i] + slots, 0)
            codes[i] = codes[i] | (entry << (target * 4))
    row = lax.broadcasted_iota(jnp.int32, plan.shape, 0)
    values = jnp.where(row == 0, widths[holders[me]], total)
    values = jnp.where(row == 2, codes[0], values)
    plan[...] = jnp.where(row == 3, codes[1], values)


def live_columns(plan, half):
    first_column = lax.axis_index("env") * half
    return first_column + lax.broadcasted_iota(jnp.int32, (1, half), 1) < plan[0:1, 0:1]


def apply_term(right, left, vector, term):
    products = jnp.dot(right[term], vector, preferred_element_type=jnp.float32)
    return jnp.dot(products.astype(jnp.bfloat16), left, preferred_element_type=jnp.float32)


def in_order(own, other):
    upper = lax.axis_index("env") > 0
    return [jnp.where(upper, other, own), jnp.where(upper, own, other)]


def own_place():
    return lax.axis_index("sec") // LINES


def columns_kernel(columns):
    columns[...] = lax.broadcasted_iota(jnp.int32, columns.shape, 1)


def first_kernel(columns, widths, holders, own, other, right, left, *rest):
    *pieces, stay, start, block_vmem = rest
    half = stay.shape[1]
    slot = lax.broadcasted_iota(jnp.int32, widths.shape, 1)
    mine = jnp.where(slot == lax.axis_index("sec"), holders[...], 0)
    sector = jnp.sum(mine, axis=1, keepdims=True)
    width = jnp.sum(jnp.where(slot == sector, widths[...], 0), axis=1, keepdims=True)
    for h, part in enumerate(in_order(own[...], other[...])):
        live = h * half + columns[0:1, :] < width
        start[h] = jnp.where(live, part, jnp.zeros_like(part))
    vector = jnp.concatenate([start[0], start[1]], axis=1)
    for term in (1, 2, 0):
        block = apply_term(right, left[0, term], vector, term).astype(jnp.bfloat16)
        if term == 0:
            stay[...] = block
        else:
            block_vmem[...] = block.reshape(block_vmem.shape)
            for step, piece in zip(STEPS, pieces):
                piece[term - 1] = block_vmem[own_place() ^ step]


def line_targets(plan, places):
    line = lax.axis_index("sec") % LINES
    codes = [jnp.max(plan[2 + i : 3 + i, :]) for i in range(2)]
    for place in range(places):
        for crossing in range(2):
            target = place * LINES + (line ^ crossing)
            entries = [(code >> (target * 4)) & (2 * LINES * places - 1) for code in codes]
            source = [entry & (LINES * places - 1) for entry in entries]
            here = [
                (entry >= LINES * places) & (slot % LINES == line)
                for entry, slot in zip(entries, source)
            ]
            yield place, crossing, here, source


def merge_kernel(plan, *rest):
    *pieces, keep, cross, table = rest
    for step, piece in zip(STEPS, pieces):
        table[own_place() ^ step] = piece[...]
    for place, crossing, here, source in line_targets(plan, keep.shape[0]):
        total = 0.0
        for i in range(2):
            block = table[source[i] // LINES, i].astype(jnp.float32)
            total = total + jnp.where(here[i], block, 0.0)
        (keep, cross)[crossing][place] = total.astype(jnp.bfloat16)


def join_kernel(keep, arrived, *outs):
    for step, out in zip(STEPS, outs):
        place = own_place() ^ step
        total = keep[place].astype(jnp.float32) + arrived[place].astype(jnp.float32)
        out[...] = total.astype(jnp.bfloat16)


def piece_rows(step, rows):
    return pl.ds(pl.multiple_of((own_place() ^ step) * rows, rows), rows)


def sum_kernel(plan, stay, *rest):
    *pieces, first = rest
    live = live_columns(plan, stay.shape[1])
    for step, piece in zip(STEPS, pieces):
        place = piece_rows(step, piece.shape[0])
        total = stay[place, :].astype(jnp.float32) + piece[...].astype(jnp.float32)
        first[place, :] = jnp.where(live, total, 0.0).astype(jnp.bfloat16)


def total_of(array):
    return jnp.sum(jnp.sum(array, axis=0, keepdims=True), axis=1, keepdims=True)


def make_tag(values, me):
    row = lax.broadcasted_iota(jnp.int32, (TAG, LANES), 0)
    lane = lax.broadcasted_iota(jnp.int32, (TAG, LANES), 1)
    spread = jnp.zeros((TAG, LANES), jnp.float32)
    for place, value in enumerate(values):
        spread = jnp.where(row // 3 == place, value, spread)
    high = spread.astype(jnp.bfloat16).astype(jnp.float32)
    middle = (spread - high).astype(jnp.bfloat16).astype(jnp.float32)
    low = spread - high - middle
    parts = jnp.where(row % 3 == 0, high, jnp.where(row % 3 == 1, middle, low))
    return jnp.where((lane == me) & (row < 3 * len(values)), parts, 0.0).astype(jnp.bfloat16)


def second_kernel(start, own, other, right, left, *rest):
    *pieces, stay, block_vmem = rest
    half = stay.shape[1]
    rows = block_vmem.shape[1]
    chunks = half // LANES
    basis = [start[h].astype(jnp.float32) for h in range(2)]
    firsts = [part.astype(jnp.float32) for part in in_order(own[...], other[...])]
    overlap = total_of(basis[0] * firsts[0]) + total_of(basis[1] * firsts[1])
    norm = total_of(basis[0] * basis[0]) + total_of(basis[1] * basis[1])
    quotient = jnp.where(norm > 0, overlap / jnp.where(norm > 0, norm, 1.0), 0.0)
    deflated = [firsts[h] - quotient * basis[h] for h in range(2)]
    rest_norm = total_of(deflated[0] * deflated[0]) + total_of(deflated[1] * deflated[1])
    vector = jnp.concatenate(deflated, axis=1).astype(jnp.bfloat16)
    tag = make_tag((overlap, norm, quotient, rest_norm), lax.axis_index("sec"))
    for piece in pieces:
        piece[pl.ds(2 * chunks * rows, TAG), :] = tag
    for term in (1, 2, 0):
        block = apply_term(right, left[0, term], vector, term)
        if term == 0:
            stay[...] = block
        else:
            block_vmem[...] = block.astype(jnp.bfloat16).reshape(block_vmem.shape)
            for step, piece in zip(STEPS, pieces):
                part = block_vmem[own_place() ^ step]
                for c in range(chunks):
                    place = pl.ds(((term - 1) * chunks + c) * rows, rows)
                    piece[place, :] = part[:, c * LANES : (c + 1) * LANES]


def read_tag(tag):
    def value(place):
        parts = [tag[3 * place + i : 3 * place + i + 1, :] for i in range(3)]
        return parts[0] + parts[1] + parts[2]

    return [value(place) for place in range(4)]


def line_quotient(overlaps, norms, line):
    inside = lax.broadcasted_iota(jnp.int32, (1, LANES), 1) % LINES == line
    overlap = total_of(jnp.where(inside, overlaps, 0.0))
    norm = total_of(jnp.where(inside, norms, 0.0))
    return jnp.where(norm > 0, overlap / jnp.where(norm > 0, norm, 1.0), 0.0)


def mix_kernel(plan, *rest):
    keep, cross, tag_out, old, new = rest[-5:]
    places, rows, half = keep.shape
    chunks = half // LANES
    tag = jnp.zeros((TAG, LANES), jnp.float32)
    for i, step in enumerate(STEPS):
        old[own_place() ^ step] = rest[i][...]
        new[own_place() ^ step] = rest[places + i][...]
        label = rest[places + i][pl.ds(2 * chunks * rows, TAG), :]
        tag = tag + label.astype(jnp.float32)
    tag_out[...] = tag.astype(jnp.bfloat16)
    cross[pl.ds(places * chunks * rows, TAG), :] = tag.astype(jnp.bfloat16)
    overlaps, norms, quotients, _ = read_tag(tag)
    shifts = quotients - line_quotient(overlaps, norms, lax.axis_index("sec") % LINES)
    lane = lax.broadcasted_iota(jnp.int32, (1, LANES), 1)
    for place, crossing, here, source in line_targets(plan, keep.shape[0]):
        total = 0.0
        for i in range(2):
            where = source[i] // LINES
            block = jnp.concatenate(
                [new[where, pl.ds((i * chunks + c) * rows, rows), :] for c in range(chunks)],
                axis=1,
            ).astype(jnp.float32)
            shift = total_of(jnp.where(lane == source[i], shifts, 0.0))
            block = block + shift * old[where, i].astype(jnp.float32)
            total = total + jnp.where(here[i], block, 0.0)
        if crossing:
            total = total.astype(jnp.bfloat16)
            for c in range(chunks):
                target = pl.ds((place * chunks + c) * rows, rows)
                cross[target, :] = total[:, c * LANES : (c + 1) * LANES]
        else:
            keep[place] = total


def join_mixed_kernel(plan, tag_line, keep, arrived, old_keep, old_arrived, *rest):
    *outs, factors = rest
    places, rows, half = keep.shape
    chunks = half // LANES
    slots = places * LINES
    me = lax.axis_index("sec")
    live_count = places * rows * plan[1:2, 0:1].astype(jnp.float32)
    tag = tag_line[...].astype(jnp.float32)
    tag = tag + arrived[pl.ds(places * chunks * rows, TAG), :].astype(jnp.float32)
    overlaps, norms, quotients, rests = read_tag(tag)
    quotient = total_of(overlaps) / total_of(norms)
    lane = lax.broadcasted_iota(jnp.int32, (1, LANES), 1)
    shifts = jnp.where(lane < slots, quotients - quotient, 0.0)
    resid_norm = total_of(rests + shifts * shifts * norms)
    scale = lax.rsqrt(resid_norm / live_count + 1e-06)
    row = lax.broadcasted_iota(jnp.int32, factors.shape, 0)
    own_shift = total_of(jnp.where(lane == me, shifts, 0.0))
    factors[...] = jnp.where(row == 0, scale, scale * own_shift)
    line = me % LINES
    shift_here = line_quotient(overlaps, norms, line) - quotient
    shift_there = line_quotient(overlaps, norms, 1 - line) - quotient
    for step, out in zip(STEPS, outs):
        place = own_place() ^ step
        starts = [pl.multiple_of((place * chunks + c) * rows, rows) for c in range(chunks)]
        block = jnp.concatenate(
            [arrived[pl.ds(start, rows), :] for start in starts], axis=1
        ).astype(jnp.float32)
        block = block + shift_there * old_arrived[place].astype(jnp.float32)
        block = block + keep[place] + shift_here * old_keep[place].astype(jnp.float32)
        out[...] = (scale * block).astype(jnp.bfloat16)


def final_kernel(plan, factors, stay, stay_2, first, *rest):
    *pieces, second, first_out = rest
    first_out[...] = first[...]
    live = live_columns(plan, stay.shape[1])
    scale, shift = factors[0:1, 0:1], factors[1:2, 0:1]
    for step, piece in zip(STEPS, pieces):
        place = piece_rows(step, piece.shape[0])
        total = scale * stay_2[place, :] + shift * stay[place, :].astype(jnp.float32)
        total = total + piece[...].astype(jnp.float32)
        second[place, :] = jnp.where(live, total, 0.0).astype(jnp.bfloat16)


SMEM = pl.BlockSpec(memory_space=pltpu.SMEM)
VMEM = pl.BlockSpec(memory_space=pltpu.VMEM)


def call(kernel, specs, outs, scratch=(), flops=0):
    return pl.pallas_call(
        kernel,
        out_shape=outs,
        in_specs=specs,
        out_specs=jax.tree.map(lambda _: VMEM, outs),
        scratch_shapes=scratch,
        compiler_params=pltpu.CompilerParams(vmem_limit_bytes=16 * 1024 * 1024),
        cost_estimate=pl.CostEstimate(flops=flops, bytes_accessed=1 << 18, transcendentals=0),
    )


def along_line(pieces, slots):
    sent = []
    for step, piece in zip(STEPS, pieces):
        pairs = [(slot, slot ^ (step * LINES)) for slot in range(slots)]
        sent.append(lax.ppermute(piece, "sec", pairs) if step else piece)
    return sent


def other_core(block):
    return lax.ppermute(block, "env", [(0, 1), (1, 0)])


def across(piece, slots):
    return lax.ppermute(piece, "sec", [(slot, slot ^ 1) for slot in range(slots)])


def on_device(amplitudes, widths, holders, left_env, right_env):
    slots_dev, right_dim, half = amplitudes.shape
    slots = holders.shape[0]
    assert slots_dev == 1
    if slots != 2 * QDOWN:
        return on_device_any(amplitudes, widths, holders, left_env, right_env)
    places = slots // LINES
    rows = right_dim // places
    dots = 6 * right_dim * half * (right_dim + 2 * half)
    block = jax.ShapeDtypeStruct((right_dim, half), jnp.bfloat16)
    wide = jax.ShapeDtypeStruct((right_dim, half), jnp.float32)
    pair = jax.ShapeDtypeStruct((2, rows, half), jnp.bfloat16)
    single = jax.ShapeDtypeStruct((rows, half), jnp.bfloat16)
    singles = jax.ShapeDtypeStruct((places, rows, half), jnp.bfloat16)
    wides = jax.ShapeDtypeStruct((places, rows, half), jnp.float32)
    chunked = rows * half // LANES
    tagged = jax.ShapeDtypeStruct((2 * chunked + TAG, LANES), jnp.bfloat16)
    crossing = jax.ShapeDtypeStruct((places * chunked + TAG, LANES), jnp.bfloat16)
    label = jax.ShapeDtypeStruct((TAG, LANES), jnp.bfloat16)
    factor_shape = jax.ShapeDtypeStruct((8, LANES), jnp.float32)
    plan_shape = jax.ShapeDtypeStruct((8, LANES), jnp.int32)
    split = [pltpu.VMEM((places, rows, half), jnp.bfloat16)]
    tables = [pltpu.VMEM((places, *shape.shape), jnp.bfloat16) for shape in (pair, tagged)]

    slot_table = [pltpu.SMEM((slots,), jnp.int32)]
    plan = call(plan_kernel, [SMEM, SMEM], plan_shape, slot_table)(widths, holders)
    both = jax.ShapeDtypeStruct((2, right_dim, half), jnp.bfloat16)
    number = jax.ShapeDtypeStruct((8, half), jnp.int32)
    columns = call(columns_kernel, [], number, flops=4 << 30)()
    *pieces, stay, start_full = call(
        first_kernel, [VMEM] * 7, (pair,) * places + (block, both), split, dots
    )(
        columns,
        widths[None],
        holders[None],
        amplitudes[0],
        other_core(amplitudes[0]),
        right_env,
        left_env,
    )
    old = along_line(pieces, slots)
    old_keep, cross = call(
        merge_kernel, [VMEM] * (1 + places), (singles, singles), tables[:1]
    )(plan, *old)
    old_arrived = across(cross, slots)
    joined = call(join_kernel, [VMEM, VMEM], (single,) * places)(old_keep, old_arrived)
    first = call(sum_kernel, [VMEM] * (2 + places), block)(
        plan, stay, *along_line(joined, slots)
    )

    *pieces, stay_2 = call(
        second_kernel, [VMEM] * 5, (tagged,) * places + (wide,), split, dots
    )(start_full, first, other_core(first), right_env, left_env)
    new = along_line(pieces, slots)
    keep, cross, tag = call(
        mix_kernel, [VMEM] * (1 + 2 * places), (wides, crossing, label), tables
    )(plan, *old, *new)
    *joined, factors = call(
        join_mixed_kernel, [VMEM] * 6, (single,) * places + (factor_shape,)
    )(plan, tag, keep, across(cross, slots), old_keep, old_arrived)
    second, first = call(final_kernel, [VMEM] * (5 + places), (block, block))(
        plan, factors, stay, stay_2, first, *along_line(joined, slots)
    )
    return first[None], second[None]


def solution(mesh):
    in_specs = (
        P(("runs", "sec"), None, "env"),
        P("runs"),
        P("runs"),
        P(("runs", "sec"), None, None, "env"),
        P("runs", None, None),
    )
    out_specs = (P(("runs", "sec"), None, "env"), P(("runs", "sec"), None, "env"))
    return jax.shard_map(
        on_device, mesh=mesh, in_specs=in_specs, out_specs=out_specs, check_vma=False
    )
```

```python
import jax
import jax.numpy as jnp
from jax import lax
from jax.experimental import pallas as pl
from jax.experimental.pallas import tpu as pltpu
from jax.sharding import PartitionSpec as P

QDOWN = 4

term_shifts = ((0, 0), (1, 0), (0, 1))


def route(holders):
    n_slots = holders.shape[0]
    sector_ids = jnp.arange(n_slots, dtype=jnp.int32)
    slot_of = jnp.argmax(holders[None, :] == sector_ids[:, None], axis=1)
    sources = []
    allowed = []
    for up, down in term_shifts[1:]:
        permitted = (holders // QDOWN - up >= 0) & (holders % QDOWN - down >= 0)
        wanted = jnp.clip(holders - QDOWN * up - down, 0, n_slots - 1)
        sources.append(slot_of[wanted])
        allowed.append(permitted)
    return sources, allowed


def contract(vector, left_env, right_env):
    products = jnp.einsum(
        "tij,jw->tiw", right_env, vector, preferred_element_type=jnp.float32
    ).astype(jnp.bfloat16)
    return jnp.einsum("tik,tkw->tiw", products, left_env, preferred_element_type=jnp.float32)


def spread(blocks, n_slots):
    terms, rows, width = blocks.shape
    pieces = blocks.reshape(terms, n_slots, rows // n_slots, width).swapaxes(0, 1)
    return lax.all_to_all(pieces, "sec", split_axis=0, concat_axis=0)


def collect(merged):
    n_slots, rows, width = merged.shape
    home = lax.all_to_all(merged, "sec", split_axis=0, concat_axis=0)
    return home.reshape(n_slots * rows, width)


def share(values, n_slots, me):
    lanes = jnp.zeros((1, 128), jnp.float32).at[0, : values.shape[0]].set(values)
    if n_slots & (n_slots - 1) or n_slots > 16:
        return lax.all_gather(lanes[0], "sec")
    table = jnp.where(jnp.arange(n_slots)[:, None] == me, lanes, 0.0)
    for offset in range(1, n_slots):
        pairs = [(i, i ^ offset) for i in range(n_slots)]
        other = lax.ppermute(lanes, "sec", pairs)
        table = jnp.where(jnp.arange(n_slots)[:, None] == (me ^ offset), other, table)
    return table


def merge(received, sources, allowed):
    total = 0.0
    for term, (source, permitted) in enumerate(zip(sources, allowed)):
        picked = received[source, term]
        total = total + jnp.where(permitted[:, None, None], picked, 0).astype(jnp.float32)
    return total


def on_device_any(amplitudes, widths, holders, left_env, right_env):
    slots_dev, right_dim, half_width = amplitudes.shape
    assert slots_dev == 1
    n_slots = holders.shape[0]
    me = lax.axis_index("sec")
    side = lax.axis_index("env")
    my_width = widths[holders[me]]
    row_index = side * half_width + jnp.arange(half_width, dtype=jnp.int32)
    live = (row_index < my_width)[None, :]
    sources, allowed = route(holders)
    envs = left_env[0]

    start = jnp.where(live, amplitudes[0], jnp.zeros_like(amplitudes[0]))
    start_full = lax.all_gather(start, "env", axis=1, tiled=True)
    outgoing = contract(start_full, envs, right_env).astype(jnp.bfloat16)
    stay = outgoing[0].astype(jnp.float32)
    received = spread(outgoing[1:], n_slots)
    arrived = collect(merge(received, sources, allowed).astype(jnp.bfloat16))
    first = jnp.where(live, stay + arrived.astype(jnp.float32), 0.0).astype(jnp.bfloat16)

    first_full = lax.all_gather(first, "env", axis=1, tiled=True).astype(jnp.float32)
    basis = start_full.astype(jnp.float32)
    overlap = jnp.sum(basis * first_full)
    norm = jnp.sum(basis * basis)
    own_quotient = jnp.where(norm > 0, overlap / jnp.where(norm > 0, norm, 1.0), 0.0)
    deflated = first_full - own_quotient * basis
    rest = jnp.sum(deflated * deflated)
    sums = share(jnp.stack([overlap, norm, own_quotient, rest]), n_slots, me)
    outgoing_2 = contract(deflated.astype(jnp.bfloat16), envs, right_env)
    received_2 = spread(outgoing_2[1:].astype(jnp.bfloat16), n_slots)

    quotient = jnp.sum(sums[:, 0]) / jnp.sum(sums[:, 1])
    shift = sums[:, 2] - quotient
    resid_norm = jnp.sum(sums[:, 3] + shift * shift * sums[:, 1])
    live_count = right_dim * jnp.sum(widths).astype(jnp.float32)
    scale = lax.rsqrt(resid_norm / live_count + 1e-06)
    mixed = received_2.astype(jnp.float32) + shift[:, None, None, None] * received.astype(
        jnp.float32
    )
    merged_2 = scale * merge(mixed, sources, allowed)
    arrived_2 = collect(merged_2.astype(jnp.bfloat16))
    stay_2 = scale * (outgoing_2[0] + (own_quotient - quotient) * stay)
    second = jnp.where(live, stay_2 + arrived_2.astype(jnp.float32), 0.0).astype(jnp.bfloat16)
    return first[None], second[None]


LANES = 128
TAG = 16
LINES = 2
STEPS = (0, 3, 2, 1)


def plan_kernel(widths, holders, plan, slot_of):
    slots = holders.shape[0]
    me = lax.axis_index("sec")
    total = jnp.int32(0)
    for s in range(slots):
        slot_of[holders[s]] = jnp.int32(s)
        total = total + widths[s]
    codes = [jnp.int32(0), jnp.int32(0)]
    for target in range(slots):
        sector = holders[target]
        has = (sector >= QDOWN, sector % QDOWN > 0)
        source = (slot_of[sector & (QDOWN - 1)], slot_of[jnp.maximum(sector - 1, 0)])
        for i in range(2):
            entry = jnp.where(has[i], source[i] + slots, 0)
            codes[i] = codes[i] | (entry << (target * 4))
    row = lax.broadcasted_iota(jnp.int32, plan.shape, 0)
    values = jnp.where(row == 0, widths[holders[me]], total)
    values = jnp.where(row == 2, codes[0], values)
    plan[...] = jnp.where(row == 3, codes[1], values)


def live_columns(plan, half):
    first_column = lax.axis_index("env") * half
    return first_column + lax.broadcasted_iota(jnp.int32, (1, half), 1) < plan[0:1, 0:1]


def apply_term(right, left, vector, term):
    products = jnp.dot(right[term], vector, preferred_element_type=jnp.float32)
    return jnp.dot(products.astype(jnp.bfloat16), left, preferred_element_type=jnp.float32)


def in_order(own, other):
    upper = lax.axis_index("env") > 0
    return [jnp.where(upper, other, own), jnp.where(upper, own, other)]


def own_place():
    return lax.axis_index("sec") // LINES


def columns_kernel(columns):
    columns[...] = lax.broadcasted_iota(jnp.int32, columns.shape, 1)


def first_kernel(columns, widths, holders, own, other, right, left, *rest):
    *pieces, start, block_vmem = rest
    half = start.shape[2]
    slot = lax.broadcasted_iota(jnp.int32, widths.shape, 1)
    mine = jnp.where(slot == lax.axis_index("sec"), holders[...], 0)
    sector = jnp.sum(mine, axis=1, keepdims=True)
    width = jnp.sum(jnp.where(slot == sector, widths[...], 0), axis=1, keepdims=True)
    for h, part in enumerate(in_order(own[...], other[...])):
        live = h * half + columns[0:1, :] < width
        start[h] = jnp.where(live, part, jnp.zeros_like(part))
    vector = jnp.concatenate([start[0], start[1]], axis=1)
    for term in (1, 2):
        block = apply_term(right, left[0, term], vector, term).astype(jnp.bfloat16)
        block_vmem[...] = block.reshape(block_vmem.shape)
        for step, piece in zip(STEPS, pieces):
            piece[term - 1] = block_vmem[own_place() ^ step]


def stay_kernel(vector, right, left, stay):
    block = apply_term(right, left[0, 0], jnp.concatenate([vector[0], vector[1]], axis=1), 0)
    stay[...] = block.astype(stay.dtype)


def line_targets(plan, places):
    line = lax.axis_index("sec") % LINES
    codes = [jnp.max(plan[2 + i : 3 + i, :]) for i in range(2)]
    for place in range(places):
        for crossing in range(2):
            target = place * LINES + (line ^ crossing)
            entries = [(code >> (target * 4)) & (2 * LINES * places - 1) for code in codes]
            source = [entry & (LINES * places - 1) for entry in entries]
            here = [
                (entry >= LINES * places) & (slot % LINES == line)
                for entry, slot in zip(entries, source)
            ]
            yield place, crossing, here, source


def merge_kernel(plan, *rest):
    *pieces, keep, cross, table = rest
    for step, piece in zip(STEPS, pieces):
        table[own_place() ^ step] = piece[...]
    for place, crossing, here, source in line_targets(plan, keep.shape[0]):
        total = 0.0
        for i in range(2):
            block = table[source[i] // LINES, i].astype(jnp.float32)
            total = total + jnp.where(here[i], block, 0.0)
        (keep, cross)[crossing][place] = total.astype(jnp.bfloat16)


def join_kernel(keep, arrived, *outs):
    for step, out in zip(STEPS, outs):
        place = own_place() ^ step
        total = keep[place].astype(jnp.float32) + arrived[place].astype(jnp.float32)
        out[...] = total.astype(jnp.bfloat16)


def piece_rows(step, rows):
    return pl.ds(pl.multiple_of((own_place() ^ step) * rows, rows), rows)


def sum_kernel(plan, stay, *rest):
    *pieces, first = rest
    live = live_columns(plan, stay.shape[1])
    for step, piece in zip(STEPS, pieces):
        place = piece_rows(step, piece.shape[0])
        total = stay[place, :].astype(jnp.float32) + piece[...].astype(jnp.float32)
        first[place, :] = jnp.where(live, total, 0.0).astype(jnp.bfloat16)


def total_of(array):
    return jnp.sum(jnp.sum(array, axis=0, keepdims=True), axis=1, keepdims=True)


def make_tag(values, me):
    row = lax.broadcasted_iota(jnp.int32, (TAG, LANES), 0)
    lane = lax.broadcasted_iota(jnp.int32, (TAG, LANES), 1)
    spread = jnp.zeros((TAG, LANES), jnp.float32)
    for place, value in enumerate(values):
        spread = jnp.where(row // 3 == place, value, spread)
    high = spread.astype(jnp.bfloat16).astype(jnp.float32)
    middle = (spread - high).astype(jnp.bfloat16).astype(jnp.float32)
    low = spread - high - middle
    parts = jnp.where(row % 3 == 0, high, jnp.where(row % 3 == 1, middle, low))
    return jnp.where((lane == me) & (row < 3 * len(values)), parts, 0.0).astype(jnp.bfloat16)


def second_kernel(start, own, other, right, left, *rest):
    *pieces, deflated_out, block_vmem = rest
    half = start.shape[2]
    rows = block_vmem.shape[1]
    chunks = half // LANES
    basis = [start[h].astype(jnp.float32) for h in range(2)]
    firsts = [part.astype(jnp.float32) for part in in_order(own[...], other[...])]
    overlap = total_of(basis[0] * firsts[0]) + total_of(basis[1] * firsts[1])
    norm = total_of(basis[0] * basis[0]) + total_of(basis[1] * basis[1])
    quotient = jnp.where(norm > 0, overlap / jnp.where(norm > 0, norm, 1.0), 0.0)
    deflated = [firsts[h] - quotient * basis[h] for h in range(2)]
    rest_norm = total_of(deflated[0] * deflated[0]) + total_of(deflated[1] * deflated[1])
    for h in range(2):
        deflated_out[h] = deflated[h].astype(jnp.bfloat16)
    vector = jnp.concatenate(deflated, axis=1).astype(jnp.bfloat16)
    tag = make_tag((overlap, norm, quotient, rest_norm), lax.axis_index("sec"))
    for piece in pieces:
        piece[pl.ds(2 * chunks * rows, TAG), :] = tag
    for term in (1, 2):
        block = apply_term(right, left[0, term], vector, term)
        block_vmem[...] = block.astype(jnp.bfloat16).reshape(block_vmem.shape)
        for step, piece in zip(STEPS, pieces):
            part = block_vmem[own_place() ^ step]
            for c in range(chunks):
                place = pl.ds(((term - 1) * chunks + c) * rows, rows)
                piece[place, :] = part[:, c * LANES : (c + 1) * LANES]


def read_tag(tag):
    def value(place):
        parts = [tag[3 * place + i : 3 * place + i + 1, :] for i in range(3)]
        return parts[0] + parts[1] + parts[2]

    return [value(place) for place in range(4)]


def line_quotient(overlaps, norms, line):
    inside = lax.broadcasted_iota(jnp.int32, (1, LANES), 1) % LINES == line
    overlap = total_of(jnp.where(inside, overlaps, 0.0))
    norm = total_of(jnp.where(inside, norms, 0.0))
    return jnp.where(norm > 0, overlap / jnp.where(norm > 0, norm, 1.0), 0.0)


def mix_kernel(plan, *rest):
    keep, cross, tag_out, old, new = rest[-5:]
    places, rows, half = keep.shape
    chunks = half // LANES
    tag = jnp.zeros((TAG, LANES), jnp.float32)
    for i, step in enumerate(STEPS):
        old[own_place() ^ step] = rest[i][...]
        new[own_place() ^ step] = rest[places + i][...]
        label = rest[places + i][pl.ds(2 * chunks * rows, TAG), :]
        tag = tag + label.astype(jnp.float32)
    tag_out[...] = tag.astype(jnp.bfloat16)
    cross[pl.ds(places * chunks * rows, TAG), :] = tag.astype(jnp.bfloat16)
    overlaps, norms, quotients, _ = read_tag(tag)
    shifts = quotients - line_quotient(overlaps, norms, lax.axis_index("sec") % LINES)
    lane = lax.broadcasted_iota(jnp.int32, (1, LANES), 1)
    for place, crossing, here, source in line_targets(plan, keep.shape[0]):
        total = 0.0
        for i in range(2):
            where = source[i] // LINES
            block = jnp.concatenate(
                [new[where, pl.ds((i * chunks + c) * rows, rows), :] for c in range(chunks)],
                axis=1,
            ).astype(jnp.float32)
            shift = total_of(jnp.where(lane == source[i], shifts, 0.0))
            block = block + shift * old[where, i].astype(jnp.float32)
            total = total + jnp.where(here[i], block, 0.0)
        if crossing:
            total = total.astype(jnp.bfloat16)
            for c in range(chunks):
                target = pl.ds((place * chunks + c) * rows, rows)
                cross[target, :] = total[:, c * LANES : (c + 1) * LANES]
        else:
            keep[place] = total


def join_mixed_kernel(plan, tag_line, keep, arrived, old_keep, old_arrived, *rest):
    *outs, factors = rest
    places, rows, half = keep.shape
    chunks = half // LANES
    slots = places * LINES
    me = lax.axis_index("sec")
    live_count = places * rows * plan[1:2, 0:1].astype(jnp.float32)
    tag = tag_line[...].astype(jnp.float32)
    tag = tag + arrived[pl.ds(places * chunks * rows, TAG), :].astype(jnp.float32)
    overlaps, norms, quotients, rests = read_tag(tag)
    quotient = total_of(overlaps) / total_of(norms)
    lane = lax.broadcasted_iota(jnp.int32, (1, LANES), 1)
    shifts = jnp.where(lane < slots, quotients - quotient, 0.0)
    resid_norm = total_of(rests + shifts * shifts * norms)
    scale = lax.rsqrt(resid_norm / live_count + 1e-06)
    row = lax.broadcasted_iota(jnp.int32, factors.shape, 0)
    own_shift = total_of(jnp.where(lane == me, shifts, 0.0))
    factors[...] = jnp.where(row == 0, scale, scale * own_shift)
    line = me % LINES
    shift_here = line_quotient(overlaps, norms, line) - quotient
    shift_there = line_quotient(overlaps, norms, 1 - line) - quotient
    for step, out in zip(STEPS, outs):
        place = own_place() ^ step
        starts = [pl.multiple_of((place * chunks + c) * rows, rows) for c in range(chunks)]
        block = jnp.concatenate(
            [arrived[pl.ds(start, rows), :] for start in starts], axis=1
        ).astype(jnp.float32)
        block = block + shift_there * old_arrived[place].astype(jnp.float32)
        block = block + keep[place] + shift_here * old_keep[place].astype(jnp.float32)
        out[...] = (scale * block).astype(jnp.bfloat16)


def final_kernel(plan, factors, stay, stay_2, first, *rest):
    *pieces, second, first_out = rest
    first_out[...] = first[...]
    live = live_columns(plan, stay.shape[1])
    scale, shift = factors[0:1, 0:1], factors[1:2, 0:1]
    for step, piece in zip(STEPS, pieces):
        place = piece_rows(step, piece.shape[0])
        total = scale * stay_2[place, :] + shift * stay[place, :].astype(jnp.float32)
        total = total + piece[...].astype(jnp.float32)
        second[place, :] = jnp.where(live, total, 0.0).astype(jnp.bfloat16)


SMEM = pl.BlockSpec(memory_space=pltpu.SMEM)
VMEM = pl.BlockSpec(memory_space=pltpu.VMEM)


def call(kernel, specs, outs, scratch=(), flops=0):
    return pl.pallas_call(
        kernel,
        out_shape=outs,
        in_specs=specs,
        out_specs=jax.tree.map(lambda _: VMEM, outs),
        scratch_shapes=scratch,
        compiler_params=pltpu.CompilerParams(vmem_limit_bytes=16 * 1024 * 1024),
        cost_estimate=pl.CostEstimate(flops=flops, bytes_accessed=1 << 18, transcendentals=0),
    )


def along_line(pieces, slots):
    sent = []
    for step, piece in zip(STEPS, pieces):
        pairs = [(slot, slot ^ (step * LINES)) for slot in range(slots)]
        sent.append(lax.ppermute(piece, "sec", pairs) if step else piece)
    return sent


def other_core(block):
    return lax.ppermute(block, "env", [(0, 1), (1, 0)])


def across(piece, slots):
    return lax.ppermute(piece, "sec", [(slot, slot ^ 1) for slot in range(slots)])


def on_device(amplitudes, widths, holders, left_env, right_env):
    slots_dev, right_dim, half = amplitudes.shape
    slots = holders.shape[0]
    assert slots_dev == 1
    if slots != 2 * QDOWN:
        return on_device_any(amplitudes, widths, holders, left_env, right_env)
    places = slots // LINES
    rows = right_dim // places
    dots = 6 * right_dim * half * (right_dim + 2 * half)
    block = jax.ShapeDtypeStruct((right_dim, half), jnp.bfloat16)
    wide = jax.ShapeDtypeStruct((right_dim, half), jnp.float32)
    pair = jax.ShapeDtypeStruct((2, rows, half), jnp.bfloat16)
    single = jax.ShapeDtypeStruct((rows, half), jnp.bfloat16)
    singles = jax.ShapeDtypeStruct((places, rows, half), jnp.bfloat16)
    wides = jax.ShapeDtypeStruct((places, rows, half), jnp.float32)
    chunked = rows * half // LANES
    tagged = jax.ShapeDtypeStruct((2 * chunked + TAG, LANES), jnp.bfloat16)
    crossing = jax.ShapeDtypeStruct((places * chunked + TAG, LANES), jnp.bfloat16)
    label = jax.ShapeDtypeStruct((TAG, LANES), jnp.bfloat16)
    factor_shape = jax.ShapeDtypeStruct((8, LANES), jnp.float32)
    plan_shape = jax.ShapeDtypeStruct((8, LANES), jnp.int32)
    split = [pltpu.VMEM((places, rows, half), jnp.bfloat16)]
    tables = [pltpu.VMEM((places, *shape.shape), jnp.bfloat16) for shape in (pair, tagged)]

    slot_table = [pltpu.SMEM((slots,), jnp.int32)]
    plan = call(plan_kernel, [SMEM, SMEM], plan_shape, slot_table)(widths, holders)
    both = jax.ShapeDtypeStruct((2, right_dim, half), jnp.bfloat16)
    number = jax.ShapeDtypeStruct((8, half), jnp.int32)
    columns = call(columns_kernel, [], number, flops=4 << 30)()
    *pieces, start_full = call(
        first_kernel, [VMEM] * 7, (pair,) * places + (both,), split, dots
    )(
        columns,
        widths[None],
        holders[None],
        amplitudes[0],
        other_core(amplitudes[0]),
        right_env,
        left_env,
    )
    old = along_line(pieces, slots)
    stay = call(stay_kernel, [VMEM] * 3, block, flops=dots // 3)(start_full, right_env, left_env)
    old_keep, cross = call(
        merge_kernel, [VMEM] * (1 + places), (singles, singles), tables[:1]
    )(plan, *old)
    old_arrived = across(cross, slots)
    joined = call(join_kernel, [VMEM, VMEM], (single,) * places)(old_keep, old_arrived)
    first = call(sum_kernel, [VMEM] * (2 + places), block)(
        plan, stay, *along_line(joined, slots)
    )

    *pieces, deflated = call(
        second_kernel, [VMEM] * 5, (tagged,) * places + (both,), split, dots
    )(start_full, first, other_core(first), right_env, left_env)
    new = along_line(pieces, slots)
    stay_2 = call(stay_kernel, [VMEM] * 3, wide, flops=dots // 3)(deflated, right_env, left_env)
    keep, cross, tag = call(
        mix_kernel, [VMEM] * (1 + 2 * places), (wides, crossing, label), tables
    )(plan, *old, *new)
    *joined, factors = call(
        join_mixed_kernel, [VMEM] * 6, (single,) * places + (factor_shape,)
    )(plan, tag, keep, across(cross, slots), old_keep, old_arrived)
    second, first = call(final_kernel, [VMEM] * (5 + places), (block, block))(
        plan, factors, stay, stay_2, first, *along_line(joined, slots)
    )
    return first[None], second[None]


def solution(mesh):
    in_specs = (
        P(("runs", "sec"), None, "env"),
        P("runs"),
        P("runs"),
        P(("runs", "sec"), None, None, "env"),
        P("runs", None, None),
    )
    out_specs = (P(("runs", "sec"), None, "env"), P(("runs", "sec"), None, "env"))
    return jax.shard_map(
        on_device, mesh=mesh, in_specs=in_specs, out_specs=out_specs, check_vma=False
    )
```

```python
import jax
import jax.numpy as jnp
from jax import lax
from jax.experimental import pallas as pl
from jax.experimental.pallas import tpu as pltpu
from jax.sharding import PartitionSpec as P

QDOWN = 4

term_shifts = ((0, 0), (1, 0), (0, 1))


def route(holders):
    n_slots = holders.shape[0]
    sector_ids = jnp.arange(n_slots, dtype=jnp.int32)
    slot_of = jnp.argmax(holders[None, :] == sector_ids[:, None], axis=1)
    sources = []
    allowed = []
    for up, down in term_shifts[1:]:
        permitted = (holders // QDOWN - up >= 0) & (holders % QDOWN - down >= 0)
        wanted = jnp.clip(holders - QDOWN * up - down, 0, n_slots - 1)
        sources.append(slot_of[wanted])
        allowed.append(permitted)
    return sources, allowed


def contract(vector, left_env, right_env):
    products = jnp.einsum(
        "tij,jw->tiw", right_env, vector, preferred_element_type=jnp.float32
    ).astype(jnp.bfloat16)
    return jnp.einsum("tik,tkw->tiw", products, left_env, preferred_element_type=jnp.float32)


def spread(blocks, n_slots):
    terms, rows, width = blocks.shape
    pieces = blocks.reshape(terms, n_slots, rows // n_slots, width).swapaxes(0, 1)
    return lax.all_to_all(pieces, "sec", split_axis=0, concat_axis=0)


def collect(merged):
    n_slots, rows, width = merged.shape
    home = lax.all_to_all(merged, "sec", split_axis=0, concat_axis=0)
    return home.reshape(n_slots * rows, width)


def share(values, n_slots, me):
    lanes = jnp.zeros((1, 128), jnp.float32).at[0, : values.shape[0]].set(values)
    if n_slots & (n_slots - 1) or n_slots > 16:
        return lax.all_gather(lanes[0], "sec")
    table = jnp.where(jnp.arange(n_slots)[:, None] == me, lanes, 0.0)
    for offset in range(1, n_slots):
        pairs = [(i, i ^ offset) for i in range(n_slots)]
        other = lax.ppermute(lanes, "sec", pairs)
        table = jnp.where(jnp.arange(n_slots)[:, None] == (me ^ offset), other, table)
    return table


def merge(received, sources, allowed):
    total = 0.0
    for term, (source, permitted) in enumerate(zip(sources, allowed)):
        picked = received[source, term]
        total = total + jnp.where(permitted[:, None, None], picked, 0).astype(jnp.float32)
    return total


def on_device_any(amplitudes, widths, holders, left_env, right_env):
    slots_dev, right_dim, half_width = amplitudes.shape
    assert slots_dev == 1
    n_slots = holders.shape[0]
    me = lax.axis_index("sec")
    side = lax.axis_index("env")
    my_width = widths[holders[me]]
    row_index = side * half_width + jnp.arange(half_width, dtype=jnp.int32)
    live = (row_index < my_width)[None, :]
    sources, allowed = route(holders)
    envs = left_env[0]

    start = jnp.where(live, amplitudes[0], jnp.zeros_like(amplitudes[0]))
    start_full = lax.all_gather(start, "env", axis=1, tiled=True)
    outgoing = contract(start_full, envs, right_env).astype(jnp.bfloat16)
    stay = outgoing[0].astype(jnp.float32)
    received = spread(outgoing[1:], n_slots)
    arrived = collect(merge(received, sources, allowed).astype(jnp.bfloat16))
    first = jnp.where(live, stay + arrived.astype(jnp.float32), 0.0).astype(jnp.bfloat16)

    first_full = lax.all_gather(first, "env", axis=1, tiled=True).astype(jnp.float32)
    basis = start_full.astype(jnp.float32)
    overlap = jnp.sum(basis * first_full)
    norm = jnp.sum(basis * basis)
    own_quotient = jnp.where(norm > 0, overlap / jnp.where(norm > 0, norm, 1.0), 0.0)
    deflated = first_full - own_quotient * basis
    rest = jnp.sum(deflated * deflated)
    sums = share(jnp.stack([overlap, norm, own_quotient, rest]), n_slots, me)
    outgoing_2 = contract(deflated.astype(jnp.bfloat16), envs, right_env)
    received_2 = spread(outgoing_2[1:].astype(jnp.bfloat16), n_slots)

    quotient = jnp.sum(sums[:, 0]) / jnp.sum(sums[:, 1])
    shift = sums[:, 2] - quotient
    resid_norm = jnp.sum(sums[:, 3] + shift * shift * sums[:, 1])
    live_count = right_dim * jnp.sum(widths).astype(jnp.float32)
    scale = lax.rsqrt(resid_norm / live_count + 1e-06)
    mixed = received_2.astype(jnp.float32) + shift[:, None, None, None] * received.astype(
        jnp.float32
    )
    merged_2 = scale * merge(mixed, sources, allowed)
    arrived_2 = collect(merged_2.astype(jnp.bfloat16))
    stay_2 = scale * (outgoing_2[0] + (own_quotient - quotient) * stay)
    second = jnp.where(live, stay_2 + arrived_2.astype(jnp.float32), 0.0).astype(jnp.bfloat16)
    return first[None], second[None]


LANES = 128
TAG = 16
LINES = 2
STEPS = (0, 3, 2, 1)
EARLY, LATE = (1, 2), (0, 3)


def plan_kernel(widths, holders, plan, slot_of):
    slots = holders.shape[0]
    me = lax.axis_index("sec")
    total = jnp.int32(0)
    for s in range(slots):
        slot_of[holders[s]] = jnp.int32(s)
        total = total + widths[s]
    codes = [jnp.int32(0), jnp.int32(0)]
    for target in range(slots):
        sector = holders[target]
        has = (sector >= QDOWN, sector % QDOWN > 0)
        source = (slot_of[sector & (QDOWN - 1)], slot_of[jnp.maximum(sector - 1, 0)])
        for i in range(2):
            entry = jnp.where(has[i], source[i] + slots, 0)
            codes[i] = codes[i] | (entry << (target * 4))
    row = lax.broadcasted_iota(jnp.int32, plan.shape, 0)
    values = jnp.where(row == 0, widths[holders[me]], total)
    values = jnp.where(row == 2, codes[0], values)
    plan[...] = jnp.where(row == 3, codes[1], values)


def live_columns(plan, half):
    first_column = lax.axis_index("env") * half
    return first_column + lax.broadcasted_iota(jnp.int32, (1, half), 1) < plan[0:1, 0:1]


def apply_term(right, left, vector, term):
    products = jnp.dot(right[term], vector, preferred_element_type=jnp.float32)
    return jnp.dot(products.astype(jnp.bfloat16), left, preferred_element_type=jnp.float32)


def in_order(own, other):
    upper = lax.axis_index("env") > 0
    return [jnp.where(upper, other, own), jnp.where(upper, own, other)]


def own_place():
    return lax.axis_index("sec") // LINES


def columns_kernel(columns):
    columns[...] = lax.broadcasted_iota(jnp.int32, columns.shape, 1)


def first_kernel(columns, widths, holders, own, other, right, left, *rest):
    *pieces, start, block_vmem = rest
    half = start.shape[2]
    slot = lax.broadcasted_iota(jnp.int32, widths.shape, 1)
    mine = jnp.where(slot == lax.axis_index("sec"), holders[...], 0)
    sector = jnp.sum(mine, axis=1, keepdims=True)
    width = jnp.sum(jnp.where(slot == sector, widths[...], 0), axis=1, keepdims=True)
    for h, part in enumerate(in_order(own[...], other[...])):
        live = h * half + columns[0:1, :] < width
        start[h] = jnp.where(live, part, jnp.zeros_like(part))
    vector = jnp.concatenate([start[0], start[1]], axis=1)
    for term in (1, 2):
        block = apply_term(right, left[0, term], vector, term).astype(jnp.bfloat16)
        block_vmem[...] = block.reshape(block_vmem.shape)
        for step, piece in zip(STEPS, pieces):
            piece[term - 1] = block_vmem[own_place() ^ step]


def stay_kernel(vector, right, left, stay):
    block = apply_term(right, left[0, 0], jnp.concatenate([vector[0], vector[1]], axis=1), 0)
    stay[...] = block.astype(stay.dtype)


def line_targets(plan, part):
    line = lax.axis_index("sec") % LINES
    places = len(STEPS)
    codes = [jnp.max(plan[2 + i : 3 + i, :]) for i in range(2)]
    for index in part:
        for crossing in range(2):
            target = (own_place() ^ STEPS[index]) * LINES + (line ^ crossing)
            entries = [(code >> (target * 4)) & (2 * LINES * places - 1) for code in codes]
            source = [entry & (LINES * places - 1) for entry in entries]
            here = [
                (entry >= LINES * places) & (slot % LINES == line)
                for entry, slot in zip(entries, source)
            ]
            yield index, crossing, here, source


def merge_targets(plan, part, table, keep, cross):
    for index, crossing, here, source in line_targets(plan, part):
        total = 0.0
        for i in range(2):
            block = table[source[i] // LINES, i].astype(jnp.float32)
            total = total + jnp.where(here[i], block, 0.0)
        (keep, cross)[crossing][part.index(index)] = total.astype(jnp.bfloat16)


def merge_early_kernel(plan, *rest):
    *pieces, table, keep, cross = rest
    for step, piece in zip(STEPS, pieces):
        table[own_place() ^ step] = piece[...]
    merge_targets(plan, EARLY, table, keep, cross)


def merge_late_kernel(plan, table, keep, cross):
    merge_targets(plan, LATE, table, keep, cross)


def join_kernel(keep, arrived, *outs):
    for i, out in enumerate(outs):
        total = keep[i].astype(jnp.float32) + arrived[i].astype(jnp.float32)
        out[...] = total.astype(jnp.bfloat16)


def piece_rows(step, rows):
    return pl.ds(pl.multiple_of((own_place() ^ step) * rows, rows), rows)


def sum_kernel(plan, stay, *rest):
    *pieces, first = rest
    live = live_columns(plan, stay.shape[1])
    for step, piece in zip(STEPS, pieces):
        place = piece_rows(step, piece.shape[0])
        total = stay[place, :].astype(jnp.float32) + piece[...].astype(jnp.float32)
        first[place, :] = jnp.where(live, total, 0.0).astype(jnp.bfloat16)


def total_of(array):
    return jnp.sum(jnp.sum(array, axis=0, keepdims=True), axis=1, keepdims=True)


def make_tag(values, me):
    row = lax.broadcasted_iota(jnp.int32, (TAG, LANES), 0)
    lane = lax.broadcasted_iota(jnp.int32, (TAG, LANES), 1)
    spread = jnp.zeros((TAG, LANES), jnp.float32)
    for place, value in enumerate(values):
        spread = jnp.where(row // 3 == place, value, spread)
    high = spread.astype(jnp.bfloat16).astype(jnp.float32)
    middle = (spread - high).astype(jnp.bfloat16).astype(jnp.float32)
    low = spread - high - middle
    parts = jnp.where(row % 3 == 0, high, jnp.where(row % 3 == 1, middle, low))
    return jnp.where((lane == me) & (row < 3 * len(values)), parts, 0.0).astype(jnp.bfloat16)


def second_kernel(start, own, other, right, left, *rest):
    *pieces, deflated_out, block_vmem = rest
    half = start.shape[2]
    rows = block_vmem.shape[1]
    chunks = half // LANES
    basis = [start[h].astype(jnp.float32) for h in range(2)]
    firsts = [part.astype(jnp.float32) for part in in_order(own[...], other[...])]
    overlap = total_of(basis[0] * firsts[0]) + total_of(basis[1] * firsts[1])
    norm = total_of(basis[0] * basis[0]) + total_of(basis[1] * basis[1])
    quotient = jnp.where(norm > 0, overlap / jnp.where(norm > 0, norm, 1.0), 0.0)
    deflated = [firsts[h] - quotient * basis[h] for h in range(2)]
    rest_norm = total_of(deflated[0] * deflated[0]) + total_of(deflated[1] * deflated[1])
    for h in range(2):
        deflated_out[h] = deflated[h].astype(jnp.bfloat16)
    vector = jnp.concatenate(deflated, axis=1).astype(jnp.bfloat16)
    tag = make_tag((overlap, norm, quotient, rest_norm), lax.axis_index("sec"))
    for piece in pieces:
        piece[pl.ds(2 * chunks * rows, TAG), :] = tag
    for term in (1, 2):
        block = apply_term(right, left[0, term], vector, term)
        block_vmem[...] = block.astype(jnp.bfloat16).reshape(block_vmem.shape)
        for step, piece in zip(STEPS, pieces):
            part = block_vmem[own_place() ^ step]
            for c in range(chunks):
                place = pl.ds(((term - 1) * chunks + c) * rows, rows)
                piece[place, :] = part[:, c * LANES : (c + 1) * LANES]


def read_tag(tag):
    def value(place):
        parts = [tag[3 * place + i : 3 * place + i + 1, :] for i in range(3)]
        return parts[0] + parts[1] + parts[2]

    return [value(place) for place in range(4)]


def line_quotient(overlaps, norms, line):
    inside = lax.broadcasted_iota(jnp.int32, (1, LANES), 1) % LINES == line
    overlap = total_of(jnp.where(inside, overlaps, 0.0))
    norm = total_of(jnp.where(inside, norms, 0.0))
    return jnp.where(norm > 0, overlap / jnp.where(norm > 0, norm, 1.0), 0.0)


def mix_kernel(plan, *rest):
    keep, early, late, tag_out, new = rest[-5:]
    old, *pieces = rest[:-5]
    places, rows, half = keep.shape
    chunks = half // LANES
    tag = jnp.zeros((TAG, LANES), jnp.float32)
    for step, piece in zip(STEPS, pieces):
        new[own_place() ^ step] = piece[...]
        label = piece[pl.ds(2 * chunks * rows, TAG), :]
        tag = tag + label.astype(jnp.float32)
    tag_out[...] = tag.astype(jnp.bfloat16)
    early[pl.ds(len(EARLY) * chunks * rows, TAG), :] = tag.astype(jnp.bfloat16)
    overlaps, norms, quotients, _ = read_tag(tag)
    shifts = quotients - line_quotient(overlaps, norms, lax.axis_index("sec") % LINES)
    lane = lax.broadcasted_iota(jnp.int32, (1, LANES), 1)
    for index, crossing, here, source in line_targets(plan, range(places)):
        total = 0.0
        for i in range(2):
            where = source[i] // LINES
            block = jnp.concatenate(
                [new[where, pl.ds((i * chunks + c) * rows, rows), :] for c in range(chunks)],
                axis=1,
            ).astype(jnp.float32)
            shift = total_of(jnp.where(lane == source[i], shifts, 0.0))
            block = block + shift * old[where, i].astype(jnp.float32)
            total = total + jnp.where(here[i], block, 0.0)
        if crossing:
            total = total.astype(jnp.bfloat16)
            out, part = (early, EARLY) if index in EARLY else (late, LATE)
            for c in range(chunks):
                target = pl.ds((part.index(index) * chunks + c) * rows, rows)
                out[target, :] = total[:, c * LANES : (c + 1) * LANES]
        else:
            keep[index] = total


def join_early_kernel(plan, tag_line, keep, arrived, old_keep, old_arrived, *rest):
    *outs, factors = rest
    places, rows, half = keep.shape
    slots = places * LINES
    me = lax.axis_index("sec")
    live_count = places * rows * plan[1:2, 0:1].astype(jnp.float32)
    tag = tag_line[...].astype(jnp.float32)
    tag = tag + arrived[pl.ds(arrived.shape[0] - TAG, TAG), :].astype(jnp.float32)
    overlaps, norms, quotients, rests = read_tag(tag)
    quotient = total_of(overlaps) / total_of(norms)
    lane = lax.broadcasted_iota(jnp.int32, (1, LANES), 1)
    shifts = jnp.where(lane < slots, quotients - quotient, 0.0)
    resid_norm = total_of(rests + shifts * shifts * norms)
    scale = lax.rsqrt(resid_norm / live_count + 1e-06)
    own_shift = total_of(jnp.where(lane == me, shifts, 0.0))
    line = me % LINES
    shift_here = line_quotient(overlaps, norms, line) - quotient
    shift_there = line_quotient(overlaps, norms, 1 - line) - quotient
    row = lax.broadcasted_iota(jnp.int32, factors.shape, 0)
    values = jnp.where(row == 0, scale, scale * own_shift)
    values = jnp.where(row == 2, shift_here, values)
    factors[...] = jnp.where(row == 3, shift_there, values)
    weights = (scale, shift_here, shift_there)
    join_mixed(EARLY, weights, keep, arrived, old_keep, old_arrived, outs)


def join_late_kernel(factors, keep, arrived, old_keep, old_arrived, *outs):
    weights = [factors[i : i + 1, 0:1] for i in (0, 2, 3)]
    join_mixed(LATE, weights, keep, arrived, old_keep, old_arrived, outs)


def join_mixed(part, weights, keep, arrived, old_keep, old_arrived, outs):
    scale, shift_here, shift_there = weights
    rows, half = outs[0].shape
    chunks = half // LANES
    for i, index in enumerate(part):
        block = jnp.concatenate(
            [arrived[pl.ds((i * chunks + c) * rows, rows), :] for c in range(chunks)], axis=1
        ).astype(jnp.float32)
        block = block + shift_there * old_arrived[i].astype(jnp.float32)
        block = block + keep[index] + shift_here * old_keep[i].astype(jnp.float32)
        outs[i][...] = (scale * block).astype(jnp.bfloat16)


def final_kernel(plan, factors, stay, stay_2, first, *rest):
    *pieces, second, first_out = rest
    first_out[...] = first[...]
    live = live_columns(plan, stay.shape[1])
    scale, shift = factors[0:1, 0:1], factors[1:2, 0:1]
    for step, piece in zip(STEPS, pieces):
        place = piece_rows(step, piece.shape[0])
        total = scale * stay_2[place, :] + shift * stay[place, :].astype(jnp.float32)
        total = total + piece[...].astype(jnp.float32)
        second[place, :] = jnp.where(live, total, 0.0).astype(jnp.bfloat16)


SMEM = pl.BlockSpec(memory_space=pltpu.SMEM)
VMEM = pl.BlockSpec(memory_space=pltpu.VMEM)


def call(kernel, specs, outs, scratch=(), flops=0):
    return pl.pallas_call(
        kernel,
        out_shape=outs,
        in_specs=specs,
        out_specs=jax.tree.map(lambda _: VMEM, outs),
        scratch_shapes=scratch,
        compiler_params=pltpu.CompilerParams(vmem_limit_bytes=16 * 1024 * 1024),
        cost_estimate=pl.CostEstimate(flops=flops, bytes_accessed=1 << 18, transcendentals=0),
    )


def along_line(pieces, slots):
    sent = []
    for step, piece in zip(STEPS, pieces):
        pairs = [(slot, slot ^ (step * LINES)) for slot in range(slots)]
        sent.append(lax.ppermute(piece, "sec", pairs) if step else piece)
    return sent


def other_core(block):
    return lax.ppermute(block, "env", [(0, 1), (1, 0)])


def across(piece, slots):
    return lax.ppermute(piece, "sec", [(slot, slot ^ 1) for slot in range(slots)])


def on_device(amplitudes, widths, holders, left_env, right_env):
    slots_dev, right_dim, half = amplitudes.shape
    slots = holders.shape[0]
    assert slots_dev == 1
    if slots != 2 * QDOWN:
        return on_device_any(amplitudes, widths, holders, left_env, right_env)
    places = slots // LINES
    rows = right_dim // places
    dots = 6 * right_dim * half * (right_dim + 2 * half)
    block = jax.ShapeDtypeStruct((right_dim, half), jnp.bfloat16)
    wide = jax.ShapeDtypeStruct((right_dim, half), jnp.float32)
    pair = jax.ShapeDtypeStruct((2, rows, half), jnp.bfloat16)
    single = jax.ShapeDtypeStruct((rows, half), jnp.bfloat16)
    wides = jax.ShapeDtypeStruct((places, rows, half), jnp.float32)
    chunked = rows * half // LANES
    tagged = jax.ShapeDtypeStruct((2 * chunked + TAG, LANES), jnp.bfloat16)
    twos = jax.ShapeDtypeStruct((2, rows, half), jnp.bfloat16)
    early = jax.ShapeDtypeStruct((2 * chunked + TAG, LANES), jnp.bfloat16)
    late = jax.ShapeDtypeStruct((2 * chunked, LANES), jnp.bfloat16)
    label = jax.ShapeDtypeStruct((TAG, LANES), jnp.bfloat16)
    factor_shape = jax.ShapeDtypeStruct((8, LANES), jnp.float32)
    plan_shape = jax.ShapeDtypeStruct((8, LANES), jnp.int32)
    split = [pltpu.VMEM((places, rows, half), jnp.bfloat16)]
    table_shape = jax.ShapeDtypeStruct((places, *pair.shape), jnp.bfloat16)
    new_table = [pltpu.VMEM((places, *tagged.shape), jnp.bfloat16)]

    slot_table = [pltpu.SMEM((slots,), jnp.int32)]
    plan = call(plan_kernel, [SMEM, SMEM], plan_shape, slot_table)(widths, holders)
    both = jax.ShapeDtypeStruct((2, right_dim, half), jnp.bfloat16)
    number = jax.ShapeDtypeStruct((8, half), jnp.int32)
    columns = call(columns_kernel, [], number, flops=4 << 30)()
    *pieces, start_full = call(
        first_kernel, [VMEM] * 7, (pair,) * places + (both,), split, dots
    )(
        columns,
        widths[None],
        holders[None],
        amplitudes[0],
        other_core(amplitudes[0]),
        right_env,
        left_env,
    )
    old = along_line(pieces, slots)
    stay = call(stay_kernel, [VMEM] * 3, block, flops=dots // 3)(start_full, right_env, left_env)
    table, keep_early, cross = call(
        merge_early_kernel, [VMEM] * (1 + places), (table_shape, twos, twos)
    )(plan, *old)
    old_early = across(cross, slots)
    keep_late, cross = call(merge_late_kernel, [VMEM] * 2, (twos, twos))(plan, table)
    old_late = across(cross, slots)
    far = call(join_kernel, [VMEM] * 2, (single,) * 2)(keep_early, old_early)
    near = call(join_kernel, [VMEM] * 2, (single,) * 2)(keep_late, old_late)
    joined = (near[0], *far, near[1])
    first = call(sum_kernel, [VMEM] * (2 + places), block)(
        plan, stay, *along_line(joined, slots)
    )

    *pieces, deflated = call(
        second_kernel, [VMEM] * 5, (tagged,) * places + (both,), split, dots
    )(start_full, first, other_core(first), right_env, left_env)
    new = along_line(pieces, slots)
    stay_2 = call(stay_kernel, [VMEM] * 3, wide, flops=dots // 3)(deflated, right_env, left_env)
    keep, *cross, tag = call(
        mix_kernel, [VMEM] * (2 + places), (wides, early, late, label), new_table
    )(plan, table, *new)
    new_early, new_late = (across(piece, slots) for piece in cross)
    *far, factors = call(join_early_kernel, [VMEM] * 6, (single, single, factor_shape))(
        plan, tag, keep, new_early, keep_early, old_early
    )
    near = call(join_late_kernel, [VMEM] * 5, (single,) * 2)(
        factors, keep, new_late, keep_late, old_late
    )
    joined = (near[0], *far, near[1])
    second, first = call(final_kernel, [VMEM] * (5 + places), (block, block))(
        plan, factors, stay, stay_2, first, *along_line(joined, slots)
    )
    return first[None], second[None]


def solution(mesh):
    in_specs = (
        P(("runs", "sec"), None, "env"),
        P("runs"),
        P("runs"),
        P(("runs", "sec"), None, None, "env"),
        P("runs", None, None),
    )
    out_specs = (P(("runs", "sec"), None, "env"), P(("runs", "sec"), None, "env"))
    return jax.shard_map(
        on_device, mesh=mesh, in_specs=in_specs, out_specs=out_specs, check_vma=False
    )
```

```python
import jax
import jax.numpy as jnp
from jax import lax
from jax.experimental import pallas as pl
from jax.experimental.pallas import tpu as pltpu
from jax.sharding import PartitionSpec as P

QDOWN = 4

term_shifts = ((0, 0), (1, 0), (0, 1))


def route(holders):
    n_slots = holders.shape[0]
    sector_ids = jnp.arange(n_slots, dtype=jnp.int32)
    slot_of = jnp.argmax(holders[None, :] == sector_ids[:, None], axis=1)
    sources = []
    allowed = []
    for up, down in term_shifts[1:]:
        permitted = (holders // QDOWN - up >= 0) & (holders % QDOWN - down >= 0)
        wanted = jnp.clip(holders - QDOWN * up - down, 0, n_slots - 1)
        sources.append(slot_of[wanted])
        allowed.append(permitted)
    return sources, allowed


def contract(vector, left_env, right_env):
    products = jnp.einsum(
        "tij,jw->tiw", right_env, vector, preferred_element_type=jnp.float32
    ).astype(jnp.bfloat16)
    return jnp.einsum("tik,tkw->tiw", products, left_env, preferred_element_type=jnp.float32)


def spread(blocks, n_slots):
    terms, rows, width = blocks.shape
    pieces = blocks.reshape(terms, n_slots, rows // n_slots, width).swapaxes(0, 1)
    return lax.all_to_all(pieces, "sec", split_axis=0, concat_axis=0)


def collect(merged):
    n_slots, rows, width = merged.shape
    home = lax.all_to_all(merged, "sec", split_axis=0, concat_axis=0)
    return home.reshape(n_slots * rows, width)


def share(values, n_slots, me):
    lanes = jnp.zeros((1, 128), jnp.float32).at[0, : values.shape[0]].set(values)
    if n_slots & (n_slots - 1) or n_slots > 16:
        return lax.all_gather(lanes[0], "sec")
    table = jnp.where(jnp.arange(n_slots)[:, None] == me, lanes, 0.0)
    for offset in range(1, n_slots):
        pairs = [(i, i ^ offset) for i in range(n_slots)]
        other = lax.ppermute(lanes, "sec", pairs)
        table = jnp.where(jnp.arange(n_slots)[:, None] == (me ^ offset), other, table)
    return table


def merge(received, sources, allowed):
    total = 0.0
    for term, (source, permitted) in enumerate(zip(sources, allowed)):
        picked = received[source, term]
        total = total + jnp.where(permitted[:, None, None], picked, 0).astype(jnp.float32)
    return total


def on_device_any(amplitudes, widths, holders, left_env, right_env):
    slots_dev, right_dim, half_width = amplitudes.shape
    assert slots_dev == 1
    n_slots = holders.shape[0]
    me = lax.axis_index("sec")
    side = lax.axis_index("env")
    my_width = widths[holders[me]]
    row_index = side * half_width + jnp.arange(half_width, dtype=jnp.int32)
    live = (row_index < my_width)[None, :]
    sources, allowed = route(holders)
    envs = left_env[0]

    start = jnp.where(live, amplitudes[0], jnp.zeros_like(amplitudes[0]))
    start_full = lax.all_gather(start, "env", axis=1, tiled=True)
    outgoing = contract(start_full, envs, right_env).astype(jnp.bfloat16)
    stay = outgoing[0].astype(jnp.float32)
    received = spread(outgoing[1:], n_slots)
    arrived = collect(merge(received, sources, allowed).astype(jnp.bfloat16))
    first = jnp.where(live, stay + arrived.astype(jnp.float32), 0.0).astype(jnp.bfloat16)

    first_full = lax.all_gather(first, "env", axis=1, tiled=True).astype(jnp.float32)
    basis = start_full.astype(jnp.float32)
    overlap = jnp.sum(basis * first_full)
    norm = jnp.sum(basis * basis)
    own_quotient = jnp.where(norm > 0, overlap / jnp.where(norm > 0, norm, 1.0), 0.0)
    deflated = first_full - own_quotient * basis
    rest = jnp.sum(deflated * deflated)
    sums = share(jnp.stack([overlap, norm, own_quotient, rest]), n_slots, me)
    outgoing_2 = contract(deflated.astype(jnp.bfloat16), envs, right_env)
    received_2 = spread(outgoing_2[1:].astype(jnp.bfloat16), n_slots)

    quotient = jnp.sum(sums[:, 0]) / jnp.sum(sums[:, 1])
    shift = sums[:, 2] - quotient
    resid_norm = jnp.sum(sums[:, 3] + shift * shift * sums[:, 1])
    live_count = right_dim * jnp.sum(widths).astype(jnp.float32)
    scale = lax.rsqrt(resid_norm / live_count + 1e-06)
    mixed = received_2.astype(jnp.float32) + shift[:, None, None, None] * received.astype(
        jnp.float32
    )
    merged_2 = scale * merge(mixed, sources, allowed)
    arrived_2 = collect(merged_2.astype(jnp.bfloat16))
    stay_2 = scale * (outgoing_2[0] + (own_quotient - quotient) * stay)
    second = jnp.where(live, stay_2 + arrived_2.astype(jnp.float32), 0.0).astype(jnp.bfloat16)
    return first[None], second[None]


LANES = 128
TAG = 16
LINES = 2
STEPS = (0, 3, 1, 2)
EARLY, LATE = (1, 2), (0, 3)


def plan_kernel(widths, holders, plan, slot_of):
    slots = holders.shape[0]
    me = lax.axis_index("sec")
    total = jnp.int32(0)
    for s in range(slots):
        slot_of[holders[s]] = jnp.int32(s)
        total = total + widths[s]
    codes = [jnp.int32(0), jnp.int32(0)]
    for target in range(slots):
        sector = holders[target]
        has = (sector >= QDOWN, sector % QDOWN > 0)
        source = (slot_of[sector & (QDOWN - 1)], slot_of[jnp.maximum(sector - 1, 0)])
        for i in range(2):
            entry = jnp.where(has[i], source[i] + slots, 0)
            codes[i] = codes[i] | (entry << (target * 4))
    row = lax.broadcasted_iota(jnp.int32, plan.shape, 0)
    values = jnp.where(row == 0, widths[holders[me]], total)
    values = jnp.where(row == 2, codes[0], values)
    plan[...] = jnp.where(row == 3, codes[1], values)


def live_columns(plan, half):
    first_column = lax.axis_index("env") * half
    return first_column + lax.broadcasted_iota(jnp.int32, (1, half), 1) < plan[0:1, 0:1]


def apply_term(right, left, vector, term):
    products = jnp.dot(right[term], vector, preferred_element_type=jnp.float32)
    return jnp.dot(products.astype(jnp.bfloat16), left, preferred_element_type=jnp.float32)


def in_order(own, other):
    upper = lax.axis_index("env") > 0
    return [jnp.where(upper, other, own), jnp.where(upper, own, other)]


def own_place():
    return lax.axis_index("sec") // LINES


def columns_kernel(columns):
    columns[...] = lax.broadcasted_iota(jnp.int32, columns.shape, 1)


def first_kernel(columns, widths, holders, own, other, right, left, *rest):
    *pieces, start, block_vmem = rest
    half = start.shape[2]
    slot = lax.broadcasted_iota(jnp.int32, widths.shape, 1)
    mine = jnp.where(slot == lax.axis_index("sec"), holders[...], 0)
    sector = jnp.sum(mine, axis=1, keepdims=True)
    width = jnp.sum(jnp.where(slot == sector, widths[...], 0), axis=1, keepdims=True)
    for h, part in enumerate(in_order(own[...], other[...])):
        live = h * half + columns[0:1, :] < width
        start[h] = jnp.where(live, part, jnp.zeros_like(part))
    vector = jnp.concatenate([start[0], start[1]], axis=1)
    for term in (1, 2):
        block = apply_term(right, left[0, term], vector, term).astype(jnp.bfloat16)
        block_vmem[...] = block.reshape(block_vmem.shape)
        for step, piece in zip(STEPS, pieces):
            piece[term - 1] = block_vmem[own_place() ^ step]


def stay_kernel(vector, right, left, stay):
    block = apply_term(right, left[0, 0], jnp.concatenate([vector[0], vector[1]], axis=1), 0)
    stay[...] = block.astype(stay.dtype)


def line_targets(plan, part):
    line = lax.axis_index("sec") % LINES
    places = len(STEPS)
    codes = [jnp.max(plan[2 + i : 3 + i, :]) for i in range(2)]
    for index in part:
        for crossing in range(2):
            target = (own_place() ^ STEPS[index]) * LINES + (line ^ crossing)
            entries = [(code >> (target * 4)) & (2 * LINES * places - 1) for code in codes]
            source = [entry & (LINES * places - 1) for entry in entries]
            here = [
                (entry >= LINES * places) & (slot % LINES == line)
                for entry, slot in zip(entries, source)
            ]
            yield index, crossing, here, source


def merge_targets(plan, part, table, keep, cross):
    for index, crossing, here, source in line_targets(plan, part):
        total = 0.0
        for i in range(2):
            block = table[source[i] // LINES, i].astype(jnp.float32)
            total = total + jnp.where(here[i], block, 0.0)
        (keep, cross)[crossing][part.index(index)] = total.astype(jnp.bfloat16)


def merge_early_kernel(plan, *rest):
    *pieces, table, keep, cross = rest
    for step, piece in zip(STEPS, pieces):
        table[own_place() ^ step] = piece[...]
    merge_targets(plan, EARLY, table, keep, cross)


def merge_late_kernel(plan, table, keep, cross):
    merge_targets(plan, LATE, table, keep, cross)


def join_kernel(keep, arrived, *outs):
    for i, out in enumerate(outs):
        total = keep[i].astype(jnp.float32) + arrived[i].astype(jnp.float32)
        out[...] = total.astype(jnp.bfloat16)


def piece_rows(step, rows):
    return pl.ds(pl.multiple_of((own_place() ^ step) * rows, rows), rows)


def sum_kernel(plan, stay, *rest):
    *pieces, first = rest
    live = live_columns(plan, stay.shape[1])
    for step, piece in zip(STEPS, pieces):
        place = piece_rows(step, piece.shape[0])
        total = stay[place, :].astype(jnp.float32) + piece[...].astype(jnp.float32)
        first[place, :] = jnp.where(live, total, 0.0).astype(jnp.bfloat16)


def total_of(array):
    return jnp.sum(jnp.sum(array, axis=0, keepdims=True), axis=1, keepdims=True)


def make_tag(values, me):
    row = lax.broadcasted_iota(jnp.int32, (TAG, LANES), 0)
    lane = lax.broadcasted_iota(jnp.int32, (TAG, LANES), 1)
    spread = jnp.zeros((TAG, LANES), jnp.float32)
    for place, value in enumerate(values):
        spread = jnp.where(row // 3 == place, value, spread)
    high = spread.astype(jnp.bfloat16).astype(jnp.float32)
    middle = (spread - high).astype(jnp.bfloat16).astype(jnp.float32)
    low = spread - high - middle
    parts = jnp.where(row % 3 == 0, high, jnp.where(row % 3 == 1, middle, low))
    return jnp.where((lane == me) & (row < 3 * len(values)), parts, 0.0).astype(jnp.bfloat16)


def second_kernel(start, own, other, right, left, *rest):
    *pieces, deflated_out, block_vmem = rest
    half = start.shape[2]
    rows = block_vmem.shape[1]
    chunks = half // LANES
    basis = [start[h].astype(jnp.float32) for h in range(2)]
    firsts = [part.astype(jnp.float32) for part in in_order(own[...], other[...])]
    overlap = total_of(basis[0] * firsts[0]) + total_of(basis[1] * firsts[1])
    norm = total_of(basis[0] * basis[0]) + total_of(basis[1] * basis[1])
    quotient = jnp.where(norm > 0, overlap / jnp.where(norm > 0, norm, 1.0), 0.0)
    deflated = [firsts[h] - quotient * basis[h] for h in range(2)]
    rest_norm = total_of(deflated[0] * deflated[0]) + total_of(deflated[1] * deflated[1])
    for h in range(2):
        deflated_out[h] = deflated[h].astype(jnp.bfloat16)
    vector = jnp.concatenate(deflated, axis=1).astype(jnp.bfloat16)
    tag = make_tag((overlap, norm, quotient, rest_norm), lax.axis_index("sec"))
    for piece in pieces:
        piece[pl.ds(2 * chunks * rows, TAG), :] = tag
    for term in (1, 2):
        block = apply_term(right, left[0, term], vector, term)
        block_vmem[...] = block.astype(jnp.bfloat16).reshape(block_vmem.shape)
        for step, piece in zip(STEPS, pieces):
            part = block_vmem[own_place() ^ step]
            for c in range(chunks):
                place = pl.ds(((term - 1) * chunks + c) * rows, rows)
                piece[place, :] = part[:, c * LANES : (c + 1) * LANES]


def read_tag(tag):
    def value(place):
        parts = [tag[3 * place + i : 3 * place + i + 1, :] for i in range(3)]
        return parts[0] + parts[1] + parts[2]

    return [value(place) for place in range(4)]


def line_quotient(overlaps, norms, line):
    inside = lax.broadcasted_iota(jnp.int32, (1, LANES), 1) % LINES == line
    overlap = total_of(jnp.where(inside, overlaps, 0.0))
    norm = total_of(jnp.where(inside, norms, 0.0))
    return jnp.where(norm > 0, overlap / jnp.where(norm > 0, norm, 1.0), 0.0)


def mix_kernel(plan, *rest):
    keep, early, late, tag_out, new = rest[-5:]
    old, *pieces = rest[:-5]
    places, rows, half = keep.shape
    chunks = half // LANES
    tag = jnp.zeros((TAG, LANES), jnp.float32)
    for step, piece in zip(STEPS, pieces):
        new[own_place() ^ step] = piece[...]
        label = piece[pl.ds(2 * chunks * rows, TAG), :]
        tag = tag + label.astype(jnp.float32)
    tag_out[...] = tag.astype(jnp.bfloat16)
    early[pl.ds(len(EARLY) * chunks * rows, TAG), :] = tag.astype(jnp.bfloat16)
    overlaps, norms, quotients, _ = read_tag(tag)
    shifts = quotients - line_quotient(overlaps, norms, lax.axis_index("sec") % LINES)
    lane = lax.broadcasted_iota(jnp.int32, (1, LANES), 1)
    for index, crossing, here, source in line_targets(plan, range(places)):
        total = 0.0
        for i in range(2):
            where = source[i] // LINES
            block = jnp.concatenate(
                [new[where, pl.ds((i * chunks + c) * rows, rows), :] for c in range(chunks)],
                axis=1,
            ).astype(jnp.float32)
            shift = total_of(jnp.where(lane == source[i], shifts, 0.0))
            block = block + shift * old[where, i].astype(jnp.float32)
            total = total + jnp.where(here[i], block, 0.0)
        if crossing:
            total = total.astype(jnp.bfloat16)
            out, part = (early, EARLY) if index in EARLY else (late, LATE)
            for c in range(chunks):
                target = pl.ds((part.index(index) * chunks + c) * rows, rows)
                out[target, :] = total[:, c * LANES : (c + 1) * LANES]
        else:
            keep[index] = total


def join_early_kernel(plan, tag_line, keep, arrived, old_keep, old_arrived, *rest):
    *outs, factors = rest
    places, rows, half = keep.shape
    slots = places * LINES
    me = lax.axis_index("sec")
    live_count = places * rows * plan[1:2, 0:1].astype(jnp.float32)
    tag = tag_line[...].astype(jnp.float32)
    tag = tag + arrived[pl.ds(arrived.shape[0] - TAG, TAG), :].astype(jnp.float32)
    overlaps, norms, quotients, rests = read_tag(tag)
    quotient = total_of(overlaps) / total_of(norms)
    lane = lax.broadcasted_iota(jnp.int32, (1, LANES), 1)
    shifts = jnp.where(lane < slots, quotients - quotient, 0.0)
    resid_norm = total_of(rests + shifts * shifts * norms)
    scale = lax.rsqrt(resid_norm / live_count + 1e-06)
    own_shift = total_of(jnp.where(lane == me, shifts, 0.0))
    line = me % LINES
    shift_here = line_quotient(overlaps, norms, line) - quotient
    shift_there = line_quotient(overlaps, norms, 1 - line) - quotient
    row = lax.broadcasted_iota(jnp.int32, factors.shape, 0)
    values = jnp.where(row == 0, scale, scale * own_shift)
    values = jnp.where(row == 2, shift_here, values)
    factors[...] = jnp.where(row == 3, shift_there, values)
    weights = (scale, shift_here, shift_there)
    join_mixed(EARLY, weights, keep, arrived, old_keep, old_arrived, outs)


def join_late_kernel(factors, keep, arrived, old_keep, old_arrived, *outs):
    weights = [factors[i : i + 1, 0:1] for i in (0, 2, 3)]
    join_mixed(LATE, weights, keep, arrived, old_keep, old_arrived, outs)


def join_mixed(part, weights, keep, arrived, old_keep, old_arrived, outs):
    scale, shift_here, shift_there = weights
    rows, half = outs[0].shape
    chunks = half // LANES
    for i, index in enumerate(part):
        block = jnp.concatenate(
            [arrived[pl.ds((i * chunks + c) * rows, rows), :] for c in range(chunks)], axis=1
        ).astype(jnp.float32)
        block = block + shift_there * old_arrived[i].astype(jnp.float32)
        block = block + keep[index] + shift_here * old_keep[i].astype(jnp.float32)
        outs[i][...] = (scale * block).astype(jnp.bfloat16)


def final_kernel(plan, factors, stay, stay_2, first, *rest):
    *pieces, second, first_out = rest
    first_out[...] = first[...]
    live = live_columns(plan, stay.shape[1])
    scale, shift = factors[0:1, 0:1], factors[1:2, 0:1]
    for step, piece in zip(STEPS, pieces):
        place = piece_rows(step, piece.shape[0])
        total = scale * stay_2[place, :] + shift * stay[place, :].astype(jnp.float32)
        total = total + piece[...].astype(jnp.float32)
        second[place, :] = jnp.where(live, total, 0.0).astype(jnp.bfloat16)


SMEM = pl.BlockSpec(memory_space=pltpu.SMEM)
VMEM = pl.BlockSpec(memory_space=pltpu.VMEM)


def call(kernel, specs, outs, scratch=(), flops=0):
    return pl.pallas_call(
        kernel,
        out_shape=outs,
        in_specs=specs,
        out_specs=jax.tree.map(lambda _: VMEM, outs),
        scratch_shapes=scratch,
        compiler_params=pltpu.CompilerParams(vmem_limit_bytes=16 * 1024 * 1024),
        cost_estimate=pl.CostEstimate(flops=flops, bytes_accessed=1 << 18, transcendentals=0),
    )


def along_line(pieces, slots):
    sent = []
    for step, piece in zip(STEPS, pieces):
        pairs = [(slot, slot ^ (step * LINES)) for slot in range(slots)]
        sent.append(lax.ppermute(piece, "sec", pairs) if step else piece)
    return sent


def other_core(block):
    return lax.ppermute(block, "env", [(0, 1), (1, 0)])


def across(piece, slots):
    return lax.ppermute(piece, "sec", [(slot, slot ^ 1) for slot in range(slots)])


def on_device(amplitudes, widths, holders, left_env, right_env):
    slots_dev, right_dim, half = amplitudes.shape
    slots = holders.shape[0]
    assert slots_dev == 1
    if slots != 2 * QDOWN:
        return on_device_any(amplitudes, widths, holders, left_env, right_env)
    places = slots // LINES
    rows = right_dim // places
    dots = 6 * right_dim * half * (right_dim + 2 * half)
    block = jax.ShapeDtypeStruct((right_dim, half), jnp.bfloat16)
    wide = jax.ShapeDtypeStruct((right_dim, half), jnp.float32)
    pair = jax.ShapeDtypeStruct((2, rows, half), jnp.bfloat16)
    single = jax.ShapeDtypeStruct((rows, half), jnp.bfloat16)
    wides = jax.ShapeDtypeStruct((places, rows, half), jnp.float32)
    chunked = rows * half // LANES
    tagged = jax.ShapeDtypeStruct((2 * chunked + TAG, LANES), jnp.bfloat16)
    twos = jax.ShapeDtypeStruct((2, rows, half), jnp.bfloat16)
    early = jax.ShapeDtypeStruct((2 * chunked + TAG, LANES), jnp.bfloat16)
    late = jax.ShapeDtypeStruct((2 * chunked, LANES), jnp.bfloat16)
    label = jax.ShapeDtypeStruct((TAG, LANES), jnp.bfloat16)
    factor_shape = jax.ShapeDtypeStruct((8, LANES), jnp.float32)
    plan_shape = jax.ShapeDtypeStruct((8, LANES), jnp.int32)
    split = [pltpu.VMEM((places, rows, half), jnp.bfloat16)]
    table_shape = jax.ShapeDtypeStruct((places, *pair.shape), jnp.bfloat16)
    new_table = [pltpu.VMEM((places, *tagged.shape), jnp.bfloat16)]

    slot_table = [pltpu.SMEM((slots,), jnp.int32)]
    plan = call(plan_kernel, [SMEM, SMEM], plan_shape, slot_table)(widths, holders)
    both = jax.ShapeDtypeStruct((2, right_dim, half), jnp.bfloat16)
    number = jax.ShapeDtypeStruct((8, half), jnp.int32)
    columns = call(columns_kernel, [], number, flops=4 << 30)()
    *pieces, start_full = call(
        first_kernel, [VMEM] * 7, (pair,) * places + (both,), split, dots
    )(
        columns,
        widths[None],
        holders[None],
        amplitudes[0],
        other_core(amplitudes[0]),
        right_env,
        left_env,
    )
    old = along_line(pieces, slots)
    stay = call(stay_kernel, [VMEM] * 3, block, flops=dots // 3)(start_full, right_env, left_env)
    table, keep_early, cross = call(
        merge_early_kernel, [VMEM] * (1 + places), (table_shape, twos, twos)
    )(plan, *old)
    old_early = across(cross, slots)
    keep_late, cross = call(merge_late_kernel, [VMEM] * 2, (twos, twos))(plan, table)
    old_late = across(cross, slots)
    far = call(join_kernel, [VMEM] * 2, (single,) * 2)(keep_early, old_early)
    near = call(join_kernel, [VMEM] * 2, (single,) * 2)(keep_late, old_late)
    joined = (near[0], *far, near[1])
    first = call(sum_kernel, [VMEM] * (2 + places), block)(
        plan, stay, *along_line(joined, slots)
    )

    *pieces, deflated = call(
        second_kernel, [VMEM] * 5, (tagged,) * places + (both,), split, dots
    )(start_full, first, other_core(first), right_env, left_env)
    new = along_line(pieces, slots)
    stay_2 = call(stay_kernel, [VMEM] * 3, wide, flops=dots // 3)(deflated, right_env, left_env)
    keep, *cross, tag = call(
        mix_kernel, [VMEM] * (2 + places), (wides, early, late, label), new_table
    )(plan, table, *new)
    new_early, new_late = (across(piece, slots) for piece in cross)
    *far, factors = call(join_early_kernel, [VMEM] * 6, (single, single, factor_shape))(
        plan, tag, keep, new_early, keep_early, old_early
    )
    near = call(join_late_kernel, [VMEM] * 5, (single,) * 2)(
        factors, keep, new_late, keep_late, old_late
    )
    joined = (near[0], *far, near[1])
    second, first = call(final_kernel, [VMEM] * (5 + places), (block, block))(
        plan, factors, stay, stay_2, first, *along_line(joined, slots)
    )
    return first[None], second[None]


def solution(mesh):
    in_specs = (
        P(("runs", "sec"), None, "env"),
        P("runs"),
        P("runs"),
        P(("runs", "sec"), None, None, "env"),
        P("runs", None, None),
    )
    out_specs = (P(("runs", "sec"), None, "env"), P(("runs", "sec"), None, "env"))
    return jax.shard_map(
        on_device, mesh=mesh, in_specs=in_specs, out_specs=out_specs, check_vma=False
    )
```

```python
import jax
import jax.numpy as jnp
from jax import lax
from jax.experimental import pallas as pl
from jax.experimental.pallas import tpu as pltpu
from jax.sharding import PartitionSpec as P

QDOWN = 4

term_shifts = ((0, 0), (1, 0), (0, 1))


def route(holders):
    n_slots = holders.shape[0]
    sector_ids = jnp.arange(n_slots, dtype=jnp.int32)
    slot_of = jnp.argmax(holders[None, :] == sector_ids[:, None], axis=1)
    sources = []
    allowed = []
    for up, down in term_shifts[1:]:
        permitted = (holders // QDOWN - up >= 0) & (holders % QDOWN - down >= 0)
        wanted = jnp.clip(holders - QDOWN * up - down, 0, n_slots - 1)
        sources.append(slot_of[wanted])
        allowed.append(permitted)
    return sources, allowed


def contract(vector, left_env, right_env):
    products = jnp.einsum(
        "tij,jw->tiw", right_env, vector, preferred_element_type=jnp.float32
    ).astype(jnp.bfloat16)
    return jnp.einsum("tik,tkw->tiw", products, left_env, preferred_element_type=jnp.float32)


def spread(blocks, n_slots):
    terms, rows, width = blocks.shape
    pieces = blocks.reshape(terms, n_slots, rows // n_slots, width).swapaxes(0, 1)
    return lax.all_to_all(pieces, "sec", split_axis=0, concat_axis=0)


def collect(merged):
    n_slots, rows, width = merged.shape
    home = lax.all_to_all(merged, "sec", split_axis=0, concat_axis=0)
    return home.reshape(n_slots * rows, width)


def share(values, n_slots, me):
    lanes = jnp.zeros((1, 128), jnp.float32).at[0, : values.shape[0]].set(values)
    if n_slots & (n_slots - 1) or n_slots > 16:
        return lax.all_gather(lanes[0], "sec")
    table = jnp.where(jnp.arange(n_slots)[:, None] == me, lanes, 0.0)
    for offset in range(1, n_slots):
        pairs = [(i, i ^ offset) for i in range(n_slots)]
        other = lax.ppermute(lanes, "sec", pairs)
        table = jnp.where(jnp.arange(n_slots)[:, None] == (me ^ offset), other, table)
    return table


def merge(received, sources, allowed):
    total = 0.0
    for term, (source, permitted) in enumerate(zip(sources, allowed)):
        picked = received[source, term]
        total = total + jnp.where(permitted[:, None, None], picked, 0).astype(jnp.float32)
    return total


def on_device_any(amplitudes, widths, holders, left_env, right_env):
    slots_dev, right_dim, half_width = amplitudes.shape
    assert slots_dev == 1
    n_slots = holders.shape[0]
    me = lax.axis_index("sec")
    side = lax.axis_index("env")
    my_width = widths[holders[me]]
    row_index = side * half_width + jnp.arange(half_width, dtype=jnp.int32)
    live = (row_index < my_width)[None, :]
    sources, allowed = route(holders)
    envs = left_env[0]

    start = jnp.where(live, amplitudes[0], jnp.zeros_like(amplitudes[0]))
    start_full = lax.all_gather(start, "env", axis=1, tiled=True)
    outgoing = contract(start_full, envs, right_env).astype(jnp.bfloat16)
    stay = outgoing[0].astype(jnp.float32)
    received = spread(outgoing[1:], n_slots)
    arrived = collect(merge(received, sources, allowed).astype(jnp.bfloat16))
    first = jnp.where(live, stay + arrived.astype(jnp.float32), 0.0).astype(jnp.bfloat16)

    first_full = lax.all_gather(first, "env", axis=1, tiled=True).astype(jnp.float32)
    basis = start_full.astype(jnp.float32)
    overlap = jnp.sum(basis * first_full)
    norm = jnp.sum(basis * basis)
    own_quotient = jnp.where(norm > 0, overlap / jnp.where(norm > 0, norm, 1.0), 0.0)
    deflated = first_full - own_quotient * basis
    rest = jnp.sum(deflated * deflated)
    sums = share(jnp.stack([overlap, norm, own_quotient, rest]), n_slots, me)
    outgoing_2 = contract(deflated.astype(jnp.bfloat16), envs, right_env)
    received_2 = spread(outgoing_2[1:].astype(jnp.bfloat16), n_slots)

    quotient = jnp.sum(sums[:, 0]) / jnp.sum(sums[:, 1])
    shift = sums[:, 2] - quotient
    resid_norm = jnp.sum(sums[:, 3] + shift * shift * sums[:, 1])
    live_count = right_dim * jnp.sum(widths).astype(jnp.float32)
    scale = lax.rsqrt(resid_norm / live_count + 1e-06)
    mixed = received_2.astype(jnp.float32) + shift[:, None, None, None] * received.astype(
        jnp.float32
    )
    merged_2 = scale * merge(mixed, sources, allowed)
    arrived_2 = collect(merged_2.astype(jnp.bfloat16))
    stay_2 = scale * (outgoing_2[0] + (own_quotient - quotient) * stay)
    second = jnp.where(live, stay_2 + arrived_2.astype(jnp.float32), 0.0).astype(jnp.bfloat16)
    return first[None], second[None]


LANES = 128
TAG = 16
LINES = 2
STEPS = (0, 3, 2, 1)
EARLY, LATE = (1,), (0, 2, 3)


def plan_kernel(widths, holders, plan, slot_of):
    slots = holders.shape[0]
    me = lax.axis_index("sec")
    total = jnp.int32(0)
    for s in range(slots):
        slot_of[holders[s]] = jnp.int32(s)
        total = total + widths[s]
    codes = [jnp.int32(0), jnp.int32(0)]
    for target in range(slots):
        sector = holders[target]
        has = (sector >= QDOWN, sector % QDOWN > 0)
        source = (slot_of[sector & (QDOWN - 1)], slot_of[jnp.maximum(sector - 1, 0)])
        for i in range(2):
            entry = jnp.where(has[i], source[i] + slots, 0)
            codes[i] = codes[i] | (entry << (target * 4))
    row = lax.broadcasted_iota(jnp.int32, plan.shape, 0)
    values = jnp.where(row == 0, widths[holders[me]], total)
    values = jnp.where(row == 2, codes[0], values)
    plan[...] = jnp.where(row == 3, codes[1], values)


def live_columns(plan, half):
    first_column = lax.axis_index("env") * half
    return first_column + lax.broadcasted_iota(jnp.int32, (1, half), 1) < plan[0:1, 0:1]


def apply_term(right, left, vector, term):
    products = jnp.dot(right[term], vector, preferred_element_type=jnp.float32)
    return jnp.dot(products.astype(jnp.bfloat16), left, preferred_element_type=jnp.float32)


def in_order(own, other):
    upper = lax.axis_index("env") > 0
    return [jnp.where(upper, other, own), jnp.where(upper, own, other)]


def own_place():
    return lax.axis_index("sec") // LINES


def columns_kernel(columns):
    columns[...] = lax.broadcasted_iota(jnp.int32, columns.shape, 1)


def first_kernel(columns, widths, holders, own, other, right, left, *rest):
    *pieces, start, block_vmem = rest
    half = start.shape[2]
    slot = lax.broadcasted_iota(jnp.int32, widths.shape, 1)
    mine = jnp.where(slot == lax.axis_index("sec"), holders[...], 0)
    sector = jnp.sum(mine, axis=1, keepdims=True)
    width = jnp.sum(jnp.where(slot == sector, widths[...], 0), axis=1, keepdims=True)
    for h, part in enumerate(in_order(own[...], other[...])):
        live = h * half + columns[0:1, :] < width
        start[h] = jnp.where(live, part, jnp.zeros_like(part))
    vector = jnp.concatenate([start[0], start[1]], axis=1)
    for term in (1, 2):
        block = apply_term(right, left[0, term], vector, term).astype(jnp.bfloat16)
        block_vmem[...] = block.reshape(block_vmem.shape)
        for step, piece in zip(STEPS, pieces):
            piece[term - 1] = block_vmem[own_place() ^ step]


def stay_kernel(vector, right, left, stay):
    block = apply_term(right, left[0, 0], jnp.concatenate([vector[0], vector[1]], axis=1), 0)
    stay[...] = block.astype(stay.dtype)


def line_targets(plan, part):
    line = lax.axis_index("sec") % LINES
    places = len(STEPS)
    codes = [jnp.max(plan[2 + i : 3 + i, :]) for i in range(2)]
    for index in part:
        for crossing in range(2):
            target = (own_place() ^ STEPS[index]) * LINES + (line ^ crossing)
            entries = [(code >> (target * 4)) & (2 * LINES * places - 1) for code in codes]
            source = [entry & (LINES * places - 1) for entry in entries]
            here = [
                (entry >= LINES * places) & (slot % LINES == line)
                for entry, slot in zip(entries, source)
            ]
            yield index, crossing, here, source


def merge_targets(plan, part, table, keep, cross):
    for index, crossing, here, source in line_targets(plan, part):
        total = 0.0
        for i in range(2):
            block = table[source[i] // LINES, i].astype(jnp.float32)
            total = total + jnp.where(here[i], block, 0.0)
        (keep, cross)[crossing][part.index(index)] = total.astype(jnp.bfloat16)


def merge_early_kernel(plan, *rest):
    *pieces, table, keep, cross = rest
    for step, piece in zip(STEPS, pieces):
        table[own_place() ^ step] = piece[...]
    merge_targets(plan, EARLY, table, keep, cross)


def merge_late_kernel(plan, table, keep, cross):
    merge_targets(plan, LATE, table, keep, cross)


def join_kernel(keep, arrived, *outs):
    for i, out in enumerate(outs):
        total = keep[i].astype(jnp.float32) + arrived[i].astype(jnp.float32)
        out[...] = total.astype(jnp.bfloat16)


def piece_rows(step, rows):
    return pl.ds(pl.multiple_of((own_place() ^ step) * rows, rows), rows)


def sum_kernel(plan, stay, *rest):
    *pieces, first = rest
    live = live_columns(plan, stay.shape[1])
    for step, piece in zip(STEPS, pieces):
        place = piece_rows(step, piece.shape[0])
        total = stay[place, :].astype(jnp.float32) + piece[...].astype(jnp.float32)
        first[place, :] = jnp.where(live, total, 0.0).astype(jnp.bfloat16)


def total_of(array):
    return jnp.sum(jnp.sum(array, axis=0, keepdims=True), axis=1, keepdims=True)


def make_tag(values, me):
    row = lax.broadcasted_iota(jnp.int32, (TAG, LANES), 0)
    lane = lax.broadcasted_iota(jnp.int32, (TAG, LANES), 1)
    spread = jnp.zeros((TAG, LANES), jnp.float32)
    for place, value in enumerate(values):
        spread = jnp.where(row // 3 == place, value, spread)
    high = spread.astype(jnp.bfloat16).astype(jnp.float32)
    middle = (spread - high).astype(jnp.bfloat16).astype(jnp.float32)
    low = spread - high - middle
    parts = jnp.where(row % 3 == 0, high, jnp.where(row % 3 == 1, middle, low))
    return jnp.where((lane == me) & (row < 3 * len(values)), parts, 0.0).astype(jnp.bfloat16)


def second_kernel(start, own, other, right, left, *rest):
    *pieces, deflated_out, block_vmem = rest
    half = start.shape[2]
    rows = block_vmem.shape[1]
    chunks = half // LANES
    basis = [start[h].astype(jnp.float32) for h in range(2)]
    firsts = [part.astype(jnp.float32) for part in in_order(own[...], other[...])]
    overlap = total_of(basis[0] * firsts[0]) + total_of(basis[1] * firsts[1])
    norm = total_of(basis[0] * basis[0]) + total_of(basis[1] * basis[1])
    quotient = jnp.where(norm > 0, overlap / jnp.where(norm > 0, norm, 1.0), 0.0)
    deflated = [firsts[h] - quotient * basis[h] for h in range(2)]
    rest_norm = total_of(deflated[0] * deflated[0]) + total_of(deflated[1] * deflated[1])
    for h in range(2):
        deflated_out[h] = deflated[h].astype(jnp.bfloat16)
    vector = jnp.concatenate(deflated, axis=1).astype(jnp.bfloat16)
    tag = make_tag((overlap, norm, quotient, rest_norm), lax.axis_index("sec"))
    for piece in pieces:
        piece[pl.ds(2 * chunks * rows, TAG), :] = tag
    for term in (1, 2):
        block = apply_term(right, left[0, term], vector, term)
        block_vmem[...] = block.astype(jnp.bfloat16).reshape(block_vmem.shape)
        for step, piece in zip(STEPS, pieces):
            part = block_vmem[own_place() ^ step]
            for c in range(chunks):
                place = pl.ds(((term - 1) * chunks + c) * rows, rows)
                piece[place, :] = part[:, c * LANES : (c + 1) * LANES]


def read_tag(tag):
    def value(place):
        parts = [tag[3 * place + i : 3 * place + i + 1, :] for i in range(3)]
        return parts[0] + parts[1] + parts[2]

    return [value(place) for place in range(4)]


def line_quotient(overlaps, norms, line):
    inside = lax.broadcasted_iota(jnp.int32, (1, LANES), 1) % LINES == line
    overlap = total_of(jnp.where(inside, overlaps, 0.0))
    norm = total_of(jnp.where(inside, norms, 0.0))
    return jnp.where(norm > 0, overlap / jnp.where(norm > 0, norm, 1.0), 0.0)


def mix_kernel(plan, *rest):
    keep, early, late, tag_out, new = rest[-5:]
    old, *pieces = rest[:-5]
    places, rows, half = keep.shape
    chunks = half // LANES
    tag = jnp.zeros((TAG, LANES), jnp.float32)
    for step, piece in zip(STEPS, pieces):
        new[own_place() ^ step] = piece[...]
        label = piece[pl.ds(2 * chunks * rows, TAG), :]
        tag = tag + label.astype(jnp.float32)
    tag_out[...] = tag.astype(jnp.bfloat16)
    early[pl.ds(len(EARLY) * chunks * rows, TAG), :] = tag.astype(jnp.bfloat16)
    overlaps, norms, quotients, _ = read_tag(tag)
    shifts = quotients - line_quotient(overlaps, norms, lax.axis_index("sec") % LINES)
    lane = lax.broadcasted_iota(jnp.int32, (1, LANES), 1)
    for index, crossing, here, source in line_targets(plan, range(places)):
        total = 0.0
        for i in range(2):
            where = source[i] // LINES
            block = jnp.concatenate(
                [new[where, pl.ds((i * chunks + c) * rows, rows), :] for c in range(chunks)],
                axis=1,
            ).astype(jnp.float32)
            shift = total_of(jnp.where(lane == source[i], shifts, 0.0))
            block = block + shift * old[where, i].astype(jnp.float32)
            total = total + jnp.where(here[i], block, 0.0)
        if crossing:
            total = total.astype(jnp.bfloat16)
            out, part = (early, EARLY) if index in EARLY else (late, LATE)
            for c in range(chunks):
                target = pl.ds((part.index(index) * chunks + c) * rows, rows)
                out[target, :] = total[:, c * LANES : (c + 1) * LANES]
        else:
            keep[index] = total


def join_early_kernel(plan, tag_line, keep, arrived, old_keep, old_arrived, *rest):
    *outs, factors = rest
    places, rows, half = keep.shape
    slots = places * LINES
    me = lax.axis_index("sec")
    live_count = places * rows * plan[1:2, 0:1].astype(jnp.float32)
    tag = tag_line[...].astype(jnp.float32)
    tag = tag + arrived[pl.ds(arrived.shape[0] - TAG, TAG), :].astype(jnp.float32)
    overlaps, norms, quotients, rests = read_tag(tag)
    quotient = total_of(overlaps) / total_of(norms)
    lane = lax.broadcasted_iota(jnp.int32, (1, LANES), 1)
    shifts = jnp.where(lane < slots, quotients - quotient, 0.0)
    resid_norm = total_of(rests + shifts * shifts * norms)
    scale = lax.rsqrt(resid_norm / live_count + 1e-06)
    own_shift = total_of(jnp.where(lane == me, shifts, 0.0))
    line = me % LINES
    shift_here = line_quotient(overlaps, norms, line) - quotient
    shift_there = line_quotient(overlaps, norms, 1 - line) - quotient
    row = lax.broadcasted_iota(jnp.int32, factors.shape, 0)
    values = jnp.where(row == 0, scale, scale * own_shift)
    values = jnp.where(row == 2, shift_here, values)
    factors[...] = jnp.where(row == 3, shift_there, values)
    weights = (scale, shift_here, shift_there)
    join_mixed(EARLY, weights, keep, arrived, old_keep, old_arrived, outs)


def join_late_kernel(factors, keep, arrived, old_keep, old_arrived, *outs):
    weights = [factors[i : i + 1, 0:1] for i in (0, 2, 3)]
    join_mixed(LATE, weights, keep, arrived, old_keep, old_arrived, outs)


def join_mixed(part, weights, keep, arrived, old_keep, old_arrived, outs):
    scale, shift_here, shift_there = weights
    rows, half = outs[0].shape
    chunks = half // LANES
    for i, index in enumerate(part):
        block = jnp.concatenate(
            [arrived[pl.ds((i * chunks + c) * rows, rows), :] for c in range(chunks)], axis=1
        ).astype(jnp.float32)
        block = block + shift_there * old_arrived[i].astype(jnp.float32)
        block = block + keep[index] + shift_here * old_keep[i].astype(jnp.float32)
        outs[i][...] = (scale * block).astype(jnp.bfloat16)


def final_kernel(plan, factors, stay, stay_2, first, *rest):
    *pieces, second, first_out = rest
    first_out[...] = first[...]
    live = live_columns(plan, stay.shape[1])
    scale, shift = factors[0:1, 0:1], factors[1:2, 0:1]
    for step, piece in zip(STEPS, pieces):
        place = piece_rows(step, piece.shape[0])
        total = scale * stay_2[place, :] + shift * stay[place, :].astype(jnp.float32)
        total = total + piece[...].astype(jnp.float32)
        second[place, :] = jnp.where(live, total, 0.0).astype(jnp.bfloat16)


SMEM = pl.BlockSpec(memory_space=pltpu.SMEM)
VMEM = pl.BlockSpec(memory_space=pltpu.VMEM)


def call(kernel, specs, outs, scratch=(), flops=0):
    return pl.pallas_call(
        kernel,
        out_shape=outs,
        in_specs=specs,
        out_specs=jax.tree.map(lambda _: VMEM, outs),
        scratch_shapes=scratch,
        compiler_params=pltpu.CompilerParams(vmem_limit_bytes=16 * 1024 * 1024),
        cost_estimate=pl.CostEstimate(flops=flops, bytes_accessed=1 << 18, transcendentals=0),
    )


def along_line(pieces, slots):
    sent = []
    for step, piece in zip(STEPS, pieces):
        pairs = [(slot, slot ^ (step * LINES)) for slot in range(slots)]
        sent.append(lax.ppermute(piece, "sec", pairs) if step else piece)
    return sent


def other_core(block):
    return lax.ppermute(block, "env", [(0, 1), (1, 0)])


def across(piece, slots):
    return lax.ppermute(piece, "sec", [(slot, slot ^ 1) for slot in range(slots)])


def on_device(amplitudes, widths, holders, left_env, right_env):
    slots_dev, right_dim, half = amplitudes.shape
    slots = holders.shape[0]
    assert slots_dev == 1
    if slots != 2 * QDOWN:
        return on_device_any(amplitudes, widths, holders, left_env, right_env)
    places = slots // LINES
    rows = right_dim // places
    dots = 6 * right_dim * half * (right_dim + 2 * half)
    block = jax.ShapeDtypeStruct((right_dim, half), jnp.bfloat16)
    wide = jax.ShapeDtypeStruct((right_dim, half), jnp.float32)
    pair = jax.ShapeDtypeStruct((2, rows, half), jnp.bfloat16)
    single = jax.ShapeDtypeStruct((rows, half), jnp.bfloat16)
    wides = jax.ShapeDtypeStruct((places, rows, half), jnp.float32)
    chunked = rows * half // LANES
    tagged = jax.ShapeDtypeStruct((2 * chunked + TAG, LANES), jnp.bfloat16)
    few = jax.ShapeDtypeStruct((len(EARLY), rows, half), jnp.bfloat16)
    most = jax.ShapeDtypeStruct((len(LATE), rows, half), jnp.bfloat16)
    early = jax.ShapeDtypeStruct((len(EARLY) * chunked + TAG, LANES), jnp.bfloat16)
    late = jax.ShapeDtypeStruct((len(LATE) * chunked, LANES), jnp.bfloat16)
    label = jax.ShapeDtypeStruct((TAG, LANES), jnp.bfloat16)
    factor_shape = jax.ShapeDtypeStruct((8, LANES), jnp.float32)
    plan_shape = jax.ShapeDtypeStruct((8, LANES), jnp.int32)
    split = [pltpu.VMEM((places, rows, half), jnp.bfloat16)]
    table_shape = jax.ShapeDtypeStruct((places, *pair.shape), jnp.bfloat16)
    new_table = [pltpu.VMEM((places, *tagged.shape), jnp.bfloat16)]

    slot_table = [pltpu.SMEM((slots,), jnp.int32)]
    plan = call(plan_kernel, [SMEM, SMEM], plan_shape, slot_table)(widths, holders)
    both = jax.ShapeDtypeStruct((2, right_dim, half), jnp.bfloat16)
    number = jax.ShapeDtypeStruct((8, half), jnp.int32)
    columns = call(columns_kernel, [], number, flops=4 << 30)()
    *pieces, start_full = call(
        first_kernel, [VMEM] * 7, (pair,) * places + (both,), split, dots
    )(
        columns,
        widths[None],
        holders[None],
        amplitudes[0],
        other_core(amplitudes[0]),
        right_env,
        left_env,
    )
    old = along_line(pieces, slots)
    stay = call(stay_kernel, [VMEM] * 3, block, flops=dots // 3)(start_full, right_env, left_env)
    table, keep_early, cross = call(
        merge_early_kernel, [VMEM] * (1 + places), (table_shape, few, few)
    )(plan, *old)
    old_early = across(cross, slots)
    keep_late, cross = call(merge_late_kernel, [VMEM] * 2, (most, most))(plan, table)
    old_late = across(cross, slots)
    far = call(join_kernel, [VMEM] * 2, (single,) * len(EARLY))(keep_early, old_early)
    near = call(join_kernel, [VMEM] * 2, (single,) * len(LATE))(keep_late, old_late)
    joined = (near[0], *far, *near[1:])
    first = call(sum_kernel, [VMEM] * (2 + places), block)(
        plan, stay, *along_line(joined, slots)
    )

    *pieces, deflated = call(
        second_kernel, [VMEM] * 5, (tagged,) * places + (both,), split, dots
    )(start_full, first, other_core(first), right_env, left_env)
    new = along_line(pieces, slots)
    stay_2 = call(stay_kernel, [VMEM] * 3, wide, flops=dots // 3)(deflated, right_env, left_env)
    keep, *cross, tag = call(
        mix_kernel, [VMEM] * (2 + places), (wides, early, late, label), new_table
    )(plan, table, *new)
    new_early, new_late = (across(piece, slots) for piece in cross)
    *far, factors = call(join_early_kernel, [VMEM] * 6, (single,) * len(EARLY) + (factor_shape,))(
        plan, tag, keep, new_early, keep_early, old_early
    )
    near = call(join_late_kernel, [VMEM] * 5, (single,) * len(LATE))(
        factors, keep, new_late, keep_late, old_late
    )
    joined = (near[0], *far, *near[1:])
    second, first = call(final_kernel, [VMEM] * (5 + places), (block, block))(
        plan, factors, stay, stay_2, first, *along_line(joined, slots)
    )
    return first[None], second[None]


def solution(mesh):
    in_specs = (
        P(("runs", "sec"), None, "env"),
        P("runs"),
        P("runs"),
        P(("runs", "sec"), None, None, "env"),
        P("runs", None, None),
    )
    out_specs = (P(("runs", "sec"), None, "env"), P(("runs", "sec"), None, "env"))
    return jax.shard_map(
        on_device, mesh=mesh, in_specs=in_specs, out_specs=out_specs, check_vma=False
    )
```

```python
import jax
import jax.numpy as jnp
from jax import lax
from jax.experimental import pallas as pl
from jax.experimental.pallas import tpu as pltpu
from jax.sharding import PartitionSpec as P

QDOWN = 4

term_shifts = ((0, 0), (1, 0), (0, 1))


def route(holders):
    n_slots = holders.shape[0]
    sector_ids = jnp.arange(n_slots, dtype=jnp.int32)
    slot_of = jnp.argmax(holders[None, :] == sector_ids[:, None], axis=1)
    sources = []
    allowed = []
    for up, down in term_shifts[1:]:
        permitted = (holders // QDOWN - up >= 0) & (holders % QDOWN - down >= 0)
        wanted = jnp.clip(holders - QDOWN * up - down, 0, n_slots - 1)
        sources.append(slot_of[wanted])
        allowed.append(permitted)
    return sources, allowed


def contract(vector, left_env, right_env):
    products = jnp.einsum(
        "tij,jw->tiw", right_env, vector, preferred_element_type=jnp.float32
    ).astype(jnp.bfloat16)
    return jnp.einsum("tik,tkw->tiw", products, left_env, preferred_element_type=jnp.float32)


def spread(blocks, n_slots):
    terms, rows, width = blocks.shape
    pieces = blocks.reshape(terms, n_slots, rows // n_slots, width).swapaxes(0, 1)
    return lax.all_to_all(pieces, "sec", split_axis=0, concat_axis=0)


def collect(merged):
    n_slots, rows, width = merged.shape
    home = lax.all_to_all(merged, "sec", split_axis=0, concat_axis=0)
    return home.reshape(n_slots * rows, width)


def share(values, n_slots, me):
    lanes = jnp.zeros((1, 128), jnp.float32).at[0, : values.shape[0]].set(values)
    if n_slots & (n_slots - 1) or n_slots > 16:
        return lax.all_gather(lanes[0], "sec")
    table = jnp.where(jnp.arange(n_slots)[:, None] == me, lanes, 0.0)
    for offset in range(1, n_slots):
        pairs = [(i, i ^ offset) for i in range(n_slots)]
        other = lax.ppermute(lanes, "sec", pairs)
        table = jnp.where(jnp.arange(n_slots)[:, None] == (me ^ offset), other, table)
    return table


def merge(received, sources, allowed):
    total = 0.0
    for term, (source, permitted) in enumerate(zip(sources, allowed)):
        picked = received[source, term]
        total = total + jnp.where(permitted[:, None, None], picked, 0).astype(jnp.float32)
    return total


def on_device_any(amplitudes, widths, holders, left_env, right_env):
    slots_dev, right_dim, half_width = amplitudes.shape
    assert slots_dev == 1
    n_slots = holders.shape[0]
    me = lax.axis_index("sec")
    side = lax.axis_index("env")
    my_width = widths[holders[me]]
    row_index = side * half_width + jnp.arange(half_width, dtype=jnp.int32)
    live = (row_index < my_width)[None, :]
    sources, allowed = route(holders)
    envs = left_env[0]

    start = jnp.where(live, amplitudes[0], jnp.zeros_like(amplitudes[0]))
    start_full = lax.all_gather(start, "env", axis=1, tiled=True)
    outgoing = contract(start_full, envs, right_env).astype(jnp.bfloat16)
    stay = outgoing[0].astype(jnp.float32)
    received = spread(outgoing[1:], n_slots)
    arrived = collect(merge(received, sources, allowed).astype(jnp.bfloat16))
    first = jnp.where(live, stay + arrived.astype(jnp.float32), 0.0).astype(jnp.bfloat16)

    first_full = lax.all_gather(first, "env", axis=1, tiled=True).astype(jnp.float32)
    basis = start_full.astype(jnp.float32)
    overlap = jnp.sum(basis * first_full)
    norm = jnp.sum(basis * basis)
    own_quotient = jnp.where(norm > 0, overlap / jnp.where(norm > 0, norm, 1.0), 0.0)
    deflated = first_full - own_quotient * basis
    rest = jnp.sum(deflated * deflated)
    sums = share(jnp.stack([overlap, norm, own_quotient, rest]), n_slots, me)
    outgoing_2 = contract(deflated.astype(jnp.bfloat16), envs, right_env)
    received_2 = spread(outgoing_2[1:].astype(jnp.bfloat16), n_slots)

    quotient = jnp.sum(sums[:, 0]) / jnp.sum(sums[:, 1])
    shift = sums[:, 2] - quotient
    resid_norm = jnp.sum(sums[:, 3] + shift * shift * sums[:, 1])
    live_count = right_dim * jnp.sum(widths).astype(jnp.float32)
    scale = lax.rsqrt(resid_norm / live_count + 1e-06)
    mixed = received_2.astype(jnp.float32) + shift[:, None, None, None] * received.astype(
        jnp.float32
    )
    merged_2 = scale * merge(mixed, sources, allowed)
    arrived_2 = collect(merged_2.astype(jnp.bfloat16))
    stay_2 = scale * (outgoing_2[0] + (own_quotient - quotient) * stay)
    second = jnp.where(live, stay_2 + arrived_2.astype(jnp.float32), 0.0).astype(jnp.bfloat16)
    return first[None], second[None]


LANES = 128
TAG = 16
LINES = 2
STEPS = (0, 3, 2, 1)
EARLY, LATE = (1, 2), (0, 3)


def plan_kernel(widths, holders, plan, slot_of):
    slots = holders.shape[0]
    me = lax.axis_index("sec")
    total = jnp.int32(0)
    for s in range(slots):
        slot_of[holders[s]] = jnp.int32(s)
        total = total + widths[s]
    codes = [jnp.int32(0), jnp.int32(0)]
    for target in range(slots):
        sector = holders[target]
        has = (sector >= QDOWN, sector % QDOWN > 0)
        source = (slot_of[sector & (QDOWN - 1)], slot_of[jnp.maximum(sector - 1, 0)])
        for i in range(2):
            entry = jnp.where(has[i], source[i] + slots, 0)
            codes[i] = codes[i] | (entry << (target * 4))
    row = lax.broadcasted_iota(jnp.int32, plan.shape, 0)
    values = jnp.where(row == 0, widths[holders[me]], total)
    values = jnp.where(row == 2, codes[0], values)
    plan[...] = jnp.where(row == 3, codes[1], values)


def live_columns(plan, half):
    first_column = lax.axis_index("env") * half
    return first_column + lax.broadcasted_iota(jnp.int32, (1, half), 1) < plan[0:1, 0:1]


def apply_term(right, left, vector, term):
    products = jnp.dot(right[term], vector, preferred_element_type=jnp.float32)
    return jnp.dot(products.astype(jnp.bfloat16), left, preferred_element_type=jnp.float32)


def in_order(own, other):
    upper = lax.axis_index("env") > 0
    return [jnp.where(upper, other, own), jnp.where(upper, own, other)]


def own_place():
    return lax.axis_index("sec") // LINES


def columns_kernel(columns):
    columns[...] = lax.broadcasted_iota(jnp.int32, columns.shape, 1)


def first_kernel(columns, widths, holders, own, other, right, left, *rest):
    *pieces, start, block_vmem = rest
    half = start.shape[2]
    slot = lax.broadcasted_iota(jnp.int32, widths.shape, 1)
    mine = jnp.where(slot == lax.axis_index("sec"), holders[...], 0)
    sector = jnp.sum(mine, axis=1, keepdims=True)
    width = jnp.sum(jnp.where(slot == sector, widths[...], 0), axis=1, keepdims=True)
    for h, part in enumerate(in_order(own[...], other[...])):
        live = h * half + columns[0:1, :] < width
        start[h] = jnp.where(live, part, jnp.zeros_like(part))
    vector = jnp.concatenate([start[0], start[1]], axis=1)
    for term in (1, 2):
        block = apply_term(right, left[0, term], vector, term).astype(jnp.bfloat16)
        block_vmem[...] = block.reshape(block_vmem.shape)
        for step, piece in zip(STEPS, pieces):
            piece[term - 1] = block_vmem[own_place() ^ step]


def stay_kernel(vector, right, left, stay):
    block = apply_term(right, left[0, 0], jnp.concatenate([vector[0], vector[1]], axis=1), 0)
    stay[...] = block.astype(stay.dtype)


def line_targets(plan, part):
    line = lax.axis_index("sec") % LINES
    places = len(STEPS)
    codes = [jnp.max(plan[2 + i : 3 + i, :]) for i in range(2)]
    for index in part:
        for crossing in range(2):
            target = (own_place() ^ STEPS[index]) * LINES + (line ^ crossing)
            entries = [(code >> (target * 4)) & (2 * LINES * places - 1) for code in codes]
            source = [entry & (LINES * places - 1) for entry in entries]
            here = [
                (entry >= LINES * places) & (slot % LINES == line)
                for entry, slot in zip(entries, source)
            ]
            yield index, crossing, here, source


def merge_targets(plan, part, table, keep, cross):
    for index, crossing, here, source in line_targets(plan, part):
        total = 0.0
        for i in range(2):
            block = table[source[i] // LINES, i].astype(jnp.float32)
            total = total + jnp.where(here[i], block, 0.0)
        (keep, cross)[crossing][part.index(index)] = total.astype(jnp.bfloat16)


def merge_early_kernel(plan, *rest):
    *pieces, table, keep, cross = rest
    for step, piece in zip(STEPS, pieces):
        table[own_place() ^ step] = piece[...]
    merge_targets(plan, EARLY, table, keep, cross)


def merge_late_kernel(plan, table, keep, cross):
    merge_targets(plan, LATE, table, keep, cross)


def join_kernel(keep, arrived, *outs):
    for i, out in enumerate(outs):
        total = keep[i].astype(jnp.float32) + arrived[i].astype(jnp.float32)
        out[...] = total.astype(jnp.bfloat16)


def piece_rows(step, rows):
    return pl.ds(pl.multiple_of((own_place() ^ step) * rows, rows), rows)


def sum_kernel(plan, stay, *rest):
    *pieces, first = rest
    live = live_columns(plan, stay.shape[1])
    for step, piece in zip(STEPS, pieces):
        place = piece_rows(step, piece.shape[0])
        total = stay[place, :].astype(jnp.float32) + piece[...].astype(jnp.float32)
        first[place, :] = jnp.where(live, total, 0.0).astype(jnp.bfloat16)


def total_of(array):
    return jnp.sum(jnp.sum(array, axis=0, keepdims=True), axis=1, keepdims=True)


def make_tag(values, me):
    row = lax.broadcasted_iota(jnp.int32, (TAG, LANES), 0)
    lane = lax.broadcasted_iota(jnp.int32, (TAG, LANES), 1)
    spread = jnp.zeros((TAG, LANES), jnp.float32)
    for place, value in enumerate(values):
        spread = jnp.where(row // 3 == place, value, spread)
    high = spread.astype(jnp.bfloat16).astype(jnp.float32)
    middle = (spread - high).astype(jnp.bfloat16).astype(jnp.float32)
    low = spread - high - middle
    parts = jnp.where(row % 3 == 0, high, jnp.where(row % 3 == 1, middle, low))
    return jnp.where((lane == me) & (row < 3 * len(values)), parts, 0.0).astype(jnp.bfloat16)


def second_kernel(start, own, other, right, left, *rest):
    *pieces, deflated_out, block_vmem = rest
    half = start.shape[2]
    rows = block_vmem.shape[1]
    chunks = half // LANES
    basis = [start[h].astype(jnp.float32) for h in range(2)]
    firsts = [part.astype(jnp.float32) for part in in_order(own[...], other[...])]
    overlap = total_of(basis[0] * firsts[0]) + total_of(basis[1] * firsts[1])
    norm = total_of(basis[0] * basis[0]) + total_of(basis[1] * basis[1])
    quotient = jnp.where(norm > 0, overlap / jnp.where(norm > 0, norm, 1.0), 0.0)
    deflated = [firsts[h] - quotient * basis[h] for h in range(2)]
    rest_norm = total_of(deflated[0] * deflated[0]) + total_of(deflated[1] * deflated[1])
    for h in range(2):
        deflated_out[h] = deflated[h].astype(jnp.bfloat16)
    vector = jnp.concatenate(deflated, axis=1).astype(jnp.bfloat16)
    tag = make_tag((overlap, norm, quotient, rest_norm), lax.axis_index("sec"))
    for piece in pieces:
        piece[pl.ds(2 * chunks * rows, TAG), :] = tag
    for term in (1, 2):
        block = apply_term(right, left[0, term], vector, term)
        block_vmem[...] = block.astype(jnp.bfloat16).reshape(block_vmem.shape)
        for step, piece in zip(STEPS, pieces):
            part = block_vmem[own_place() ^ step]
            for c in range(chunks):
                place = pl.ds(((term - 1) * chunks + c) * rows, rows)
                piece[place, :] = part[:, c * LANES : (c + 1) * LANES]


def read_tag(tag):
    def value(place):
        parts = [tag[3 * place + i : 3 * place + i + 1, :] for i in range(3)]
        return parts[0] + parts[1] + parts[2]

    return [value(place) for place in range(4)]


def line_quotient(overlaps, norms, line):
    inside = lax.broadcasted_iota(jnp.int32, (1, LANES), 1) % LINES == line
    overlap = total_of(jnp.where(inside, overlaps, 0.0))
    norm = total_of(jnp.where(inside, norms, 0.0))
    return jnp.where(norm > 0, overlap / jnp.where(norm > 0, norm, 1.0), 0.0)


def mix_kernel(plan, *rest):
    keep, early, late, tag_out, new = rest[-5:]
    old, *pieces = rest[:-5]
    places, rows, half = keep.shape
    chunks = half // LANES
    tag = jnp.zeros((TAG, LANES), jnp.float32)
    for step, piece in zip(STEPS, pieces):
        new[own_place() ^ step] = piece[...]
        label = piece[pl.ds(2 * chunks * rows, TAG), :]
        tag = tag + label.astype(jnp.float32)
    tag_out[...] = tag.astype(jnp.bfloat16)
    early[pl.ds(len(EARLY) * chunks * rows, TAG), :] = tag.astype(jnp.bfloat16)
    overlaps, norms, quotients, _ = read_tag(tag)
    shifts = quotients - line_quotient(overlaps, norms, lax.axis_index("sec") % LINES)
    lane = lax.broadcasted_iota(jnp.int32, (1, LANES), 1)
    for index, crossing, here, source in line_targets(plan, range(places)):
        total = 0.0
        for i in range(2):
            where = source[i] // LINES
            block = jnp.concatenate(
                [new[where, pl.ds((i * chunks + c) * rows, rows), :] for c in range(chunks)],
                axis=1,
            ).astype(jnp.float32)
            shift = total_of(jnp.where(lane == source[i], shifts, 0.0))
            block = block + shift * old[where, i].astype(jnp.float32)
            total = total + jnp.where(here[i], block, 0.0)
        if crossing:
            total = total.astype(jnp.bfloat16)
            out, part = (early, EARLY) if index in EARLY else (late, LATE)
            for c in range(chunks):
                target = pl.ds((part.index(index) * chunks + c) * rows, rows)
                out[target, :] = total[:, c * LANES : (c + 1) * LANES]
        else:
            keep[index] = total


def join_early_kernel(plan, tag_line, keep, arrived, old_keep, old_arrived, *rest):
    *outs, factors = rest
    places, rows, half = keep.shape
    slots = places * LINES
    me = lax.axis_index("sec")
    live_count = places * rows * plan[1:2, 0:1].astype(jnp.float32)
    tag = tag_line[...].astype(jnp.float32)
    tag = tag + arrived[pl.ds(arrived.shape[0] - TAG, TAG), :].astype(jnp.float32)
    overlaps, norms, quotients, rests = read_tag(tag)
    quotient = total_of(overlaps) / total_of(norms)
    lane = lax.broadcasted_iota(jnp.int32, (1, LANES), 1)
    shifts = jnp.where(lane < slots, quotients - quotient, 0.0)
    resid_norm = total_of(rests + shifts * shifts * norms)
    scale = lax.rsqrt(resid_norm / live_count + 1e-06)
    own_shift = total_of(jnp.where(lane == me, shifts, 0.0))
    line = me % LINES
    shift_here = line_quotient(overlaps, norms, line) - quotient
    shift_there = line_quotient(overlaps, norms, 1 - line) - quotient
    row = lax.broadcasted_iota(jnp.int32, factors.shape, 0)
    values = jnp.where(row == 0, scale, scale * own_shift)
    values = jnp.where(row == 2, shift_here, values)
    factors[...] = jnp.where(row == 3, shift_there, values)
    weights = (scale, shift_here, shift_there)
    join_mixed(EARLY, weights, keep, arrived, old_keep, old_arrived, outs)


def join_late_kernel(factors, keep, arrived, old_keep, old_arrived, *outs):
    weights = [factors[i : i + 1, 0:1] for i in (0, 2, 3)]
    join_mixed(LATE, weights, keep, arrived, old_keep, old_arrived, outs)


def join_mixed(part, weights, keep, arrived, old_keep, old_arrived, outs):
    scale, shift_here, shift_there = weights
    rows, half = outs[0].shape
    chunks = half // LANES
    for i, index in enumerate(part):
        block = jnp.concatenate(
            [arrived[pl.ds((i * chunks + c) * rows, rows), :] for c in range(chunks)], axis=1
        ).astype(jnp.float32)
        block = block + shift_there * old_arrived[i].astype(jnp.float32)
        block = block + keep[index] + shift_here * old_keep[i].astype(jnp.float32)
        outs[i][...] = (scale * block).astype(jnp.bfloat16)


def final_kernel(plan, factors, stay, stay_2, first, *rest):
    *pieces, second, first_out = rest
    first_out[...] = first[...]
    live = live_columns(plan, stay.shape[1])
    scale, shift = factors[0:1, 0:1], factors[1:2, 0:1]
    for step, piece in zip(STEPS, pieces):
        place = piece_rows(step, piece.shape[0])
        total = scale * stay_2[place, :] + shift * stay[place, :].astype(jnp.float32)
        total = total + piece[...].astype(jnp.float32)
        second[place, :] = jnp.where(live, total, 0.0).astype(jnp.bfloat16)


SMEM = pl.BlockSpec(memory_space=pltpu.SMEM)
VMEM = pl.BlockSpec(memory_space=pltpu.VMEM)


def call(kernel, specs, outs, scratch=(), flops=0):
    return pl.pallas_call(
        kernel,
        out_shape=outs,
        in_specs=specs,
        out_specs=jax.tree.map(lambda _: VMEM, outs),
        scratch_shapes=scratch,
        compiler_params=pltpu.CompilerParams(vmem_limit_bytes=16 * 1024 * 1024),
        cost_estimate=pl.CostEstimate(flops=flops, bytes_accessed=1 << 18, transcendentals=0),
    )


def along_line(pieces, slots):
    sent = []
    for step, piece in zip(STEPS, pieces):
        pairs = [(slot, slot ^ (step * LINES)) for slot in range(slots)]
        sent.append(lax.ppermute(piece, "sec", pairs) if step else piece)
    return sent


def other_core(block):
    return lax.ppermute(block, "env", [(0, 1), (1, 0)])


def across(piece, slots):
    return lax.ppermute(piece, "sec", [(slot, slot ^ 1) for slot in range(slots)])


def on_device(amplitudes, widths, holders, left_env, right_env):
    slots_dev, right_dim, half = amplitudes.shape
    slots = holders.shape[0]
    assert slots_dev == 1
    if slots != 2 * QDOWN:
        return on_device_any(amplitudes, widths, holders, left_env, right_env)
    places = slots // LINES
    rows = right_dim // places
    dots = 6 * right_dim * half * (right_dim + 2 * half)
    block = jax.ShapeDtypeStruct((right_dim, half), jnp.bfloat16)
    wide = jax.ShapeDtypeStruct((right_dim, half), jnp.float32)
    pair = jax.ShapeDtypeStruct((2, rows, half), jnp.bfloat16)
    single = jax.ShapeDtypeStruct((rows, half), jnp.bfloat16)
    wides = jax.ShapeDtypeStruct((places, rows, half), jnp.float32)
    chunked = rows * half // LANES
    tagged = jax.ShapeDtypeStruct((2 * chunked + TAG, LANES), jnp.bfloat16)
    twos = jax.ShapeDtypeStruct((2, rows, half), jnp.bfloat16)
    early = jax.ShapeDtypeStruct((2 * chunked + TAG, LANES), jnp.bfloat16)
    late = jax.ShapeDtypeStruct((2 * chunked, LANES), jnp.bfloat16)
    label = jax.ShapeDtypeStruct((TAG, LANES), jnp.bfloat16)
    factor_shape = jax.ShapeDtypeStruct((8, LANES), jnp.float32)
    plan_shape = jax.ShapeDtypeStruct((8, LANES), jnp.int32)
    split = [pltpu.VMEM((places, rows, half), jnp.bfloat16)]
    table_shape = jax.ShapeDtypeStruct((places, *pair.shape), jnp.bfloat16)
    new_table = [pltpu.VMEM((places, *tagged.shape), jnp.bfloat16)]

    slot_table = [pltpu.SMEM((slots,), jnp.int32)]
    plan = call(plan_kernel, [SMEM, SMEM], plan_shape, slot_table)(widths, holders)
    both = jax.ShapeDtypeStruct((2, right_dim, half), jnp.bfloat16)
    number = jax.ShapeDtypeStruct((8, half), jnp.int32)
    columns = call(columns_kernel, [], number, flops=4 << 30)()
    *pieces, start_full = call(
        first_kernel, [VMEM] * 7, (pair,) * places + (both,), split, dots
    )(
        columns,
        widths[None],
        holders[None],
        amplitudes[0],
        other_core(amplitudes[0]),
        right_env,
        left_env,
    )
    old = along_line(pieces, slots)
    stay = call(stay_kernel, [VMEM] * 3, block, flops=dots // 3)(start_full, right_env, left_env)
    table, keep_early, cross = call(
        merge_early_kernel, [VMEM] * (1 + places), (table_shape, twos, twos)
    )(plan, *old)
    old_early = across(cross, slots)
    keep_late, cross = call(merge_late_kernel, [VMEM] * 2, (twos, twos))(plan, table)
    old_early, cross = lax.optimization_barrier((old_early, cross))
    old_late = across(cross, slots)
    far = call(join_kernel, [VMEM] * 2, (single,) * 2)(keep_early, old_early)
    near = call(join_kernel, [VMEM] * 2, (single,) * 2)(keep_late, old_late)
    joined = (near[0], *far, near[1])
    first = call(sum_kernel, [VMEM] * (2 + places), block)(
        plan, stay, *along_line(joined, slots)
    )

    *pieces, deflated = call(
        second_kernel, [VMEM] * 5, (tagged,) * places + (both,), split, dots
    )(start_full, first, other_core(first), right_env, left_env)
    new = along_line(pieces, slots)
    stay_2 = call(stay_kernel, [VMEM] * 3, wide, flops=dots // 3)(deflated, right_env, left_env)
    keep, *cross, tag = call(
        mix_kernel, [VMEM] * (2 + places), (wides, early, late, label), new_table
    )(plan, table, *new)
    new_early, cross_late = lax.optimization_barrier((across(cross[0], slots), cross[1]))
    new_late = across(cross_late, slots)
    *far, factors = call(join_early_kernel, [VMEM] * 6, (single, single, factor_shape))(
        plan, tag, keep, new_early, keep_early, old_early
    )
    near = call(join_late_kernel, [VMEM] * 5, (single,) * 2)(
        factors, keep, new_late, keep_late, old_late
    )
    joined = (near[0], *far, near[1])
    second, first = call(final_kernel, [VMEM] * (5 + places), (block, block))(
        plan, factors, stay, stay_2, first, *along_line(joined, slots)
    )
    return first[None], second[None]


def solution(mesh):
    in_specs = (
        P(("runs", "sec"), None, "env"),
        P("runs"),
        P("runs"),
        P(("runs", "sec"), None, None, "env"),
        P("runs", None, None),
    )
    out_specs = (P(("runs", "sec"), None, "env"), P(("runs", "sec"), None, "env"))
    return jax.shard_map(
        on_device, mesh=mesh, in_specs=in_specs, out_specs=out_specs, check_vma=False
    )
```

```python
import jax
import jax.numpy as jnp
from jax import lax
from jax.experimental import pallas as pl
from jax.experimental.pallas import tpu as pltpu
from jax.sharding import PartitionSpec as P

QDOWN = 4

term_shifts = ((0, 0), (1, 0), (0, 1))


def route(holders):
    n_slots = holders.shape[0]
    sector_ids = jnp.arange(n_slots, dtype=jnp.int32)
    slot_of = jnp.argmax(holders[None, :] == sector_ids[:, None], axis=1)
    sources = []
    allowed = []
    for up, down in term_shifts[1:]:
        permitted = (holders // QDOWN - up >= 0) & (holders % QDOWN - down >= 0)
        wanted = jnp.clip(holders - QDOWN * up - down, 0, n_slots - 1)
        sources.append(slot_of[wanted])
        allowed.append(permitted)
    return sources, allowed


def contract(vector, left_env, right_env):
    products = jnp.einsum(
        "tij,jw->tiw", right_env, vector, preferred_element_type=jnp.float32
    ).astype(jnp.bfloat16)
    return jnp.einsum("tik,tkw->tiw", products, left_env, preferred_element_type=jnp.float32)


def spread(blocks, n_slots):
    terms, rows, width = blocks.shape
    pieces = blocks.reshape(terms, n_slots, rows // n_slots, width).swapaxes(0, 1)
    return lax.all_to_all(pieces, "sec", split_axis=0, concat_axis=0)


def collect(merged):
    n_slots, rows, width = merged.shape
    home = lax.all_to_all(merged, "sec", split_axis=0, concat_axis=0)
    return home.reshape(n_slots * rows, width)


def share(values, n_slots, me):
    lanes = jnp.zeros((1, 128), jnp.float32).at[0, : values.shape[0]].set(values)
    if n_slots & (n_slots - 1) or n_slots > 16:
        return lax.all_gather(lanes[0], "sec")
    table = jnp.where(jnp.arange(n_slots)[:, None] == me, lanes, 0.0)
    for offset in range(1, n_slots):
        pairs = [(i, i ^ offset) for i in range(n_slots)]
        other = lax.ppermute(lanes, "sec", pairs)
        table = jnp.where(jnp.arange(n_slots)[:, None] == (me ^ offset), other, table)
    return table


def merge(received, sources, allowed):
    total = 0.0
    for term, (source, permitted) in enumerate(zip(sources, allowed)):
        picked = received[source, term]
        total = total + jnp.where(permitted[:, None, None], picked, 0).astype(jnp.float32)
    return total


def on_device_any(amplitudes, widths, holders, left_env, right_env):
    slots_dev, right_dim, half_width = amplitudes.shape
    assert slots_dev == 1
    n_slots = holders.shape[0]
    me = lax.axis_index("sec")
    side = lax.axis_index("env")
    my_width = widths[holders[me]]
    row_index = side * half_width + jnp.arange(half_width, dtype=jnp.int32)
    live = (row_index < my_width)[None, :]
    sources, allowed = route(holders)
    envs = left_env[0]

    start = jnp.where(live, amplitudes[0], jnp.zeros_like(amplitudes[0]))
    start_full = lax.all_gather(start, "env", axis=1, tiled=True)
    outgoing = contract(start_full, envs, right_env).astype(jnp.bfloat16)
    stay = outgoing[0].astype(jnp.float32)
    received = spread(outgoing[1:], n_slots)
    arrived = collect(merge(received, sources, allowed).astype(jnp.bfloat16))
    first = jnp.where(live, stay + arrived.astype(jnp.float32), 0.0).astype(jnp.bfloat16)

    first_full = lax.all_gather(first, "env", axis=1, tiled=True).astype(jnp.float32)
    basis = start_full.astype(jnp.float32)
    overlap = jnp.sum(basis * first_full)
    norm = jnp.sum(basis * basis)
    own_quotient = jnp.where(norm > 0, overlap / jnp.where(norm > 0, norm, 1.0), 0.0)
    deflated = first_full - own_quotient * basis
    rest = jnp.sum(deflated * deflated)
    sums = share(jnp.stack([overlap, norm, own_quotient, rest]), n_slots, me)
    outgoing_2 = contract(deflated.astype(jnp.bfloat16), envs, right_env)
    received_2 = spread(outgoing_2[1:].astype(jnp.bfloat16), n_slots)

    quotient = jnp.sum(sums[:, 0]) / jnp.sum(sums[:, 1])
    shift = sums[:, 2] - quotient
    resid_norm = jnp.sum(sums[:, 3] + shift * shift * sums[:, 1])
    live_count = right_dim * jnp.sum(widths).astype(jnp.float32)
    scale = lax.rsqrt(resid_norm / live_count + 1e-06)
    mixed = received_2.astype(jnp.float32) + shift[:, None, None, None] * received.astype(
        jnp.float32
    )
    merged_2 = scale * merge(mixed, sources, allowed)
    arrived_2 = collect(merged_2.astype(jnp.bfloat16))
    stay_2 = scale * (outgoing_2[0] + (own_quotient - quotient) * stay)
    second = jnp.where(live, stay_2 + arrived_2.astype(jnp.float32), 0.0).astype(jnp.bfloat16)
    return first[None], second[None]


LANES = 128
TAG = 16
LINES = 2
STEPS = (0, 3, 2, 1)
EARLY, LATE = (1, 2), (0, 3)


def plan_kernel(widths, holders, plan, slot_of):
    slots = holders.shape[0]
    me = lax.axis_index("sec")
    total = jnp.int32(0)
    for s in range(slots):
        slot_of[holders[s]] = jnp.int32(s)
        total = total + widths[s]
    codes = [jnp.int32(0), jnp.int32(0)]
    for target in range(slots):
        sector = holders[target]
        has = (sector >= QDOWN, sector % QDOWN > 0)
        source = (slot_of[sector & (QDOWN - 1)], slot_of[jnp.maximum(sector - 1, 0)])
        for i in range(2):
            entry = jnp.where(has[i], source[i] + slots, 0)
            codes[i] = codes[i] | (entry << (target * 4))
    row = lax.broadcasted_iota(jnp.int32, plan.shape, 0)
    values = jnp.where(row == 0, widths[holders[me]], total)
    values = jnp.where(row == 2, codes[0], values)
    plan[...] = jnp.where(row == 3, codes[1], values)


def live_columns(plan, half):
    first_column = lax.axis_index("env") * half
    return first_column + lax.broadcasted_iota(jnp.int32, (1, half), 1) < plan[0:1, 0:1]


def contract_right(right, vector, first, terms):
    rows = right.shape[1]
    stacked = right[pl.ds(first, terms)].reshape(terms * rows, rows)
    products = jnp.dot(stacked, vector, preferred_element_type=jnp.float32)
    return products.astype(jnp.bfloat16)


def contract_left(products, left):
    return jnp.dot(products, left, preferred_element_type=jnp.float32)


def in_order(own, other):
    upper = lax.axis_index("env") > 0
    return [jnp.where(upper, other, own), jnp.where(upper, own, other)]


def own_place():
    return lax.axis_index("sec") // LINES


def columns_kernel(columns):
    columns[...] = lax.broadcasted_iota(jnp.int32, columns.shape, 1)


def first_kernel(columns, widths, holders, own, other, right, left, *rest):
    *pieces, start, block_vmem = rest
    half = start.shape[2]
    slot = lax.broadcasted_iota(jnp.int32, widths.shape, 1)
    mine = jnp.where(slot == lax.axis_index("sec"), holders[...], 0)
    sector = jnp.sum(mine, axis=1, keepdims=True)
    width = jnp.sum(jnp.where(slot == sector, widths[...], 0), axis=1, keepdims=True)
    for h, part in enumerate(in_order(own[...], other[...])):
        live = h * half + columns[0:1, :] < width
        start[h] = jnp.where(live, part, jnp.zeros_like(part))
    vector = jnp.concatenate([start[0], start[1]], axis=1)
    products = contract_right(right, vector, 1, 2)
    rows = products.shape[0] // 2
    for term in (1, 2):
        block = contract_left(products[(term - 1) * rows : term * rows], left[0, term])
        block = block.astype(jnp.bfloat16)
        block_vmem[...] = block.reshape(block_vmem.shape)
        for step, piece in zip(STEPS, pieces):
            piece[term - 1] = block_vmem[own_place() ^ step]


def stay_kernel(vector, right, left, stay):
    products = contract_right(right, jnp.concatenate([vector[0], vector[1]], axis=1), 0, 1)
    block = contract_left(products, left[0, 0])
    stay[...] = block.astype(stay.dtype)


def line_targets(plan, part):
    line = lax.axis_index("sec") % LINES
    places = len(STEPS)
    codes = [jnp.max(plan[2 + i : 3 + i, :]) for i in range(2)]
    for index in part:
        for crossing in range(2):
            target = (own_place() ^ STEPS[index]) * LINES + (line ^ crossing)
            entries = [(code >> (target * 4)) & (2 * LINES * places - 1) for code in codes]
            source = [entry & (LINES * places - 1) for entry in entries]
            here = [
                (entry >= LINES * places) & (slot % LINES == line)
                for entry, slot in zip(entries, source)
            ]
            yield index, crossing, here, source


def merge_targets(plan, part, table, keep, cross):
    for index, crossing, here, source in line_targets(plan, part):
        total = 0.0
        for i in range(2):
            block = table[source[i] // LINES, i].astype(jnp.float32)
            total = total + jnp.where(here[i], block, 0.0)
        (keep, cross)[crossing][part.index(index)] = total.astype(jnp.bfloat16)


def merge_early_kernel(plan, *rest):
    *pieces, table, keep, cross = rest
    for step, piece in zip(STEPS, pieces):
        table[own_place() ^ step] = piece[...]
    merge_targets(plan, EARLY, table, keep, cross)


def merge_late_kernel(plan, table, keep, cross):
    merge_targets(plan, LATE, table, keep, cross)


def join_kernel(keep, arrived, *outs):
    for i, out in enumerate(outs):
        total = keep[i].astype(jnp.float32) + arrived[i].astype(jnp.float32)
        out[...] = total.astype(jnp.bfloat16)


def piece_rows(step, rows):
    return pl.ds(pl.multiple_of((own_place() ^ step) * rows, rows), rows)


def sum_kernel(plan, stay, *rest):
    *pieces, first = rest
    live = live_columns(plan, stay.shape[1])
    for step, piece in zip(STEPS, pieces):
        place = piece_rows(step, piece.shape[0])
        total = stay[place, :].astype(jnp.float32) + piece[...].astype(jnp.float32)
        first[place, :] = jnp.where(live, total, 0.0).astype(jnp.bfloat16)


def total_of(array):
    return jnp.sum(jnp.sum(array, axis=0, keepdims=True), axis=1, keepdims=True)


def make_tag(values, me):
    row = lax.broadcasted_iota(jnp.int32, (TAG, LANES), 0)
    lane = lax.broadcasted_iota(jnp.int32, (TAG, LANES), 1)
    spread = jnp.zeros((TAG, LANES), jnp.float32)
    for place, value in enumerate(values):
        spread = jnp.where(row // 3 == place, value, spread)
    high = spread.astype(jnp.bfloat16).astype(jnp.float32)
    middle = (spread - high).astype(jnp.bfloat16).astype(jnp.float32)
    low = spread - high - middle
    parts = jnp.where(row % 3 == 0, high, jnp.where(row % 3 == 1, middle, low))
    return jnp.where((lane == me) & (row < 3 * len(values)), parts, 0.0).astype(jnp.bfloat16)


def second_kernel(start, own, other, right, left, *rest):
    *pieces, deflated_out, block_vmem = rest
    half = start.shape[2]
    rows = block_vmem.shape[1]
    chunks = half // LANES
    basis = [start[h].astype(jnp.float32) for h in range(2)]
    firsts = [part.astype(jnp.float32) for part in in_order(own[...], other[...])]
    overlap = total_of(basis[0] * firsts[0]) + total_of(basis[1] * firsts[1])
    norm = total_of(basis[0] * basis[0]) + total_of(basis[1] * basis[1])
    quotient = jnp.where(norm > 0, overlap / jnp.where(norm > 0, norm, 1.0), 0.0)
    deflated = [firsts[h] - quotient * basis[h] for h in range(2)]
    rest_norm = total_of(deflated[0] * deflated[0]) + total_of(deflated[1] * deflated[1])
    for h in range(2):
        deflated_out[h] = deflated[h].astype(jnp.bfloat16)
    vector = jnp.concatenate(deflated, axis=1).astype(jnp.bfloat16)
    tag = make_tag((overlap, norm, quotient, rest_norm), lax.axis_index("sec"))
    for piece in pieces:
        piece[pl.ds(2 * chunks * rows, TAG), :] = tag
    products = contract_right(right, vector, 1, 2)
    right_rows = products.shape[0] // 2
    for term in (1, 2):
        block = contract_left(
            products[(term - 1) * right_rows : term * right_rows], left[0, term]
        )
        block_vmem[...] = block.astype(jnp.bfloat16).reshape(block_vmem.shape)
        for step, piece in zip(STEPS, pieces):
            part = block_vmem[own_place() ^ step]
            for c in range(chunks):
                place = pl.ds(((term - 1) * chunks + c) * rows, rows)
                piece[place, :] = part[:, c * LANES : (c + 1) * LANES]


def read_tag(tag):
    def value(place):
        parts = [tag[3 * place + i : 3 * place + i + 1, :] for i in range(3)]
        return parts[0] + parts[1] + parts[2]

    return [value(place) for place in range(4)]


def line_quotient(overlaps, norms, line):
    inside = lax.broadcasted_iota(jnp.int32, (1, LANES), 1) % LINES == line
    overlap = total_of(jnp.where(inside, overlaps, 0.0))
    norm = total_of(jnp.where(inside, norms, 0.0))
    return jnp.where(norm > 0, overlap / jnp.where(norm > 0, norm, 1.0), 0.0)


def mix_targets(plan, part, old, new, tag, keep, cross):
    rows, half = keep.shape[1:]
    chunks = half // LANES
    overlaps, norms, quotients, _ = read_tag(tag)
    shifts = quotients - line_quotient(overlaps, norms, lax.axis_index("sec") % LINES)
    lane = lax.broadcasted_iota(jnp.int32, (1, LANES), 1)
    for index, crossing, here, source in line_targets(plan, part):
        position = part.index(index)
        total = 0.0
        for i in range(2):
            where = source[i] // LINES
            block = jnp.concatenate(
                [new[where, pl.ds((i * chunks + c) * rows, rows), :] for c in range(chunks)],
                axis=1,
            ).astype(jnp.float32)
            shift = total_of(jnp.where(lane == source[i], shifts, 0.0))
            block = block + shift * old[where, i].astype(jnp.float32)
            total = total + jnp.where(here[i], block, 0.0)
        if crossing:
            total = total.astype(jnp.bfloat16)
            for c in range(chunks):
                target = pl.ds((position * chunks + c) * rows, rows)
                cross[target, :] = total[:, c * LANES : (c + 1) * LANES]
        else:
            keep[position] = total


def mix_early_kernel(plan, old, *rest):
    *pieces, new, keep, cross, tag_out = rest
    tag = jnp.zeros((TAG, LANES), jnp.float32)
    for step, piece in zip(STEPS, pieces):
        new[own_place() ^ step] = piece[...]
        tag = tag + piece[pl.ds(piece.shape[0] - TAG, TAG), :].astype(jnp.float32)
    tag_out[...] = tag.astype(jnp.bfloat16)
    cross[pl.ds(cross.shape[0] - TAG, TAG), :] = tag.astype(jnp.bfloat16)
    mix_targets(plan, EARLY, old, new, tag, keep, cross)


def mix_late_kernel(plan, old, new, tag, keep, cross):
    mix_targets(plan, LATE, old, new, tag[...].astype(jnp.float32), keep, cross)


def join_early_kernel(plan, tag_line, keep, arrived, old_keep, old_arrived, *rest):
    *outs, factors = rest
    rows = keep.shape[1]
    places = len(STEPS)
    slots = places * LINES
    me = lax.axis_index("sec")
    live_count = places * rows * plan[1:2, 0:1].astype(jnp.float32)
    tag = tag_line[...].astype(jnp.float32)
    tag = tag + arrived[pl.ds(arrived.shape[0] - TAG, TAG), :].astype(jnp.float32)
    overlaps, norms, quotients, rests = read_tag(tag)
    quotient = total_of(overlaps) / total_of(norms)
    lane = lax.broadcasted_iota(jnp.int32, (1, LANES), 1)
    shifts = jnp.where(lane < slots, quotients - quotient, 0.0)
    resid_norm = total_of(rests + shifts * shifts * norms)
    scale = lax.rsqrt(resid_norm / live_count + 1e-06)
    own_shift = total_of(jnp.where(lane == me, shifts, 0.0))
    line = me % LINES
    shift_here = line_quotient(overlaps, norms, line) - quotient
    shift_there = line_quotient(overlaps, norms, 1 - line) - quotient
    row = lax.broadcasted_iota(jnp.int32, factors.shape, 0)
    values = jnp.where(row == 0, scale, scale * own_shift)
    values = jnp.where(row == 2, shift_here, values)
    factors[...] = jnp.where(row == 3, shift_there, values)
    weights = (scale, shift_here, shift_there)
    join_mixed(weights, keep, arrived, old_keep, old_arrived, outs)


def join_late_kernel(factors, keep, arrived, old_keep, old_arrived, *outs):
    weights = [factors[i : i + 1, 0:1] for i in (0, 2, 3)]
    join_mixed(weights, keep, arrived, old_keep, old_arrived, outs)


def join_mixed(weights, keep, arrived, old_keep, old_arrived, outs):
    scale, shift_here, shift_there = weights
    rows, half = outs[0].shape
    chunks = half // LANES
    for i, out in enumerate(outs):
        block = jnp.concatenate(
            [arrived[pl.ds((i * chunks + c) * rows, rows), :] for c in range(chunks)], axis=1
        ).astype(jnp.float32)
        block = block + shift_there * old_arrived[i].astype(jnp.float32)
        block = block + keep[i] + shift_here * old_keep[i].astype(jnp.float32)
        out[...] = (scale * block).astype(jnp.bfloat16)


def final_kernel(plan, factors, stay, stay_2, first, *rest):
    *pieces, second, first_out = rest
    first_out[...] = first[...]
    live = live_columns(plan, stay.shape[1])
    scale, shift = factors[0:1, 0:1], factors[1:2, 0:1]
    for step, piece in zip(STEPS, pieces):
        place = piece_rows(step, piece.shape[0])
        total = scale * stay_2[place, :] + shift * stay[place, :].astype(jnp.float32)
        total = total + piece[...].astype(jnp.float32)
        second[place, :] = jnp.where(live, total, 0.0).astype(jnp.bfloat16)


SMEM = pl.BlockSpec(memory_space=pltpu.SMEM)
VMEM = pl.BlockSpec(memory_space=pltpu.VMEM)


def call(kernel, specs, outs, scratch=(), flops=0):
    return pl.pallas_call(
        kernel,
        out_shape=outs,
        in_specs=specs,
        out_specs=jax.tree.map(lambda _: VMEM, outs),
        scratch_shapes=scratch,
        compiler_params=pltpu.CompilerParams(vmem_limit_bytes=16 * 1024 * 1024),
        cost_estimate=pl.CostEstimate(flops=flops, bytes_accessed=1 << 18, transcendentals=0),
    )


def along_line(pieces, slots):
    sent = []
    for step, piece in zip(STEPS, pieces):
        pairs = [(slot, slot ^ (step * LINES)) for slot in range(slots)]
        sent.append(lax.ppermute(piece, "sec", pairs) if step else piece)
    return sent


def other_core(block):
    return lax.ppermute(block, "env", [(0, 1), (1, 0)])


def across(piece, slots):
    return lax.ppermute(piece, "sec", [(slot, slot ^ 1) for slot in range(slots)])


def on_device(amplitudes, widths, holders, left_env, right_env):
    slots_dev, right_dim, half = amplitudes.shape
    slots = holders.shape[0]
    assert slots_dev == 1
    if slots != 2 * QDOWN:
        return on_device_any(amplitudes, widths, holders, left_env, right_env)
    places = slots // LINES
    rows = right_dim // places
    dots = 6 * right_dim * half * (right_dim + 2 * half)
    block = jax.ShapeDtypeStruct((right_dim, half), jnp.bfloat16)
    wide = jax.ShapeDtypeStruct((right_dim, half), jnp.float32)
    pair = jax.ShapeDtypeStruct((2, rows, half), jnp.bfloat16)
    single = jax.ShapeDtypeStruct((rows, half), jnp.bfloat16)
    wides = jax.ShapeDtypeStruct((2, rows, half), jnp.float32)
    chunked = rows * half // LANES
    tagged = jax.ShapeDtypeStruct((2 * chunked + TAG, LANES), jnp.bfloat16)
    twos = jax.ShapeDtypeStruct((2, rows, half), jnp.bfloat16)
    early = jax.ShapeDtypeStruct((2 * chunked + TAG, LANES), jnp.bfloat16)
    late = jax.ShapeDtypeStruct((2 * chunked, LANES), jnp.bfloat16)
    label = jax.ShapeDtypeStruct((TAG, LANES), jnp.bfloat16)
    factor_shape = jax.ShapeDtypeStruct((8, LANES), jnp.float32)
    plan_shape = jax.ShapeDtypeStruct((8, LANES), jnp.int32)
    split = [pltpu.VMEM((places, rows, half), jnp.bfloat16)]
    table_shape = jax.ShapeDtypeStruct((places, *pair.shape), jnp.bfloat16)
    new_shape = jax.ShapeDtypeStruct((places, *tagged.shape), jnp.bfloat16)

    slot_table = [pltpu.SMEM((slots,), jnp.int32)]
    plan = call(plan_kernel, [SMEM, SMEM], plan_shape, slot_table)(widths, holders)
    both = jax.ShapeDtypeStruct((2, right_dim, half), jnp.bfloat16)
    number = jax.ShapeDtypeStruct((8, half), jnp.int32)
    columns = call(columns_kernel, [], number, flops=4 << 30)()
    *pieces, start_full = call(
        first_kernel, [VMEM] * 7, (pair,) * places + (both,), split, dots
    )(
        columns,
        widths[None],
        holders[None],
        amplitudes[0],
        other_core(amplitudes[0]),
        right_env,
        left_env,
    )
    old = along_line(pieces, slots)
    stay = call(stay_kernel, [VMEM] * 3, block, flops=dots // 3)(start_full, right_env, left_env)
    table, keep_early, cross = call(
        merge_early_kernel, [VMEM] * (1 + places), (table_shape, twos, twos)
    )(plan, *old)
    old_early = across(cross, slots)
    keep_late, cross = call(merge_late_kernel, [VMEM] * 2, (twos, twos))(plan, table)
    old_late = across(cross, slots)
    far = call(join_kernel, [VMEM] * 2, (single,) * 2)(keep_early, old_early)
    near = call(join_kernel, [VMEM] * 2, (single,) * 2)(keep_late, old_late)
    joined = (near[0], *far, near[1])
    first = call(sum_kernel, [VMEM] * (2 + places), block)(
        plan, stay, *along_line(joined, slots)
    )

    *pieces, deflated = call(
        second_kernel, [VMEM] * 5, (tagged,) * places + (both,), split, dots
    )(start_full, first, other_core(first), right_env, left_env)
    new = along_line(pieces, slots)
    stay_2 = call(stay_kernel, [VMEM] * 3, wide, flops=dots // 3)(deflated, right_env, left_env)
    new_table, wide_early, cross, tag = call(
        mix_early_kernel, [VMEM] * (2 + places), (new_shape, wides, early, label)
    )(plan, table, *new)
    new_early = across(cross, slots)
    wide_late, cross = call(mix_late_kernel, [VMEM] * 4, (wides, late))(plan, table, new_table, tag)
    new_late = across(cross, slots)
    *far, factors = call(join_early_kernel, [VMEM] * 6, (single, single, factor_shape))(
        plan, tag, wide_early, new_early, keep_early, old_early
    )
    near = call(join_late_kernel, [VMEM] * 5, (single,) * 2)(
        factors, wide_late, new_late, keep_late, old_late
    )
    joined = (near[0], *far, near[1])
    second, first = call(final_kernel, [VMEM] * (5 + places), (block, block))(
        plan, factors, stay, stay_2, first, *along_line(joined, slots)
    )
    return first[None], second[None]


def solution(mesh):
    in_specs = (
        P(("runs", "sec"), None, "env"),
        P("runs"),
        P("runs"),
        P(("runs", "sec"), None, None, "env"),
        P("runs", None, None),
    )
    out_specs = (P(("runs", "sec"), None, "env"), P(("runs", "sec"), None, "env"))
    return jax.shard_map(
        on_device, mesh=mesh, in_specs=in_specs, out_specs=out_specs, check_vma=False
    )
```

```python
import jax
import jax.numpy as jnp
from jax import lax
from jax.experimental import pallas as pl
from jax.experimental.pallas import tpu as pltpu
from jax.sharding import PartitionSpec as P

QDOWN = 4

term_shifts = ((0, 0), (1, 0), (0, 1))


def route(holders):
    n_slots = holders.shape[0]
    sector_ids = jnp.arange(n_slots, dtype=jnp.int32)
    slot_of = jnp.argmax(holders[None, :] == sector_ids[:, None], axis=1)
    sources = []
    allowed = []
    for up, down in term_shifts[1:]:
        permitted = (holders // QDOWN - up >= 0) & (holders % QDOWN - down >= 0)
        wanted = jnp.clip(holders - QDOWN * up - down, 0, n_slots - 1)
        sources.append(slot_of[wanted])
        allowed.append(permitted)
    return sources, allowed


def contract(vector, left_env, right_env):
    products = jnp.einsum(
        "tij,jw->tiw", right_env, vector, preferred_element_type=jnp.float32
    ).astype(jnp.bfloat16)
    return jnp.einsum("tik,tkw->tiw", products, left_env, preferred_element_type=jnp.float32)


def spread(blocks, n_slots):
    terms, rows, width = blocks.shape
    pieces = blocks.reshape(terms, n_slots, rows // n_slots, width).swapaxes(0, 1)
    return lax.all_to_all(pieces, "sec", split_axis=0, concat_axis=0)


def collect(merged):
    n_slots, rows, width = merged.shape
    home = lax.all_to_all(merged, "sec", split_axis=0, concat_axis=0)
    return home.reshape(n_slots * rows, width)


def share(values, n_slots, me):
    lanes = jnp.zeros((1, 128), jnp.float32).at[0, : values.shape[0]].set(values)
    if n_slots & (n_slots - 1) or n_slots > 16:
        return lax.all_gather(lanes[0], "sec")
    table = jnp.where(jnp.arange(n_slots)[:, None] == me, lanes, 0.0)
    for offset in range(1, n_slots):
        pairs = [(i, i ^ offset) for i in range(n_slots)]
        other = lax.ppermute(lanes, "sec", pairs)
        table = jnp.where(jnp.arange(n_slots)[:, None] == (me ^ offset), other, table)
    return table


def merge(received, sources, allowed):
    total = 0.0
    for term, (source, permitted) in enumerate(zip(sources, allowed)):
        picked = received[source, term]
        total = total + jnp.where(permitted[:, None, None], picked, 0).astype(jnp.float32)
    return total


def on_device_any(amplitudes, widths, holders, left_env, right_env):
    slots_dev, right_dim, half_width = amplitudes.shape
    assert slots_dev == 1
    n_slots = holders.shape[0]
    me = lax.axis_index("sec")
    side = lax.axis_index("env")
    my_width = widths[holders[me]]
    row_index = side * half_width + jnp.arange(half_width, dtype=jnp.int32)
    live = (row_index < my_width)[None, :]
    sources, allowed = route(holders)
    envs = left_env[0]

    start = jnp.where(live, amplitudes[0], jnp.zeros_like(amplitudes[0]))
    start_full = lax.all_gather(start, "env", axis=1, tiled=True)
    outgoing = contract(start_full, envs, right_env).astype(jnp.bfloat16)
    stay = outgoing[0].astype(jnp.float32)
    received = spread(outgoing[1:], n_slots)
    arrived = collect(merge(received, sources, allowed).astype(jnp.bfloat16))
    first = jnp.where(live, stay + arrived.astype(jnp.float32), 0.0).astype(jnp.bfloat16)

    first_full = lax.all_gather(first, "env", axis=1, tiled=True).astype(jnp.float32)
    basis = start_full.astype(jnp.float32)
    overlap = jnp.sum(basis * first_full)
    norm = jnp.sum(basis * basis)
    own_quotient = jnp.where(norm > 0, overlap / jnp.where(norm > 0, norm, 1.0), 0.0)
    deflated = first_full - own_quotient * basis
    rest = jnp.sum(deflated * deflated)
    sums = share(jnp.stack([overlap, norm, own_quotient, rest]), n_slots, me)
    outgoing_2 = contract(deflated.astype(jnp.bfloat16), envs, right_env)
    received_2 = spread(outgoing_2[1:].astype(jnp.bfloat16), n_slots)

    quotient = jnp.sum(sums[:, 0]) / jnp.sum(sums[:, 1])
    shift = sums[:, 2] - quotient
    resid_norm = jnp.sum(sums[:, 3] + shift * shift * sums[:, 1])
    live_count = right_dim * jnp.sum(widths).astype(jnp.float32)
    scale = lax.rsqrt(resid_norm / live_count + 1e-06)
    mixed = received_2.astype(jnp.float32) + shift[:, None, None, None] * received.astype(
        jnp.float32
    )
    merged_2 = scale * merge(mixed, sources, allowed)
    arrived_2 = collect(merged_2.astype(jnp.bfloat16))
    stay_2 = scale * (outgoing_2[0] + (own_quotient - quotient) * stay)
    second = jnp.where(live, stay_2 + arrived_2.astype(jnp.float32), 0.0).astype(jnp.bfloat16)
    return first[None], second[None]


LANES = 128
TAG = 16
LINES = 2
STEPS = (0, 3, 2, 1)
EARLY, LATE = (1, 2), (0, 3)


def plan_kernel(widths, holders, plan, slot_of):
    slots = holders.shape[0]
    me = lax.axis_index("sec")
    total = jnp.int32(0)
    for s in range(slots):
        slot_of[holders[s]] = jnp.int32(s)
        total = total + widths[s]
    codes = [jnp.int32(0), jnp.int32(0)]
    for target in range(slots):
        sector = holders[target]
        has = (sector >= QDOWN, sector % QDOWN > 0)
        source = (slot_of[sector & (QDOWN - 1)], slot_of[jnp.maximum(sector - 1, 0)])
        for i in range(2):
            entry = jnp.where(has[i], source[i] + slots, 0)
            codes[i] = codes[i] | (entry << (target * 4))
    row = lax.broadcasted_iota(jnp.int32, plan.shape, 0)
    values = jnp.where(row == 0, widths[holders[me]], total)
    values = jnp.where(row == 2, codes[0], values)
    plan[...] = jnp.where(row == 3, codes[1], values)


def live_columns(plan, half):
    first_column = lax.axis_index("env") * half
    return first_column + lax.broadcasted_iota(jnp.int32, (1, half), 1) < plan[0:1, 0:1]


def contract_right(right, vector, first, terms):
    rows = right.shape[1]
    stacked = right[pl.ds(first, terms)].reshape(terms * rows, rows)
    products = jnp.dot(stacked, vector, preferred_element_type=jnp.float32)
    return products.astype(jnp.bfloat16)


def contract_left(products, left):
    return jnp.dot(products, left, preferred_element_type=jnp.float32)


def in_order(own, other):
    upper = lax.axis_index("env") > 0
    return [jnp.where(upper, other, own), jnp.where(upper, own, other)]


def own_place():
    return lax.axis_index("sec") // LINES


def columns_kernel(columns):
    columns[...] = lax.broadcasted_iota(jnp.int32, columns.shape, 1)


def first_kernel(columns, widths, holders, own, other, right, left, *rest):
    *pieces, start, block_vmem = rest
    half = start.shape[2]
    slot = lax.broadcasted_iota(jnp.int32, widths.shape, 1)
    mine = jnp.where(slot == lax.axis_index("sec"), holders[...], 0)
    sector = jnp.sum(mine, axis=1, keepdims=True)
    width = jnp.sum(jnp.where(slot == sector, widths[...], 0), axis=1, keepdims=True)
    for h, part in enumerate(in_order(own[...], other[...])):
        live = h * half + columns[0:1, :] < width
        start[h] = jnp.where(live, part, jnp.zeros_like(part))
    vector = jnp.concatenate([start[0], start[1]], axis=1)
    products = contract_right(right, vector, 1, 2)
    rows = products.shape[0] // 2
    for term in (1, 2):
        block = contract_left(products[(term - 1) * rows : term * rows], left[0, term])
        block = block.astype(jnp.bfloat16)
        block_vmem[...] = block.reshape(block_vmem.shape)
        for step, piece in zip(STEPS, pieces):
            piece[term - 1] = block_vmem[own_place() ^ step]


def stay_kernel(vector, right, left, stay):
    products = contract_right(right, jnp.concatenate([vector[0], vector[1]], axis=1), 0, 1)
    block = contract_left(products, left[0, 0])
    stay[...] = block.astype(stay.dtype)


def line_targets(plan, part):
    line = lax.axis_index("sec") % LINES
    places = len(STEPS)
    codes = [jnp.max(plan[2 + i : 3 + i, :]) for i in range(2)]
    for index in part:
        for crossing in range(2):
            target = (own_place() ^ STEPS[index]) * LINES + (line ^ crossing)
            entries = [(code >> (target * 4)) & (2 * LINES * places - 1) for code in codes]
            source = [entry & (LINES * places - 1) for entry in entries]
            here = [
                (entry >= LINES * places) & (slot % LINES == line)
                for entry, slot in zip(entries, source)
            ]
            yield index, crossing, here, source


def merge_targets(plan, part, table, keep, cross):
    for index, crossing, here, source in line_targets(plan, part):
        total = 0.0
        for i in range(2):
            block = table[source[i] // LINES, i].astype(jnp.float32)
            total = total + jnp.where(here[i], block, 0.0)
        (keep, cross)[crossing][part.index(index)] = total.astype(jnp.bfloat16)


def merge_early_kernel(plan, *rest):
    *pieces, table, keep, cross = rest
    for step, piece in zip(STEPS, pieces):
        table[own_place() ^ step] = piece[...]
    merge_targets(plan, EARLY, table, keep, cross)


def merge_late_kernel(plan, table, keep, cross):
    merge_targets(plan, LATE, table, keep, cross)


def join_kernel(keep, arrived, *outs):
    for i, out in enumerate(outs):
        total = keep[i].astype(jnp.float32) + arrived[i].astype(jnp.float32)
        out[...] = total.astype(jnp.bfloat16)


def piece_rows(step, rows):
    return pl.ds(pl.multiple_of((own_place() ^ step) * rows, rows), rows)


def sum_kernel(plan, stay, *rest):
    *pieces, first = rest
    live = live_columns(plan, stay.shape[1])
    for step, piece in zip(STEPS, pieces):
        place = piece_rows(step, piece.shape[0])
        total = stay[place, :].astype(jnp.float32) + piece[...].astype(jnp.float32)
        first[place, :] = jnp.where(live, total, 0.0).astype(jnp.bfloat16)


def total_of(array):
    return jnp.sum(jnp.sum(array, axis=0, keepdims=True), axis=1, keepdims=True)


def make_tag(values, me):
    row = lax.broadcasted_iota(jnp.int32, (TAG, LANES), 0)
    lane = lax.broadcasted_iota(jnp.int32, (TAG, LANES), 1)
    spread = jnp.zeros((TAG, LANES), jnp.float32)
    for place, value in enumerate(values):
        spread = jnp.where(row // 3 == place, value, spread)
    high = spread.astype(jnp.bfloat16).astype(jnp.float32)
    middle = (spread - high).astype(jnp.bfloat16).astype(jnp.float32)
    low = spread - high - middle
    parts = jnp.where(row % 3 == 0, high, jnp.where(row % 3 == 1, middle, low))
    return jnp.where((lane == me) & (row < 3 * len(values)), parts, 0.0).astype(jnp.bfloat16)


def second_kernel(start, own, other, right, left, *rest):
    *pieces, deflated_out, block_vmem = rest
    half = start.shape[2]
    rows = block_vmem.shape[1]
    chunks = half // LANES
    basis = [start[h].astype(jnp.float32) for h in range(2)]
    firsts = [part.astype(jnp.float32) for part in in_order(own[...], other[...])]
    overlap = total_of(basis[0] * firsts[0]) + total_of(basis[1] * firsts[1])
    norm = total_of(basis[0] * basis[0]) + total_of(basis[1] * basis[1])
    quotient = jnp.where(norm > 0, overlap / jnp.where(norm > 0, norm, 1.0), 0.0)
    deflated = [firsts[h] - quotient * basis[h] for h in range(2)]
    rest_norm = total_of(deflated[0] * deflated[0]) + total_of(deflated[1] * deflated[1])
    for h in range(2):
        deflated_out[h] = deflated[h].astype(jnp.bfloat16)
    vector = jnp.concatenate(deflated, axis=1).astype(jnp.bfloat16)
    tag = make_tag((overlap, norm, quotient, rest_norm), lax.axis_index("sec"))
    for piece in pieces:
        piece[pl.ds(2 * chunks * rows, TAG), :] = tag
    products = contract_right(right, vector, 1, 2)
    right_rows = products.shape[0] // 2
    for term in (1, 2):
        block = contract_left(
            products[(term - 1) * right_rows : term * right_rows], left[0, term]
        )
        block_vmem[...] = block.astype(jnp.bfloat16).reshape(block_vmem.shape)
        for step, piece in zip(STEPS, pieces):
            part = block_vmem[own_place() ^ step]
            for c in range(chunks):
                place = pl.ds(((term - 1) * chunks + c) * rows, rows)
                piece[place, :] = part[:, c * LANES : (c + 1) * LANES]


def read_tag(tag):
    def value(place):
        parts = [tag[3 * place + i : 3 * place + i + 1, :] for i in range(3)]
        return parts[0] + parts[1] + parts[2]

    return [value(place) for place in range(4)]


def line_quotient(overlaps, norms, line):
    inside = lax.broadcasted_iota(jnp.int32, (1, LANES), 1) % LINES == line
    overlap = total_of(jnp.where(inside, overlaps, 0.0))
    norm = total_of(jnp.where(inside, norms, 0.0))
    return jnp.where(norm > 0, overlap / jnp.where(norm > 0, norm, 1.0), 0.0)


def mix_kernel(plan, *rest):
    keep, early, late, tag_out, new = rest[-5:]
    old, *pieces = rest[:-5]
    places, rows, half = keep.shape
    chunks = half // LANES
    tag = jnp.zeros((TAG, LANES), jnp.float32)
    for step, piece in zip(STEPS, pieces):
        new[own_place() ^ step] = piece[...]
        label = piece[pl.ds(2 * chunks * rows, TAG), :]
        tag = tag + label.astype(jnp.float32)
    tag_out[...] = tag.astype(jnp.bfloat16)
    early[pl.ds(len(EARLY) * chunks * rows, TAG), :] = tag.astype(jnp.bfloat16)
    overlaps, norms, quotients, _ = read_tag(tag)
    shifts = quotients - line_quotient(overlaps, norms, lax.axis_index("sec") % LINES)
    lane = lax.broadcasted_iota(jnp.int32, (1, LANES), 1)
    for index, crossing, here, source in line_targets(plan, range(places)):
        total = 0.0
        for i in range(2):
            where = source[i] // LINES
            block = jnp.concatenate(
                [new[where, pl.ds((i * chunks + c) * rows, rows), :] for c in range(chunks)],
                axis=1,
            ).astype(jnp.float32)
            shift = total_of(jnp.where(lane == source[i], shifts, 0.0))
            block = block + shift * old[where, i].astype(jnp.float32)
            total = total + jnp.where(here[i], block, 0.0)
        if crossing:
            total = total.astype(jnp.bfloat16)
            out, part = (early, EARLY) if index in EARLY else (late, LATE)
            for c in range(chunks):
                target = pl.ds((part.index(index) * chunks + c) * rows, rows)
                out[target, :] = total[:, c * LANES : (c + 1) * LANES]
        else:
            keep[index] = total


def join_early_kernel(plan, tag_line, keep, arrived, old_keep, old_arrived, *rest):
    *outs, factors = rest
    places, rows, half = keep.shape
    slots = places * LINES
    me = lax.axis_index("sec")
    live_count = places * rows * plan[1:2, 0:1].astype(jnp.float32)
    tag = tag_line[...].astype(jnp.float32)
    tag = tag + arrived[pl.ds(arrived.shape[0] - TAG, TAG), :].astype(jnp.float32)
    overlaps, norms, quotients, rests = read_tag(tag)
    quotient = total_of(overlaps) / total_of(norms)
    lane = lax.broadcasted_iota(jnp.int32, (1, LANES), 1)
    shifts = jnp.where(lane < slots, quotients - quotient, 0.0)
    resid_norm = total_of(rests + shifts * shifts * norms)
    scale = lax.rsqrt(resid_norm / live_count + 1e-06)
    own_shift = total_of(jnp.where(lane == me, shifts, 0.0))
    line = me % LINES
    shift_here = line_quotient(overlaps, norms, line) - quotient
    shift_there = line_quotient(overlaps, norms, 1 - line) - quotient
    row = lax.broadcasted_iota(jnp.int32, factors.shape, 0)
    values = jnp.where(row == 0, scale, scale * own_shift)
    values = jnp.where(row == 2, shift_here, values)
    factors[...] = jnp.where(row == 3, shift_there, values)
    weights = (scale, shift_here, shift_there)
    join_mixed(EARLY, weights, keep, arrived, old_keep, old_arrived, outs)


def join_late_kernel(factors, keep, arrived, old_keep, old_arrived, *outs):
    weights = [factors[i : i + 1, 0:1] for i in (0, 2, 3)]
    join_mixed(LATE, weights, keep, arrived, old_keep, old_arrived, outs)


def join_mixed(part, weights, keep, arrived, old_keep, old_arrived, outs):
    scale, shift_here, shift_there = weights
    rows, half = outs[0].shape
    chunks = half // LANES
    for i, index in enumerate(part):
        block = jnp.concatenate(
            [arrived[pl.ds((i * chunks + c) * rows, rows), :] for c in range(chunks)], axis=1
        ).astype(jnp.float32)
        block = block + shift_there * old_arrived[i].astype(jnp.float32)
        block = block + keep[index] + shift_here * old_keep[i].astype(jnp.float32)
        outs[i][...] = (scale * block).astype(jnp.bfloat16)


def final_kernel(plan, factors, stay, stay_2, first, *rest):
    *pieces, second, first_out = rest
    first_out[...] = first[...]
    live = live_columns(plan, stay.shape[1])
    scale, shift = factors[0:1, 0:1], factors[1:2, 0:1]
    for step, piece in zip(STEPS, pieces):
        place = piece_rows(step, piece.shape[0])
        total = scale * stay_2[place, :] + shift * stay[place, :].astype(jnp.float32)
        total = total + piece[...].astype(jnp.float32)
        second[place, :] = jnp.where(live, total, 0.0).astype(jnp.bfloat16)


SMEM = pl.BlockSpec(memory_space=pltpu.SMEM)
VMEM = pl.BlockSpec(memory_space=pltpu.VMEM)


def call(kernel, specs, outs, scratch=(), flops=0):
    return pl.pallas_call(
        kernel,
        out_shape=outs,
        in_specs=specs,
        out_specs=jax.tree.map(lambda _: VMEM, outs),
        scratch_shapes=scratch,
        compiler_params=pltpu.CompilerParams(vmem_limit_bytes=16 * 1024 * 1024),
        cost_estimate=pl.CostEstimate(flops=flops, bytes_accessed=1 << 18, transcendentals=0),
    )


def along_line(pieces, slots):
    sent = []
    for step, piece in zip(STEPS, pieces):
        pairs = [(slot, slot ^ (step * LINES)) for slot in range(slots)]
        sent.append(lax.ppermute(piece, "sec", pairs) if step else piece)
    return sent


def other_core(block):
    return lax.ppermute(block, "env", [(0, 1), (1, 0)])


def across(piece, slots):
    return lax.ppermute(piece, "sec", [(slot, slot ^ 1) for slot in range(slots)])


def on_device(amplitudes, widths, holders, left_env, right_env):
    slots_dev, right_dim, half = amplitudes.shape
    slots = holders.shape[0]
    assert slots_dev == 1
    if slots != 2 * QDOWN:
        return on_device_any(amplitudes, widths, holders, left_env, right_env)
    places = slots // LINES
    rows = right_dim // places
    dots = 6 * right_dim * half * (right_dim + 2 * half)
    block = jax.ShapeDtypeStruct((right_dim, half), jnp.bfloat16)
    wide = jax.ShapeDtypeStruct((right_dim, half), jnp.float32)
    pair = jax.ShapeDtypeStruct((2, rows, half), jnp.bfloat16)
    single = jax.ShapeDtypeStruct((rows, half), jnp.bfloat16)
    wides = jax.ShapeDtypeStruct((places, rows, half), jnp.float32)
    chunked = rows * half // LANES
    tagged = jax.ShapeDtypeStruct((2 * chunked + TAG, LANES), jnp.bfloat16)
    twos = jax.ShapeDtypeStruct((2, rows, half), jnp.bfloat16)
    early = jax.ShapeDtypeStruct((2 * chunked + TAG, LANES), jnp.bfloat16)
    late = jax.ShapeDtypeStruct((2 * chunked, LANES), jnp.bfloat16)
    label = jax.ShapeDtypeStruct((TAG, LANES), jnp.bfloat16)
    factor_shape = jax.ShapeDtypeStruct((8, LANES), jnp.float32)
    plan_shape = jax.ShapeDtypeStruct((8, LANES), jnp.int32)
    split = [pltpu.VMEM((places, rows, half), jnp.bfloat16)]
    table_shape = jax.ShapeDtypeStruct((places, *pair.shape), jnp.bfloat16)
    new_table = [pltpu.VMEM((places, *tagged.shape), jnp.bfloat16)]

    slot_table = [pltpu.SMEM((slots,), jnp.int32)]
    plan = call(plan_kernel, [SMEM, SMEM], plan_shape, slot_table)(widths, holders)
    both = jax.ShapeDtypeStruct((2, right_dim, half), jnp.bfloat16)
    number = jax.ShapeDtypeStruct((8, half), jnp.int32)
    columns = call(columns_kernel, [], number, flops=4 << 30)()
    *pieces, start_full = call(
        first_kernel, [VMEM] * 7, (pair,) * places + (both,), split, dots
    )(
        columns,
        widths[None],
        holders[None],
        amplitudes[0],
        other_core(amplitudes[0]),
        right_env,
        left_env,
    )
    old = along_line(pieces, slots)
    stay = call(stay_kernel, [VMEM] * 3, block, flops=dots // 3)(start_full, right_env, left_env)
    table, keep_early, cross = call(
        merge_early_kernel, [VMEM] * (1 + places), (table_shape, twos, twos)
    )(plan, *old)
    old_early = across(cross, slots)
    keep_late, cross = call(merge_late_kernel, [VMEM] * 2, (twos, twos))(plan, table)
    old_late = across(cross, slots)
    far = call(join_kernel, [VMEM] * 2, (single,) * 2)(keep_early, old_early)
    near = call(join_kernel, [VMEM] * 2, (single,) * 2)(keep_late, old_late)
    joined = (near[0], *far, near[1])
    first = call(sum_kernel, [VMEM] * (2 + places), block)(
        plan, stay, *along_line(joined, slots)
    )

    *pieces, deflated = call(
        second_kernel, [VMEM] * 5, (tagged,) * places + (both,), split, dots
    )(start_full, first, other_core(first), right_env, left_env)
    new = along_line(pieces, slots)
    stay_2 = call(stay_kernel, [VMEM] * 3, wide, flops=dots // 3)(deflated, right_env, left_env)
    keep, *cross, tag = call(
        mix_kernel, [VMEM] * (2 + places), (wides, early, late, label), new_table
    )(plan, table, *new)
    new_early, new_late = (across(piece, slots) for piece in cross)
    *far, factors = call(join_early_kernel, [VMEM] * 6, (single, single, factor_shape))(
        plan, tag, keep, new_early, keep_early, old_early
    )
    near = call(join_late_kernel, [VMEM] * 5, (single,) * 2)(
        factors, keep, new_late, keep_late, old_late
    )
    joined = (near[0], *far, near[1])
    second, first = call(final_kernel, [VMEM] * (5 + places), (block, block))(
        plan, factors, stay, stay_2, first, *along_line(joined, slots)
    )
    return first[None], second[None]


def solution(mesh):
    in_specs = (
        P(("runs", "sec"), None, "env"),
        P("runs"),
        P("runs"),
        P(("runs", "sec"), None, None, "env"),
        P("runs", None, None),
    )
    out_specs = (P(("runs", "sec"), None, "env"), P(("runs", "sec"), None, "env"))
    return jax.shard_map(
        on_device, mesh=mesh, in_specs=in_specs, out_specs=out_specs, check_vma=False
    )
```

```python
import jax
import jax.numpy as jnp
from jax import lax
from jax.experimental import pallas as pl
from jax.experimental.pallas import tpu as pltpu
from jax.sharding import PartitionSpec as P

QDOWN = 4

term_shifts = ((0, 0), (1, 0), (0, 1))


def route(holders):
    n_slots = holders.shape[0]
    sector_ids = jnp.arange(n_slots, dtype=jnp.int32)
    slot_of = jnp.argmax(holders[None, :] == sector_ids[:, None], axis=1)
    sources = []
    allowed = []
    for up, down in term_shifts[1:]:
        permitted = (holders // QDOWN - up >= 0) & (holders % QDOWN - down >= 0)
        wanted = jnp.clip(holders - QDOWN * up - down, 0, n_slots - 1)
        sources.append(slot_of[wanted])
        allowed.append(permitted)
    return sources, allowed


def contract(vector, left_env, right_env):
    products = jnp.einsum(
        "tij,jw->tiw", right_env, vector, preferred_element_type=jnp.float32
    ).astype(jnp.bfloat16)
    return jnp.einsum("tik,tkw->tiw", products, left_env, preferred_element_type=jnp.float32)


def spread(blocks, n_slots):
    terms, rows, width = blocks.shape
    pieces = blocks.reshape(terms, n_slots, rows // n_slots, width).swapaxes(0, 1)
    return lax.all_to_all(pieces, "sec", split_axis=0, concat_axis=0)


def collect(merged):
    n_slots, rows, width = merged.shape
    home = lax.all_to_all(merged, "sec", split_axis=0, concat_axis=0)
    return home.reshape(n_slots * rows, width)


def share(values, n_slots, me):
    lanes = jnp.zeros((1, 128), jnp.float32).at[0, : values.shape[0]].set(values)
    if n_slots & (n_slots - 1) or n_slots > 16:
        return lax.all_gather(lanes[0], "sec")
    table = jnp.where(jnp.arange(n_slots)[:, None] == me, lanes, 0.0)
    for offset in range(1, n_slots):
        pairs = [(i, i ^ offset) for i in range(n_slots)]
        other = lax.ppermute(lanes, "sec", pairs)
        table = jnp.where(jnp.arange(n_slots)[:, None] == (me ^ offset), other, table)
    return table


def merge(received, sources, allowed):
    total = 0.0
    for term, (source, permitted) in enumerate(zip(sources, allowed)):
        picked = received[source, term]
        total = total + jnp.where(permitted[:, None, None], picked, 0).astype(jnp.float32)
    return total


def on_device_any(amplitudes, widths, holders, left_env, right_env):
    slots_dev, right_dim, half_width = amplitudes.shape
    assert slots_dev == 1
    n_slots = holders.shape[0]
    me = lax.axis_index("sec")
    side = lax.axis_index("env")
    my_width = widths[holders[me]]
    row_index = side * half_width + jnp.arange(half_width, dtype=jnp.int32)
    live = (row_index < my_width)[None, :]
    sources, allowed = route(holders)
    envs = left_env[0]

    start = jnp.where(live, amplitudes[0], jnp.zeros_like(amplitudes[0]))
    start_full = lax.all_gather(start, "env", axis=1, tiled=True)
    outgoing = contract(start_full, envs, right_env).astype(jnp.bfloat16)
    stay = outgoing[0].astype(jnp.float32)
    received = spread(outgoing[1:], n_slots)
    arrived = collect(merge(received, sources, allowed).astype(jnp.bfloat16))
    first = jnp.where(live, stay + arrived.astype(jnp.float32), 0.0).astype(jnp.bfloat16)

    first_full = lax.all_gather(first, "env", axis=1, tiled=True).astype(jnp.float32)
    basis = start_full.astype(jnp.float32)
    overlap = jnp.sum(basis * first_full)
    norm = jnp.sum(basis * basis)
    own_quotient = jnp.where(norm > 0, overlap / jnp.where(norm > 0, norm, 1.0), 0.0)
    deflated = first_full - own_quotient * basis
    rest = jnp.sum(deflated * deflated)
    sums = share(jnp.stack([overlap, norm, own_quotient, rest]), n_slots, me)
    outgoing_2 = contract(deflated.astype(jnp.bfloat16), envs, right_env)
    received_2 = spread(outgoing_2[1:].astype(jnp.bfloat16), n_slots)

    quotient = jnp.sum(sums[:, 0]) / jnp.sum(sums[:, 1])
    shift = sums[:, 2] - quotient
    resid_norm = jnp.sum(sums[:, 3] + shift * shift * sums[:, 1])
    live_count = right_dim * jnp.sum(widths).astype(jnp.float32)
    scale = lax.rsqrt(resid_norm / live_count + 1e-06)
    mixed = received_2.astype(jnp.float32) + shift[:, None, None, None] * received.astype(
        jnp.float32
    )
    merged_2 = scale * merge(mixed, sources, allowed)
    arrived_2 = collect(merged_2.astype(jnp.bfloat16))
    stay_2 = scale * (outgoing_2[0] + (own_quotient - quotient) * stay)
    second = jnp.where(live, stay_2 + arrived_2.astype(jnp.float32), 0.0).astype(jnp.bfloat16)
    return first[None], second[None]


LANES = 128
TAG = 16
LINES = 2
STEPS = (0, 3, 2, 1)
EARLY, LATE = (1, 2), (0, 3)


def plan_kernel(widths, holders, plan, slot_of):
    slots = holders.shape[0]
    me = lax.axis_index("sec")
    total = jnp.int32(0)
    for s in range(slots):
        slot_of[holders[s]] = jnp.int32(s)
        total = total + widths[s]
    codes = [jnp.int32(0), jnp.int32(0)]
    for target in range(slots):
        sector = holders[target]
        has = (sector >= QDOWN, sector % QDOWN > 0)
        source = (slot_of[sector & (QDOWN - 1)], slot_of[jnp.maximum(sector - 1, 0)])
        for i in range(2):
            entry = jnp.where(has[i], source[i] + slots, 0)
            codes[i] = codes[i] | (entry << (target * 4))
    row = lax.broadcasted_iota(jnp.int32, plan.shape, 0)
    values = jnp.where(row == 0, widths[holders[me]], total)
    values = jnp.where(row == 2, codes[0], values)
    plan[...] = jnp.where(row == 3, codes[1], values)


def live_columns(plan, half):
    first_column = lax.axis_index("env") * half
    return first_column + lax.broadcasted_iota(jnp.int32, (1, half), 1) < plan[0:1, 0:1]


def contract_right(right, vector, first, terms):
    rows = right.shape[1]
    stacked = right[pl.ds(first, terms)].reshape(terms * rows, rows)
    products = jnp.dot(stacked, vector, preferred_element_type=jnp.float32)
    return products.astype(jnp.bfloat16)


def contract_left(products, left):
    return jnp.dot(products, left, preferred_element_type=jnp.float32)


def in_order(own, other):
    upper = lax.axis_index("env") > 0
    return [jnp.where(upper, other, own), jnp.where(upper, own, other)]


def own_place():
    return lax.axis_index("sec") // LINES


def columns_kernel(columns):
    columns[...] = lax.broadcasted_iota(jnp.int32, columns.shape, 1)


def first_kernel(columns, widths, holders, own, other, right, left, *rest):
    *pieces, start, block_vmem = rest
    half = start.shape[2]
    slot = lax.broadcasted_iota(jnp.int32, widths.shape, 1)
    mine = jnp.where(slot == lax.axis_index("sec"), holders[...], 0)
    sector = jnp.sum(mine, axis=1, keepdims=True)
    width = jnp.sum(jnp.where(slot == sector, widths[...], 0), axis=1, keepdims=True)
    for h, part in enumerate(in_order(own[...], other[...])):
        live = h * half + columns[0:1, :] < width
        start[h] = jnp.where(live, part, jnp.zeros_like(part))
    vector = jnp.concatenate([start[0], start[1]], axis=1)
    products = contract_right(right, vector, 1, 2)
    rows = products.shape[0] // 2
    for term in (1, 2):
        block = contract_left(products[(term - 1) * rows : term * rows], left[0, term])
        block = block.astype(jnp.bfloat16)
        block_vmem[...] = block.reshape(block_vmem.shape)
        for step, piece in zip(STEPS, pieces):
            piece[term - 1] = block_vmem[own_place() ^ step]


def stay_kernel(vector, right, left, stay):
    products = contract_right(right, jnp.concatenate([vector[0], vector[1]], axis=1), 0, 1)
    block = contract_left(products, left[0, 0])
    stay[...] = block.astype(stay.dtype)


def line_targets(plan, part):
    line = lax.axis_index("sec") % LINES
    places = len(STEPS)
    codes = [jnp.max(plan[2 + i : 3 + i, :]) for i in range(2)]
    for index in part:
        for crossing in range(2):
            target = (own_place() ^ STEPS[index]) * LINES + (line ^ crossing)
            entries = [(code >> (target * 4)) & (2 * LINES * places - 1) for code in codes]
            source = [entry & (LINES * places - 1) for entry in entries]
            here = [
                (entry >= LINES * places) & (slot % LINES == line)
                for entry, slot in zip(entries, source)
            ]
            yield index, crossing, here, source


def merge_targets(plan, part, table, keep, cross):
    for index, crossing, here, source in line_targets(plan, part):
        total = 0.0
        for i in range(2):
            block = table[source[i] // LINES, i].astype(jnp.float32)
            total = total + jnp.where(here[i], block, 0.0)
        (keep, cross)[crossing][part.index(index)] = total.astype(jnp.bfloat16)


def merge_early_kernel(plan, *rest):
    *pieces, table, keep, cross = rest
    for step, piece in zip(STEPS, pieces):
        table[own_place() ^ step] = piece[...]
    merge_targets(plan, EARLY, table, keep, cross)


def merge_late_kernel(plan, table, keep, cross):
    merge_targets(plan, LATE, table, keep, cross)


def join_kernel(keep, arrived, *outs):
    for i, out in enumerate(outs):
        total = keep[i].astype(jnp.float32) + arrived[i].astype(jnp.float32)
        out[...] = total.astype(jnp.bfloat16)


def piece_rows(step, rows):
    return pl.ds(pl.multiple_of((own_place() ^ step) * rows, rows), rows)


def sum_kernel(plan, stay, *rest):
    *pieces, first = rest
    live = live_columns(plan, stay.shape[1])
    for step, piece in zip(STEPS, pieces):
        place = piece_rows(step, piece.shape[0])
        total = stay[place, :].astype(jnp.float32) + piece[...].astype(jnp.float32)
        first[place, :] = jnp.where(live, total, 0.0).astype(jnp.bfloat16)


def total_of(array):
    return jnp.sum(jnp.sum(array, axis=0, keepdims=True), axis=1, keepdims=True)


def make_tag(values, me):
    row = lax.broadcasted_iota(jnp.int32, (TAG, LANES), 0)
    lane = lax.broadcasted_iota(jnp.int32, (TAG, LANES), 1)
    spread = jnp.zeros((TAG, LANES), jnp.float32)
    for place, value in enumerate(values):
        spread = jnp.where(row // 3 == place, value, spread)
    high = spread.astype(jnp.bfloat16).astype(jnp.float32)
    middle = (spread - high).astype(jnp.bfloat16).astype(jnp.float32)
    low = spread - high - middle
    parts = jnp.where(row % 3 == 0, high, jnp.where(row % 3 == 1, middle, low))
    return jnp.where((lane == me) & (row < 3 * len(values)), parts, 0.0).astype(jnp.bfloat16)


def second_kernel(start, own, other, right, left, *rest):
    *pieces, deflated_out, block_vmem = rest
    half = start.shape[2]
    rows = block_vmem.shape[1]
    chunks = half // LANES
    basis = [start[h].astype(jnp.float32) for h in range(2)]
    firsts = [part.astype(jnp.float32) for part in in_order(own[...], other[...])]
    overlap = total_of(basis[0] * firsts[0]) + total_of(basis[1] * firsts[1])
    norm = total_of(basis[0] * basis[0]) + total_of(basis[1] * basis[1])
    quotient = jnp.where(norm > 0, overlap / jnp.where(norm > 0, norm, 1.0), 0.0)
    deflated = [firsts[h] - quotient * basis[h] for h in range(2)]
    rest_norm = total_of(deflated[0] * deflated[0]) + total_of(deflated[1] * deflated[1])
    for h in range(2):
        deflated_out[h] = deflated[h].astype(jnp.bfloat16)
    vector = jnp.concatenate(deflated, axis=1).astype(jnp.bfloat16)
    tag = make_tag((overlap, norm, quotient, rest_norm), lax.axis_index("sec"))
    for piece in pieces:
        piece[pl.ds(2 * chunks * rows, TAG), :] = tag
    products = contract_right(right, vector, 1, 2)
    right_rows = products.shape[0] // 2
    for term in (1, 2):
        block = contract_left(
            products[(term - 1) * right_rows : term * right_rows], left[0, term]
        )
        block_vmem[...] = block.astype(jnp.bfloat16).reshape(block_vmem.shape)
        for step, piece in zip(STEPS, pieces):
            part = block_vmem[own_place() ^ step]
            for c in range(chunks):
                place = pl.ds(((term - 1) * chunks + c) * rows, rows)
                piece[place, :] = part[:, c * LANES : (c + 1) * LANES]


def read_tag(tag):
    def value(place):
        parts = [tag[3 * place + i : 3 * place + i + 1, :] for i in range(3)]
        return parts[0] + parts[1] + parts[2]

    return [value(place) for place in range(4)]


def line_quotient(overlaps, norms, line):
    inside = lax.broadcasted_iota(jnp.int32, (1, LANES), 1) % LINES == line
    overlap = total_of(jnp.where(inside, overlaps, 0.0))
    norm = total_of(jnp.where(inside, norms, 0.0))
    return jnp.where(norm > 0, overlap / jnp.where(norm > 0, norm, 1.0), 0.0)


def mix_kernel(plan, *rest):
    keep, early, late, tag_out, new = rest[-5:]
    old, *pieces = rest[:-5]
    places, rows, half = keep.shape
    chunks = half // LANES
    tag = jnp.zeros((TAG, LANES), jnp.float32)
    for step, piece in zip(STEPS, pieces):
        new[own_place() ^ step] = piece[...]
        label = piece[pl.ds(2 * chunks * rows, TAG), :]
        tag = tag + label.astype(jnp.float32)
    tag_out[...] = tag.astype(jnp.bfloat16)
    early[pl.ds(len(EARLY) * chunks * rows, TAG), :] = tag.astype(jnp.bfloat16)
    overlaps, norms, quotients, _ = read_tag(tag)
    shifts = quotients - line_quotient(overlaps, norms, lax.axis_index("sec") % LINES)
    lane = lax.broadcasted_iota(jnp.int32, (1, LANES), 1)
    for index, crossing, here, source in line_targets(plan, range(places)):
        total = 0.0
        for i in range(2):
            where = source[i] // LINES
            block = jnp.concatenate(
                [new[where, pl.ds((i * chunks + c) * rows, rows), :] for c in range(chunks)],
                axis=1,
            ).astype(jnp.float32)
            shift = total_of(jnp.where(lane == source[i], shifts, 0.0))
            block = block + shift * old[where, i].astype(jnp.float32)
            total = total + jnp.where(here[i], block, 0.0)
        if crossing:
            total = total.astype(jnp.bfloat16)
            out, part = (early, EARLY) if index in EARLY else (late, LATE)
            for c in range(chunks):
                target = pl.ds((part.index(index) * chunks + c) * rows, rows)
                out[target, :] = total[:, c * LANES : (c + 1) * LANES]
        else:
            keep[index] = total


def join_early_kernel(plan, tag_line, keep, arrived, old_keep, old_arrived, *rest):
    *outs, factors = rest
    places, rows, half = keep.shape
    slots = places * LINES
    me = lax.axis_index("sec")
    live_count = places * rows * plan[1:2, 0:1].astype(jnp.float32)
    tag = tag_line[...].astype(jnp.float32)
    tag = tag + arrived[pl.ds(arrived.shape[0] - TAG, TAG), :].astype(jnp.float32)
    overlaps, norms, quotients, rests = read_tag(tag)
    quotient = total_of(overlaps) / total_of(norms)
    lane = lax.broadcasted_iota(jnp.int32, (1, LANES), 1)
    shifts = jnp.where(lane < slots, quotients - quotient, 0.0)
    resid_norm = total_of(rests + shifts * shifts * norms)
    scale = lax.rsqrt(resid_norm / live_count + 1e-06)
    own_shift = total_of(jnp.where(lane == me, shifts, 0.0))
    line = me % LINES
    shift_here = line_quotient(overlaps, norms, line) - quotient
    shift_there = line_quotient(overlaps, norms, 1 - line) - quotient
    row = lax.broadcasted_iota(jnp.int32, factors.shape, 0)
    values = jnp.where(row == 0, scale, scale * own_shift)
    values = jnp.where(row == 2, shift_here, values)
    factors[...] = jnp.where(row == 3, shift_there, values)
    weights = (scale, shift_here, shift_there)
    join_mixed(EARLY, weights, keep, arrived, old_keep, old_arrived, outs)


def join_late_kernel(factors, keep, arrived, old_keep, old_arrived, *outs):
    weights = [factors[i : i + 1, 0:1] for i in (0, 2, 3)]
    join_mixed(LATE, weights, keep, arrived, old_keep, old_arrived, outs)


def join_mixed(part, weights, keep, arrived, old_keep, old_arrived, outs):
    scale, shift_here, shift_there = weights
    rows, half = outs[0].shape
    chunks = half // LANES
    for i, index in enumerate(part):
        block = jnp.concatenate(
            [arrived[pl.ds((i * chunks + c) * rows, rows), :] for c in range(chunks)], axis=1
        ).astype(jnp.float32)
        block = block + shift_there * old_arrived[i].astype(jnp.float32)
        block = block + keep[index] + shift_here * old_keep[i].astype(jnp.float32)
        outs[i][...] = (scale * block).astype(jnp.bfloat16)


def write_kernel(block, out):
    out[...] = block[...]


def final_kernel(plan, factors, stay, stay_2, *rest):
    *pieces, second = rest
    live = live_columns(plan, stay.shape[1])
    scale, shift = factors[0:1, 0:1], factors[1:2, 0:1]
    for step, piece in zip(STEPS, pieces):
        place = piece_rows(step, piece.shape[0])
        total = scale * stay_2[place, :] + shift * stay[place, :].astype(jnp.float32)
        total = total + piece[...].astype(jnp.float32)
        second[place, :] = jnp.where(live, total, 0.0).astype(jnp.bfloat16)


SMEM = pl.BlockSpec(memory_space=pltpu.SMEM)
VMEM = pl.BlockSpec(memory_space=pltpu.VMEM)


def call(kernel, specs, outs, scratch=(), flops=0):
    return pl.pallas_call(
        kernel,
        out_shape=outs,
        in_specs=specs,
        out_specs=jax.tree.map(lambda _: VMEM, outs),
        scratch_shapes=scratch,
        compiler_params=pltpu.CompilerParams(vmem_limit_bytes=16 * 1024 * 1024),
        cost_estimate=pl.CostEstimate(flops=flops, bytes_accessed=1 << 18, transcendentals=0),
    )


def along_line(pieces, slots):
    sent = []
    for step, piece in zip(STEPS, pieces):
        pairs = [(slot, slot ^ (step * LINES)) for slot in range(slots)]
        sent.append(lax.ppermute(piece, "sec", pairs) if step else piece)
    return sent


def other_core(block):
    return lax.ppermute(block, "env", [(0, 1), (1, 0)])


def across(piece, slots):
    return lax.ppermute(piece, "sec", [(slot, slot ^ 1) for slot in range(slots)])


def on_device(amplitudes, widths, holders, left_env, right_env):
    slots_dev, right_dim, half = amplitudes.shape
    slots = holders.shape[0]
    assert slots_dev == 1
    if slots != 2 * QDOWN:
        return on_device_any(amplitudes, widths, holders, left_env, right_env)
    places = slots // LINES
    rows = right_dim // places
    dots = 6 * right_dim * half * (right_dim + 2 * half)
    block = jax.ShapeDtypeStruct((right_dim, half), jnp.bfloat16)
    wide = jax.ShapeDtypeStruct((right_dim, half), jnp.float32)
    pair = jax.ShapeDtypeStruct((2, rows, half), jnp.bfloat16)
    single = jax.ShapeDtypeStruct((rows, half), jnp.bfloat16)
    wides = jax.ShapeDtypeStruct((places, rows, half), jnp.float32)
    chunked = rows * half // LANES
    tagged = jax.ShapeDtypeStruct((2 * chunked + TAG, LANES), jnp.bfloat16)
    twos = jax.ShapeDtypeStruct((2, rows, half), jnp.bfloat16)
    early = jax.ShapeDtypeStruct((2 * chunked + TAG, LANES), jnp.bfloat16)
    late = jax.ShapeDtypeStruct((2 * chunked, LANES), jnp.bfloat16)
    label = jax.ShapeDtypeStruct((TAG, LANES), jnp.bfloat16)
    factor_shape = jax.ShapeDtypeStruct((8, LANES), jnp.float32)
    plan_shape = jax.ShapeDtypeStruct((8, LANES), jnp.int32)
    split = [pltpu.VMEM((places, rows, half), jnp.bfloat16)]
    table_shape = jax.ShapeDtypeStruct((places, *pair.shape), jnp.bfloat16)
    new_table = [pltpu.VMEM((places, *tagged.shape), jnp.bfloat16)]

    slot_table = [pltpu.SMEM((slots,), jnp.int32)]
    plan = call(plan_kernel, [SMEM, SMEM], plan_shape, slot_table)(widths, holders)
    both = jax.ShapeDtypeStruct((2, right_dim, half), jnp.bfloat16)
    number = jax.ShapeDtypeStruct((8, half), jnp.int32)
    columns = call(columns_kernel, [], number, flops=4 << 30)()
    *pieces, start_full = call(
        first_kernel, [VMEM] * 7, (pair,) * places + (both,), split, dots
    )(
        columns,
        widths[None],
        holders[None],
        amplitudes[0],
        other_core(amplitudes[0]),
        right_env,
        left_env,
    )
    old = along_line(pieces, slots)
    stay = call(stay_kernel, [VMEM] * 3, block, flops=dots // 3)(start_full, right_env, left_env)
    table, keep_early, cross = call(
        merge_early_kernel, [VMEM] * (1 + places), (table_shape, twos, twos)
    )(plan, *old)
    old_early = across(cross, slots)
    keep_late, cross = call(merge_late_kernel, [VMEM] * 2, (twos, twos))(plan, table)
    old_late = across(cross, slots)
    far = call(join_kernel, [VMEM] * 2, (single,) * 2)(keep_early, old_early)
    near = call(join_kernel, [VMEM] * 2, (single,) * 2)(keep_late, old_late)
    joined = (near[0], *far, near[1])
    first = call(sum_kernel, [VMEM] * (2 + places), block)(
        plan, stay, *along_line(joined, slots)
    )

    *pieces, deflated = call(
        second_kernel, [VMEM] * 5, (tagged,) * places + (both,), split, dots
    )(start_full, first, other_core(first), right_env, left_env)
    new = along_line(pieces, slots)
    written = call(write_kernel, [VMEM], block)(first)
    new, first = lax.optimization_barrier((new, written))
    stay_2 = call(stay_kernel, [VMEM] * 3, wide, flops=dots // 3)(deflated, right_env, left_env)
    keep, *cross, tag = call(
        mix_kernel, [VMEM] * (2 + places), (wides, early, late, label), new_table
    )(plan, table, *new)
    new_early, new_late = (across(piece, slots) for piece in cross)
    *far, factors = call(join_early_kernel, [VMEM] * 6, (single, single, factor_shape))(
        plan, tag, keep, new_early, keep_early, old_early
    )
    near = call(join_late_kernel, [VMEM] * 5, (single,) * 2)(
        factors, keep, new_late, keep_late, old_late
    )
    joined = (near[0], *far, near[1])
    second = call(final_kernel, [VMEM] * (4 + places), block)(
        plan, factors, stay, stay_2, *along_line(joined, slots)
    )
    return first[None], second[None]


def solution(mesh):
    in_specs = (
        P(("runs", "sec"), None, "env"),
        P("runs"),
        P("runs"),
        P(("runs", "sec"), None, None, "env"),
        P("runs", None, None),
    )
    out_specs = (P(("runs", "sec"), None, "env"), P(("runs", "sec"), None, "env"))
    return jax.shard_map(
        on_device, mesh=mesh, in_specs=in_specs, out_specs=out_specs, check_vma=False
    )
```

```python
import jax
import jax.numpy as jnp
from jax import lax
from jax.experimental import pallas as pl
from jax.experimental.pallas import tpu as pltpu
from jax.sharding import PartitionSpec as P

QDOWN = 4

term_shifts = ((0, 0), (1, 0), (0, 1))


def route(holders):
    n_slots = holders.shape[0]
    sector_ids = jnp.arange(n_slots, dtype=jnp.int32)
    slot_of = jnp.argmax(holders[None, :] == sector_ids[:, None], axis=1)
    sources = []
    allowed = []
    for up, down in term_shifts[1:]:
        permitted = (holders // QDOWN - up >= 0) & (holders % QDOWN - down >= 0)
        wanted = jnp.clip(holders - QDOWN * up - down, 0, n_slots - 1)
        sources.append(slot_of[wanted])
        allowed.append(permitted)
    return sources, allowed


def contract(vector, left_env, right_env):
    products = jnp.einsum(
        "tij,jw->tiw", right_env, vector, preferred_element_type=jnp.float32
    ).astype(jnp.bfloat16)
    return jnp.einsum("tik,tkw->tiw", products, left_env, preferred_element_type=jnp.float32)


def spread(blocks, n_slots):
    terms, rows, width = blocks.shape
    pieces = blocks.reshape(terms, n_slots, rows // n_slots, width).swapaxes(0, 1)
    return lax.all_to_all(pieces, "sec", split_axis=0, concat_axis=0)


def collect(merged):
    n_slots, rows, width = merged.shape
    home = lax.all_to_all(merged, "sec", split_axis=0, concat_axis=0)
    return home.reshape(n_slots * rows, width)


def share(values, n_slots, me):
    lanes = jnp.zeros((1, 128), jnp.float32).at[0, : values.shape[0]].set(values)
    if n_slots & (n_slots - 1) or n_slots > 16:
        return lax.all_gather(lanes[0], "sec")
    table = jnp.where(jnp.arange(n_slots)[:, None] == me, lanes, 0.0)
    for offset in range(1, n_slots):
        pairs = [(i, i ^ offset) for i in range(n_slots)]
        other = lax.ppermute(lanes, "sec", pairs)
        table = jnp.where(jnp.arange(n_slots)[:, None] == (me ^ offset), other, table)
    return table


def merge(received, sources, allowed):
    total = 0.0
    for term, (source, permitted) in enumerate(zip(sources, allowed)):
        picked = received[source, term]
        total = total + jnp.where(permitted[:, None, None], picked, 0).astype(jnp.float32)
    return total


def on_device_any(amplitudes, widths, holders, left_env, right_env):
    slots_dev, right_dim, half_width = amplitudes.shape
    assert slots_dev == 1
    n_slots = holders.shape[0]
    me = lax.axis_index("sec")
    side = lax.axis_index("env")
    my_width = widths[holders[me]]
    row_index = side * half_width + jnp.arange(half_width, dtype=jnp.int32)
    live = (row_index < my_width)[None, :]
    sources, allowed = route(holders)
    envs = left_env[0]

    start = jnp.where(live, amplitudes[0], jnp.zeros_like(amplitudes[0]))
    start_full = lax.all_gather(start, "env", axis=1, tiled=True)
    outgoing = contract(start_full, envs, right_env).astype(jnp.bfloat16)
    stay = outgoing[0].astype(jnp.float32)
    received = spread(outgoing[1:], n_slots)
    arrived = collect(merge(received, sources, allowed).astype(jnp.bfloat16))
    first = jnp.where(live, stay + arrived.astype(jnp.float32), 0.0).astype(jnp.bfloat16)

    first_full = lax.all_gather(first, "env", axis=1, tiled=True).astype(jnp.float32)
    basis = start_full.astype(jnp.float32)
    overlap = jnp.sum(basis * first_full)
    norm = jnp.sum(basis * basis)
    own_quotient = jnp.where(norm > 0, overlap / jnp.where(norm > 0, norm, 1.0), 0.0)
    deflated = first_full - own_quotient * basis
    rest = jnp.sum(deflated * deflated)
    sums = share(jnp.stack([overlap, norm, own_quotient, rest]), n_slots, me)
    outgoing_2 = contract(deflated.astype(jnp.bfloat16), envs, right_env)
    received_2 = spread(outgoing_2[1:].astype(jnp.bfloat16), n_slots)

    quotient = jnp.sum(sums[:, 0]) / jnp.sum(sums[:, 1])
    shift = sums[:, 2] - quotient
    resid_norm = jnp.sum(sums[:, 3] + shift * shift * sums[:, 1])
    live_count = right_dim * jnp.sum(widths).astype(jnp.float32)
    scale = lax.rsqrt(resid_norm / live_count + 1e-06)
    mixed = received_2.astype(jnp.float32) + shift[:, None, None, None] * received.astype(
        jnp.float32
    )
    merged_2 = scale * merge(mixed, sources, allowed)
    arrived_2 = collect(merged_2.astype(jnp.bfloat16))
    stay_2 = scale * (outgoing_2[0] + (own_quotient - quotient) * stay)
    second = jnp.where(live, stay_2 + arrived_2.astype(jnp.float32), 0.0).astype(jnp.bfloat16)
    return first[None], second[None]


LANES = 128
TAG = 16
LINES = 2
STEPS = (0, 2, 3, 1)
EARLY, LATE = (1, 2), (0, 3)


def plan_kernel(widths, holders, plan, slot_of):
    slots = holders.shape[0]
    me = lax.axis_index("sec")
    total = jnp.int32(0)
    for s in range(slots):
        slot_of[holders[s]] = jnp.int32(s)
        total = total + widths[s]
    codes = [jnp.int32(0), jnp.int32(0)]
    for target in range(slots):
        sector = holders[target]
        has = (sector >= QDOWN, sector % QDOWN > 0)
        source = (slot_of[sector & (QDOWN - 1)], slot_of[jnp.maximum(sector - 1, 0)])
        for i in range(2):
            entry = jnp.where(has[i], source[i] + slots, 0)
            codes[i] = codes[i] | (entry << (target * 4))
    row = lax.broadcasted_iota(jnp.int32, plan.shape, 0)
    values = jnp.where(row == 0, widths[holders[me]], total)
    values = jnp.where(row == 2, codes[0], values)
    plan[...] = jnp.where(row == 3, codes[1], values)


def live_columns(plan, half):
    first_column = lax.axis_index("env") * half
    return first_column + lax.broadcasted_iota(jnp.int32, (1, half), 1) < plan[0:1, 0:1]


def contract_right(right, vector, first, terms):
    rows = right.shape[1]
    stacked = right[pl.ds(first, terms)].reshape(terms * rows, rows)
    products = jnp.dot(stacked, vector, preferred_element_type=jnp.float32)
    return products.astype(jnp.bfloat16)


def contract_left(products, left):
    return jnp.dot(products, left, preferred_element_type=jnp.float32)


def in_order(own, other):
    upper = lax.axis_index("env") > 0
    return [jnp.where(upper, other, own), jnp.where(upper, own, other)]


def own_place():
    return lax.axis_index("sec") // LINES


def columns_kernel(columns):
    columns[...] = lax.broadcasted_iota(jnp.int32, columns.shape, 1)


def first_kernel(columns, widths, holders, own, other, right, left, *rest):
    *pieces, start, block_vmem = rest
    half = start.shape[2]
    slot = lax.broadcasted_iota(jnp.int32, widths.shape, 1)
    mine = jnp.where(slot == lax.axis_index("sec"), holders[...], 0)
    sector = jnp.sum(mine, axis=1, keepdims=True)
    width = jnp.sum(jnp.where(slot == sector, widths[...], 0), axis=1, keepdims=True)
    for h, part in enumerate(in_order(own[...], other[...])):
        live = h * half + columns[0:1, :] < width
        start[h] = jnp.where(live, part, jnp.zeros_like(part))
    vector = jnp.concatenate([start[0], start[1]], axis=1)
    products = contract_right(right, vector, 1, 2)
    rows = products.shape[0] // 2
    for term in (1, 2):
        block = contract_left(products[(term - 1) * rows : term * rows], left[0, term])
        block = block.astype(jnp.bfloat16)
        block_vmem[...] = block.reshape(block_vmem.shape)
        for step, piece in zip(STEPS, pieces):
            piece[term - 1] = block_vmem[own_place() ^ step]


def stay_kernel(vector, right, left, stay):
    products = contract_right(right, jnp.concatenate([vector[0], vector[1]], axis=1), 0, 1)
    block = contract_left(products, left[0, 0])
    stay[...] = block.astype(stay.dtype)


def line_targets(plan, part):
    line = lax.axis_index("sec") % LINES
    places = len(STEPS)
    codes = [jnp.max(plan[2 + i : 3 + i, :]) for i in range(2)]
    for index in part:
        for crossing in range(2):
            target = (own_place() ^ STEPS[index]) * LINES + (line ^ crossing)
            entries = [(code >> (target * 4)) & (2 * LINES * places - 1) for code in codes]
            source = [entry & (LINES * places - 1) for entry in entries]
            here = [
                (entry >= LINES * places) & (slot % LINES == line)
                for entry, slot in zip(entries, source)
            ]
            yield index, crossing, here, source


def merge_targets(plan, part, table, keep, cross):
    for index, crossing, here, source in line_targets(plan, part):
        total = 0.0
        for i in range(2):
            block = table[source[i] // LINES, i].astype(jnp.float32)
            total = total + jnp.where(here[i], block, 0.0)
        (keep, cross)[crossing][part.index(index)] = total.astype(jnp.bfloat16)


def merge_early_kernel(plan, *rest):
    *pieces, table, keep, cross = rest
    for step, piece in zip(STEPS, pieces):
        table[own_place() ^ step] = piece[...]
    merge_targets(plan, EARLY, table, keep, cross)


def merge_late_kernel(plan, table, keep, cross):
    merge_targets(plan, LATE, table, keep, cross)


def join_kernel(keep, arrived, *outs):
    for i, out in enumerate(outs):
        total = keep[i].astype(jnp.float32) + arrived[i].astype(jnp.float32)
        out[...] = total.astype(jnp.bfloat16)


def piece_rows(step, rows):
    return pl.ds(pl.multiple_of((own_place() ^ step) * rows, rows), rows)


def sum_kernel(plan, stay, *rest):
    *pieces, first = rest
    live = live_columns(plan, stay.shape[1])
    for step, piece in zip(STEPS, pieces):
        place = piece_rows(step, piece.shape[0])
        total = stay[place, :].astype(jnp.float32) + piece[...].astype(jnp.float32)
        first[place, :] = jnp.where(live, total, 0.0).astype(jnp.bfloat16)


def total_of(array):
    return jnp.sum(jnp.sum(array, axis=0, keepdims=True), axis=1, keepdims=True)


def make_tag(values, me):
    row = lax.broadcasted_iota(jnp.int32, (TAG, LANES), 0)
    lane = lax.broadcasted_iota(jnp.int32, (TAG, LANES), 1)
    spread = jnp.zeros((TAG, LANES), jnp.float32)
    for place, value in enumerate(values):
        spread = jnp.where(row // 3 == place, value, spread)
    high = spread.astype(jnp.bfloat16).astype(jnp.float32)
    middle = (spread - high).astype(jnp.bfloat16).astype(jnp.float32)
    low = spread - high - middle
    parts = jnp.where(row % 3 == 0, high, jnp.where(row % 3 == 1, middle, low))
    return jnp.where((lane == me) & (row < 3 * len(values)), parts, 0.0).astype(jnp.bfloat16)


def second_kernel(start, own, other, right, left, *rest):
    *pieces, deflated_out, block_vmem = rest
    half = start.shape[2]
    rows = block_vmem.shape[1]
    chunks = half // LANES
    basis = [start[h].astype(jnp.float32) for h in range(2)]
    firsts = [part.astype(jnp.float32) for part in in_order(own[...], other[...])]
    overlap = total_of(basis[0] * firsts[0]) + total_of(basis[1] * firsts[1])
    norm = total_of(basis[0] * basis[0]) + total_of(basis[1] * basis[1])
    quotient = jnp.where(norm > 0, overlap / jnp.where(norm > 0, norm, 1.0), 0.0)
    deflated = [firsts[h] - quotient * basis[h] for h in range(2)]
    rest_norm = total_of(deflated[0] * deflated[0]) + total_of(deflated[1] * deflated[1])
    for h in range(2):
        deflated_out[h] = deflated[h].astype(jnp.bfloat16)
    vector = jnp.concatenate(deflated, axis=1).astype(jnp.bfloat16)
    tag = make_tag((overlap, norm, quotient, rest_norm), lax.axis_index("sec"))
    for piece in pieces:
        piece[pl.ds(2 * chunks * rows, TAG), :] = tag
    products = contract_right(right, vector, 1, 2)
    right_rows = products.shape[0] // 2
    for term in (1, 2):
        block = contract_left(
            products[(term - 1) * right_rows : term * right_rows], left[0, term]
        )
        block_vmem[...] = block.astype(jnp.bfloat16).reshape(block_vmem.shape)
        for step, piece in zip(STEPS, pieces):
            part = block_vmem[own_place() ^ step]
            for c in range(chunks):
                place = pl.ds(((term - 1) * chunks + c) * rows, rows)
                piece[place, :] = part[:, c * LANES : (c + 1) * LANES]


def read_tag(tag):
    def value(place):
        parts = [tag[3 * place + i : 3 * place + i + 1, :] for i in range(3)]
        return parts[0] + parts[1] + parts[2]

    return [value(place) for place in range(4)]


def line_quotient(overlaps, norms, line):
    inside = lax.broadcasted_iota(jnp.int32, (1, LANES), 1) % LINES == line
    overlap = total_of(jnp.where(inside, overlaps, 0.0))
    norm = total_of(jnp.where(inside, norms, 0.0))
    return jnp.where(norm > 0, overlap / jnp.where(norm > 0, norm, 1.0), 0.0)


def mix_kernel(plan, *rest):
    keep, early, late, tag_out, new = rest[-5:]
    old, *pieces = rest[:-5]
    places, rows, half = keep.shape
    chunks = half // LANES
    tag = jnp.zeros((TAG, LANES), jnp.float32)
    for step, piece in zip(STEPS, pieces):
        new[own_place() ^ step] = piece[...]
        label = piece[pl.ds(2 * chunks * rows, TAG), :]
        tag = tag + label.astype(jnp.float32)
    tag_out[...] = tag.astype(jnp.bfloat16)
    early[pl.ds(len(EARLY) * chunks * rows, TAG), :] = tag.astype(jnp.bfloat16)
    overlaps, norms, quotients, _ = read_tag(tag)
    shifts = quotients - line_quotient(overlaps, norms, lax.axis_index("sec") % LINES)
    lane = lax.broadcasted_iota(jnp.int32, (1, LANES), 1)
    for index, crossing, here, source in line_targets(plan, range(places)):
        total = 0.0
        for i in range(2):
            where = source[i] // LINES
            block = jnp.concatenate(
                [new[where, pl.ds((i * chunks + c) * rows, rows), :] for c in range(chunks)],
                axis=1,
            ).astype(jnp.float32)
            shift = total_of(jnp.where(lane == source[i], shifts, 0.0))
            block = block + shift * old[where, i].astype(jnp.float32)
            total = total + jnp.where(here[i], block, 0.0)
        if crossing:
            total = total.astype(jnp.bfloat16)
            out, part = (early, EARLY) if index in EARLY else (late, LATE)
            for c in range(chunks):
                target = pl.ds((part.index(index) * chunks + c) * rows, rows)
                out[target, :] = total[:, c * LANES : (c + 1) * LANES]
        else:
            keep[index] = total


def join_early_kernel(plan, tag_line, keep, arrived, old_keep, old_arrived, *rest):
    *outs, factors = rest
    places, rows, half = keep.shape
    slots = places * LINES
    me = lax.axis_index("sec")
    live_count = places * rows * plan[1:2, 0:1].astype(jnp.float32)
    tag = tag_line[...].astype(jnp.float32)
    tag = tag + arrived[pl.ds(arrived.shape[0] - TAG, TAG), :].astype(jnp.float32)
    overlaps, norms, quotients, rests = read_tag(tag)
    quotient = total_of(overlaps) / total_of(norms)
    lane = lax.broadcasted_iota(jnp.int32, (1, LANES), 1)
    shifts = jnp.where(lane < slots, quotients - quotient, 0.0)
    resid_norm = total_of(rests + shifts * shifts * norms)
    scale = lax.rsqrt(resid_norm / live_count + 1e-06)
    own_shift = total_of(jnp.where(lane == me, shifts, 0.0))
    line = me % LINES
    shift_here = line_quotient(overlaps, norms, line) - quotient
    shift_there = line_quotient(overlaps, norms, 1 - line) - quotient
    row = lax.broadcasted_iota(jnp.int32, factors.shape, 0)
    values = jnp.where(row == 0, scale, scale * own_shift)
    values = jnp.where(row == 2, shift_here, values)
    factors[...] = jnp.where(row == 3, shift_there, values)
    weights = (scale, shift_here, shift_there)
    join_mixed(EARLY, weights, keep, arrived, old_keep, old_arrived, outs)


def join_late_kernel(factors, keep, arrived, old_keep, old_arrived, *outs):
    weights = [factors[i : i + 1, 0:1] for i in (0, 2, 3)]
    join_mixed(LATE, weights, keep, arrived, old_keep, old_arrived, outs)


def join_mixed(part, weights, keep, arrived, old_keep, old_arrived, outs):
    scale, shift_here, shift_there = weights
    rows, half = outs[0].shape
    chunks = half // LANES
    for i, index in enumerate(part):
        block = jnp.concatenate(
            [arrived[pl.ds((i * chunks + c) * rows, rows), :] for c in range(chunks)], axis=1
        ).astype(jnp.float32)
        block = block + shift_there * old_arrived[i].astype(jnp.float32)
        block = block + keep[index] + shift_here * old_keep[i].astype(jnp.float32)
        outs[i][...] = (scale * block).astype(jnp.bfloat16)


def final_kernel(plan, factors, stay, stay_2, first, *rest):
    *pieces, second, first_out = rest
    first_out[...] = first[...]
    live = live_columns(plan, stay.shape[1])
    scale, shift = factors[0:1, 0:1], factors[1:2, 0:1]
    for step, piece in zip(STEPS, pieces):
        place = piece_rows(step, piece.shape[0])
        total = scale * stay_2[place, :] + shift * stay[place, :].astype(jnp.float32)
        total = total + piece[...].astype(jnp.float32)
        second[place, :] = jnp.where(live, total, 0.0).astype(jnp.bfloat16)


SMEM = pl.BlockSpec(memory_space=pltpu.SMEM)
VMEM = pl.BlockSpec(memory_space=pltpu.VMEM)


def call(kernel, specs, outs, scratch=(), flops=0):
    return pl.pallas_call(
        kernel,
        out_shape=outs,
        in_specs=specs,
        out_specs=jax.tree.map(lambda _: VMEM, outs),
        scratch_shapes=scratch,
        compiler_params=pltpu.CompilerParams(vmem_limit_bytes=16 * 1024 * 1024),
        cost_estimate=pl.CostEstimate(flops=flops, bytes_accessed=1 << 18, transcendentals=0),
    )


def along_line(pieces, slots):
    sent = []
    for step, piece in zip(STEPS, pieces):
        pairs = [(slot, slot ^ (step * LINES)) for slot in range(slots)]
        sent.append(lax.ppermute(piece, "sec", pairs) if step else piece)
    return sent


def other_core(block):
    return lax.ppermute(block, "env", [(0, 1), (1, 0)])


def across(piece, slots):
    return lax.ppermute(piece, "sec", [(slot, slot ^ 1) for slot in range(slots)])


def on_device(amplitudes, widths, holders, left_env, right_env):
    slots_dev, right_dim, half = amplitudes.shape
    slots = holders.shape[0]
    assert slots_dev == 1
    if slots != 2 * QDOWN:
        return on_device_any(amplitudes, widths, holders, left_env, right_env)
    places = slots // LINES
    rows = right_dim // places
    dots = 6 * right_dim * half * (right_dim + 2 * half)
    block = jax.ShapeDtypeStruct((right_dim, half), jnp.bfloat16)
    wide = jax.ShapeDtypeStruct((right_dim, half), jnp.float32)
    pair = jax.ShapeDtypeStruct((2, rows, half), jnp.bfloat16)
    single = jax.ShapeDtypeStruct((rows, half), jnp.bfloat16)
    wides = jax.ShapeDtypeStruct((places, rows, half), jnp.float32)
    chunked = rows * half // LANES
    tagged = jax.ShapeDtypeStruct((2 * chunked + TAG, LANES), jnp.bfloat16)
    twos = jax.ShapeDtypeStruct((2, rows, half), jnp.bfloat16)
    early = jax.ShapeDtypeStruct((2 * chunked + TAG, LANES), jnp.bfloat16)
    late = jax.ShapeDtypeStruct((2 * chunked, LANES), jnp.bfloat16)
    label = jax.ShapeDtypeStruct((TAG, LANES), jnp.bfloat16)
    factor_shape = jax.ShapeDtypeStruct((8, LANES), jnp.float32)
    plan_shape = jax.ShapeDtypeStruct((8, LANES), jnp.int32)
    split = [pltpu.VMEM((places, rows, half), jnp.bfloat16)]
    table_shape = jax.ShapeDtypeStruct((places, *pair.shape), jnp.bfloat16)
    new_table = [pltpu.VMEM((places, *tagged.shape), jnp.bfloat16)]

    slot_table = [pltpu.SMEM((slots,), jnp.int32)]
    plan = call(plan_kernel, [SMEM, SMEM], plan_shape, slot_table)(widths, holders)
    both = jax.ShapeDtypeStruct((2, right_dim, half), jnp.bfloat16)
    number = jax.ShapeDtypeStruct((8, half), jnp.int32)
    columns = call(columns_kernel, [], number, flops=4 << 30)()
    *pieces, start_full = call(
        first_kernel, [VMEM] * 7, (pair,) * places + (both,), split, dots
    )(
        columns,
        widths[None],
        holders[None],
        amplitudes[0],
        other_core(amplitudes[0]),
        right_env,
        left_env,
    )
    old = along_line(pieces, slots)
    stay = call(stay_kernel, [VMEM] * 3, block, flops=dots // 3)(start_full, right_env, left_env)
    table, keep_early, cross = call(
        merge_early_kernel, [VMEM] * (1 + places), (table_shape, twos, twos)
    )(plan, *old)
    old_early = across(cross, slots)
    keep_late, cross = call(merge_late_kernel, [VMEM] * 2, (twos, twos))(plan, table)
    old_late = across(cross, slots)
    far = call(join_kernel, [VMEM] * 2, (single,) * 2)(keep_early, old_early)
    near = call(join_kernel, [VMEM] * 2, (single,) * 2)(keep_late, old_late)
    joined = (near[0], *far, near[1])
    first = call(sum_kernel, [VMEM] * (2 + places), block)(
        plan, stay, *along_line(joined, slots)
    )

    *pieces, deflated = call(
        second_kernel, [VMEM] * 5, (tagged,) * places + (both,), split, dots
    )(start_full, first, other_core(first), right_env, left_env)
    new = along_line(pieces, slots)
    stay_2 = call(stay_kernel, [VMEM] * 3, wide, flops=dots // 3)(deflated, right_env, left_env)
    keep, *cross, tag = call(
        mix_kernel, [VMEM] * (2 + places), (wides, early, late, label), new_table
    )(plan, table, *new)
    new_early, new_late = (across(piece, slots) for piece in cross)
    *far, factors = call(join_early_kernel, [VMEM] * 6, (single, single, factor_shape))(
        plan, tag, keep, new_early, keep_early, old_early
    )
    near = call(join_late_kernel, [VMEM] * 5, (single,) * 2)(
        factors, keep, new_late, keep_late, old_late
    )
    joined = (near[0], *far, near[1])
    second, first = call(final_kernel, [VMEM] * (5 + places), (block, block))(
        plan, factors, stay, stay_2, first, *along_line(joined, slots)
    )
    return first[None], second[None]


def solution(mesh):
    in_specs = (
        P(("runs", "sec"), None, "env"),
        P("runs"),
        P("runs"),
        P(("runs", "sec"), None, None, "env"),
        P("runs", None, None),
    )
    out_specs = (P(("runs", "sec"), None, "env"), P(("runs", "sec"), None, "env"))
    return jax.shard_map(
        on_device, mesh=mesh, in_specs=in_specs, out_specs=out_specs, check_vma=False
    )
```
